32 devices in a mesh: dp: 16 (over z, y, x), branch: 2 (over core).
Axes of the slice: x: 2, y: 2, z: 4, core: 2. Of those that a mesh axis runs over, the one named last changes fastest.
Arguments:
- tokens: bfloat16 [28672, 768], P(('dp', 'branch')), may hold values from -6 to 6
- lengths: int32 [64, 4], P('dp'), may hold values from 32 to 112, as said below
- cotangent: bfloat16 [28672, 768], P(('dp', 'branch')), may hold values from -6 to 6
- ln_gain: float32 [768], replicated, may hold values from 0.1 to 1.9
- w_qkv: bfloat16 [768, 2304], replicated, may hold values from -0.21875 to 0.21875
- b_qkv: float32 [2304], replicated, may hold values from -3 to 3
- q_gain: float32 [64], replicated, may hold values from 0.1 to 1.9
- k_gain: float32 [64], replicated, may hold values from 0.1 to 1.9
- w_o: bfloat16 [768, 768], replicated, may hold values from -1.75 to 1.75
- b_o: float32 [768], replicated, may hold values from -2 to 2
- w_in: bfloat16 [768, 3072], replicated, may hold values from -0.21875 to 0.21875
- b_in: float32 [3072], replicated, may hold values from -3 to 3
- w_out: bfloat16 [3072, 768], replicated, may hold values from -0.109375 to 0.109375
- b_out: float32 [768], replicated, may hold values from -2 to 2
Outputs:
- output: bfloat16 [28672, 768], P(('dp', 'branch'))
- grad_tokens: bfloat16 [28672, 768], P(('dp', 'branch'))
- grad_ln_gain: float32 [768], replicated
- grad_w_qkv: float32 [768, 2304], P('dp')
- grad_b_qkv: float32 [2304], replicated
- grad_q_gain: float32 [64], replicated
- grad_k_gain: float32 [64], replicated
- grad_w_o: float32 [768, 768], P('dp')
- grad_b_o: float32 [768], replicated
- grad_w_in: float32 [768, 3072], P('dp')
- grad_b_in: float32 [3072], replicated
- grad_w_out: float32 [3072, 768], P('dp')
- grad_b_out: float32 [768], replicated
The draws below stay inside these ranges and needn't reach their ends.
Inputs may be any that keep to these rules, and one draw needn't show every extreme that they name: `lengths`: each entry is the patch count of one image of a sequence; a sequence's images lie in order from its first position, and its remaining positions are padding.
All inputs are finite; a program needn't handle non-finite values.
Results may differ from the reference program's by a relative error of at most 0.012.
Values may be sent and summed in bfloat16 or wider, within the bound.
A program may use at most 320 MiB of HBM per device.

```python
import jax
import jax.numpy as jnp
from jax import lax

D = 768
HEAD = 64
FF = 3072
SEQ = 448
IMAGES = 4
SEQ_DEV = 4
SEQS = 64
TOKENS = 28672
N_DP = 16


def draw_lengths(key, part):
    key = jax.random.fold_in(key, 11)
    first_key, second_key = jax.random.split(key, 2)
    most_len = SEQ // IMAGES
    least_len = max(1, SEQ // 14)
    counts = jax.random.randint(first_key, (SEQS, IMAGES), least_len, most_len + 1).astype(jnp.int32)
    places = jnp.arange(SEQS * IMAGES, dtype=jnp.int32).reshape(SEQS, IMAGES)
    picks = jax.random.randint(second_key, (2,), 0, SEQS * IMAGES).astype(jnp.int32)
    counts = jnp.where(places == picks[0], most_len, counts)
    counts = jnp.where((places == picks[1]) & (places != picks[0]), least_len, counts)
    return counts.astype(jnp.int32)


def steps_of(key, dims, pieces, low, high):
    gain = 1.0
    for dim, blocks in pieces:
        steps = jax.random.uniform(jax.random.fold_in(jax.random.fold_in(key, 6), dim), (blocks,), jnp.float32, low / len(pieces), high / len(pieces))
        gain = gain * jnp.repeat(jnp.exp(steps), dims[dim] // blocks).reshape((-1,) + (1,) * (len(dims) - 1 - dim))
    return gain


def centred(key, shape, scale, limit, pieces=(), held_as=jnp.bfloat16):
    factor_of = steps_of(key, shape, pieces, -0.22, 0.18) if pieces else 1.0
    values = jax.random.normal(key, shape, jnp.float32) * scale * factor_of
    return jnp.minimum(jnp.maximum(values, -limit), limit).astype(held_as)


def setup_inputs(seed: int = 0) -> dict:
    keys = jax.random.split(jax.random.key(seed), 15)
    return {
        "tokens": centred(keys[0], (TOKENS, D), 1.0, 6.0, ((0, 32),)),
        "lengths": draw_lengths(jax.random.fold_in(keys[14], 71), 0),
        "cotangent": centred(keys[2], (TOKENS, D), 1.0, 6.0, ((0, 32),)),
        "ln_gain": jnp.clip(1.0 + 0.18 * jax.random.normal(keys[3], (D,), jnp.float32), 0.1, 1.9),
        "w_qkv": centred(keys[4], (D, 3 * D), D ** -0.5, 0.21875),
        "b_qkv": centred(keys[5], (3 * D,), 0.5, 3.0, (), jnp.float32),
        "q_gain": jnp.clip(1.0 + 0.18 * jax.random.normal(keys[6], (HEAD,), jnp.float32), 0.1, 1.9),
        "k_gain": jnp.clip(1.0 + 0.18 * jax.random.normal(keys[7], (HEAD,), jnp.float32), 0.1, 1.9),
        "w_o": centred(keys[8], (D, D), (D // 64) ** -0.5, 1.75),
        "b_o": centred(keys[9], (D,), 0.3, 2.0, (), jnp.float32),
        "w_in": centred(keys[10], (D, FF), D ** -0.5, 0.21875),
        "b_in": centred(keys[11], (FF,), 0.5, 3.0, (), jnp.float32),
        "w_out": centred(keys[12], (FF, D), FF ** -0.5, 0.109375),
        "b_out": centred(keys[13], (D,), 0.3, 2.0, (), jnp.float32),
    }


HIGH = lax.Precision.HIGHEST
EPS = 1e-06
NEG = -1e+30
SCALE = 0.125

@jax.custom_vjp
def low(v):
    return lax.optimization_barrier(v.astype(jnp.bfloat16)).astype(jnp.float32)

@jax.custom_vjp
def low_back(v):
    return v

def low_keep(v):
    return (low(v), None)

def low_pass(kept, grad):
    return (grad,)

def back_keep(v):
    return (v, None)

def back_low(kept, grad):
    return (low(grad),)
low.defvjp(low_keep, low_pass)
low_back.defvjp(back_keep, back_low)

def norm_rows(values, gain_vec):
    row_mean = lax.optimization_barrier(jnp.mean(values, axis=-1, keepdims=True))
    centered = values - row_mean
    spread = lax.optimization_barrier(jnp.mean(centered * centered, axis=-1, keepdims=True))
    return centered * lax.rsqrt(spread + EPS) * gain_vec

def image_ids(lengths):
    image_ends = jnp.cumsum(lengths, axis=1).astype(jnp.int32)
    places = jnp.arange(SEQ, dtype=jnp.int32)
    passed = lax.optimization_barrier(jnp.sum((places[None, :, None] >= image_ends[:, None, :]).astype(jnp.int32), axis=2)).astype(jnp.int32)
    return jnp.where(places[None, :] < image_ends[:, -1:], passed, -1).astype(jnp.int32)

def layer_group(group_rows, lengths, ln_gain, w_qkv, b_qkv, q_gain, k_gain, w_o, b_o, w_in, b_in, w_out, b_out):
    row_count = group_rows.shape[0]
    model_width = group_rows.shape[1]
    seq_count = row_count // SEQ
    head_count = model_width // HEAD
    image_of = image_ids(lengths)
    normed = low(norm_rows(group_rows, ln_gain))
    projected = low_back(jnp.dot(normed, w_qkv, precision=HIGH) + b_qkv)
    query_raw = projected[:, :model_width].reshape(row_count, head_count, HEAD)
    key_raw = projected[:, model_width:2 * model_width].reshape(row_count, head_count, HEAD)
    queries = low(norm_rows(query_raw, q_gain)).reshape(seq_count, SEQ, head_count, HEAD)
    key_heads = low(norm_rows(key_raw, k_gain)).reshape(seq_count, SEQ, head_count, HEAD)
    values = low(projected[:, 2 * model_width:]).reshape(seq_count, SEQ, head_count, HEAD)
    scores = low_back(jnp.einsum('sqhd,skhd->shqk', queries, key_heads, precision=HIGH) * SCALE)
    same_image = image_of[:, None, :, None] == image_of[:, None, None, :]
    scores = jnp.where(same_image, scores, NEG)
    largest = lax.optimization_barrier(jnp.max(scores, axis=-1, keepdims=True))
    exponent = jnp.exp(scores - largest)
    attn_probs = low(exponent / lax.optimization_barrier(jnp.sum(exponent, axis=-1, keepdims=True)))
    mixed = jnp.einsum('shqk,skhd->sqhd', attn_probs, values, precision=HIGH).reshape(row_count, model_width)
    mixed = low(low_back(mixed))
    attended = low(jnp.dot(mixed, w_o, precision=HIGH) + b_o)
    pre_act = low_back(jnp.dot(normed, w_in, precision=HIGH) + b_in)
    hidden = low(jax.nn.gelu(pre_act))
    fed_out = low(jnp.dot(hidden, w_out, precision=HIGH) + b_out)
    valid_rows = (image_of.reshape(row_count) >= 0).astype(jnp.float32)[:, None]
    return group_rows + valid_rows * (attended + fed_out)

def reference(tokens, lengths, cotangent, ln_gain, w_qkv, b_qkv, q_gain, k_gain, w_o, b_o, w_in, b_in, w_out, b_out):
    params = (ln_gain.astype(jnp.float32), w_qkv.astype(jnp.float32), b_qkv.astype(jnp.float32), q_gain.astype(jnp.float32), k_gain.astype(jnp.float32), w_o.astype(jnp.float32), b_o.astype(jnp.float32), w_in.astype(jnp.float32), b_in.astype(jnp.float32), w_out.astype(jnp.float32), b_out.astype(jnp.float32))
    inputs = tokens.astype(jnp.float32)
    groups = lengths.reshape(N_DP, SEQ_DEV, IMAGES)
    group_step = jax.checkpoint(layer_group)

    def forward(inputs, params):

        def one_group(scan_carry, scan_item):
            return (scan_carry, group_step(scan_item[0], scan_item[1], *params))
        start = jnp.zeros((), jnp.float32)
        _, group_outs = lax.scan(one_group, start, (inputs.reshape(N_DP, SEQ_DEV * SEQ, D), groups))
        return group_outs.reshape(TOKENS, D)
    output, pull_back = jax.vjp(forward, inputs, params)
    grad_inputs, weight_grads = pull_back(cotangent.astype(jnp.float32))
    g_ln, g_wqkv, g_bqkv, g_qgain, g_kgain, g_wo, g_bo, g_win, g_bin, g_wout, g_bout = weight_grads
    return (output.astype(jnp.bfloat16), grad_inputs.astype(jnp.bfloat16), g_ln, g_wqkv, g_bqkv, g_qgain, g_kgain, g_wo, g_bo, g_win, g_bin, g_wout, g_bout)
```

```python
import functools
import math

import jax
import jax.numpy as jnp
from jax import lax
from jax.experimental import pallas as pl
from jax.experimental.pallas import tpu as pltpu
from jax.sharding import PartitionSpec as P

HEAD = 64
SEQ = 448
IMAGES = 4
SLOT = SEQ // IMAGES
KEYS = 128
GROUP = 256
EPS = 1e-06
SCALE = 0.125
TILE = 224
F32 = jnp.float32
BF16 = jnp.bfloat16
GELU_A = math.sqrt(2.0 / math.pi)
GELU_B = 0.044715


def dot(left, right, left_dim=1, right_dim=0):
    return lax.dot_general(
        left, right, (((left_dim,), (right_dim,)), ((), ())), preferred_element_type=F32
    )


def slot_positions(lens):
    row = lax.broadcasted_iota(jnp.int32, (SEQ, 1), 0)
    held = jnp.full((SEQ, 1), -1, jnp.int32)
    start = jnp.int32(0)
    for image in range(IMAGES):
        place = row - SLOT * image
        held = jnp.where((place >= 0) & (place < lens[image]), place + start, held)
        start = start + lens[image]
    return held


def position_slots(lens):
    row = lax.broadcasted_iota(jnp.int32, (SEQ, 1), 0)
    held = jnp.full((SEQ, 1), -1, jnp.int32)
    start = jnp.int32(0)
    for image in range(IMAGES):
        place = row - start
        held = jnp.where((place >= 0) & (place < lens[image]), place + SLOT * image, held)
        start = start + lens[image]
    return held


def one_hot(index):
    lanes = lax.broadcasted_iota(jnp.int32, (SEQ, SEQ), 1)
    return jnp.where(lanes == index, 1.0, 0.0).astype(BF16)


def row_stats(values):
    centered = values - jnp.mean(values, axis=1, keepdims=True)
    spread = jnp.mean(centered * centered, axis=1, keepdims=True)
    inverse = lax.rsqrt(spread + EPS)
    return centered * inverse, inverse


def gelu_pair(pre, grad):
    square = pre * pre
    bent = jnp.tanh(pre * (GELU_A + (GELU_A * GELU_B) * square))
    half = 0.5 * pre
    up = 1.0 + bent
    hidden = half * up
    slope = half * (GELU_A + (3.0 * GELU_A * GELU_B) * square)
    return hidden, (up * (0.5 + (1.0 - bent) * slope)) * grad


def layer_kernel(
    lengths_ref, tokens_hbm, cot_hbm, ln_gain_ref, w_qkv_hbm, b_qkv_ref, q_gain_ref, k_gain_ref,
    w_o_hbm, b_o_ref, w_in_hbm, b_in_ref, w_out_hbm, b_out_ref,
    output_hbm, grad_tokens_hbm, pieces_hbm, small_ref,
    wqkv, wo, win, wout, tok, cot, packed, grow, normed, flipped, hid, gpre,
    fed, gnorm, qs, ks, vs, gm, nq, nk, rq, rk, dq, dk, mixed, stage,
    load_sem, piece_sem, done_sem,
):
    rows, width = tok.shape
    hidden_width = w_in_hbm.shape[1]
    chunks = hidden_width // width
    groups = width // GROUP
    seqs = rows // SEQ
    images = seqs * IMAGES
    tiles = rows // TILE
    base = lax.axis_index("branch") * seqs

    def load(source, target, slot):
        copy = pltpu.make_async_copy(source, target, load_sem.at[slot])
        copy.start()
        return copy

    token_copy = load(tokens_hbm, tok, 0)
    cot_copy = load(cot_hbm, cot, 1)
    in_copies, out_copies, qkv_copies = [], [], []
    for f in range(chunks):
        cols = pl.ds(f * width, width)
        in_copies.append(load(w_in_hbm.at[:, cols], win.at[f], 2 + 2 * f))
        out_copies.append(load(w_out_hbm.at[cols, :], wout.at[f], 3 + 2 * f))
    for hg in range(groups):
        qkv_copies.append([
            load(
                w_qkv_hbm.at[:, pl.ds(t * width + hg * GROUP, GROUP)],
                wqkv.at[hg, :, pl.ds(t * GROUP, GROUP)],
                2 + 2 * chunks + 3 * hg + t,
            )
            for t in range(3)
        ])
    o_copy = load(w_o_hbm, wo, 2 + 2 * chunks + 3 * groups)

    small_ref[...] = jnp.zeros_like(small_ref)
    sent = []

    def emit(value):
        index = len(sent)
        slot = index % 2
        if index >= 2:
            sent[index - 2].wait()
        stage[slot] = value.astype(BF16)
        copy = pltpu.make_async_copy(stage.at[slot], pieces_hbm.at[index], piece_sem.at[slot])
        copy.start()
        sent.append(copy)

    ones_row = jnp.where(lax.broadcasted_iota(jnp.int32, (16, rows), 0) == 0, 1.0, 0.0)
    flipped[pl.ds(width, 16), :] = ones_row.astype(BF16)

    lens = [[lengths_ref[base + s, j] for j in range(IMAGES)] for s in range(seqs)]
    token_copy.wait()
    cot_copy.wait()
    grad_sum = jnp.zeros((1, width), F32)
    for s in range(seqs):
        span = pl.ds(s * SEQ, SEQ)
        pick = one_hot(slot_positions(lens[s]))
        rows_here = dot(pick, tok[span, :])
        packed[span, :] = rows_here.astype(BF16)
        unit, _ = row_stats(rows_here)
        normed[span, :] = (unit * ln_gain_ref[...]).astype(BF16)
        grads_here = dot(pick, cot[span, :])
        grow[span, :] = grads_here.astype(BF16)
        grad_sum = grad_sum + jnp.sum(grads_here, axis=0, keepdims=True)
    small_ref[pl.ds(2, 1), pl.ds(width, width)] = grad_sum
    eye = jnp.where(
        lax.broadcasted_iota(jnp.int32, (GROUP, GROUP), 0)
        == lax.broadcasted_iota(jnp.int32, (GROUP, GROUP), 1),
        1.0,
        0.0,
    ).astype(BF16)
    for part in range(groups):
        lanes = pl.ds(part * GROUP, GROUP)
        flipped[lanes, :] = dot(eye, normed[:, lanes], 1, 1).astype(BF16)

    for f in range(chunks):
        in_copies[f].wait()
        out_copies[f].wait()
        bias = b_in_ref[:, pl.ds(f * width, width)]
        for t in range(tiles):
            span = pl.ds(t * TILE, TILE)
            pre = dot(normed[span, :], win[f]) + bias
            back = dot(grow[span, :], wout[f], 1, 1)
            hidden, grad_pre = gelu_pair(pre, back)
            hidden, grad_pre = hidden.astype(BF16), grad_pre.astype(BF16)
            hid[span, :] = hidden
            gpre[span, :] = grad_pre
            up = dot(hidden, wout[f])
            down = dot(grad_pre, win[f], 1, 1)
            if f == 0:
                fed[span, :] = up
                gnorm[span, :] = down
            else:
                fed[span, :] += up
                gnorm[span, :] += down
        emit(dot(hid[...], grow[...], 0, 0))
        weights = dot(flipped[...], gpre[...])
        emit(weights[:width])
        small_ref[pl.ds(0, 1), pl.ds(f * width, width)] = weights[width : width + 1]

    for hg in range(groups):
        for copy in qkv_copies[hg]:
            copy.wait()
        if hg == 0:
            o_copy.wait()
        same_head = (
            lax.broadcasted_iota(jnp.int32, (GROUP, GROUP), 0) // HEAD
            == lax.broadcasted_iota(jnp.int32, (GROUP, GROUP), 1) // HEAD
        )
        average = jnp.where(same_head, 1.0 / HEAD, 0.0).astype(BF16)

        def head_mean(values, split):
            high = values.astype(BF16)
            mean = dot(high, average)
            if split:
                mean = mean + dot((values - high.astype(F32)).astype(BF16), average)
            return mean

        def head_norm(raw):
            centered = raw - head_mean(raw, True)
            inverse = lax.rsqrt(head_mean(centered * centered, False) + EPS)
            return centered * inverse, inverse

        q_gain = jnp.concatenate([q_gain_ref[...]] * (GROUP // HEAD), axis=1)
        k_gain = jnp.concatenate([k_gain_ref[...]] * (GROUP // HEAD), axis=1)
        bias_q = b_qkv_ref[:, pl.ds(hg * GROUP, GROUP)]
        bias_k = b_qkv_ref[:, pl.ds(width + hg * GROUP, GROUP)]
        bias_v = b_qkv_ref[:, pl.ds(2 * width + hg * GROUP, GROUP)]
        for t in range(tiles):
            span = pl.ds(t * TILE, TILE)
            raw = dot(normed[span, :], wqkv[hg])
            unit, inverse = head_norm(raw[:, :GROUP] + bias_q)
            nq[span, :] = unit
            rq[span, :] = inverse
            qs[span, :] = (unit * q_gain).astype(BF16) * SCALE
            unit, inverse = head_norm(raw[:, GROUP : 2 * GROUP] + bias_k)
            nk[span, :] = unit
            rk[span, :] = inverse
            ks[span, :] = (unit * k_gain).astype(BF16)
            vs[span, :] = (raw[:, 2 * GROUP :] + bias_v).astype(BF16)
            gm[span, :] = dot(grow[span, :], wo[pl.ds(hg * GROUP, GROUP), :], 1, 1).astype(BF16)
        if hg == 0:
            ks[pl.ds(rows, KEYS - SLOT), :] = jnp.zeros((KEYS - SLOT, GROUP), BF16)
            vs[pl.ds(rows, KEYS - SLOT), :] = jnp.zeros((KEYS - SLOT, GROUP), BF16)

        lane = lax.broadcasted_iota(jnp.int32, (1, KEYS), 1)
        first_head = jnp.where(lane < HEAD, 1.0, 0.0).astype(BF16)
        second_head = jnp.where(lane < HEAD, 0.0, 1.0).astype(BF16)

        def two_heads(block):
            return jnp.concatenate([block * first_head, block * second_head], axis=0)

        def side_by_side(block):
            return jnp.concatenate([block[:SLOT], block[SLOT:]], axis=1)

        def one_image(image, carry):
            start = pl.multiple_of(image * SLOT, 16)
            span = pl.ds(start, SLOT)
            window = pl.ds(start, KEYS)
            count = lengths_ref[base + image // IMAGES, lax.rem(image, IMAGES)]
            seen = lane < count
            for pair in range(GROUP // KEYS):
                lanes = pl.ds(pair * KEYS, KEYS)
                query = two_heads(qs[span, lanes])
                grad = two_heads(gm[span, lanes])
                key, value = ks[window, lanes], vs[window, lanes]
                weight = jnp.where(seen, jnp.exp(dot(query, key, 1, 1)), 0.0)
                probs = weight / jnp.sum(weight, axis=1, keepdims=True)
                grad_probs = dot(grad, value, 1, 1)
                inner = jnp.sum(probs * grad_probs, axis=1, keepdims=True)
                grad_scores = (probs * (grad_probs - inner)).astype(BF16)
                probs_low = probs.astype(BF16)
                mixed[span, pl.ds(hg * GROUP + pair * KEYS, KEYS)] = dot(
                    side_by_side(probs_low), two_heads(value)
                ).astype(BF16)
                dq[span, lanes] = dot(side_by_side(grad_scores), two_heads(key)) * SCALE
                dk[span, lanes] = dot(grad_scores, query, 0, 0)[:SLOT]
                gpre[span, pl.ds(2 * GROUP + pair * KEYS, KEYS)] = dot(probs_low, grad, 0, 0)[
                    :SLOT
                ].astype(BF16)
            return carry

        lax.fori_loop(0, images, one_image, 0)

        gain_sums = [jnp.zeros((1, GROUP), F32), jnp.zeros((1, GROUP), F32)]
        for t in range(tiles):
            span = pl.ds(t * TILE, TILE)
            for side, (grad_ref, unit_ref, inverse_ref, gain) in enumerate(
                ((dq, nq, rq, q_gain), (dk, nk, rk, k_gain))
            ):
                grad, unit = grad_ref[span, :], unit_ref[span, :]
                gain_sums[side] = gain_sums[side] + jnp.sum(grad * unit, axis=0, keepdims=True)
                grad = grad * gain
                back = grad - head_mean(grad, True) - unit * head_mean(grad * unit, False)
                gpre[span, pl.ds(side * GROUP, GROUP)] = (back * inverse_ref[span, :]).astype(BF16)
            gnorm[span, :] += dot(gpre[span, :], wqkv[hg], 1, 1)
        for side in range(2):
            small_ref[pl.ds(3, 1), pl.ds((2 * hg + side) * GROUP, GROUP)] = gain_sums[side]
        weights = dot(flipped[...], gpre[...])
        emit(weights[:width])
        small_ref[pl.ds(1, 1), pl.ds(hg * width, width)] = weights[width : width + 1]

    emit(dot(mixed[...], grow[...], 0, 0))

    gain_grad = jnp.zeros((1, width), F32)
    for s in range(seqs):
        span = pl.ds(s * SEQ, SEQ)
        place = position_slots(lens[s])
        put = one_hot(place)
        padding = jnp.where(place < 0, 1.0, 0.0)
        attended = (dot(mixed[span, :], wo[...]) + b_o_ref[...]).astype(BF16).astype(F32)
        fed_here = (fed[span, :] + b_out_ref[...]).astype(BF16).astype(F32)
        rows_here = packed[span, :].astype(F32)
        result = (rows_here + (attended + fed_here)).astype(BF16)
        tok[span, :] = (dot(put, result) + padding * tok[span, :].astype(F32)).astype(BF16)
        unit, inverse = row_stats(rows_here)
        grad = gnorm[span, :]
        gain_grad = gain_grad + jnp.sum(grad * unit, axis=0, keepdims=True)
        grad = grad * ln_gain_ref[...]
        back = grad - jnp.mean(grad, axis=1, keepdims=True)
        back = (back - unit * jnp.mean(grad * unit, axis=1, keepdims=True)) * inverse
        result = (grow[span, :].astype(F32) + back).astype(BF16)
        cot[span, :] = (dot(put, result) + padding * cot[span, :].astype(F32)).astype(BF16)
    small_ref[pl.ds(2, 1), pl.ds(0, width)] = gain_grad
    finals = [
        pltpu.make_async_copy(tok, output_hbm, done_sem.at[0]),
        pltpu.make_async_copy(cot, grad_tokens_hbm, done_sem.at[1]),
    ]
    for copy in finals:
        copy.start()
    for copy in sent[-2:] + finals:
        copy.wait()


def local(tokens, lengths, cotangent, ln_gain, w_qkv, b_qkv, q_gain, k_gain, w_o, b_o, w_in, b_in, w_out, b_out):
    rows, width = tokens.shape
    hidden_width = w_in.shape[1]
    chunks = hidden_width // width
    groups = width // GROUP
    piece_count = 2 * chunks + groups + 1
    anywhere = pl.BlockSpec(memory_space=pl.ANY)
    vmem = pl.BlockSpec(memory_space=pltpu.VMEM)
    wide = lambda *shape: pltpu.VMEM(shape, F32)
    slim = lambda *shape: pltpu.VMEM(shape, BF16)
    extra = KEYS - SLOT
    output, grad_tokens, pieces, small = pl.pallas_call(
        layer_kernel,
        out_shape=(
            jax.ShapeDtypeStruct(tokens.shape, BF16),
            jax.ShapeDtypeStruct(tokens.shape, BF16),
            jax.ShapeDtypeStruct((piece_count, width, width), BF16),
            jax.ShapeDtypeStruct((8, hidden_width), F32),
        ),
        in_specs=[
            pl.BlockSpec(memory_space=pltpu.SMEM), anywhere, anywhere, vmem, anywhere, vmem, vmem, vmem,
            anywhere, vmem, anywhere, vmem, anywhere, vmem,
        ],
        out_specs=(anywhere, anywhere, anywhere, vmem),
        scratch_shapes=[
            slim(groups, width, width), slim(width, width), slim(chunks, width, width),
            slim(chunks, width, width), slim(rows, width), slim(rows, width), slim(rows, width),
            slim(rows, width), slim(rows, width), slim(width + 16, rows), slim(rows, width),
            slim(rows, width), wide(rows, width), wide(rows, width), slim(rows, GROUP),
            slim(rows + extra, GROUP), slim(rows + extra, GROUP), slim(rows, GROUP),
            wide(rows, GROUP), wide(rows, GROUP), wide(rows, GROUP), wide(rows, GROUP),
            wide(rows, GROUP), wide(rows, GROUP), slim(rows, width), slim(2, width, width),
            pltpu.SemaphoreType.DMA((3 + 2 * chunks + 3 * groups,)),
            pltpu.SemaphoreType.DMA((2,)), pltpu.SemaphoreType.DMA((2,)),
        ],
        compiler_params=pltpu.CompilerParams(vmem_limit_bytes=60 << 20),
    )(
        lengths, tokens, cotangent, ln_gain[None], w_qkv, b_qkv[None], q_gain[None], k_gain[None],
        w_o, b_o[None], w_in, b_in[None], w_out, b_out[None],
    )

    def scatter(block, dim):
        part = lax.psum_scatter(block, "dp", scatter_dimension=dim, tiled=True)
        return lax.psum(part, "branch").astype(F32)

    grad_out = scatter(pieces[0 : 2 * chunks : 2].reshape(hidden_width, width), 0)
    others = scatter(jnp.concatenate([pieces[1 : 2 * chunks : 2], pieces[2 * chunks :]]), 1)
    grad_in = jnp.concatenate([others[f] for f in range(chunks)], axis=1)
    qkv = others[chunks : chunks + groups].reshape(groups, -1, 3, GROUP)
    grad_qkv = qkv.transpose(1, 2, 0, 3).reshape(-1, 3 * width)
    small = lax.psum(small, ("dp", "branch"))
    bias_qkv = small[1, : 3 * width].reshape(groups, 3, GROUP).transpose(1, 0, 2).reshape(-1)
    gains = small[3, : 2 * width].reshape(groups, 2, GROUP // HEAD, HEAD).sum(axis=(0, 2))
    return (
        output, grad_tokens, small[2, :width], grad_qkv, bias_qkv, gains[0], gains[1],
        others[chunks + groups], small[2, width : 2 * width], grad_in, small[0], grad_out,
        small[2, width : 2 * width],
    )


def solution(mesh):
    rows, split, whole = P(("dp", "branch"), None), P("dp", None), P()
    return jax.shard_map(
        local,
        mesh=mesh,
        in_specs=(rows, split, rows) + (whole,) * 11,
        out_specs=(
            rows, rows, whole, split, whole, whole, whole, split, whole, split, whole, split, whole,
        ),
        check_vma=False,
    )
```

```python
import functools
import math

import jax
import jax.numpy as jnp
from jax import lax
from jax.experimental import pallas as pl
from jax.experimental.pallas import tpu as pltpu
from jax.sharding import PartitionSpec as P

HEAD = 64
SEQ = 448
IMAGES = 4
SLOT = SEQ // IMAGES
KEYS = 128
GROUP = 256
EPS = 1e-06
SCALE = 0.125
TILE = 224
F32 = jnp.float32
BF16 = jnp.bfloat16
GELU_A = math.sqrt(2.0 / math.pi)
GELU_B = 0.044715


def dot(left, right, left_dim=1, right_dim=0):
    return lax.dot_general(
        left, right, (((left_dim,), (right_dim,)), ((), ())), preferred_element_type=F32
    )


def slot_positions(lens):
    row = lax.broadcasted_iota(jnp.int32, (SEQ, 1), 0)
    held = jnp.full((SEQ, 1), -1, jnp.int32)
    start = jnp.int32(0)
    for image in range(IMAGES):
        place = row - SLOT * image
        held = jnp.where((place >= 0) & (place < lens[image]), place + start, held)
        start = start + lens[image]
    return held


def position_slots(lens):
    row = lax.broadcasted_iota(jnp.int32, (SEQ, 1), 0)
    held = jnp.full((SEQ, 1), -1, jnp.int32)
    start = jnp.int32(0)
    for image in range(IMAGES):
        place = row - start
        held = jnp.where((place >= 0) & (place < lens[image]), place + SLOT * image, held)
        start = start + lens[image]
    return held


def one_hot(index):
    lanes = lax.broadcasted_iota(jnp.int32, (SEQ, SEQ), 1)
    return jnp.where(lanes == index, 1.0, 0.0).astype(BF16)


def row_stats(values):
    centered = values - jnp.mean(values, axis=1, keepdims=True)
    spread = jnp.mean(centered * centered, axis=1, keepdims=True)
    inverse = lax.rsqrt(spread + EPS)
    return centered * inverse, inverse


def gelu_pair(pre, grad):
    square = pre * pre
    bent = jnp.tanh(pre * (GELU_A + (GELU_A * GELU_B) * square))
    half = 0.5 * pre
    up = 1.0 + bent
    hidden = half * up
    slope = half * (GELU_A + (3.0 * GELU_A * GELU_B) * square)
    return hidden, (up * (0.5 + (1.0 - bent) * slope)) * grad


MESH = pl.DeviceIdType.MESH
BLOCK = 48
CORE, FIRST, SECOND, THIRD, FOURTH, TWIN = range(6)
AGES = (1, 3, 2, 1, 1, 1)


class Piece:
    def __init__(self, index, shard, order):
        self.index, self.shard, self.order = index, shard, order
        self.stage, self.copy, self.point = CORE, None, 0


class Exchange:
    def __init__(self, refs, chunks):
        (self.both, self.inbox, self.acc, self.in1, self.in2, self.in3, self.in4, self.osum,
         self.oin3, self.oin4, self.fin, self.small, self.small_in, self.send_sem, self.recv_sem) = refs
        self.chunks = chunks
        self.dp, self.core = lax.axis_index("dp"), lax.axis_index("branch")
        self.bits = {
            "x": lax.rem(self.dp, 2),
            "y": lax.rem(self.dp // 2, 2),
            "z0": lax.rem(self.dp // 4, 2),
            "z1": lax.rem(self.dp // 8, 2),
        }
        self.far = {
            axis: (self.dp + step - 2 * step * self.bits[axis], self.core)
            for axis, step in (("x", 1), ("y", 2), ("z0", 4), ("z1", 8))
        }
        self.far["core"] = (self.dp, 1 - self.core)
        self.pieces, self.point, self.flights = [], 0, 0
        self.small_stage, self.small_copy = 0, None
        self.merged = 0

    def greet(self):
        barrier = pltpu.get_barrier_semaphore()
        for device in self.far.values():
            pl.semaphore_signal(barrier, inc=1, device_id=device, device_id_type=MESH)
        pl.semaphore_wait(barrier, len(self.far))

    def send(self, source, target, axis):
        copy = pltpu.make_async_remote_copy(
            src_ref=source, dst_ref=target, send_sem=self.send_sem.at[self.flights],
            recv_sem=self.recv_sem.at[self.flights], device_id=self.far[axis], device_id_type=MESH,
        )
        self.flights += 1
        copy.start()
        return copy

    def start(self, value, shard, order, by_row_block):
        for piece in self.pieces:
            if piece.stage == CORE:
                self.advance(piece)
        piece = Piece(len(self.pieces), shard, order)
        slot = piece.index % 2
        half = value.shape[1] // 2
        for block in range(16):
            place = block
            if by_row_block:
                x, y, z0, z1 = block % 2, block // 2 % 2, block // 4 % 2, block // 8
                first, second = (x, y) if order == "xy" else (y, x)
                place = 8 * first + 4 * second + 2 * z0 + z1
            for side in range(2):
                self.both[slot, side, place] = value[
                    BLOCK * block : BLOCK * (block + 1), half * side : half * (side + 1)
                ].astype(BF16)
        piece.copy = self.send(self.both.at[slot, 1 - self.core], self.inbox.at[slot], "core")
        piece.point = self.point
        self.pieces.append(piece)

    def halve(self, piece, held, held_at, arrived, count, axis, target):
        near = self.bits[axis] * count
        away = (1 - self.bits[axis]) * count
        span = pl.ds(away, count)
        arrived[span] = arrived[span] + held[pl.ds(held_at + away, count)]
        piece.copy = self.send(arrived.at[span], target, axis)
        span = pl.ds(near, count)
        arrived[span] = arrived[span] + held[pl.ds(held_at + near, count)]

    def advance(self, piece):
        piece.copy.wait()
        piece.point = self.point
        k, shard = piece.index, piece.shard
        one, two = piece.order
        acc = self.acc.at[k % 4]
        if piece.stage == CORE:
            for other in self.pieces:
                assert other.index != k - 4 or other.stage > FIRST
            own, arrived = self.both.at[k % 2, self.core], self.inbox.at[k % 2]
            away = pl.ds((1 - self.bits[one]) * 8, 8)
            acc[away] = own[away] + arrived[away]
            piece.copy = self.send(acc.at[away], self.in1.at[k], one)
            near = pl.ds(self.bits[one] * 8, 8)
            acc[near] = own[near] + arrived[near]
        elif piece.stage == FIRST:
            self.halve(piece, acc, self.bits[one] * 8, self.in1.at[k], 4, two, self.in2.at[k])
        elif piece.stage == SECOND:
            held, held_at = self.in1.at[k], self.bits[two] * 4
            if isinstance(shard, int):
                self.halve(piece, held, held_at, self.in2.at[k], 2, "z0", self.in3.at[shard])
            else:
                plane = shard[0]
                place = plane % 2 * 2 + plane // 2
                self.osum[place] = self.in2[k] + held[pl.ds(held_at, 4)]
                self.merged += 1
                if self.merged < self.chunks:
                    piece.stage = TWIN
                    piece.copy = None
                else:
                    far = pl.ds((1 - self.bits["z0"]) * 2, 2)
                    piece.copy = self.send(self.osum.at[far], self.oin3, "z0")
        elif piece.stage == THIRD:
            if isinstance(shard, int):
                self.halve(
                    piece, self.in2.at[k], self.bits["z0"] * 2, self.in3.at[shard], 1, "z1",
                    self.in4.at[shard],
                )
            else:
                self.halve(
                    piece, self.osum, self.bits["z0"] * 2, self.oin3, 1, "z1", self.oin4
                )
        elif piece.stage == FOURTH:
            if isinstance(shard, int):
                final = self.fin.at[self.core, pl.ds(shard, 1)]
                final[...] = self.in4[shard] + self.in3[shard, pl.ds(self.bits["z1"], 1)]
            else:
                final = self.fin.at[self.core, pl.ds(self.fin.shape[1] - 4, 4)]
                final[...] = self.oin4[0] + self.oin3[self.bits["z1"]]
            piece.copy = self.send(final, final, "core")
        else:
            piece.copy = None
        piece.stage += 1

    def start_small(self):
        self.small_copy = self.send(self.small, self.small_in.at[0], "core")

    def advance_small(self):
        if self.small_copy is None:
            return
        self.small_copy.wait()
        self.small[...] = self.small[...] + self.small_in[self.small_stage]
        self.small_stage += 1
        self.small_copy = None
        if self.small_stage < 5:
            axis = ("core", "x", "y", "z0", "z1")[self.small_stage]
            self.small_copy = self.send(self.small, self.small_in.at[self.small_stage], axis)

    def progress(self):
        self.point += 1
        for piece in self.pieces:
            if piece.stage <= TWIN and self.point - piece.point >= AGES[piece.stage]:
                self.advance(piece)

    def drain(self):
        while self.small_copy is not None or any(piece.stage <= TWIN for piece in self.pieces):
            self.point += 1
            for piece in self.pieces:
                if piece.stage <= TWIN:
                    self.advance(piece)
            self.advance_small()


def layer_kernel(
    wired,
    lengths_ref, tokens_hbm, cot_hbm, ln_gain_ref, w_qkv_hbm, b_qkv_ref, q_gain_ref, k_gain_ref,
    w_o_hbm, b_o_ref, w_in_hbm, b_in_ref, w_out_hbm, b_out_ref,
    output_hbm, grad_tokens_hbm, pieces_hbm, small_hbm,
    wqkv, wo, win, wout, tok, cot, packed, grow, normed, flipped, hid, gpre,
    fed, gnorm, qs, ks, vs, gm, nq, nk, rq, rk, dq, dk, mixed, small_ref,
    load_sem, done_sem, *refs,
):
    rows, width = tok.shape
    hidden_width = w_in_hbm.shape[1]
    chunks = hidden_width // width
    groups = width // GROUP
    seqs = rows // SEQ
    images = seqs * IMAGES
    tiles = rows // TILE
    base = lax.axis_index("branch") * seqs

    def load(source, target, slot):
        copy = pltpu.make_async_copy(source, target, load_sem.at[slot])
        copy.start()
        return copy

    token_copy = load(tokens_hbm, tok, 0)
    cot_copy = load(cot_hbm, cot, 1)
    in_copies, out_copies, qkv_copies = [], [], []
    for f in range(chunks):
        cols = pl.ds(f * width, width)
        in_copies.append(load(w_in_hbm.at[:, cols], win.at[f], 2 + 2 * f))
        out_copies.append(load(w_out_hbm.at[cols, :], wout.at[f], 3 + 2 * f))
    for hg in range(groups):
        qkv_copies.append([
            load(
                w_qkv_hbm.at[:, pl.ds(t * width + hg * GROUP, GROUP)],
                wqkv.at[hg, :, pl.ds(t * GROUP, GROUP)],
                2 + 2 * chunks + 3 * hg + t,
            )
            for t in range(3)
        ])
    o_copy = load(w_o_hbm, wo, 2 + 2 * chunks + 3 * groups)

    small_ref[...] = jnp.zeros_like(small_ref)
    sent = []
    net = None
    if wired:
        net = Exchange(refs[:11] + (small_ref,) + refs[11:], chunks)
        net.greet()
    else:
        stage, piece_sem = refs

    def emit(value, shard, order="xy", by_row_block=True):
        if wired:
            net.start(value, shard, order, by_row_block)
            return
        index = len(sent)
        slot = index % 2
        if index >= 2:
            sent[index - 2].wait()
        stage[slot] = value.astype(BF16)
        target = pieces_hbm.at[shard if isinstance(shard, int) else chunks + groups + 1 + shard[0]]
        copy = pltpu.make_async_copy(stage.at[slot], target, piece_sem.at[slot])
        copy.start()
        sent.append(copy)

    def point():
        if wired:
            net.progress()

    ones_row = jnp.where(lax.broadcasted_iota(jnp.int32, (16, rows), 0) == 0, 1.0, 0.0)
    flipped[pl.ds(width, 16), :] = ones_row.astype(BF16)

    lens = [[lengths_ref[base + s, j] for j in range(IMAGES)] for s in range(seqs)]
    token_copy.wait()
    cot_copy.wait()
    grad_sum = jnp.zeros((1, width), F32)
    for s in range(seqs):
        span = pl.ds(s * SEQ, SEQ)
        pick = one_hot(slot_positions(lens[s]))
        rows_here = dot(pick, tok[span, :])
        packed[span, :] = rows_here.astype(BF16)
        unit, _ = row_stats(rows_here)
        normed[span, :] = (unit * ln_gain_ref[...].reshape(1, width)).astype(BF16)
        grads_here = dot(pick, cot[span, :])
        grow[span, :] = grads_here.astype(BF16)
        grad_sum = grad_sum + jnp.sum(grads_here, axis=0, keepdims=True)
    small_ref[pl.ds(7, 1), pl.ds(0, width)] = grad_sum
    eye = jnp.where(
        lax.broadcasted_iota(jnp.int32, (GROUP, GROUP), 0)
        == lax.broadcasted_iota(jnp.int32, (GROUP, GROUP), 1),
        1.0,
        0.0,
    ).astype(BF16)
    for part in range(groups):
        lanes = pl.ds(part * GROUP, GROUP)
        flipped[lanes, :] = dot(eye, normed[:, lanes], 1, 1).astype(BF16)

    def emit_w_out(f):
        emit(dot(hid[f % 2], grow[...], 0, 0), (f,), "yx", False)

    def emit_w_in(f):
        weights = dot(flipped[...], gpre[f % 2])
        emit(weights[:width], f, "xy")
        small_ref[pl.ds(f, 1), pl.ds(0, width)] = weights[width : width + 1]

    for f in range(chunks):
        in_copies[f].wait()
        out_copies[f].wait()
        bias = b_in_ref[...].reshape(1, hidden_width)[:, f * width : (f + 1) * width]
        for t in range(tiles):
            span = pl.ds(t * TILE, TILE)
            pre = dot(normed[span, :], win[f]) + bias
            back = dot(grow[span, :], wout[f], 1, 1)
            hidden, grad_pre = gelu_pair(pre, back)
            hidden, grad_pre = hidden.astype(BF16), grad_pre.astype(BF16)
            hid[f % 2, span, :] = hidden
            gpre[f % 2, span, :] = grad_pre
            up = dot(hidden, wout[f])
            down = dot(grad_pre, win[f], 1, 1)
            if f == 0:
                fed[span, :] = up
                gnorm[span, :] = down
            else:
                fed[span, :] += up
                gnorm[span, :] += down
            if f > 0 and t == 0:
                emit_w_out(f - 1)
            if f > 0 and t == 2:
                emit_w_in(f - 1)
            point()

    for hg in range(groups):
        for copy in qkv_copies[hg]:
            copy.wait()
        if hg == 0:
            o_copy.wait()
        same_head = (
            lax.broadcasted_iota(jnp.int32, (GROUP, GROUP), 0) // HEAD
            == lax.broadcasted_iota(jnp.int32, (GROUP, GROUP), 1) // HEAD
        )
        average = jnp.where(same_head, 1.0 / HEAD, 0.0).astype(BF16)

        def head_mean(values, split):
            high = values.astype(BF16)
            mean = dot(high, average)
            if split:
                mean = mean + dot((values - high.astype(F32)).astype(BF16), average)
            return mean

        def head_norm(raw):
            centered = raw - head_mean(raw, True)
            inverse = lax.rsqrt(head_mean(centered * centered, False) + EPS)
            return centered * inverse, inverse

        q_gain = jnp.concatenate([q_gain_ref[...].reshape(1, HEAD)] * (GROUP // HEAD), axis=1)
        k_gain = jnp.concatenate([k_gain_ref[...].reshape(1, HEAD)] * (GROUP // HEAD), axis=1)
        b_qkv = b_qkv_ref[...].reshape(1, 3 * width)
        bias_q, bias_k, bias_v = (
            b_qkv[:, t * width + hg * GROUP : t * width + (hg + 1) * GROUP] for t in range(3)
        )
        gproj = gpre.at[hg % 2]
        for t in range(tiles):
            span = pl.ds(t * TILE, TILE)
            raw = dot(normed[span, :], wqkv[hg])
            unit, inverse = head_norm(raw[:, :GROUP] + bias_q)
            nq[span, :] = unit
            rq[span, :] = inverse
            qs[span, :] = (unit * q_gain).astype(BF16) * SCALE
            unit, inverse = head_norm(raw[:, GROUP : 2 * GROUP] + bias_k)
            nk[span, :] = unit
            rk[span, :] = inverse
            ks[span, :] = (unit * k_gain).astype(BF16)
            vs[span, :] = (raw[:, 2 * GROUP :] + bias_v).astype(BF16)
            gm[span, :] = dot(grow[span, :], wo[pl.ds(hg * GROUP, GROUP), :], 1, 1).astype(BF16)
            if t % 2 == 1:
                point()
        if hg == 0:
            ks[pl.ds(rows, KEYS - SLOT), :] = jnp.zeros((KEYS - SLOT, GROUP), BF16)
            vs[pl.ds(rows, KEYS - SLOT), :] = jnp.zeros((KEYS - SLOT, GROUP), BF16)

        lane = lax.broadcasted_iota(jnp.int32, (1, KEYS), 1)
        first_head = jnp.where(lane < HEAD, 1.0, 0.0).astype(BF16)
        second_head = jnp.where(lane < HEAD, 0.0, 1.0).astype(BF16)

        def two_heads(block):
            return jnp.concatenate([block * first_head, block * second_head], axis=0)

        def side_by_side(block):
            return jnp.concatenate([block[:SLOT], block[SLOT:]], axis=1)

        def one_image(image, carry):
            start = pl.multiple_of(image * SLOT, 16)
            span = pl.ds(start, SLOT)
            window = pl.ds(start, KEYS)
            count = lengths_ref[base + image // IMAGES, lax.rem(image, IMAGES)]
            seen = lane < count
            for pair in range(GROUP // KEYS):
                lanes = pl.ds(pair * KEYS, KEYS)
                query = two_heads(qs[span, lanes])
                grad = two_heads(gm[span, lanes])
                key, value = ks[window, lanes], vs[window, lanes]
                weight = jnp.where(seen, jnp.exp(dot(query, key, 1, 1)), 0.0)
                probs = weight / jnp.sum(weight, axis=1, keepdims=True)
                grad_probs = dot(grad, value, 1, 1)
                inner = jnp.sum(probs * grad_probs, axis=1, keepdims=True)
                grad_scores = (probs * (grad_probs - inner)).astype(BF16)
                probs_low = probs.astype(BF16)
                mixed[span, pl.ds(hg * GROUP + pair * KEYS, KEYS)] = dot(
                    side_by_side(probs_low), two_heads(value)
                ).astype(BF16)
                dq[span, lanes] = dot(side_by_side(grad_scores), two_heads(key)) * SCALE
                dk[span, lanes] = dot(grad_scores, query, 0, 0)[:SLOT]
                gproj[span, pl.ds(2 * GROUP + pair * KEYS, KEYS)] = dot(probs_low, grad, 0, 0)[
                    :SLOT
                ].astype(BF16)
            return carry

        if hg == 0:
            emit_w_out(chunks - 1)
        lax.fori_loop(0, images // 2, one_image, 0)
        point()
        if hg == 0:
            emit_w_in(chunks - 1)
        lax.fori_loop(images // 2, images, one_image, 0)
        point()
        if hg == groups - 1:
            emit(dot(mixed[...], grow[...], 0, 0), chunks + groups, "yx")

        gain_sums = [jnp.zeros((1, GROUP), F32), jnp.zeros((1, GROUP), F32)]
        for t in range(tiles):
            span = pl.ds(t * TILE, TILE)
            for side, (grad_ref, unit_ref, inverse_ref, gain) in enumerate(
                ((dq, nq, rq, q_gain), (dk, nk, rk, k_gain))
            ):
                grad, unit = grad_ref[span, :], unit_ref[span, :]
                gain_sums[side] = gain_sums[side] + jnp.sum(grad * unit, axis=0, keepdims=True)
                grad = grad * gain
                back = grad - head_mean(grad, True) - unit * head_mean(grad * unit, False)
                gproj[span, pl.ds(side * GROUP, GROUP)] = (back * inverse_ref[span, :]).astype(BF16)
            if t == 1:
                point()
        for side in range(2):
            small_ref[pl.ds(3 + side, 1), pl.ds(width, GROUP)] += gain_sums[side]
        weights = dot(flipped[...], gproj[...])
        emit(weights[:width], chunks + hg, "xy" if hg % 2 == 0 else "yx")
        small_ref[pl.ds(4 + hg, 1), pl.ds(0, width)] = weights[width : width + 1]
        for t in range(tiles):
            span = pl.ds(t * TILE, TILE)
            gnorm[span, :] += dot(gproj[span, :], wqkv[hg], 1, 1)
            if t % 2 == 1:
                point()

    ln_gain = ln_gain_ref[...].reshape(1, width)
    b_o = b_o_ref[...].reshape(1, width)
    b_out = b_out_ref[...].reshape(1, width)
    gain_grad = jnp.zeros((1, width), F32)
    for s in range(seqs):
        span = pl.ds(s * SEQ, SEQ)
        unit, inverse = row_stats(packed[span, :].astype(F32))
        grad = gnorm[span, :]
        gain_grad = gain_grad + jnp.sum(grad * unit, axis=0, keepdims=True)
        grad = grad * ln_gain
        back = grad - jnp.mean(grad, axis=1, keepdims=True)
        back = (back - unit * jnp.mean(grad * unit, axis=1, keepdims=True)) * inverse
        normed[span, :] = (grow[span, :].astype(F32) + back).astype(BF16)
    for t in range(width // GROUP):
        small_ref[pl.ds(t, 1), pl.ds(width, GROUP)] = gain_grad[:, t * GROUP : (t + 1) * GROUP]
    if wired:
        net.start_small()
    point()
    finals = []
    for s in range(seqs):
        span = pl.ds(s * SEQ, SEQ)
        place = position_slots(lens[s])
        put = one_hot(place)
        padding = jnp.where(place < 0, 1.0, 0.0)
        attended = (dot(mixed[span, :], wo[...]) + b_o).astype(BF16).astype(F32)
        fed_here = (fed[span, :] + b_out).astype(BF16).astype(F32)
        result = (packed[span, :].astype(F32) + (attended + fed_here)).astype(BF16)
        tok[span, :] = (dot(put, result) + padding * tok[span, :].astype(F32)).astype(BF16)
        finals.append(
            pltpu.make_async_copy(tok.at[span], output_hbm.at[span], done_sem.at[2 * s])
        )
        finals[-1].start()
        if wired:
            net.advance_small()
        point()
        grads = dot(put, normed[span, :]) + padding * cot[span, :].astype(F32)
        cot[span, :] = grads.astype(BF16)
        finals.append(
            pltpu.make_async_copy(cot.at[span], grad_tokens_hbm.at[span], done_sem.at[2 * s + 1])
        )
        finals[-1].start()
        if wired:
            net.advance_small()
        point()
    if wired:
        net.drain()
        finals.append(pltpu.make_async_copy(net.fin, pieces_hbm, done_sem.at[2 * seqs]))
        finals[-1].start()
    finals.append(pltpu.make_async_copy(small_ref, small_hbm, done_sem.at[2 * seqs + 1]))
    finals[-1].start()
    for copy in sent[-2:] + finals:
        copy.wait()


def split_lanes(block, groups):
    width = block.shape[1] // 3
    return jnp.concatenate(
        [
            block[:, hg * width + t * GROUP : hg * width + (t + 1) * GROUP]
            for t in range(3)
            for hg in range(groups)
        ],
        axis=1,
    )


def fold_heads(gains):
    return sum(gains[:, h * HEAD : (h + 1) * HEAD] for h in range(GROUP // HEAD))


def small_parts(small, chunks, groups, width):
    b_in = jnp.concatenate([small[f : f + 1, :width] for f in range(chunks)], axis=1)
    b_qkv = jnp.concatenate([small[4 + hg : 5 + hg, :width] for hg in range(groups)], axis=1)
    ln = jnp.concatenate([small[t : t + 1, width:] for t in range(width // GROUP)], axis=1)
    gains = [fold_heads(small[3 + side : 4 + side, width:]) for side in range(2)]
    return ln, split_lanes(b_qkv, groups), gains[0], gains[1], small[7:8, :width], b_in


def finish_kernel(
    rows_hbm, grads_hbm, fin, small, output_hbm, grad_tokens_hbm, g_ln, g_qkv, g_b_qkv, g_q, g_k,
    g_o, g_b_o, g_in, g_b_in, g_out, g_b_out, sem,
):
    copies = [
        pltpu.make_async_copy(rows_hbm, output_hbm, sem.at[0]),
        pltpu.make_async_copy(grads_hbm, grad_tokens_hbm, sem.at[1]),
    ]
    for copy in copies:
        copy.start()
    width = g_o.shape[1]
    half = width // 2
    chunks, groups = g_in.shape[1] // width, width // GROUP

    def whole(shard):
        return jnp.concatenate([fin[side, shard].astype(F32) for side in range(2)], axis=1)

    for f in range(chunks):
        g_in[:, f * width : (f + 1) * width] = whole(f)
    qkv = jnp.concatenate([whole(chunks + hg) for hg in range(groups)], axis=1)
    g_qkv[...] = split_lanes(qkv, groups)
    g_o[...] = whole(chunks + groups)
    for j in range(4):
        g_out[j * BLOCK : (j + 1) * BLOCK, :] = whole(chunks + groups + 1 + j)
    ln, b_qkv, q, k, b_out, b_in = small_parts(small[...], chunks, groups, width)
    for ref, value in (
        (g_ln, ln), (g_b_qkv, b_qkv), (g_q, q), (g_k, k), (g_b_o, b_out), (g_b_in, b_in), (g_b_out, b_out)
    ):
        ref[...] = value.reshape(value.shape[1])
    for copy in copies:
        copy.wait()


def local(n_dp, tokens, lengths, cotangent, ln_gain, w_qkv, b_qkv, q_gain, k_gain, w_o, b_o, w_in, b_in, w_out, b_out):
    rows, width = tokens.shape
    hidden_width = w_in.shape[1]
    chunks = hidden_width // width
    groups = width // GROUP
    seqs = rows // SEQ
    shards = chunks + groups + 1
    pieces_in_all = shards + chunks
    wired = n_dp * BLOCK == width and n_dp == 4 * chunks
    anywhere = pl.BlockSpec(memory_space=pl.ANY)
    vmem = pl.BlockSpec(memory_space=pltpu.VMEM)
    wide = lambda *shape: pltpu.VMEM(shape, F32)
    slim = lambda *shape: pltpu.VMEM(shape, BF16)
    extra = KEYS - SLOT
    half = width // 2
    if wired:
        pieces_shape = (2, shards + 4, BLOCK, half)
        flights = 6 * shards + 3 * chunks + 3 + 5
        others = [
            slim(2, 2, 16, BLOCK, half), slim(2, 16, BLOCK, half), slim(4, 16, BLOCK, half),
            slim(pieces_in_all, 8, BLOCK, half), slim(pieces_in_all, 4, BLOCK, half),
            slim(shards, 2, BLOCK, half), slim(shards, 1, BLOCK, half), slim(4, 4, BLOCK, half),
            slim(2, 4, BLOCK, half), slim(1, 4, BLOCK, half), slim(2, shards + 4, BLOCK, half),
            wide(5, 8, width + GROUP), pltpu.SemaphoreType.DMA((flights,)),
            pltpu.SemaphoreType.DMA((flights,)),
        ]
        settings = dict(collective_id=0, has_side_effects=True)
    else:
        pieces_shape = (pieces_in_all, width, width)
        others = [slim(2, width, width), pltpu.SemaphoreType.DMA((2,))]
        settings = {}
    output, grad_tokens, pieces, small = pl.pallas_call(
        functools.partial(layer_kernel, wired),
        out_shape=(
            jax.ShapeDtypeStruct(tokens.shape, BF16),
            jax.ShapeDtypeStruct(tokens.shape, BF16),
            jax.ShapeDtypeStruct(pieces_shape, BF16),
            jax.ShapeDtypeStruct((8, width + GROUP), F32),
        ),
        in_specs=[
            pl.BlockSpec(memory_space=pltpu.SMEM), anywhere, anywhere, vmem, anywhere, vmem, vmem, vmem,
            anywhere, vmem, anywhere, vmem, anywhere, vmem,
        ],
        out_specs=(anywhere, anywhere, anywhere, anywhere),
        scratch_shapes=[
            slim(groups, width, width), slim(width, width), slim(chunks, width, width),
            slim(chunks, width, width), slim(rows, width), slim(rows, width), slim(rows, width),
            slim(rows, width), slim(rows, width), slim(width + 16, rows), slim(2, rows, width),
            slim(2, rows, width), wide(rows, width), wide(rows, width), slim(rows, GROUP),
            slim(rows + extra, GROUP), slim(rows + extra, GROUP), slim(rows, GROUP),
            wide(rows, GROUP), wide(rows, GROUP), wide(rows, GROUP), wide(rows, GROUP),
            wide(rows, GROUP), wide(rows, GROUP), slim(rows, width), wide(8, width + GROUP),
            pltpu.SemaphoreType.DMA((3 + 2 * chunks + 3 * groups,)),
            pltpu.SemaphoreType.DMA((2 * seqs + 2,)),
        ] + others,
        compiler_params=pltpu.CompilerParams(vmem_limit_bytes=62 << 20, **settings),
    )(
        lengths, tokens, cotangent, ln_gain, w_qkv, b_qkv, q_gain, k_gain,
        w_o, b_o, w_in, b_in, w_out, b_out,
    )
    if wired:
        shape = lambda *dims: jax.ShapeDtypeStruct(dims, F32)
        return pl.pallas_call(
            finish_kernel,
            out_shape=(
                jax.ShapeDtypeStruct(tokens.shape, BF16), jax.ShapeDtypeStruct(tokens.shape, BF16),
                shape(width), shape(BLOCK, 3 * width), shape(3 * width), shape(HEAD), shape(HEAD),
                shape(BLOCK, width), shape(width), shape(BLOCK, hidden_width), shape(hidden_width),
                shape(4 * BLOCK, width), shape(width),
            ),
            in_specs=[anywhere, anywhere, vmem, vmem],
            out_specs=(anywhere, anywhere) + (vmem,) * 11,
            scratch_shapes=[pltpu.SemaphoreType.DMA((2,))],
        )(output, grad_tokens, pieces, small)

    def scatter(block, dim):
        part = lax.psum_scatter(block, "dp", scatter_dimension=dim, tiled=True)
        return lax.psum(part, "branch").astype(F32)

    grad_out = scatter(pieces[shards:].reshape(hidden_width, width), 0)
    reduced = scatter(pieces[:shards], 1)
    grad_in = jnp.concatenate([reduced[f] for f in range(chunks)], axis=1)
    qkv = jnp.concatenate([reduced[chunks + hg] for hg in range(groups)], axis=1)
    small = lax.psum(small, ("dp", "branch"))
    ln, g_b_qkv, g_q, g_k, g_b_out, g_b_in = (
        part[0] for part in small_parts(small, chunks, groups, width)
    )
    return (
        output, grad_tokens, ln, split_lanes(qkv, groups), g_b_qkv, g_q, g_k,
        reduced[chunks + groups], g_b_out, grad_in, g_b_in, grad_out, g_b_out,
    )


def solution(mesh):
    rows, split, whole = P(("dp", "branch"), None), P("dp", None), P()
    return jax.shard_map(
        functools.partial(local, mesh.shape["dp"]),
        mesh=mesh,
        in_specs=(rows, split, rows) + (whole,) * 11,
        out_specs=(
            rows, rows, whole, split, whole, whole, whole, split, whole, split, whole, split, whole,
        ),
        check_vma=False,
    )
```

```python
import functools
import math

import jax
import jax.numpy as jnp
from jax import lax
from jax.experimental import pallas as pl
from jax.experimental.pallas import tpu as pltpu
from jax.sharding import PartitionSpec as P

HEAD = 64
SEQ = 448
IMAGES = 4
SLOT = SEQ // IMAGES
KEYS = 128
GROUP = 256
EPS = 1e-06
SCALE = 0.125
F32 = jnp.float32
BF16 = jnp.bfloat16
GELU_A = math.sqrt(2.0 / math.pi)
GELU_B = 0.044715


def dot(left, right, left_dim=1, right_dim=0):
    return lax.dot_general(
        left, right, (((left_dim,), (right_dim,)), ((), ())), preferred_element_type=F32
    )


def slot_positions(lens):
    row = lax.broadcasted_iota(jnp.int32, (SEQ, 1), 0)
    held = jnp.full((SEQ, 1), -1, jnp.int32)
    start = jnp.int32(0)
    for image in range(IMAGES):
        place = row - SLOT * image
        held = jnp.where((place >= 0) & (place < lens[image]), place + start, held)
        start = start + lens[image]
    return held


def position_slots(lens):
    row = lax.broadcasted_iota(jnp.int32, (SEQ, 1), 0)
    held = jnp.full((SEQ, 1), -1, jnp.int32)
    start = jnp.int32(0)
    for image in range(IMAGES):
        place = row - start
        held = jnp.where((place >= 0) & (place < lens[image]), place + SLOT * image, held)
        start = start + lens[image]
    return held


def one_hot(index):
    lanes = lax.broadcasted_iota(jnp.int32, (SEQ, SEQ), 1)
    return jnp.where(lanes == index, 1.0, 0.0).astype(BF16)


def row_stats(values):
    centered = values - jnp.mean(values, axis=1, keepdims=True)
    spread = jnp.mean(centered * centered, axis=1, keepdims=True)
    inverse = lax.rsqrt(spread + EPS)
    return centered * inverse, inverse


def gelu_pair(pre, grad):
    square = pre * pre
    bent = jnp.tanh(pre * (GELU_A + (GELU_A * GELU_B) * square))
    half = 0.5 * pre
    up = 1.0 + bent
    hidden = half * up
    slope = half * (GELU_A + (3.0 * GELU_A * GELU_B) * square)
    return hidden, (up * (0.5 + (1.0 - bent) * slope)) * grad


MESH = pl.DeviceIdType.MESH
BLOCK = 48
CORE, FIRST, SECOND, THIRD, FOURTH, TWIN = range(6)
AGES = (4, 5, 3, 2, 2, 1)
LATE_AGES = (1, 2, 1, 1, 1, 1)
SLOTS = 4
HELD = 3


class Piece:
    def __init__(self, index, shard, order):
        self.index, self.shard, self.order = index, shard, order
        self.stage, self.copy, self.point = CORE, None, 0


class Exchange:
    def __init__(self, refs, chunks):
        (self.both, self.inbox, self.acc, self.in1, self.in2, self.in3, self.in4, self.osum,
         self.oin3, self.oin4, self.fin, self.small, self.small_in, self.send_sem, self.recv_sem) = refs
        self.chunks = chunks
        self.dp, self.core = lax.axis_index("dp"), lax.axis_index("branch")
        self.bits = {
            "x": lax.rem(self.dp, 2),
            "y": lax.rem(self.dp // 2, 2),
            "z0": lax.rem(self.dp // 4, 2),
            "z1": lax.rem(self.dp // 8, 2),
        }
        self.far = {
            axis: (self.dp + step - 2 * step * self.bits[axis], self.core)
            for axis, step in (("x", 1), ("y", 2), ("z0", 4), ("z1", 8))
        }
        self.far["core"] = (self.dp, 1 - self.core)
        self.pieces, self.point, self.flights = [], 0, 0
        self.small_stage, self.small_copy = 0, None
        self.merged = 0
        self.ages = AGES

    def greet(self):
        barrier = pltpu.get_barrier_semaphore()
        for device in self.far.values():
            pl.semaphore_signal(barrier, inc=1, device_id=device, device_id_type=MESH)
        pl.semaphore_wait(barrier, len(self.far))

    def send(self, source, target, axis):
        copy = pltpu.make_async_remote_copy(
            src_ref=source, dst_ref=target, send_sem=self.send_sem.at[self.flights],
            recv_sem=self.recv_sem.at[self.flights], device_id=self.far[axis], device_id_type=MESH,
        )
        self.flights += 1
        copy.start()
        return copy

    def start(self, value, shard, order, by_row_block):
        piece = Piece(len(self.pieces), shard, order)
        for other in self.pieces:
            if other.stage == CORE and other.index <= piece.index - SLOTS // 2:
                self.advance(other)
        slot = piece.index % SLOTS
        half = value.shape[1] // 2
        for block in range(16):
            place = block
            if by_row_block:
                x, y, z0, z1 = block % 2, block // 2 % 2, block // 4 % 2, block // 8
                first, second = (x, y) if order == "xy" else (y, x)
                place = 8 * first + 4 * second + 2 * z0 + z1
            for side in range(2):
                self.both[slot, side, place] = value[
                    BLOCK * block : BLOCK * (block + 1), half * side : half * (side + 1)
                ].astype(BF16)
        piece.copy = self.send(self.both.at[slot, 1 - self.core], self.inbox.at[slot], "core")
        piece.point = self.point
        self.pieces.append(piece)

    def halve(self, piece, held, held_at, arrived, count, axis, target):
        near = self.bits[axis] * count
        away = (1 - self.bits[axis]) * count
        span = pl.ds(away, count)
        arrived[span] = arrived[span] + held[pl.ds(held_at + away, count)]
        piece.copy = self.send(arrived.at[span], target, axis)
        span = pl.ds(near, count)
        arrived[span] = arrived[span] + held[pl.ds(held_at + near, count)]

    def advance(self, piece):
        piece.copy.wait()
        piece.point = self.point
        k, shard = piece.index, piece.shard
        one, two = piece.order
        acc = self.acc.at[k % 4]
        if piece.stage == CORE:
            for other in self.pieces:
                assert other.index != k - 4 or other.stage > FIRST
            own, arrived = self.both.at[k % SLOTS, self.core], self.inbox.at[k % SLOTS]
            away = pl.ds((1 - self.bits[one]) * 8, 8)
            acc[away] = own[away] + arrived[away]
            piece.copy = self.send(acc.at[away], self.in1.at[k], one)
            near = pl.ds(self.bits[one] * 8, 8)
            acc[near] = own[near] + arrived[near]
        elif piece.stage == FIRST:
            self.halve(piece, acc, self.bits[one] * 8, self.in1.at[k], 4, two, self.in2.at[k])
        elif piece.stage == SECOND:
            held, held_at = self.in1.at[k], self.bits[two] * 4
            if isinstance(shard, int):
                self.halve(piece, held, held_at, self.in2.at[k], 2, "z0", self.in3.at[shard])
            else:
                plane = shard[0]
                place = plane % 2 * 2 + plane // 2
                self.osum[place] = self.in2[k] + held[pl.ds(held_at, 4)]
                self.merged += 1
                if self.merged < self.chunks:
                    piece.stage = TWIN
                    piece.copy = None
                else:
                    far = pl.ds((1 - self.bits["z0"]) * 2, 2)
                    piece.copy = self.send(self.osum.at[far], self.oin3, "z0")
        elif piece.stage == THIRD:
            if isinstance(shard, int):
                self.halve(
                    piece, self.in2.at[k], self.bits["z0"] * 2, self.in3.at[shard], 1, "z1",
                    self.in4.at[shard],
                )
            else:
                self.halve(
                    piece, self.osum, self.bits["z0"] * 2, self.oin3, 1, "z1", self.oin4
                )
        elif piece.stage == FOURTH:
            if isinstance(shard, int):
                final = self.fin.at[self.core, pl.ds(shard, 1)]
                final[...] = self.in4[shard] + self.in3[shard, pl.ds(self.bits["z1"], 1)]
            else:
                final = self.fin.at[self.core, pl.ds(self.fin.shape[1] - 4, 4)]
                final[...] = self.oin4[0] + self.oin3[self.bits["z1"]]
            piece.copy = self.send(final, final, "core")
        else:
            piece.copy = None
        piece.stage += 1

    def start_small(self):
        self.small_copy = self.send(self.small, self.small_in.at[0], "core")

    def advance_small(self):
        if self.small_copy is None:
            return
        self.small_copy.wait()
        self.small[...] = self.small[...] + self.small_in[self.small_stage]
        self.small_stage += 1
        self.small_copy = None
        if self.small_stage < 5:
            axis = ("core", "x", "y", "z0", "z1")[self.small_stage]
            self.small_copy = self.send(self.small, self.small_in.at[self.small_stage], axis)

    def progress(self):
        self.point += 1
        for piece in self.pieces:
            if piece.stage <= TWIN and self.point - piece.point >= self.ages[piece.stage]:
                self.advance(piece)

    def drain(self):
        while self.small_copy is not None or any(piece.stage <= TWIN for piece in self.pieces):
            self.point += 1
            for piece in self.pieces:
                if piece.stage <= TWIN:
                    self.advance(piece)
            self.advance_small()


def layer_kernel(
    wired,
    lengths_ref, tokens_hbm, cot_hbm, ln_gain_ref, w_qkv_hbm, b_qkv_ref, q_gain_ref, k_gain_ref,
    w_o_hbm, b_o_ref, w_in_hbm, b_in_ref, w_out_hbm, b_out_ref,
    output_hbm, grad_tokens_hbm, pieces_hbm, small_hbm,
    wqkv, wo, win, wout, tok, cot, packed, grow, normed, flipped, hid_even, gpre_even,
    fed, gnorm, qs, ks, vs, gm, nq, nk, rq, rk, dq, dk, small_ref, turned,
    load_sem, done_sem, *refs,
):
    rows, width = tok.shape
    hidden_width = w_in_hbm.shape[1]
    chunks = hidden_width // width
    groups = width // GROUP
    seqs = rows // SEQ
    images = seqs * IMAGES
    base = lax.axis_index("branch") * seqs
    hid, gpre, mixed = (hid_even, tok), (gpre_even, cot), hid_even

    def load(source, target, slot):
        copy = pltpu.make_async_copy(source, target, load_sem.at[slot])
        copy.start()
        return copy

    token_copy = load(tokens_hbm, tok, 0)
    cot_copy = load(cot_hbm, cot, 1)
    in_copies, out_copies, qkv_copies = [], [], []

    def load_chunk(f):
        cols = pl.ds(f * width, width)
        in_copies.append(load(w_in_hbm.at[:, cols], win.at[f % HELD], 2 + 2 * f))
        out_copies.append(load(w_out_hbm.at[cols, :], wout.at[f % HELD], 3 + 2 * f))

    for f in range(HELD):
        load_chunk(f)
    for hg in range(groups):
        qkv_copies.append([
            load(
                w_qkv_hbm.at[:, pl.ds(t * width + hg * GROUP, GROUP)],
                wqkv.at[hg, :, pl.ds(t * GROUP, GROUP)],
                2 + 2 * chunks + 3 * hg + t,
            )
            for t in range(3)
        ])
    o_copy = load(w_o_hbm, wo, 2 + 2 * chunks + 3 * groups)

    small_ref[...] = jnp.zeros_like(small_ref)
    sent = []
    net = None
    if wired:
        net = Exchange(refs[:11] + (small_ref,) + refs[11:], chunks)
        net.greet()
    else:
        stage, piece_sem = refs

    def emit(value, shard, order="xy", by_row_block=True):
        if wired:
            net.start(value, shard, order, by_row_block)
            return
        index = len(sent)
        slot = index % 2
        if index >= 2:
            sent[index - 2].wait()
        stage[slot] = value.astype(BF16)
        target = pieces_hbm.at[shard if isinstance(shard, int) else chunks + groups + 1 + shard[0]]
        copy = pltpu.make_async_copy(stage.at[slot], target, piece_sem.at[slot])
        copy.start()
        sent.append(copy)

    def point():
        if wired:
            net.progress()

    ones_row = jnp.where(lax.broadcasted_iota(jnp.int32, (16, rows), 0) == 0, 1.0, 0.0)
    flipped[pl.ds(width, 16), :] = ones_row.astype(BF16)

    lens = [[lengths_ref[base + s, j] for j in range(IMAGES)] for s in range(seqs)]
    token_copy.wait()
    cot_copy.wait()
    grad_sum = jnp.zeros((1, width), F32)
    for s in range(seqs):
        span = pl.ds(s * SEQ, SEQ)
        pick = one_hot(slot_positions(lens[s]))
        rows_here = dot(pick, tok[span, :])
        packed[span, :] = rows_here.astype(BF16)
        unit, _ = row_stats(rows_here)
        normed[span, :] = (unit * ln_gain_ref[...].reshape(1, width)).astype(BF16)
        grads_here = dot(pick, cot[span, :])
        grow[span, :] = grads_here.astype(BF16)
        grad_sum = grad_sum + jnp.sum(grads_here, axis=0, keepdims=True)
    small_ref[pl.ds(7, 1), pl.ds(0, width)] = grad_sum
    eye = jnp.where(
        lax.broadcasted_iota(jnp.int32, (GROUP, GROUP), 0)
        == lax.broadcasted_iota(jnp.int32, (GROUP, GROUP), 1),
        1.0,
        0.0,
    ).astype(BF16)

    def flip(source, target):
        for part in range(groups):
            lanes = pl.ds(part * GROUP, GROUP)
            target[lanes, :] = dot(eye, source[:, lanes], 1, 1).astype(BF16)

    flip(normed, flipped)

    def chunk_results(f, step):
        slot = f % 2
        if step == 0:
            for part in range(groups):
                lanes = pl.ds(part * GROUP, GROUP)
                up = dot(hid[slot][...], wout[f % HELD, :, lanes])
                fed[:, lanes] = up if f == 0 else fed[:, lanes] + up
            flip(hid[slot], turned)
        elif step == 1:
            emit(dot(turned[...], grow[...]), (f,), "yx", False)
        else:
            for part in range(groups):
                lanes = pl.ds(part * GROUP, GROUP)
                down = dot(gpre[slot][...], win[f % HELD, lanes, :], 1, 1)
                gnorm[:, lanes] = down if f == 0 else gnorm[:, lanes] + down
            weights = dot(flipped[...], gpre[slot][...])
            emit(weights[:width], f, "xy")
            small_ref[pl.ds(f, 1), pl.ds(0, width)] = weights[width : width + 1]

    for f in range(chunks):
        in_copies[f].wait()
        out_copies[f].wait()
        bias = b_in_ref[...].reshape(1, hidden_width)[:, f * width : (f + 1) * width]
        for c in range(groups):
            lanes = pl.ds(c * GROUP, GROUP)
            pre = dot(normed[...], win[f % HELD, :, lanes]) + bias[:, c * GROUP : (c + 1) * GROUP]
            back = dot(grow[...], wout[f % HELD, lanes, :], 1, 1)
            if f > 0:
                chunk_results(f - 1, c)
            hidden, grad_pre = gelu_pair(pre, back)
            hid[f % 2][:, lanes] = hidden.astype(BF16)
            gpre[f % 2][:, lanes] = grad_pre.astype(BF16)
            point()
        if 0 < f <= chunks - HELD:
            load_chunk(f - 1 + HELD)

    for hg in range(groups):
        for copy in qkv_copies[hg]:
            copy.wait()
        if hg == 0:
            o_copy.wait()
        same_head = (
            lax.broadcasted_iota(jnp.int32, (GROUP, GROUP), 0) // HEAD
            == lax.broadcasted_iota(jnp.int32, (GROUP, GROUP), 1) // HEAD
        )
        average = jnp.where(same_head, 1.0 / HEAD, 0.0).astype(BF16)

        def head_mean(values, split):
            high = values.astype(BF16)
            mean = dot(high, average)
            if split:
                mean = mean + dot((values - high.astype(F32)).astype(BF16), average)
            return mean

        def head_norm(raw):
            centered = raw - head_mean(raw, True)
            inverse = lax.rsqrt(head_mean(centered * centered, False) + EPS)
            return centered * inverse, inverse

        q_gain = jnp.concatenate([q_gain_ref[...].reshape(1, HEAD)] * (GROUP // HEAD), axis=1)
        k_gain = jnp.concatenate([k_gain_ref[...].reshape(1, HEAD)] * (GROUP // HEAD), axis=1)
        b_qkv = b_qkv_ref[...].reshape(1, 3 * width)
        bias_q, bias_k, bias_v = (
            b_qkv[:, t * width + hg * GROUP : t * width + (hg + 1) * GROUP] for t in range(3)
        )
        gproj = gpre[hg % 2]
        if hg == 0:
            chunk_results(chunks - 1, 0)
            token_copy = load(tokens_hbm, tok, 0)
        if hg == groups - 1:
            cot_copy = load(cot_hbm, cot, 1)
        if wired and hg == groups - 1:
            net.ages = LATE_AGES
        raw = dot(normed[...], wqkv[hg, :, pl.ds(0, GROUP)]) + bias_q
        unit, inverse = head_norm(raw)
        nq[...] = unit
        rq[...] = inverse
        qs[...] = (unit * q_gain).astype(BF16) * SCALE
        point()
        raw = dot(normed[...], wqkv[hg, :, pl.ds(GROUP, GROUP)]) + bias_k
        unit, inverse = head_norm(raw)
        nk[...] = unit
        rk[...] = inverse
        ks[pl.ds(0, rows), :] = (unit * k_gain).astype(BF16)
        raw = dot(normed[...], wqkv[hg, :, pl.ds(2 * GROUP, GROUP)]) + bias_v
        vs[pl.ds(0, rows), :] = raw.astype(BF16)
        gm[...] = dot(grow[...], wo[pl.ds(hg * GROUP, GROUP), :], 1, 1).astype(BF16)
        point()
        if hg == 0:
            ks[pl.ds(rows, KEYS - SLOT), :] = jnp.zeros((KEYS - SLOT, GROUP), BF16)
            vs[pl.ds(rows, KEYS - SLOT), :] = jnp.zeros((KEYS - SLOT, GROUP), BF16)

        lane = lax.broadcasted_iota(jnp.int32, (1, KEYS), 1)
        first_head = jnp.where(lane < HEAD, 1.0, 0.0).astype(BF16)
        second_head = jnp.where(lane < HEAD, 0.0, 1.0).astype(BF16)

        def two_heads(block):
            return jnp.concatenate([block * first_head, block * second_head], axis=0)

        def side_by_side(block):
            return jnp.concatenate([block[:SLOT], block[SLOT:]], axis=1)

        def one_image(image):
            start = pl.multiple_of(image * SLOT, 16)
            span = pl.ds(start, SLOT)
            window = pl.ds(start, KEYS)
            count = lengths_ref[base + image // IMAGES, lax.rem(image, IMAGES)]
            seen = lane < count
            for pair in range(GROUP // KEYS):
                lanes = pl.ds(pair * KEYS, KEYS)
                query = two_heads(qs[span, lanes])
                grad = two_heads(gm[span, lanes])
                key, value = ks[window, lanes], vs[window, lanes]
                weight = jnp.where(seen, jnp.exp(dot(query, key, 1, 1)), 0.0)
                probs = weight / jnp.sum(weight, axis=1, keepdims=True)
                grad_probs = dot(grad, value, 1, 1)
                inner = jnp.sum(probs * grad_probs, axis=1, keepdims=True)
                grad_scores = (probs * (grad_probs - inner)).astype(BF16)
                probs_low = probs.astype(BF16)
                mixed[span, pl.ds(hg * GROUP + pair * KEYS, KEYS)] = dot(
                    side_by_side(probs_low), two_heads(value)
                ).astype(BF16)
                dq[span, lanes] = dot(side_by_side(grad_scores), two_heads(key)) * SCALE
                dk[span, lanes] = dot(grad_scores, query, 0, 0)[:SLOT]
                gproj[span, pl.ds(2 * GROUP + pair * KEYS, KEYS)] = dot(probs_low, grad, 0, 0)[
                    :SLOT
                ].astype(BF16)

        def two_images(step, carry):
            one_image(2 * step)
            one_image(2 * step + 1)
            return carry

        if hg == 0:
            chunk_results(chunks - 1, 1)
        lax.fori_loop(0, images // 4, two_images, 0)
        point()
        if hg == 0:
            chunk_results(chunks - 1, 2)
        lax.fori_loop(images // 4, images // 2, two_images, 0)
        point()
        if hg == groups - 1:
            flip(mixed, turned)
            emit(dot(turned[...], grow[...]), chunks + groups, "yx")

        gain_sums = []
        for side, (grad_ref, unit_ref, inverse_ref, gain) in enumerate(
            ((dq, nq, rq, q_gain), (dk, nk, rk, k_gain))
        ):
            grad, unit = grad_ref[...], unit_ref[...]
            gain_sums.append(jnp.sum(grad * unit, axis=0, keepdims=True))
            grad = grad * gain
            back = grad - head_mean(grad, True) - unit * head_mean(grad * unit, False)
            gproj[:, pl.ds(side * GROUP, GROUP)] = (back * inverse_ref[...]).astype(BF16)
            if side == 0:
                point()
        for side in range(2):
            small_ref[pl.ds(3 + side, 1), pl.ds(width, GROUP)] += gain_sums[side]
        weights = dot(flipped[...], gproj[...])
        emit(weights[:width], chunks + hg, "xy" if hg % 2 == 0 else "yx")
        small_ref[pl.ds(4 + hg, 1), pl.ds(0, width)] = weights[width : width + 1]
        point()
        for part in range(groups):
            lanes = pl.ds(part * GROUP, GROUP)
            gnorm[:, lanes] += dot(gproj[...], wqkv[hg, lanes, :], 1, 1)
        point()

    ln_gain = ln_gain_ref[...].reshape(1, width)
    b_o = b_o_ref[...].reshape(1, width)
    b_out = b_out_ref[...].reshape(1, width)
    gain_grad = jnp.zeros((1, width), F32)
    for s in range(seqs):
        span = pl.ds(s * SEQ, SEQ)
        unit, inverse = row_stats(packed[span, :].astype(F32))
        grad = gnorm[span, :]
        gain_grad = gain_grad + jnp.sum(grad * unit, axis=0, keepdims=True)
        grad = grad * ln_gain
        back = grad - jnp.mean(grad, axis=1, keepdims=True)
        back = (back - unit * jnp.mean(grad * unit, axis=1, keepdims=True)) * inverse
        normed[span, :] = (grow[span, :].astype(F32) + back).astype(BF16)
    for t in range(width // GROUP):
        small_ref[pl.ds(t, 1), pl.ds(width, GROUP)] = gain_grad[:, t * GROUP : (t + 1) * GROUP]
    if wired:
        net.start_small()
    point()
    finals = []
    token_copy.wait()
    cot_copy.wait()
    for s in range(seqs):
        span = pl.ds(s * SEQ, SEQ)
        place = position_slots(lens[s])
        put = one_hot(place)
        padding = jnp.where(place < 0, 1.0, 0.0)
        attended = (dot(mixed[span, :], wo[...]) + b_o).astype(BF16).astype(F32)
        fed_here = (fed[span, :] + b_out).astype(BF16).astype(F32)
        result = (packed[span, :].astype(F32) + (attended + fed_here)).astype(BF16)
        tok[span, :] = (dot(put, result) + padding * tok[span, :].astype(F32)).astype(BF16)
        finals.append(
            pltpu.make_async_copy(tok.at[span], output_hbm.at[span], done_sem.at[2 * s])
        )
        finals[-1].start()
        if wired:
            net.advance_small()
        point()
        grads = dot(put, normed[span, :]) + padding * cot[span, :].astype(F32)
        cot[span, :] = grads.astype(BF16)
        finals.append(
            pltpu.make_async_copy(cot.at[span], grad_tokens_hbm.at[span], done_sem.at[2 * s + 1])
        )
        finals[-1].start()
        if wired:
            net.advance_small()
        point()
    if wired:
        net.drain()
        finals.append(pltpu.make_async_copy(net.fin, pieces_hbm, done_sem.at[2 * seqs]))
        finals[-1].start()
    finals.append(pltpu.make_async_copy(small_ref, small_hbm, done_sem.at[2 * seqs + 1]))
    finals[-1].start()
    for copy in sent[-2:] + finals:
        copy.wait()


def split_lanes(block, groups):
    width = block.shape[1] // 3
    return jnp.concatenate(
        [
            block[:, hg * width + t * GROUP : hg * width + (t + 1) * GROUP]
            for t in range(3)
            for hg in range(groups)
        ],
        axis=1,
    )


def fold_heads(gains):
    return sum(gains[:, h * HEAD : (h + 1) * HEAD] for h in range(GROUP // HEAD))


def small_parts(small, chunks, groups, width):
    b_in = jnp.concatenate([small[f : f + 1, :width] for f in range(chunks)], axis=1)
    b_qkv = jnp.concatenate([small[4 + hg : 5 + hg, :width] for hg in range(groups)], axis=1)
    ln = jnp.concatenate([small[t : t + 1, width:] for t in range(width // GROUP)], axis=1)
    gains = [fold_heads(small[3 + side : 4 + side, width:]) for side in range(2)]
    return ln, split_lanes(b_qkv, groups), gains[0], gains[1], small[7:8, :width], b_in


def finish_kernel(
    rows_hbm, grads_hbm, fin, small, output_hbm, grad_tokens_hbm, g_ln, g_qkv, g_b_qkv, g_q, g_k,
    g_o, g_b_o, g_in, g_b_in, g_out, g_b_out, held, sem,
):
    ends = ((rows_hbm, output_hbm), (grads_hbm, grad_tokens_hbm))
    comes = [pltpu.make_async_copy(ends[i][0], held.at[i], sem.at[0, i]) for i in range(2)]
    goes = [pltpu.make_async_copy(held.at[i], ends[i][1], sem.at[1, i]) for i in range(2)]
    for copy in comes:
        copy.start()
    width = g_o.shape[1]
    half = width // 2
    chunks, groups = g_in.shape[1] // width, width // GROUP

    def whole(shard):
        return jnp.concatenate([fin[side, shard].astype(F32) for side in range(2)], axis=1)

    for come, go in zip(comes, goes):
        come.wait()
        go.start()
    for f in range(chunks):
        g_in[:, f * width : (f + 1) * width] = whole(f)
    qkv = jnp.concatenate([whole(chunks + hg) for hg in range(groups)], axis=1)
    g_qkv[...] = split_lanes(qkv, groups)
    g_o[...] = whole(chunks + groups)
    for j in range(4):
        g_out[j * BLOCK : (j + 1) * BLOCK, :] = whole(chunks + groups + 1 + j)
    ln, b_qkv, q, k, b_out, b_in = small_parts(small[...], chunks, groups, width)
    for ref, value in (
        (g_ln, ln), (g_b_qkv, b_qkv), (g_q, q), (g_k, k), (g_b_o, b_out), (g_b_in, b_in), (g_b_out, b_out)
    ):
        ref[...] = value.reshape(value.shape[1])
    for copy in goes:
        copy.wait()


def local(n_dp, tokens, lengths, cotangent, ln_gain, w_qkv, b_qkv, q_gain, k_gain, w_o, b_o, w_in, b_in, w_out, b_out):
    rows, width = tokens.shape
    hidden_width = w_in.shape[1]
    chunks = hidden_width // width
    groups = width // GROUP
    seqs = rows // SEQ
    shards = chunks + groups + 1
    pieces_in_all = shards + chunks
    wired = n_dp * BLOCK == width and n_dp == 4 * chunks
    anywhere = pl.BlockSpec(memory_space=pl.ANY)
    vmem = pl.BlockSpec(memory_space=pltpu.VMEM)
    wide = lambda *shape: pltpu.VMEM(shape, F32)
    slim = lambda *shape: pltpu.VMEM(shape, BF16)
    extra = KEYS - SLOT
    half = width // 2
    if wired:
        pieces_shape = (2, shards + 4, BLOCK, half)
        flights = 6 * shards + 3 * chunks + 3 + 5
        others = [
            slim(4, 2, 16, BLOCK, half), slim(4, 16, BLOCK, half), slim(4, 16, BLOCK, half),
            slim(pieces_in_all, 8, BLOCK, half), slim(pieces_in_all, 4, BLOCK, half),
            slim(shards, 2, BLOCK, half), slim(shards, 1, BLOCK, half), slim(4, 4, BLOCK, half),
            slim(2, 4, BLOCK, half), slim(1, 4, BLOCK, half), slim(2, shards + 4, BLOCK, half),
            wide(5, 8, width + GROUP), pltpu.SemaphoreType.DMA((flights,)),
            pltpu.SemaphoreType.DMA((flights,)),
        ]
        settings = dict(collective_id=0, has_side_effects=True)
    else:
        pieces_shape = (pieces_in_all, width, width)
        others = [slim(2, width, width), pltpu.SemaphoreType.DMA((2,))]
        settings = {}
    output, grad_tokens, pieces, small = pl.pallas_call(
        functools.partial(layer_kernel, wired),
        out_shape=(
            jax.ShapeDtypeStruct(tokens.shape, BF16),
            jax.ShapeDtypeStruct(tokens.shape, BF16),
            jax.ShapeDtypeStruct(pieces_shape, BF16),
            jax.ShapeDtypeStruct((8, width + GROUP), F32),
        ),
        in_specs=[
            pl.BlockSpec(memory_space=pltpu.SMEM), anywhere, anywhere, vmem, anywhere, vmem, vmem, vmem,
            anywhere, vmem, anywhere, vmem, anywhere, vmem,
        ],
        out_specs=(anywhere, anywhere, anywhere, anywhere),
        scratch_shapes=[
            slim(groups, width, width), slim(width, width), slim(HELD, width, width),
            slim(HELD, width, width), slim(rows, width), slim(rows, width), slim(rows, width),
            slim(rows, width), slim(rows, width), slim(width + 16, rows), slim(rows, width),
            slim(rows, width), wide(rows, width), wide(rows, width), slim(rows, GROUP),
            slim(rows + extra, GROUP), slim(rows + extra, GROUP), slim(rows, GROUP),
            wide(rows, GROUP), wide(rows, GROUP), wide(rows, GROUP), wide(rows, GROUP),
            wide(rows, GROUP), wide(rows, GROUP), wide(8, width + GROUP), slim(width, rows),
            pltpu.SemaphoreType.DMA((3 + 2 * chunks + 3 * groups,)),
            pltpu.SemaphoreType.DMA((2 * seqs + 2,)),
        ] + others,
        compiler_params=pltpu.CompilerParams(vmem_limit_bytes=62 << 20, **settings),
    )(
        lengths, tokens, cotangent, ln_gain, w_qkv, b_qkv, q_gain, k_gain,
        w_o, b_o, w_in, b_in, w_out, b_out,
    )
    if wired:
        shape = lambda *dims: jax.ShapeDtypeStruct(dims, F32)
        return pl.pallas_call(
            finish_kernel,
            out_shape=(
                jax.ShapeDtypeStruct(tokens.shape, BF16), jax.ShapeDtypeStruct(tokens.shape, BF16),
                shape(width), shape(BLOCK, 3 * width), shape(3 * width), shape(HEAD), shape(HEAD),
                shape(BLOCK, width), shape(width), shape(BLOCK, hidden_width), shape(hidden_width),
                shape(4 * BLOCK, width), shape(width),
            ),
            in_specs=[anywhere, anywhere, vmem, vmem],
            out_specs=(anywhere, anywhere) + (vmem,) * 11,
            scratch_shapes=[slim(2, rows, width), pltpu.SemaphoreType.DMA((2, 2))],
        )(output, grad_tokens, pieces, small)

    def scatter(block, dim):
        part = lax.psum_scatter(block, "dp", scatter_dimension=dim, tiled=True)
        return lax.psum(part, "branch").astype(F32)

    grad_out = scatter(pieces[shards:].reshape(hidden_width, width), 0)
    reduced = scatter(pieces[:shards], 1)
    grad_in = jnp.concatenate([reduced[f] for f in range(chunks)], axis=1)
    qkv = jnp.concatenate([reduced[chunks + hg] for hg in range(groups)], axis=1)
    small = lax.psum(small, ("dp", "branch"))
    ln, g_b_qkv, g_q, g_k, g_b_out, g_b_in = (
        part[0] for part in small_parts(small, chunks, groups, width)
    )
    return (
        output, grad_tokens, ln, split_lanes(qkv, groups), g_b_qkv, g_q, g_k,
        reduced[chunks + groups], g_b_out, grad_in, g_b_in, grad_out, g_b_out,
    )


def solution(mesh):
    rows, split, whole = P(("dp", "branch"), None), P("dp", None), P()
    return jax.shard_map(
        functools.partial(local, mesh.shape["dp"]),
        mesh=mesh,
        in_specs=(rows, split, rows) + (whole,) * 11,
        out_specs=(
            rows, rows, whole, split, whole, whole, whole, split, whole, split, whole, split, whole,
        ),
        check_vma=False,
    )
```

```python
import functools
import math

import jax
import jax.numpy as jnp
from jax import lax
from jax.experimental import pallas as pl
from jax.experimental.pallas import tpu as pltpu
from jax.sharding import PartitionSpec as P

HEAD = 64
SEQ = 448
IMAGES = 4
SLOT = SEQ // IMAGES
KEYS = 128
GROUP = 256
EPS = 1e-06
SCALE = 0.125
F32 = jnp.float32
BF16 = jnp.bfloat16
GELU_A = math.sqrt(2.0 / math.pi)
GELU_B = 0.044715


def dot(left, right, left_dim=1, right_dim=0):
    return lax.dot_general(
        left, right, (((left_dim,), (right_dim,)), ((), ())), preferred_element_type=F32
    )


def slot_positions(lens):
    row = lax.broadcasted_iota(jnp.int32, (SEQ, 1), 0)
    held = jnp.full((SEQ, 1), -1, jnp.int32)
    start = jnp.int32(0)
    for image in range(IMAGES):
        place = row - SLOT * image
        held = jnp.where((place >= 0) & (place < lens[image]), place + start, held)
        start = start + lens[image]
    return held


def position_slots(lens):
    row = lax.broadcasted_iota(jnp.int32, (SEQ, 1), 0)
    held = jnp.full((SEQ, 1), -1, jnp.int32)
    start = jnp.int32(0)
    for image in range(IMAGES):
        place = row - start
        held = jnp.where((place >= 0) & (place < lens[image]), place + SLOT * image, held)
        start = start + lens[image]
    return held


def one_hot(index):
    lanes = lax.broadcasted_iota(jnp.int32, (SEQ, SEQ), 1)
    return jnp.where(lanes == index, 1.0, 0.0).astype(BF16)


def row_stats(values):
    centered = values - jnp.mean(values, axis=1, keepdims=True)
    spread = jnp.mean(centered * centered, axis=1, keepdims=True)
    inverse = lax.rsqrt(spread + EPS)
    return centered * inverse, inverse


def gelu_pair(pre, grad):
    square = pre * pre
    bent = jnp.tanh(pre * (GELU_A + (GELU_A * GELU_B) * square))
    half = 0.5 * pre
    up = 1.0 + bent
    hidden = half * up
    slope = half * (GELU_A + (3.0 * GELU_A * GELU_B) * square)
    return hidden, (up * (0.5 + (1.0 - bent) * slope)) * grad


MESH = pl.DeviceIdType.MESH
BLOCK = 48
CORE, FIRST, SECOND, THIRD, FOURTH, TWIN = range(6)
AGES = (1, 2, 1, 1, 1, 1)
HELD = 3


class Piece:
    def __init__(self, index, shard, order):
        self.index, self.shard, self.order = index, shard, order
        self.stage, self.copy, self.point = CORE, None, 0


class Exchange:
    def __init__(self, refs, chunks):
        (self.pieces_hbm, self.acc, self.inbox, self.in1, self.in2, self.in3, self.in4, self.osum,
         self.oin3, self.oin4, self.fin, self.small, self.small_in, self.own_sem, self.send_sem, self.recv_sem) = refs
        self.chunks = chunks
        self.dp, self.core = lax.axis_index("dp"), lax.axis_index("branch")
        self.bits = {
            "x": lax.rem(self.dp, 2),
            "y": lax.rem(self.dp // 2, 2),
            "z0": lax.rem(self.dp // 4, 2),
            "z1": lax.rem(self.dp // 8, 2),
        }
        self.far = {
            axis: (self.dp + step - 2 * step * self.bits[axis], self.core)
            for axis, step in (("x", 1), ("y", 2), ("z0", 4), ("z1", 8))
        }
        self.far["core"] = (self.dp, 1 - self.core)
        self.pieces, self.point, self.flights = [], 0, 0
        self.small_stage, self.small_copy = 0, None
        self.merged = 0

    def greet(self):
        barrier = pltpu.get_barrier_semaphore()
        for device in self.far.values():
            pl.semaphore_signal(barrier, inc=1, device_id=device, device_id_type=MESH)
        pl.semaphore_wait(barrier, len(self.far))

    def send(self, source, target, axis):
        copy = pltpu.make_async_remote_copy(
            src_ref=source, dst_ref=target, send_sem=self.send_sem.at[self.flights],
            recv_sem=self.recv_sem.at[self.flights], device_id=self.far[axis], device_id_type=MESH,
        )
        self.flights += 1
        copy.start()
        return copy

    def start(self, shard, order):
        k = len(self.pieces)
        piece = Piece(k, shard, order)
        piece.own = pltpu.make_async_copy(
            self.pieces_hbm.at[k, self.core], self.acc.at[k], self.own_sem.at[k]
        )
        piece.own.start()
        piece.copy = self.send(self.pieces_hbm.at[k, 1 - self.core], self.inbox.at[k], "core")
        self.pieces.append(piece)

    def halve(self, piece, held, held_at, arrived, count, axis, target):
        near = self.bits[axis] * count
        away = (1 - self.bits[axis]) * count
        span = pl.ds(away, count)
        arrived[span] = arrived[span] + held[pl.ds(held_at + away, count)]
        piece.copy = self.send(arrived.at[span], target, axis)
        span = pl.ds(near, count)
        arrived[span] = arrived[span] + held[pl.ds(held_at + near, count)]

    def advance(self, piece):
        piece.copy.wait()
        piece.point = self.point
        k, shard = piece.index, piece.shard
        one, two = piece.order
        acc = self.acc.at[k]
        if piece.stage == CORE:
            piece.own.wait()
            acc, arrived = self.acc.at[k], self.inbox.at[k]
            away = pl.ds((1 - self.bits[one]) * 8, 8)
            acc[away] = acc[away] + arrived[away]
            piece.copy = self.send(acc.at[away], self.in1.at[k], one)
            near = pl.ds(self.bits[one] * 8, 8)
            acc[near] = acc[near] + arrived[near]
        elif piece.stage == FIRST:
            self.halve(piece, acc, self.bits[one] * 8, self.in1.at[k], 4, two, self.in2.at[k])
        elif piece.stage == SECOND:
            held, held_at = self.in1.at[k], self.bits[two] * 4
            if isinstance(shard, int):
                self.halve(piece, held, held_at, self.in2.at[k], 2, "z0", self.in3.at[shard])
            else:
                plane = shard[0]
                place = plane % 2 * 2 + plane // 2
                self.osum[place] = self.in2[k] + held[pl.ds(held_at, 4)]
                self.merged += 1
                if self.merged < self.chunks:
                    piece.stage = TWIN
                    piece.copy = None
                else:
                    far = pl.ds((1 - self.bits["z0"]) * 2, 2)
                    piece.copy = self.send(self.osum.at[far], self.oin3, "z0")
        elif piece.stage == THIRD:
            if isinstance(shard, int):
                self.halve(
                    piece, self.in2.at[k], self.bits["z0"] * 2, self.in3.at[shard], 1, "z1",
                    self.in4.at[shard],
                )
            else:
                self.halve(
                    piece, self.osum, self.bits["z0"] * 2, self.oin3, 1, "z1", self.oin4
                )
        elif piece.stage == FOURTH:
            if isinstance(shard, int):
                final = self.fin.at[self.core, pl.ds(shard, 1)]
                final[...] = self.in4[shard] + self.in3[shard, pl.ds(self.bits["z1"], 1)]
            else:
                final = self.fin.at[self.core, pl.ds(self.fin.shape[1] - 4, 4)]
                final[...] = self.oin4[0] + self.oin3[self.bits["z1"]]
            piece.copy = self.send(final, final, "core")
        else:
            piece.copy = None
        piece.stage += 1

    def start_small(self):
        self.small_copy = self.send(self.small, self.small_in.at[0], "core")

    def advance_small(self):
        if self.small_copy is None:
            return
        self.small_copy.wait()
        self.small[...] = self.small[...] + self.small_in[self.small_stage]
        self.small_stage += 1
        self.small_copy = None
        if self.small_stage < 5:
            axis = ("core", "x", "y", "z0", "z1")[self.small_stage]
            self.small_copy = self.send(self.small, self.small_in.at[self.small_stage], axis)

    def progress(self):
        self.point += 1
        for piece in self.pieces:
            due = piece.index + sum(AGES[: piece.stage + 1])
            if piece.stage <= TWIN and self.point >= due:
                self.advance(piece)

    def drain(self):
        while self.small_copy is not None or any(piece.stage <= TWIN for piece in self.pieces):
            self.progress()
            self.advance_small()


def layer_kernel(
    wired, plan,
    lengths_ref, tokens_hbm, cot_hbm, ln_gain_ref, w_qkv_hbm, b_qkv_ref, q_gain_ref, k_gain_ref,
    w_o_hbm, b_o_ref, w_in_hbm, b_in_ref, w_out_hbm, b_out_ref,
    output_hbm, grad_tokens_hbm, pieces_hbm, small_hbm,
    wqkv, wo, win, wout, tok, cot, packed, grow, normed, flipped, hid_even, gpre_even,
    fed, gnorm, qs, ks, vs, gm, nq, nk, rq, rk, dq, dk, small_ref, turned,
    load_sem, done_sem, stage, piece_sem,
):
    rows, width = tok.shape
    hidden_width = w_in_hbm.shape[1]
    chunks = hidden_width // width
    groups = width // GROUP
    seqs = rows // SEQ
    images = seqs * IMAGES
    base = lax.axis_index("branch") * seqs
    hid, gpre, mixed = (hid_even, tok), (gpre_even, cot), hid_even

    def load(source, target, slot):
        copy = pltpu.make_async_copy(source, target, load_sem.at[slot])
        copy.start()
        return copy

    token_copy = load(tokens_hbm, tok, 0)
    cot_copy = load(cot_hbm, cot, 1)
    in_copies, out_copies, qkv_copies = [], [], []

    def load_chunk(f):
        cols = pl.ds(f * width, width)
        in_copies.append(load(w_in_hbm.at[:, cols], win.at[f % HELD], 2 + 2 * f))
        out_copies.append(load(w_out_hbm.at[cols, :], wout.at[f % HELD], 3 + 2 * f))

    for f in range(HELD):
        load_chunk(f)
    for hg in range(groups):
        qkv_copies.append([
            load(
                w_qkv_hbm.at[:, pl.ds(t * width + hg * GROUP, GROUP)],
                wqkv.at[hg, :, pl.ds(t * GROUP, GROUP)],
                2 + 2 * chunks + 3 * hg + t,
            )
            for t in range(3)
        ])
    o_copy = load(w_o_hbm, wo, 2 + 2 * chunks + 3 * groups)

    small_ref[...] = jnp.zeros_like(small_ref)
    sent = []

    def emit(value, shard, order="xy", by_row_block=True):
        index = len(sent)
        slot = index % 2
        if index >= 2:
            sent[index - 2].wait()
        if wired:
            half = width // 2
            for block in range(16):
                place = block
                if by_row_block:
                    x, y, z0, z1 = block % 2, block // 2 % 2, block // 4 % 2, block // 8
                    first, second = (x, y) if order == "xy" else (y, x)
                    place = 8 * first + 4 * second + 2 * z0 + z1
                for side in range(2):
                    stage[slot, side, place] = value[
                        BLOCK * block : BLOCK * (block + 1), half * side : half * (side + 1)
                    ].astype(BF16)
            target = pieces_hbm.at[index]
            plan.append((shard, order))
        else:
            stage[slot] = value.astype(BF16)
            target = pieces_hbm.at[
                shard if isinstance(shard, int) else chunks + groups + 1 + shard[0]
            ]
        copy = pltpu.make_async_copy(stage.at[slot], target, piece_sem.at[slot])
        copy.start()
        sent.append(copy)

    ones_row = jnp.where(lax.broadcasted_iota(jnp.int32, (16, rows), 0) == 0, 1.0, 0.0)
    flipped[pl.ds(width, 16), :] = ones_row.astype(BF16)

    lens = [[lengths_ref[base + s, j] for j in range(IMAGES)] for s in range(seqs)]
    token_copy.wait()
    cot_copy.wait()
    grad_sum = jnp.zeros((1, width), F32)
    for s in range(seqs):
        span = pl.ds(s * SEQ, SEQ)
        pick = one_hot(slot_positions(lens[s]))
        rows_here = dot(pick, tok[span, :])
        packed[span, :] = rows_here.astype(BF16)
        unit, _ = row_stats(rows_here)
        normed[span, :] = (unit * ln_gain_ref[...].reshape(1, width)).astype(BF16)
        grads_here = dot(pick, cot[span, :])
        grow[span, :] = grads_here.astype(BF16)
        grad_sum = grad_sum + jnp.sum(grads_here, axis=0, keepdims=True)
    small_ref[pl.ds(7, 1), pl.ds(0, width)] = grad_sum
    eye = jnp.where(
        lax.broadcasted_iota(jnp.int32, (GROUP, GROUP), 0)
        == lax.broadcasted_iota(jnp.int32, (GROUP, GROUP), 1),
        1.0,
        0.0,
    ).astype(BF16)

    def flip(source, target):
        for part in range(groups):
            lanes = pl.ds(part * GROUP, GROUP)
            target[lanes, :] = dot(eye, source[:, lanes], 1, 1).astype(BF16)

    flip(normed, flipped)

    def chunk_results(f, step):
        slot = f % 2
        if step == 0:
            for part in range(groups):
                lanes = pl.ds(part * GROUP, GROUP)
                up = dot(hid[slot][...], wout[f % HELD, :, lanes])
                fed[:, lanes] = up if f == 0 else fed[:, lanes] + up
            flip(hid[slot], turned)
        elif step == 1:
            emit(dot(turned[...], grow[...]), (f,), "yx", False)
        else:
            for part in range(groups):
                lanes = pl.ds(part * GROUP, GROUP)
                down = dot(gpre[slot][...], win[f % HELD, lanes, :], 1, 1)
                gnorm[:, lanes] = down if f == 0 else gnorm[:, lanes] + down
            weights = dot(flipped[...], gpre[slot][...])
            emit(weights[:width], f, "xy")
            small_ref[pl.ds(f, 1), pl.ds(0, width)] = weights[width : width + 1]

    for f in range(chunks):
        in_copies[f].wait()
        out_copies[f].wait()
        bias = b_in_ref[...].reshape(1, hidden_width)[:, f * width : (f + 1) * width]
        for c in range(groups):
            lanes = pl.ds(c * GROUP, GROUP)
            pre = dot(normed[...], win[f % HELD, :, lanes]) + bias[:, c * GROUP : (c + 1) * GROUP]
            back = dot(grow[...], wout[f % HELD, lanes, :], 1, 1)
            if f > 0:
                chunk_results(f - 1, c)
            hidden, grad_pre = gelu_pair(pre, back)
            hid[f % 2][:, lanes] = hidden.astype(BF16)
            gpre[f % 2][:, lanes] = grad_pre.astype(BF16)
        if 0 < f <= chunks - HELD:
            load_chunk(f - 1 + HELD)

    for hg in range(groups):
        for copy in qkv_copies[hg]:
            copy.wait()
        if hg == 0:
            o_copy.wait()
        same_head = (
            lax.broadcasted_iota(jnp.int32, (GROUP, GROUP), 0) // HEAD
            == lax.broadcasted_iota(jnp.int32, (GROUP, GROUP), 1) // HEAD
        )
        average = jnp.where(same_head, 1.0 / HEAD, 0.0).astype(BF16)

        def head_mean(values, split):
            high = values.astype(BF16)
            mean = dot(high, average)
            if split:
                mean = mean + dot((values - high.astype(F32)).astype(BF16), average)
            return mean

        def head_norm(raw):
            centered = raw - head_mean(raw, True)
            inverse = lax.rsqrt(head_mean(centered * centered, False) + EPS)
            return centered * inverse, inverse

        q_gain = jnp.concatenate([q_gain_ref[...].reshape(1, HEAD)] * (GROUP // HEAD), axis=1)
        k_gain = jnp.concatenate([k_gain_ref[...].reshape(1, HEAD)] * (GROUP // HEAD), axis=1)
        b_qkv = b_qkv_ref[...].reshape(1, 3 * width)
        bias_q, bias_k, bias_v = (
            b_qkv[:, t * width + hg * GROUP : t * width + (hg + 1) * GROUP] for t in range(3)
        )
        gproj = gpre[hg % 2]
        if hg == 0:
            chunk_results(chunks - 1, 0)
            token_copy = load(tokens_hbm, tok, 0)
        if hg == groups - 1:
            cot_copy = load(cot_hbm, cot, 1)
        raw = dot(normed[...], wqkv[hg, :, pl.ds(0, GROUP)]) + bias_q
        unit, inverse = head_norm(raw)
        nq[...] = unit
        rq[...] = inverse
        qs[...] = (unit * q_gain).astype(BF16) * SCALE
        raw = dot(normed[...], wqkv[hg, :, pl.ds(GROUP, GROUP)]) + bias_k
        unit, inverse = head_norm(raw)
        nk[...] = unit
        rk[...] = inverse
        ks[pl.ds(0, rows), :] = (unit * k_gain).astype(BF16)
        raw = dot(normed[...], wqkv[hg, :, pl.ds(2 * GROUP, GROUP)]) + bias_v
        vs[pl.ds(0, rows), :] = raw.astype(BF16)
        gm[...] = dot(grow[...], wo[pl.ds(hg * GROUP, GROUP), :], 1, 1).astype(BF16)
        if hg == 0:
            ks[pl.ds(rows, KEYS - SLOT), :] = jnp.zeros((KEYS - SLOT, GROUP), BF16)
            vs[pl.ds(rows, KEYS - SLOT), :] = jnp.zeros((KEYS - SLOT, GROUP), BF16)

        lane = lax.broadcasted_iota(jnp.int32, (1, KEYS), 1)
        first_head = jnp.where(lane < HEAD, 1.0, 0.0).astype(BF16)
        second_head = jnp.where(lane < HEAD, 0.0, 1.0).astype(BF16)

        def two_heads(block):
            return jnp.concatenate([block * first_head, block * second_head], axis=0)

        def side_by_side(block):
            return jnp.concatenate([block[:SLOT], block[SLOT:]], axis=1)

        def one_image(image):
            start = pl.multiple_of(image * SLOT, 16)
            span = pl.ds(start, SLOT)
            window = pl.ds(start, KEYS)
            count = lengths_ref[base + image // IMAGES, lax.rem(image, IMAGES)]
            seen = lane < count
            for pair in range(GROUP // KEYS):
                lanes = pl.ds(pair * KEYS, KEYS)
                query = two_heads(qs[span, lanes])
                grad = two_heads(gm[span, lanes])
                key, value = ks[window, lanes], vs[window, lanes]
                weight = jnp.where(seen, jnp.exp(dot(query, key, 1, 1)), 0.0)
                probs = weight / jnp.sum(weight, axis=1, keepdims=True)
                grad_probs = dot(grad, value, 1, 1)
                inner = jnp.sum(probs * grad_probs, axis=1, keepdims=True)
                grad_scores = (probs * (grad_probs - inner)).astype(BF16)
                probs_low = probs.astype(BF16)
                mixed[span, pl.ds(hg * GROUP + pair * KEYS, KEYS)] = dot(
                    side_by_side(probs_low), two_heads(value)
                ).astype(BF16)
                dq[span, lanes] = dot(side_by_side(grad_scores), two_heads(key)) * SCALE
                dk[span, lanes] = dot(grad_scores, query, 0, 0)[:SLOT]
                gproj[span, pl.ds(2 * GROUP + pair * KEYS, KEYS)] = dot(probs_low, grad, 0, 0)[
                    :SLOT
                ].astype(BF16)

        def two_images(step, carry):
            one_image(2 * step)
            one_image(2 * step + 1)
            return carry

        if hg == 0:
            chunk_results(chunks - 1, 1)
        lax.fori_loop(0, images // 4, two_images, 0)
        if hg == 0:
            chunk_results(chunks - 1, 2)
        lax.fori_loop(images // 4, images // 2, two_images, 0)
        if hg == groups - 1:
            flip(mixed, turned)
            emit(dot(turned[...], grow[...]), chunks + groups, "yx")

        gain_sums = []
        for side, (grad_ref, unit_ref, inverse_ref, gain) in enumerate(
            ((dq, nq, rq, q_gain), (dk, nk, rk, k_gain))
        ):
            grad, unit = grad_ref[...], unit_ref[...]
            gain_sums.append(jnp.sum(grad * unit, axis=0, keepdims=True))
            grad = grad * gain
            back = grad - head_mean(grad, True) - unit * head_mean(grad * unit, False)
            gproj[:, pl.ds(side * GROUP, GROUP)] = (back * inverse_ref[...]).astype(BF16)
        for side in range(2):
            small_ref[pl.ds(3 + side, 1), pl.ds(width, GROUP)] += gain_sums[side]
        weights = dot(flipped[...], gproj[...])
        emit(weights[:width], chunks + hg, "xy" if hg % 2 == 0 else "yx")
        small_ref[pl.ds(4 + hg, 1), pl.ds(0, width)] = weights[width : width + 1]
        for part in range(groups):
            lanes = pl.ds(part * GROUP, GROUP)
            gnorm[:, lanes] += dot(gproj[...], wqkv[hg, lanes, :], 1, 1)

    ln_gain = ln_gain_ref[...].reshape(1, width)
    b_o = b_o_ref[...].reshape(1, width)
    b_out = b_out_ref[...].reshape(1, width)
    gain_grad = jnp.zeros((1, width), F32)
    for s in range(seqs):
        span = pl.ds(s * SEQ, SEQ)
        unit, inverse = row_stats(packed[span, :].astype(F32))
        grad = gnorm[span, :]
        gain_grad = gain_grad + jnp.sum(grad * unit, axis=0, keepdims=True)
        grad = grad * ln_gain
        back = grad - jnp.mean(grad, axis=1, keepdims=True)
        back = (back - unit * jnp.mean(grad * unit, axis=1, keepdims=True)) * inverse
        normed[span, :] = (grow[span, :].astype(F32) + back).astype(BF16)
    for t in range(width // GROUP):
        small_ref[pl.ds(t, 1), pl.ds(width, GROUP)] = gain_grad[:, t * GROUP : (t + 1) * GROUP]
    finals = []
    token_copy.wait()
    cot_copy.wait()
    for s in range(seqs):
        span = pl.ds(s * SEQ, SEQ)
        place = position_slots(lens[s])
        put = one_hot(place)
        padding = jnp.where(place < 0, 1.0, 0.0)
        attended = (dot(mixed[span, :], wo[...]) + b_o).astype(BF16).astype(F32)
        fed_here = (fed[span, :] + b_out).astype(BF16).astype(F32)
        result = (packed[span, :].astype(F32) + (attended + fed_here)).astype(BF16)
        tok[span, :] = (dot(put, result) + padding * tok[span, :].astype(F32)).astype(BF16)
        finals.append(
            pltpu.make_async_copy(tok.at[span], output_hbm.at[span], done_sem.at[2 * s])
        )
        finals[-1].start()
        grads = dot(put, normed[span, :]) + padding * cot[span, :].astype(F32)
        cot[span, :] = grads.astype(BF16)
        finals.append(
            pltpu.make_async_copy(cot.at[span], grad_tokens_hbm.at[span], done_sem.at[2 * s + 1])
        )
        finals[-1].start()
    finals.append(pltpu.make_async_copy(small_ref, small_hbm, done_sem.at[2 * seqs + 1]))
    finals[-1].start()
    for copy in sent[-2:] + finals:
        copy.wait()


def exchange_kernel(plan, chunks, pieces_hbm, small, fin_hbm, small_hbm, own_small, fin, *refs):
    done_sem, refs = refs[-1], refs[:-1]
    own_small[...] = small[...]
    net = Exchange((pieces_hbm,) + refs[:9] + (fin, own_small) + refs[9:], chunks)
    net.greet()
    for shard, order in plan:
        net.start(shard, order)
    net.start_small()
    net.drain()
    copies = [
        pltpu.make_async_copy(fin, fin_hbm, done_sem.at[0]),
        pltpu.make_async_copy(own_small, small_hbm, done_sem.at[1]),
    ]
    for copy in copies:
        copy.start()
    for copy in copies:
        copy.wait()


def split_lanes(block, groups):
    width = block.shape[1] // 3
    return jnp.concatenate(
        [
            block[:, hg * width + t * GROUP : hg * width + (t + 1) * GROUP]
            for t in range(3)
            for hg in range(groups)
        ],
        axis=1,
    )


def fold_heads(gains):
    return sum(gains[:, h * HEAD : (h + 1) * HEAD] for h in range(GROUP // HEAD))


def small_parts(small, chunks, groups, width):
    b_in = jnp.concatenate([small[f : f + 1, :width] for f in range(chunks)], axis=1)
    b_qkv = jnp.concatenate([small[4 + hg : 5 + hg, :width] for hg in range(groups)], axis=1)
    ln = jnp.concatenate([small[t : t + 1, width:] for t in range(width // GROUP)], axis=1)
    gains = [fold_heads(small[3 + side : 4 + side, width:]) for side in range(2)]
    return ln, split_lanes(b_qkv, groups), gains[0], gains[1], small[7:8, :width], b_in


def finish_kernel(
    fin, small, g_ln, g_qkv, g_b_qkv, g_q, g_k, g_o, g_b_o, g_in, g_b_in, g_out, g_b_out
):
    width = g_o.shape[1]
    half = width // 2
    chunks, groups = g_in.shape[1] // width, width // GROUP

    def whole(shard):
        return jnp.concatenate([fin[side, shard].astype(F32) for side in range(2)], axis=1)

    for f in range(chunks):
        g_in[:, f * width : (f + 1) * width] = whole(f)
    qkv = jnp.concatenate([whole(chunks + hg) for hg in range(groups)], axis=1)
    g_qkv[...] = split_lanes(qkv, groups)
    g_o[...] = whole(chunks + groups)
    for j in range(4):
        g_out[j * BLOCK : (j + 1) * BLOCK, :] = whole(chunks + groups + 1 + j)
    ln, b_qkv, q, k, b_out, b_in = small_parts(small[...], chunks, groups, width)
    for ref, value in (
        (g_ln, ln), (g_b_qkv, b_qkv), (g_q, q), (g_k, k), (g_b_o, b_out), (g_b_in, b_in), (g_b_out, b_out)
    ):
        ref[...] = value.reshape(value.shape[1])


def local(n_dp, tokens, lengths, cotangent, ln_gain, w_qkv, b_qkv, q_gain, k_gain, w_o, b_o, w_in, b_in, w_out, b_out):
    rows, width = tokens.shape
    hidden_width = w_in.shape[1]
    chunks = hidden_width // width
    groups = width // GROUP
    seqs = rows // SEQ
    shards = chunks + groups + 1
    pieces_in_all = shards + chunks
    wired = n_dp * BLOCK == width and n_dp == 4 * chunks
    anywhere = pl.BlockSpec(memory_space=pl.ANY)
    vmem = pl.BlockSpec(memory_space=pltpu.VMEM)
    wide = lambda *shape: pltpu.VMEM(shape, F32)
    slim = lambda *shape: pltpu.VMEM(shape, BF16)
    extra = KEYS - SLOT
    half = width // 2
    if wired:
        pieces_shape = (pieces_in_all, 2, 16, BLOCK, half)
        stage = slim(2, 2, 16, BLOCK, half)
    else:
        pieces_shape = (pieces_in_all, width, width)
        stage = slim(2, width, width)
    plan = []
    output, grad_tokens, pieces, small = pl.pallas_call(
        functools.partial(layer_kernel, wired, plan),
        out_shape=(
            jax.ShapeDtypeStruct(tokens.shape, BF16),
            jax.ShapeDtypeStruct(tokens.shape, BF16),
            jax.ShapeDtypeStruct(pieces_shape, BF16),
            jax.ShapeDtypeStruct((8, width + GROUP), F32),
        ),
        in_specs=[
            pl.BlockSpec(memory_space=pltpu.SMEM), anywhere, anywhere, vmem, anywhere, vmem, vmem, vmem,
            anywhere, vmem, anywhere, vmem, anywhere, vmem,
        ],
        out_specs=(anywhere, anywhere, anywhere, anywhere),
        scratch_shapes=[
            slim(groups, width, width), slim(width, width), slim(HELD, width, width),
            slim(HELD, width, width), slim(rows, width), slim(rows, width), slim(rows, width),
            slim(rows, width), slim(rows, width), slim(width + 16, rows), slim(rows, width),
            slim(rows, width), wide(rows, width), wide(rows, width), slim(rows, GROUP),
            slim(rows + extra, GROUP), slim(rows + extra, GROUP), slim(rows, GROUP),
            wide(rows, GROUP), wide(rows, GROUP), wide(rows, GROUP), wide(rows, GROUP),
            wide(rows, GROUP), wide(rows, GROUP), wide(8, width + GROUP), slim(width, rows),
            pltpu.SemaphoreType.DMA((3 + 2 * chunks + 3 * groups,)),
            pltpu.SemaphoreType.DMA((2 * seqs + 2,)), stage, pltpu.SemaphoreType.DMA((2,)),
        ],
        compiler_params=pltpu.CompilerParams(vmem_limit_bytes=60 << 20),
    )(
        lengths, tokens, cotangent, ln_gain, w_qkv, b_qkv, q_gain, k_gain,
        w_o, b_o, w_in, b_in, w_out, b_out,
    )
    if wired:
        shape = lambda *dims: jax.ShapeDtypeStruct(dims, F32)
        flights = 6 * shards + 3 * chunks + 3 + 5
        fin, small = pl.pallas_call(
            functools.partial(exchange_kernel, tuple(plan), chunks),
            out_shape=(
                jax.ShapeDtypeStruct((2, shards + 4, BLOCK, half), BF16), shape(8, width + GROUP)
            ),
            in_specs=[anywhere, vmem],
            out_specs=(anywhere, anywhere),
            scratch_shapes=[
                wide(8, width + GROUP), slim(2, shards + 4, BLOCK, half),
                slim(pieces_in_all, 16, BLOCK, half), slim(pieces_in_all, 16, BLOCK, half),
                slim(pieces_in_all, 8, BLOCK, half), slim(pieces_in_all, 4, BLOCK, half),
                slim(shards, 2, BLOCK, half), slim(shards, 1, BLOCK, half), slim(4, 4, BLOCK, half),
                slim(2, 4, BLOCK, half), slim(1, 4, BLOCK, half), wide(5, 8, width + GROUP),
                pltpu.SemaphoreType.DMA((pieces_in_all,)), pltpu.SemaphoreType.DMA((flights,)),
                pltpu.SemaphoreType.DMA((flights,)), pltpu.SemaphoreType.DMA((2,)),
            ],
            compiler_params=pltpu.CompilerParams(
                vmem_limit_bytes=48 << 20, collective_id=0, has_side_effects=True
            ),
        )(pieces, small)
        grads = pl.pallas_call(
            finish_kernel,
            out_shape=(
                shape(width), shape(BLOCK, 3 * width), shape(3 * width), shape(HEAD), shape(HEAD),
                shape(BLOCK, width), shape(width), shape(BLOCK, hidden_width), shape(hidden_width),
                shape(4 * BLOCK, width), shape(width),
            ),
            in_specs=[vmem, vmem],
            out_specs=(vmem,) * 11,
        )(fin, small)
        return (output, grad_tokens) + tuple(grads)

    def scatter(block, dim):
        part = lax.psum_scatter(block, "dp", scatter_dimension=dim, tiled=True)
        return lax.psum(part, "branch").astype(F32)

    grad_out = scatter(pieces[shards:].reshape(hidden_width, width), 0)
    reduced = scatter(pieces[:shards], 1)
    grad_in = jnp.concatenate([reduced[f] for f in range(chunks)], axis=1)
    qkv = jnp.concatenate([reduced[chunks + hg] for hg in range(groups)], axis=1)
    small = lax.psum(small, ("dp", "branch"))
    ln, g_b_qkv, g_q, g_k, g_b_out, g_b_in = (
        part[0] for part in small_parts(small, chunks, groups, width)
    )
    return (
        output, grad_tokens, ln, split_lanes(qkv, groups), g_b_qkv, g_q, g_k,
        reduced[chunks + groups], g_b_out, grad_in, g_b_in, grad_out, g_b_out,
    )


def solution(mesh):
    rows, split, whole = P(("dp", "branch"), None), P("dp", None), P()
    return jax.shard_map(
        functools.partial(local, mesh.shape["dp"]),
        mesh=mesh,
        in_specs=(rows, split, rows) + (whole,) * 11,
        out_specs=(
            rows, rows, whole, split, whole, whole, whole, split, whole, split, whole, split, whole,
        ),
        check_vma=False,
    )
```

```python
import functools
import math

import jax
import jax.numpy as jnp
from jax import lax
from jax.experimental import pallas as pl
from jax.experimental.pallas import tpu as pltpu
from jax.sharding import PartitionSpec as P

HEAD = 64
SEQ = 448
IMAGES = 4
SLOT = SEQ // IMAGES
KEYS = 128
GROUP = 256
EPS = 1e-06
SCALE = 0.125
F32 = jnp.float32
BF16 = jnp.bfloat16
GELU_A = math.sqrt(2.0 / math.pi)
GELU_B = 0.044715


def dot(left, right, left_dim=1, right_dim=0):
    return lax.dot_general(
        left, right, (((left_dim,), (right_dim,)), ((), ())), preferred_element_type=F32
    )


def slot_positions(lens):
    row = lax.broadcasted_iota(jnp.int32, (SEQ, 1), 0)
    held = jnp.full((SEQ, 1), -1, jnp.int32)
    start = jnp.int32(0)
    for image in range(IMAGES):
        place = row - SLOT * image
        held = jnp.where((place >= 0) & (place < lens[image]), place + start, held)
        start = start + lens[image]
    return held


def position_slots(lens):
    row = lax.broadcasted_iota(jnp.int32, (SEQ, 1), 0)
    held = jnp.full((SEQ, 1), -1, jnp.int32)
    start = jnp.int32(0)
    for image in range(IMAGES):
        place = row - start
        held = jnp.where((place >= 0) & (place < lens[image]), place + SLOT * image, held)
        start = start + lens[image]
    return held


def one_hot(index):
    lanes = lax.broadcasted_iota(jnp.int32, (SEQ, SEQ), 1)
    return jnp.where(lanes == index, 1.0, 0.0).astype(BF16)


def row_stats(values):
    centered = values - jnp.mean(values, axis=1, keepdims=True)
    spread = jnp.mean(centered * centered, axis=1, keepdims=True)
    inverse = lax.rsqrt(spread + EPS)
    return centered * inverse, inverse


def gelu_pair(pre, grad):
    square = pre * pre
    bent = jnp.tanh(pre * (GELU_A + (GELU_A * GELU_B) * square))
    half = 0.5 * pre
    up = 1.0 + bent
    hidden = half * up
    slope = half * (GELU_A + (3.0 * GELU_A * GELU_B) * square)
    return hidden, (up * (0.5 + (1.0 - bent) * slope)) * grad


MESH = pl.DeviceIdType.MESH
BLOCK = 48
SLOTS = 4
XY, YX = ("x", "y", "z0", "z1"), ("y", "x", "z0", "z1")
ZX, ZY = ("z0", "z1", "x", "y"), ("z0", "z1", "y", "x")
RATES = {"core": 200e3, "x": 42e3, "y": 42e3, "z0": 42e3, "z1": 21e3}
LATENCY = 1.5


class Piece:
    def __init__(self, index, shard, axes):
        self.index, self.shard, self.axes = index, shard, axes
        self.stage, self.copy, self.eta, self.own = 0, None, 0.0, None


class Small:
    def __init__(self):
        self.stage, self.copy, self.eta = 0, None, 0.0


class Exchange:
    def __init__(self, refs, chunks):
        (self.both, self.inbox, self.in1, self.in2, self.in3, self.in4, self.osum, self.oin3,
         self.oin4, self.fin, self.small, self.small_in, self.own_sem, self.send_sem,
         self.recv_sem) = refs
        self.chunks = chunks
        self.dp, self.core = lax.axis_index("dp"), lax.axis_index("branch")
        self.bits = {
            "x": lax.rem(self.dp, 2),
            "y": lax.rem(self.dp // 2, 2),
            "z0": lax.rem(self.dp // 4, 2),
            "z1": lax.rem(self.dp // 8, 2),
        }
        self.far = {
            axis: (self.dp + step - 2 * step * self.bits[axis], self.core)
            for axis, step in (("x", 1), ("y", 2), ("z0", 4), ("z1", 8))
        }
        self.far["core"] = (self.dp, 1 - self.core)
        self.pieces, self.items, self.parked = [], [], []
        self.flights, self.merged, self.now, self.free = 0, 0, 0.0, {}

    def greet(self):
        barrier = pltpu.get_barrier_semaphore()
        for device in self.far.values():
            pl.semaphore_signal(barrier, inc=1, device_id=device, device_id_type=MESH)
        pl.semaphore_wait(barrier, len(self.far))

    def send(self, item, source, target, axis):
        copy = pltpu.make_async_remote_copy(
            src_ref=source, dst_ref=target, send_sem=self.send_sem.at[self.flights],
            recv_sem=self.recv_sem.at[self.flights], device_id=self.far[axis], device_id_type=MESH,
        )
        self.flights += 1
        copy.start()
        link = axis[0]
        size = source.dtype.itemsize * math.prod(source.shape)
        self.free[link] = max(self.free.get(link, 0.0), self.now) + size / RATES[axis]
        item.copy, item.eta = copy, self.free[link] + LATENCY

    def fetch_own(self, piece):
        k = piece.index
        piece.own = pltpu.make_async_copy(
            self.parked[k].at[self.core], self.both.at[k % SLOTS, 0], self.own_sem.at[k]
        )
        piece.own.start()

    def start_parked(self, source, shard, axes):
        piece = Piece(len(self.pieces), shard, axes)
        self.parked.append(source)
        if piece.index < SLOTS:
            self.fetch_own(piece)
        self.send(piece, source.at[1 - self.core], self.inbox.at[piece.index], "core")
        self.pieces.append(piece)
        self.items.append(piece)

    def start(self, value, shard, axes):
        piece = Piece(len(self.pieces), shard, axes)
        while self.pieces[piece.index - SLOTS].stage == 0:
            self.advance(min(self.under_way(), key=lambda item: item.eta))
        slot = piece.index % SLOTS
        for side, role in ((0, self.core), (1, 1 - self.core)):
            put_blocks(value, self.both.at[slot, role], side, axes)
        self.send(piece, self.both.at[slot, 1], self.inbox.at[piece.index], "core")
        self.pieces.append(piece)
        self.items.append(piece)

    def halve(self, piece, held, held_at, arrived, count, axis, target):
        near = self.bits[axis] * count
        away = (1 - self.bits[axis]) * count
        span = pl.ds(away, count)
        arrived[span] = arrived[span] + held[pl.ds(held_at + away, count)]
        self.send(piece, arrived.at[span], target, axis)
        span = pl.ds(near, count)
        arrived[span] = arrived[span] + held[pl.ds(held_at + near, count)]

    def advance(self, piece):
        piece.copy.wait()
        self.now = max(self.now, piece.eta)
        piece.copy = None
        if isinstance(piece, Small):
            self.advance_small(piece)
            return
        k, shard, axes = piece.index, piece.shard, piece.axes
        whole = isinstance(shard, int)
        if piece.stage == 0:
            if piece.own is not None:
                piece.own.wait()
            own, arrived = self.both.at[k % SLOTS, 0], self.inbox.at[k]
            self.halve(piece, own, 0, arrived, 8, axes[0], self.in1.at[k])
            if k + SLOTS < len(self.parked):
                self.fetch_own(self.pieces[k + SLOTS])
        elif piece.stage == 1:
            self.halve(
                piece, self.inbox.at[k], self.bits[axes[0]] * 8, self.in1.at[k], 4, axes[1],
                self.in2.at[k],
            )
        elif piece.stage == 2 and whole:
            self.halve(
                piece, self.in1.at[k], self.bits[axes[1]] * 4, self.in2.at[k], 2, axes[2],
                self.in3.at[shard],
            )
        elif piece.stage == 2:
            place = shard[0] % 2 * 2 + shard[0] // 2
            self.osum[place] = self.in2[k] + self.in1[k, pl.ds(self.bits[axes[1]] * 4, 4)]
            self.merged += 1
            if self.merged < self.chunks:
                piece.stage = 5
            else:
                far = pl.ds((1 - self.bits["z0"]) * 2, 2)
                self.send(piece, self.osum.at[far], self.oin3, "z0")
        elif piece.stage == 3 and whole:
            self.halve(
                piece, self.in2.at[k], self.bits[axes[2]] * 2, self.in3.at[shard], 1, axes[3],
                self.in4.at[shard],
            )
        elif piece.stage == 3:
            self.halve(piece, self.osum, self.bits["z0"] * 2, self.oin3, 1, "z1", self.oin4)
        elif piece.stage == 4:
            if whole:
                final = self.fin.at[self.core, pl.ds(shard, 1)]
                final[...] = self.in4[shard] + self.in3[shard, pl.ds(self.bits[axes[3]], 1)]
            else:
                final = self.fin.at[self.core, pl.ds(self.fin.shape[1] - 4, 4)]
                final[...] = self.oin4[0] + self.oin3[self.bits["z1"]]
            self.send(piece, final, final, "core")
        piece.stage += 1

    def start_small(self):
        item = Small()
        self.send(item, self.small, self.small_in.at[0], "core")
        self.items.append(item)

    def advance_small(self, item):
        self.small[...] = self.small[...] + self.small_in[item.stage]
        item.stage += 1
        if item.stage < 5:
            axis = ("core", "x", "y", "z0", "z1")[item.stage]
            self.send(item, self.small, self.small_in.at[item.stage], axis)

    def under_way(self):
        return [item for item in self.items if item.copy is not None]

    def progress(self, cost):
        self.now += cost
        while True:
            due = [item for item in self.under_way() if item.eta <= self.now]
            if not due:
                return
            self.advance(min(due, key=lambda item: item.eta))

    def drain(self):
        while self.under_way():
            self.advance(min(self.under_way(), key=lambda item: item.eta))


def put_blocks(value, target, side, axes):
    half = value.shape[1] // 2
    for block in range(16):
        place = block
        if axes is not None and len(axes) == 4:
            bit = dict(x=block % 2, y=block // 2 % 2, z0=block // 4 % 2, z1=block // 8)
            place = sum(bit[axis] << (3 - i) for i, axis in enumerate(axes))
        target[place] = value[
            BLOCK * block : BLOCK * (block + 1), half * side : half * (side + 1)
        ].astype(BF16)


def make_flip():
    eye = jnp.where(
        lax.broadcasted_iota(jnp.int32, (GROUP, GROUP), 0)
        == lax.broadcasted_iota(jnp.int32, (GROUP, GROUP), 1),
        1.0,
        0.0,
    ).astype(BF16)

    def flip(source, target):
        for part in range(source.shape[1] // GROUP):
            lanes = pl.ds(part * GROUP, GROUP)
            target[lanes, :] = dot(eye, source[:, lanes], 1, 1).astype(BF16)

    return flip


class Parking:
    def __init__(self, wired, stage, target, sem):
        self.wired, self.stage, self.target, self.sem = wired, stage, target, sem
        self.sent = []

    def put(self, value, index, axes):
        slot = len(self.sent) % 2
        if len(self.sent) >= 2:
            self.sent[-2].wait()
        if self.wired:
            for side in range(2):
                put_blocks(value, self.stage.at[slot, side], side, axes)
        else:
            self.stage[slot] = value.astype(BF16)
        copy = pltpu.make_async_copy(self.stage.at[slot], self.target.at[index], self.sem.at[slot])
        copy.start()
        self.sent.append(copy)

    def finish(self):
        for copy in self.sent[-2:]:
            copy.wait()


def w_in_axes(f):
    return ZX if f == 1 else XY


def mlp_kernel(
    wired, lengths_ref, tokens_hbm, cot_hbm, ln_gain_ref, w_in_hbm, b_in_ref, w_out_hbm, b_out_ref,
    normed_hbm, flipped_hbm, packed_hbm, grow_hbm, fed_hbm, gnorm_hbm, pieces_hbm, small_ref,
    win, wout, tok, cot, packed, grow, normed, flipped, turned, hid, gpre, fed, gnorm, stage,
    load_sem, store_sem, piece_sem,
):
    rows, width = tok.shape
    hidden_width = w_in_hbm.shape[1]
    chunks = hidden_width // width
    groups = width // GROUP
    seqs = rows // SEQ
    base = lax.axis_index("branch") * seqs
    stores = []

    def load(source, target, slot):
        copy = pltpu.make_async_copy(source, target, load_sem.at[slot])
        copy.start()
        return copy

    def store(source, target):
        copy = pltpu.make_async_copy(source, target, store_sem.at[len(stores)])
        copy.start()
        stores.append(copy)

    token_copy = load(tokens_hbm, tok, 0)
    cot_copy = load(cot_hbm, cot, 1)
    in_copies, out_copies = [], []
    for f in range(chunks):
        cols = pl.ds(f * width, width)
        in_copies.append(load(w_in_hbm.at[:, cols], win.at[:, cols], 2 + 2 * f))
        out_copies.append(load(w_out_hbm.at[cols, :], wout.at[cols, :], 3 + 2 * f))
    parking = Parking(wired, stage, pieces_hbm, piece_sem)
    small_ref[...] = jnp.zeros_like(small_ref)
    ones_row = jnp.where(lax.broadcasted_iota(jnp.int32, (16, rows), 0) == 0, 1.0, 0.0)
    flipped[pl.ds(width, 16), :] = ones_row.astype(BF16)
    flip = make_flip()

    token_copy.wait()
    cot_copy.wait()
    grad_sum = jnp.zeros((1, width), F32)
    for s in range(seqs):
        span = pl.ds(s * SEQ, SEQ)
        pick = one_hot(slot_positions([lengths_ref[base + s, j] for j in range(IMAGES)]))
        rows_here = dot(pick, tok[span, :])
        packed[span, :] = rows_here.astype(BF16)
        unit, _ = row_stats(rows_here)
        normed[span, :] = (unit * ln_gain_ref[...].reshape(1, width)).astype(BF16)
        grads_here = dot(pick, cot[span, :])
        grow[span, :] = grads_here.astype(BF16)
        grad_sum = grad_sum + jnp.sum(grads_here, axis=0, keepdims=True)
    small_ref[pl.ds(7, 1), pl.ds(0, width)] = grad_sum
    flip(normed, flipped)
    for source, target in (
        (normed, normed_hbm), (flipped, flipped_hbm), (packed, packed_hbm), (grow, grow_hbm)
    ):
        store(source, target)

    def chunk_grads(f, step):
        cols = pl.ds(f * width, width)
        if step == 0:
            flip(hid.at[:, cols], turned)
        elif step == 1:
            parking.put(dot(turned[...], grow[...]), chunks + f, None)
        else:
            weights = dot(flipped[...], gpre[:, cols])
            parking.put(weights[:width], f, w_in_axes(f))
            small_ref[pl.ds(f, 1), pl.ds(0, width)] = weights[width : width + 1]

    b_in = b_in_ref[...].reshape(1, hidden_width)
    for f in range(chunks):
        in_copies[f].wait()
        out_copies[f].wait()
        for c in range(groups):
            place = f * width + c * GROUP
            lanes = pl.ds(place, GROUP)
            pre = dot(normed[...], win[:, lanes]) + b_in[:, place : place + GROUP]
            back = dot(grow[...], wout[lanes, :], 1, 1)
            if f > 0:
                chunk_grads(f - 1, c)
            hidden, grad_pre = gelu_pair(pre, back)
            hid[:, lanes] = hidden.astype(BF16)
            gpre[:, lanes] = grad_pre.astype(BF16)
    for step in range(3):
        chunk_grads(chunks - 1, step)
    b_out = b_out_ref[...].reshape(1, width)
    for part in range(groups):
        lanes = pl.ds(part * GROUP, GROUP)
        up = dot(hid[...], wout[:, lanes]) + b_out[:, part * GROUP : (part + 1) * GROUP]
        fed[:, lanes] = up.astype(BF16)
        gnorm[:, lanes] = dot(gpre[...], win[lanes, :], 1, 1)
    store(fed, fed_hbm)
    store(gnorm, gnorm_hbm)
    for copy in stores:
        copy.wait()
    parking.finish()


def attention_kernel(
    wired, chunks,
    lengths_ref, tokens_hbm, cot_hbm, normed_hbm, flipped_hbm, packed_hbm, grow_hbm, fed_hbm,
    gnorm_hbm, mlp_hbm, mlp_small, ln_gain_ref, w_qkv_hbm, b_qkv_ref, q_gain_ref, k_gain_ref,
    w_o_hbm, b_o_ref,
    output_hbm, grad_tokens_hbm, pieces_hbm, small_hbm,
    wqkv, wo, tok, cot, packed, grow, normed, flipped, fed, gnorm, gprojs, mixed, turned,
    qs, ks, vs, gm, nq, nk, rq, rk, dq, dk, small_ref, load_sem, done_sem, *refs,
):
    rows, width = tok.shape
    groups = width // GROUP
    seqs = rows // SEQ
    images = seqs * IMAGES
    base = lax.axis_index("branch") * seqs
    loads = {}

    def load(name, source, target):
        copy = pltpu.make_async_copy(source, target, load_sem.at[len(loads)])
        copy.start()
        loads[name] = copy

    load("normed", normed_hbm, normed)
    for hg in range(groups):
        for t in range(3):
            load(
                (hg, t),
                w_qkv_hbm.at[:, pl.ds(t * width + hg * GROUP, GROUP)],
                wqkv.at[hg, :, pl.ds(t * GROUP, GROUP)],
            )
        if hg == 0:
            load("grow", grow_hbm, grow)
            load("wo", w_o_hbm, wo)
            load("flipped", flipped_hbm, flipped)
    for name, source, target in (
        ("gnorm", gnorm_hbm, gnorm), ("packed", packed_hbm, packed), ("fed", fed_hbm, fed),
        ("tok", tokens_hbm, tok), ("cot", cot_hbm, cot),
    ):
        load(name, source, target)

    small_ref[...] = mlp_small[...]
    net, parking = None, None
    if wired:
        net = Exchange(refs[:10] + (small_ref,) + refs[10:], chunks)
        net.greet()
        for f in range(chunks):
            net.start_parked(mlp_hbm.at[f], f, w_in_axes(f))
            net.start_parked(mlp_hbm.at[chunks + f], (f,), YX[:2])
    else:
        parking = Parking(False, refs[0], pieces_hbm, refs[1])

    def emit(value, index, axes):
        if wired:
            net.start(value, chunks + index, axes)
        else:
            parking.put(value, index, axes)

    def point(cost):
        if wired:
            net.progress(cost)

    flip = make_flip()
    same_head = (
        lax.broadcasted_iota(jnp.int32, (GROUP, GROUP), 0) // HEAD
        == lax.broadcasted_iota(jnp.int32, (GROUP, GROUP), 1) // HEAD
    )
    average = jnp.where(same_head, 1.0 / HEAD, 0.0).astype(BF16)
    q_gain = jnp.concatenate([q_gain_ref[...].reshape(1, HEAD)] * (GROUP // HEAD), axis=1)
    k_gain = jnp.concatenate([k_gain_ref[...].reshape(1, HEAD)] * (GROUP // HEAD), axis=1)
    b_qkv = b_qkv_ref[...].reshape(1, 3 * width)
    lane = lax.broadcasted_iota(jnp.int32, (1, KEYS), 1)
    first_head = jnp.where(lane < HEAD, 1.0, 0.0).astype(BF16)
    second_head = jnp.where(lane < HEAD, 0.0, 1.0).astype(BF16)

    def head_mean(values, split):
        high = values.astype(BF16)
        mean = dot(high, average)
        if split:
            mean = mean + dot((values - high.astype(F32)).astype(BF16), average)
        return mean

    def head_norm(raw):
        centered = raw - head_mean(raw, True)
        inverse = lax.rsqrt(head_mean(centered * centered, False) + EPS)
        return centered * inverse, inverse

    def two_heads(block):
        return jnp.concatenate([block * first_head, block * second_head], axis=0)

    def side_by_side(block):
        return jnp.concatenate([block[:SLOT], block[SLOT:]], axis=1)

    ks[pl.ds(rows, KEYS - SLOT), :] = jnp.zeros((KEYS - SLOT, GROUP), BF16)
    vs[pl.ds(rows, KEYS - SLOT), :] = jnp.zeros((KEYS - SLOT, GROUP), BF16)

    for hg in range(groups):
        gproj = gprojs.at[hg]
        bias_q, bias_k, bias_v = (
            b_qkv[:, t * width + hg * GROUP : t * width + (hg + 1) * GROUP] for t in range(3)
        )
        if hg == 0:
            loads["normed"].wait()
        loads[hg, 0].wait()
        raw = dot(normed[...], wqkv[hg, :, pl.ds(0, GROUP)]) + bias_q
        unit, inverse = head_norm(raw)
        nq[...] = unit
        rq[...] = inverse
        qs[...] = (unit * q_gain).astype(BF16) * SCALE
        point(1.8)
        loads[hg, 1].wait()
        raw = dot(normed[...], wqkv[hg, :, pl.ds(GROUP, GROUP)]) + bias_k
        unit, inverse = head_norm(raw)
        nk[...] = unit
        rk[...] = inverse
        ks[pl.ds(0, rows), :] = (unit * k_gain).astype(BF16)
        point(1.8)
        loads[hg, 2].wait()
        if hg == 0:
            loads["grow"].wait()
            loads["wo"].wait()
        raw = dot(normed[...], wqkv[hg, :, pl.ds(2 * GROUP, GROUP)]) + bias_v
        vs[pl.ds(0, rows), :] = raw.astype(BF16)
        gm[...] = dot(grow[...], wo[pl.ds(hg * GROUP, GROUP), :], 1, 1).astype(BF16)
        point(1.8)

        def one_image(image):
            start = image * SLOT
            span = pl.ds(start, SLOT)
            window = pl.ds(start, KEYS)
            seen = lane < lengths_ref[base + image // IMAGES, image % IMAGES]
            for pair in range(GROUP // KEYS):
                lanes = pl.ds(pair * KEYS, KEYS)
                query = two_heads(qs[span, lanes])
                grad = two_heads(gm[span, lanes])
                key, value = ks[window, lanes], vs[window, lanes]
                weight = jnp.where(seen, jnp.exp(dot(query, key, 1, 1)), 0.0)
                probs = weight / jnp.sum(weight, axis=1, keepdims=True)
                grad_probs = dot(grad, value, 1, 1)
                inner = jnp.sum(probs * grad_probs, axis=1, keepdims=True)
                grad_scores = (probs * (grad_probs - inner)).astype(BF16)
                probs_low = probs.astype(BF16)
                mixed[span, pl.ds(hg * GROUP + pair * KEYS, KEYS)] = dot(
                    side_by_side(probs_low), two_heads(value)
                ).astype(BF16)
                dq[span, lanes] = dot(side_by_side(grad_scores), two_heads(key)) * SCALE
                dk[span, lanes] = dot(grad_scores, query, 0, 0)[:SLOT]
                gproj[span, pl.ds(2 * GROUP + pair * KEYS, KEYS)] = dot(probs_low, grad, 0, 0)[
                    :SLOT
                ].astype(BF16)

        for image in range(0, images, 2):
            one_image(image)
            one_image(image + 1)
            point(1.5)
        if hg == 0:
            loads["flipped"].wait()
        if hg == groups - 1:
            flip(mixed, turned)
            emit(dot(turned[...], grow[...]), groups, YX)
            point(2.5)

        gain_sums = []
        for side, (grad_ref, unit_ref, inverse_ref, gain) in enumerate(
            ((dq, nq, rq, q_gain), (dk, nk, rk, k_gain))
        ):
            grad, unit = grad_ref[...], unit_ref[...]
            gain_sums.append(jnp.sum(grad * unit, axis=0, keepdims=True))
            grad = grad * gain
            back = grad - head_mean(grad, True) - unit * head_mean(grad * unit, False)
            gproj[:, pl.ds(side * GROUP, GROUP)] = (back * inverse_ref[...]).astype(BF16)
            point(1.0)
        for side in range(2):
            small_ref[pl.ds(3 + side, 1), pl.ds(width, GROUP)] += gain_sums[side]
        weights = dot(flipped[...], gproj[...])
        emit(weights[:width], hg, (ZY, YX, XY)[hg % 3])
        small_ref[pl.ds(4 + hg, 1), pl.ds(0, width)] = weights[width : width + 1]
        point(2.2)

    loads["gnorm"].wait()
    for hg in range(groups):
        for part in range(groups):
            lanes = pl.ds(part * GROUP, GROUP)
            gnorm[:, lanes] += dot(gprojs[hg], wqkv[hg, lanes, :], 1, 1)
        point(1.9)
    ln_gain = ln_gain_ref[...].reshape(1, width)
    b_o = b_o_ref[...].reshape(1, width)
    gain_grad = jnp.zeros((1, width), F32)
    loads["packed"].wait()
    for s in range(seqs):
        span = pl.ds(s * SEQ, SEQ)
        unit, inverse = row_stats(packed[span, :].astype(F32))
        grad = gnorm[span, :]
        gain_grad = gain_grad + jnp.sum(grad * unit, axis=0, keepdims=True)
        grad = grad * ln_gain
        back = grad - jnp.mean(grad, axis=1, keepdims=True)
        back = (back - unit * jnp.mean(grad * unit, axis=1, keepdims=True)) * inverse
        normed[span, :] = (grow[span, :].astype(F32) + back).astype(BF16)
    for t in range(width // GROUP):
        small_ref[pl.ds(t, 1), pl.ds(width, GROUP)] = gain_grad[:, t * GROUP : (t + 1) * GROUP]
    if wired:
        net.start_small()
    point(1.5)
    finals = []
    for name in ("tok", "cot", "fed"):
        loads[name].wait()

    def hand_over(source, target):
        copy = pltpu.make_async_copy(source, target, done_sem.at[len(finals)])
        copy.start()
        finals.append(copy)

    for s in range(seqs):
        span = pl.ds(s * SEQ, SEQ)
        place = position_slots([lengths_ref[base + s, j] for j in range(IMAGES)])
        put = one_hot(place)
        padding = jnp.where(place < 0, 1.0, 0.0)
        attended = (dot(mixed[span, :], wo[...]) + b_o).astype(BF16).astype(F32)
        result = packed[span, :].astype(F32) + (attended + fed[span, :].astype(F32))
        result = dot(put, result.astype(BF16)) + padding * tok[span, :].astype(F32)
        tok[span, :] = result.astype(BF16)
        hand_over(tok.at[span], output_hbm.at[span])
        point(1.2)
        grads = dot(put, normed[span, :]) + padding * cot[span, :].astype(F32)
        cot[span, :] = grads.astype(BF16)
        hand_over(cot.at[span], grad_tokens_hbm.at[span])
        point(0.8)
    if wired:
        net.drain()
        hand_over(net.fin, pieces_hbm)
    else:
        parking.finish()
    hand_over(small_ref, small_hbm)
    for copy in finals:
        copy.wait()


def split_lanes(block, groups):
    width = block.shape[1] // 3
    return jnp.concatenate(
        [
            block[:, hg * width + t * GROUP : hg * width + (t + 1) * GROUP]
            for t in range(3)
            for hg in range(groups)
        ],
        axis=1,
    )


def fold_heads(gains):
    return sum(gains[:, h * HEAD : (h + 1) * HEAD] for h in range(GROUP // HEAD))


def small_parts(small, chunks, groups, width):
    b_in = jnp.concatenate([small[f : f + 1, :width] for f in range(chunks)], axis=1)
    b_qkv = jnp.concatenate([small[4 + hg : 5 + hg, :width] for hg in range(groups)], axis=1)
    ln = jnp.concatenate([small[t : t + 1, width:] for t in range(width // GROUP)], axis=1)
    gains = [fold_heads(small[3 + side : 4 + side, width:]) for side in range(2)]
    return ln, split_lanes(b_qkv, groups), gains[0], gains[1], small[7:8, :width], b_in


def finish_kernel(
    rows_hbm, grads_hbm, fin_hbm, small_hbm, output_hbm, grad_tokens_hbm, g_ln, g_qkv, g_b_qkv,
    g_q, g_k, g_o, g_b_o, g_in, g_b_in, g_out, g_b_out, held, fin, small, sem,
):
    comes = [
        pltpu.make_async_copy(source, target, sem.at[0, i])
        for i, (source, target) in enumerate(
            ((rows_hbm, held.at[0]), (grads_hbm, held.at[1]), (fin_hbm, fin), (small_hbm, small))
        )
    ]
    goes = [
        pltpu.make_async_copy(held.at[i], target, sem.at[1, i])
        for i, target in enumerate((output_hbm, grad_tokens_hbm))
    ]
    for copy in comes:
        copy.start()
    width = g_o.shape[1]
    chunks, groups = g_in.shape[1] // width, width // GROUP
    for come, go in zip(comes, goes):
        come.wait()
        go.start()
    for come in comes[2:]:
        come.wait()

    def whole(shard):
        return jnp.concatenate([fin[side, shard].astype(F32) for side in range(2)], axis=1)

    for f in range(chunks):
        g_in[:, f * width : (f + 1) * width] = whole(f)
    qkv = jnp.concatenate([whole(chunks + hg) for hg in range(groups)], axis=1)
    g_qkv[...] = split_lanes(qkv, groups)
    g_o[...] = whole(chunks + groups)
    for j in range(4):
        g_out[j * BLOCK : (j + 1) * BLOCK, :] = whole(chunks + groups + 1 + j)
    ln, b_qkv, q, k, b_out, b_in = small_parts(small[...], chunks, groups, width)
    for ref, value in (
        (g_ln, ln), (g_b_qkv, b_qkv), (g_q, q), (g_k, k), (g_b_o, b_out), (g_b_in, b_in), (g_b_out, b_out)
    ):
        ref[...] = value.reshape(value.shape[1])
    for copy in goes:
        copy.wait()


def local(n_dp, tokens, lengths, cotangent, ln_gain, w_qkv, b_qkv, q_gain, k_gain, w_o, b_o, w_in, b_in, w_out, b_out):
    rows, width = tokens.shape
    hidden_width = w_in.shape[1]
    chunks = hidden_width // width
    groups = width // GROUP
    seqs = rows // SEQ
    shards = chunks + groups + 1
    everyone = shards + chunks
    wired = n_dp * BLOCK == width and n_dp == 4 * chunks
    half = width // 2
    extra = KEYS - SLOT
    anywhere = pl.BlockSpec(memory_space=pl.ANY)
    vmem = pl.BlockSpec(memory_space=pltpu.VMEM)
    smem = pl.BlockSpec(memory_space=pltpu.SMEM)
    wide = lambda *shape: pltpu.VMEM(shape, F32)
    slim = lambda *shape: pltpu.VMEM(shape, BF16)
    flags = lambda *shape: pltpu.SemaphoreType.DMA(shape)
    low = lambda *shape: jax.ShapeDtypeStruct(shape, BF16)
    full = lambda *shape: jax.ShapeDtypeStruct(shape, F32)
    small_shape = (8, width + GROUP)
    piece_shape = (2, 16, BLOCK, half) if wired else (width, width)

    normed, flipped, packed, grow, fed, gnorm, mlp_pieces, small = pl.pallas_call(
        functools.partial(mlp_kernel, wired),
        out_shape=(
            low(rows, width), low(width + 16, rows), low(rows, width), low(rows, width),
            low(rows, width), full(rows, width), low(2 * chunks, *piece_shape), full(*small_shape),
        ),
        in_specs=[smem, anywhere, anywhere, vmem, anywhere, vmem, anywhere, vmem],
        out_specs=(anywhere,) * 7 + (vmem,),
        scratch_shapes=[
            slim(width, hidden_width), slim(hidden_width, width), slim(rows, width),
            slim(rows, width), slim(rows, width), slim(rows, width), slim(rows, width),
            slim(width + 16, rows), slim(width, rows), slim(rows, hidden_width),
            slim(rows, hidden_width), slim(rows, width), wide(rows, width), slim(2, *piece_shape),
            flags(2 + 2 * chunks), flags(6), flags(2),
        ],
        compiler_params=pltpu.CompilerParams(vmem_limit_bytes=58 << 20),
    )(lengths, tokens, cotangent, ln_gain, w_in, b_in, w_out, b_out)

    if wired:
        out_piece = low(2, shards + 4, BLOCK, half)
        flights = 6 * shards + 3 * chunks + 3 + 5
        others = [
            slim(SLOTS, 2, 16, BLOCK, half), slim(everyone, 16, BLOCK, half),
            slim(everyone, 8, BLOCK, half), slim(everyone, 4, BLOCK, half),
            slim(shards, 2, BLOCK, half), slim(shards, 1, BLOCK, half), slim(4, 4, BLOCK, half),
            slim(2, 4, BLOCK, half), slim(1, 4, BLOCK, half), slim(2, shards + 4, BLOCK, half),
            wide(5, *small_shape), flags(2 * chunks), flags(flights), flags(flights),
        ]
        settings = dict(collective_id=0, has_side_effects=True)
    else:
        out_piece = low(groups + 1, width, width)
        others = [slim(2, *piece_shape), flags(2)]
        settings = {}
    output, grad_tokens, pieces, small = pl.pallas_call(
        functools.partial(attention_kernel, wired, chunks),
        out_shape=(low(rows, width), low(rows, width), out_piece, full(*small_shape)),
        in_specs=[smem] + [anywhere] * 9 + [vmem, vmem, anywhere, vmem, vmem, vmem, anywhere, vmem],
        out_specs=(anywhere,) * 4,
        scratch_shapes=[
            slim(groups, width, width), slim(width, width), slim(rows, width), slim(rows, width),
            slim(rows, width), slim(rows, width), slim(rows, width), slim(width + 16, rows),
            slim(rows, width), wide(rows, width), slim(groups, rows, width), slim(rows, width),
            slim(width, rows), slim(rows, GROUP), slim(rows + extra, GROUP),
            slim(rows + extra, GROUP), slim(rows, GROUP), wide(rows, GROUP), wide(rows, GROUP),
            wide(rows, GROUP), wide(rows, GROUP), wide(rows, GROUP), wide(rows, GROUP),
            wide(*small_shape), flags(9 + 3 * groups), flags(2 * seqs + 2),
        ]
        + others,
        compiler_params=pltpu.CompilerParams(vmem_limit_bytes=62 << 20, **settings),
    )(
        lengths, tokens, cotangent, normed, flipped, packed, grow, fed, gnorm, mlp_pieces, small,
        ln_gain, w_qkv, b_qkv, q_gain, k_gain, w_o, b_o,
    )

    if wired:
        return pl.pallas_call(
            finish_kernel,
            out_shape=(
                low(rows, width), low(rows, width), full(width), full(BLOCK, 3 * width),
                full(3 * width), full(HEAD), full(HEAD), full(BLOCK, width), full(width),
                full(BLOCK, hidden_width), full(hidden_width), full(4 * BLOCK, width), full(width),
            ),
            in_specs=[anywhere] * 4,
            out_specs=(anywhere, anywhere) + (vmem,) * 11,
            scratch_shapes=[
                slim(2, rows, width), slim(2, shards + 4, BLOCK, half), wide(*small_shape),
                flags(2, 4),
            ],
        )(output, grad_tokens, pieces, small)

    def scatter(block, dim):
        part = lax.psum_scatter(block, "dp", scatter_dimension=dim, tiled=True)
        return lax.psum(part, "branch").astype(F32)

    grad_out = scatter(mlp_pieces[chunks:].reshape(hidden_width, width), 0)
    reduced = scatter(jnp.concatenate([mlp_pieces[:chunks], pieces]), 1)
    grad_in = jnp.concatenate([reduced[f] for f in range(chunks)], axis=1)
    qkv = jnp.concatenate([reduced[chunks + hg] for hg in range(groups)], axis=1)
    small = lax.psum(small, ("dp", "branch"))
    ln, g_b_qkv, g_q, g_k, g_b_out, g_b_in = (
        part[0] for part in small_parts(small, chunks, groups, width)
    )
    return (
        output, grad_tokens, ln, split_lanes(qkv, groups), g_b_qkv, g_q, g_k,
        reduced[chunks + groups], g_b_out, grad_in, g_b_in, grad_out, g_b_out,
    )


def solution(mesh):
    rows, split, whole = P(("dp", "branch"), None), P("dp", None), P()
    return jax.shard_map(
        functools.partial(local, mesh.shape["dp"]),
        mesh=mesh,
        in_specs=(rows, split, rows) + (whole,) * 11,
        out_specs=(
            rows, rows, whole, split, whole, whole, whole, split, whole, split, whole, split, whole,
        ),
        check_vma=False,
    )
```

```python
import functools
import math

import jax
import jax.numpy as jnp
from jax import lax
from jax.experimental import pallas as pl
from jax.experimental.pallas import tpu as pltpu
from jax.sharding import PartitionSpec as P

HEAD = 64
SEQ = 448
IMAGES = 4
SLOT = SEQ // IMAGES
KEYS = 128
GROUP = 256
EPS = 1e-06
SCALE = 0.125
F32 = jnp.float32
BF16 = jnp.bfloat16
GELU_A = math.sqrt(2.0 / math.pi)
GELU_B = 0.044715


def dot(left, right, left_dim=1, right_dim=0):
    return lax.dot_general(
        left, right, (((left_dim,), (right_dim,)), ((), ())), preferred_element_type=F32
    )


def slot_positions(lens):
    row = lax.broadcasted_iota(jnp.int32, (SEQ, 1), 0)
    held = jnp.full((SEQ, 1), -1, jnp.int32)
    start = jnp.int32(0)
    for image in range(IMAGES):
        place = row - SLOT * image
        held = jnp.where((place >= 0) & (place < lens[image]), place + start, held)
        start = start + lens[image]
    return held


def position_slots(lens):
    row = lax.broadcasted_iota(jnp.int32, (SEQ, 1), 0)
    held = jnp.full((SEQ, 1), -1, jnp.int32)
    start = jnp.int32(0)
    for image in range(IMAGES):
        place = row - start
        held = jnp.where((place >= 0) & (place < lens[image]), place + SLOT * image, held)
        start = start + lens[image]
    return held


def one_hot(index):
    lanes = lax.broadcasted_iota(jnp.int32, (SEQ, SEQ), 1)
    return jnp.where(lanes == index, 1.0, 0.0).astype(BF16)


def row_stats(values):
    centered = values - jnp.mean(values, axis=1, keepdims=True)
    spread = jnp.mean(centered * centered, axis=1, keepdims=True)
    inverse = lax.rsqrt(spread + EPS)
    return centered * inverse, inverse


def gelu_pair(pre, grad):
    square = pre * pre
    bent = jnp.tanh(pre * (GELU_A + (GELU_A * GELU_B) * square))
    half = 0.5 * pre
    up = 1.0 + bent
    hidden = half * up
    slope = half * (GELU_A + (3.0 * GELU_A * GELU_B) * square)
    return hidden, (up * (0.5 + (1.0 - bent) * slope)) * grad


MESH = pl.DeviceIdType.MESH
BLOCK = 48
SLOTS = 2
RING = 8
XY, YX = ("x", "y", "z0", "z1"), ("y", "x", "z0", "z1")
ZX, ZY = ("z0", "z1", "x", "y"), ("z0", "z1", "y", "x")
RATES = {"core": 400e3, "x": 38e3, "y": 38e3, "z0": 38e3, "z1": 19e3}
LATENCY = 2.5


class Piece:
    def __init__(self, index, shard, axes):
        self.index, self.shard, self.axes = index, shard, axes
        self.stage, self.copy, self.eta = 0, None, 0.0


class Small:
    def __init__(self):
        self.stage, self.copy, self.eta = 0, None, 0.0


class Exchange:
    def __init__(self, refs, chunks):
        (self.both, self.inbox, self.in1, self.in2, self.in3, self.in4, self.osum, self.oin3,
         self.oin4, self.fin, self.small, self.small_in, self.send_sem, self.recv_sem) = refs
        self.chunks = chunks
        self.dp, self.core = lax.axis_index("dp"), lax.axis_index("branch")
        self.bits = {
            "x": lax.rem(self.dp, 2),
            "y": lax.rem(self.dp // 2, 2),
            "z0": lax.rem(self.dp // 4, 2),
            "z1": lax.rem(self.dp // 8, 2),
        }
        self.far = {
            axis: (self.dp + step - 2 * step * self.bits[axis], self.core)
            for axis, step in (("x", 1), ("y", 2), ("z0", 4), ("z1", 8))
        }
        self.far["core"] = (self.dp, 1 - self.core)
        self.pieces, self.items = [], []
        self.flights, self.merged, self.now, self.free = 0, 0, 0.0, {}

    def greet(self):
        barrier = pltpu.get_barrier_semaphore()
        for device in self.far.values():
            pl.semaphore_signal(barrier, inc=1, device_id=device, device_id_type=MESH)
        pl.semaphore_wait(barrier, len(self.far))

    def send(self, item, source, target, axis):
        copy = pltpu.make_async_remote_copy(
            src_ref=source, dst_ref=target, send_sem=self.send_sem.at[self.flights],
            recv_sem=self.recv_sem.at[self.flights], device_id=self.far[axis], device_id_type=MESH,
        )
        self.flights += 1
        copy.start()
        link = axis[0]
        size = source.dtype.itemsize * math.prod(source.shape)
        self.free[link] = max(self.free.get(link, 0.0), self.now) + size / RATES[axis]
        item.copy, item.eta = copy, self.free[link] + LATENCY

    def start(self, value, shard, axes):
        piece = Piece(len(self.pieces), shard, axes)
        for behind, stage in ((SLOTS, 1), (RING - SLOTS, 2)):
            while piece.index >= behind and self.pieces[piece.index - behind].stage < stage:
                self.advance(min(self.under_way(), key=lambda item: item.eta))
        slot = piece.index % SLOTS
        for side, role in ((0, self.core), (1, 1 - self.core)):
            put_blocks(value, self.both.at[slot, role], side, axes)
        self.send(piece, self.both.at[slot, 1], self.inbox.at[piece.index % RING], "core")
        self.pieces.append(piece)
        self.items.append(piece)

    def halve(self, piece, held, held_at, arrived, count, axis, target):
        near = self.bits[axis] * count
        away = (1 - self.bits[axis]) * count
        span = pl.ds(away, count)
        arrived[span] = arrived[span] + held[pl.ds(held_at + away, count)]
        self.send(piece, arrived.at[span], target, axis)
        span = pl.ds(near, count)
        arrived[span] = arrived[span] + held[pl.ds(held_at + near, count)]

    def advance(self, piece):
        piece.copy.wait()
        self.now = max(self.now, piece.eta)
        piece.copy = None
        if isinstance(piece, Small):
            self.advance_small(piece)
            return
        k, shard, axes = piece.index, piece.shard, piece.axes
        whole = isinstance(shard, int)
        if piece.stage == 0:
            own, arrived = self.both.at[k % SLOTS, 0], self.inbox.at[k % RING]
            self.halve(piece, own, 0, arrived, 8, axes[0], self.in1.at[k])
        elif piece.stage == 1:
            self.halve(
                piece, self.inbox.at[k % RING], self.bits[axes[0]] * 8, self.in1.at[k], 4, axes[1],
                self.in2.at[k],
            )
        elif piece.stage == 2 and whole:
            self.halve(
                piece, self.in1.at[k], self.bits[axes[1]] * 4, self.in2.at[k], 2, axes[2],
                self.in3.at[shard],
            )
        elif piece.stage == 2:
            place = shard[0] % 2 * 2 + shard[0] // 2
            self.osum[place] = self.in2[k] + self.in1[k, pl.ds(self.bits[axes[1]] * 4, 4)]
            self.merged += 1
            if self.merged < self.chunks:
                piece.stage = 5
            else:
                far = pl.ds((1 - self.bits["z0"]) * 2, 2)
                self.send(piece, self.osum.at[far], self.oin3, "z0")
        elif piece.stage == 3 and whole:
            self.halve(
                piece, self.in2.at[k], self.bits[axes[2]] * 2, self.in3.at[shard], 1, axes[3],
                self.in4.at[shard],
            )
        elif piece.stage == 3:
            self.halve(piece, self.osum, self.bits["z0"] * 2, self.oin3, 1, "z1", self.oin4)
        elif piece.stage == 4:
            if whole:
                final = self.fin.at[self.core, pl.ds(shard, 1)]
                final[...] = self.in4[shard] + self.in3[shard, pl.ds(self.bits[axes[3]], 1)]
            else:
                final = self.fin.at[self.core, pl.ds(self.fin.shape[1] - 4, 4)]
                final[...] = self.oin4[0] + self.oin3[self.bits["z1"]]
            self.send(piece, final, final, "core")
        piece.stage += 1

    def start_small(self):
        item = Small()
        self.send(item, self.small, self.small_in.at[0], "core")
        self.items.append(item)

    def advance_small(self, item):
        self.small[...] = self.small[...] + self.small_in[item.stage]
        item.stage += 1
        if item.stage < 5:
            axis = ("core", "x", "y", "z0", "z1")[item.stage]
            self.send(item, self.small, self.small_in.at[item.stage], axis)

    def under_way(self):
        return [item for item in self.items if item.copy is not None]

    def progress(self, cost):
        self.now += cost
        while True:
            due = [item for item in self.under_way() if item.eta <= self.now]
            if not due:
                return
            self.advance(min(due, key=lambda item: item.eta))

    def drain(self):
        while self.under_way():
            self.advance(min(self.under_way(), key=lambda item: item.eta))


def put_blocks(value, target, side, axes):
    half = value.shape[1] // 2
    for block in range(16):
        place = block
        if axes is not None and len(axes) == 4:
            bit = dict(x=block % 2, y=block // 2 % 2, z0=block // 4 % 2, z1=block // 8)
            place = sum(bit[axis] << (3 - i) for i, axis in enumerate(axes))
        target[place] = value[
            BLOCK * block : BLOCK * (block + 1), half * side : half * (side + 1)
        ].astype(BF16)


def make_flip():
    eye = jnp.where(
        lax.broadcasted_iota(jnp.int32, (GROUP, GROUP), 0)
        == lax.broadcasted_iota(jnp.int32, (GROUP, GROUP), 1),
        1.0,
        0.0,
    ).astype(BF16)

    def flip(source, target):
        for part in range(source.shape[1] // GROUP):
            lanes = pl.ds(part * GROUP, GROUP)
            target[lanes, :] = dot(eye, source[:, lanes], 1, 1).astype(BF16)

    return flip


class Parking:
    def __init__(self, stage, target, sem):
        self.stage, self.target, self.sem = stage, target, sem
        self.sent = []

    def put(self, value, index):
        slot = len(self.sent) % 2
        if len(self.sent) >= 2:
            self.sent[-2].wait()
        self.stage[slot] = value.astype(BF16)
        copy = pltpu.make_async_copy(self.stage.at[slot], self.target.at[index], self.sem.at[slot])
        copy.start()
        self.sent.append(copy)

    def finish(self):
        for copy in self.sent[-2:]:
            copy.wait()


def layer_kernel(
    wired,
    lengths_ref, tokens_hbm, cot_hbm, ln_gain_ref, w_qkv_hbm, b_qkv_ref, q_gain_ref, k_gain_ref,
    w_o_hbm, b_o_ref, w_in_hbm, b_in_ref, w_out_hbm, b_out_ref,
    output_hbm, grad_tokens_hbm, pieces_hbm, small_hbm,
    weights, tok, cot, packed, grow, normed, hid_even, gpre_even, hid_odd, gpre_odd,
    flipped, turned, fed, gnorm, qs, ks, vs, gm, rk, dq, dk, small_ref,
    load_sem, done_sem, *refs,
):
    rows, width = tok.shape
    hidden_width = w_in_hbm.shape[1]
    chunks = hidden_width // width
    groups = width // GROUP
    seqs = rows // SEQ
    images = seqs * IMAGES
    base = lax.axis_index("branch") * seqs
    assert chunks == 4 and groups == 3
    hid, gpre = (hid_even, hid_odd), (gpre_even, gpre_odd)
    mixed, gprojs = tok, (hid_even, gpre_even, cot)
    w_in = [weights.at[f % 3] for f in range(chunks)]
    w_out = [weights.at[3 + f % 3] for f in range(chunks)]
    w_qkv, w_o = [weights.at[1], weights.at[4], weights.at[2]], weights.at[5]
    nq, rq, nk = (fed.at[:, pl.ds(part * GROUP, GROUP)] for part in range(3))
    loads = {}

    def load(name, source, target):
        copy = pltpu.make_async_copy(source, target, load_sem.at[len(loads)])
        copy.start()
        loads[name] = copy

    def load_chunk(f):
        cols = pl.ds(f * width, width)
        load(("in", f), w_in_hbm.at[:, cols], w_in[f])
        load(("out", f), w_out_hbm.at[cols, :], w_out[f])

    def load_qkv(hg):
        for t in range(3):
            load(
                ("qkv", hg, t),
                w_qkv_hbm.at[:, pl.ds(t * width + hg * GROUP, GROUP)],
                w_qkv[hg].at[:, pl.ds(t * GROUP, GROUP)],
            )

    load("tok", tokens_hbm, tok)
    load("cot", cot_hbm, cot)
    for f in range(3):
        load_chunk(f)
    small_ref[...] = jnp.zeros_like(small_ref)
    net, parking = None, None
    if wired:
        net = Exchange(refs[:10] + (small_ref,) + refs[10:], chunks)
        net.greet()
    else:
        parking = Parking(refs[0], pieces_hbm, refs[1])

    def emit(value, shard, axes):
        if wired:
            net.start(value, shard, axes)
        else:
            parking.put(value, shard if isinstance(shard, int) else chunks + groups + 1 + shard[0])

    def point(cost):
        if wired:
            net.progress(cost)

    def cost(amount):
        if wired:
            net.now += amount

    def lanes_of(part):
        return pl.ds(part * GROUP, GROUP)

    ones_row = jnp.where(lax.broadcasted_iota(jnp.int32, (16, rows), 0) == 0, 1.0, 0.0)
    flipped[pl.ds(width, 16), :] = ones_row.astype(BF16)
    eye = jnp.where(
        lax.broadcasted_iota(jnp.int32, (GROUP, GROUP), 0)
        == lax.broadcasted_iota(jnp.int32, (GROUP, GROUP), 1),
        1.0,
        0.0,
    ).astype(BF16)

    def flip(source, target, part):
        target[lanes_of(part), :] = dot(eye, source[:, lanes_of(part)], 1, 1).astype(BF16)

    loads["tok"].wait()
    loads["cot"].wait()
    grad_sum = jnp.zeros((1, width), F32)
    for s in range(seqs):
        span = pl.ds(s * SEQ, SEQ)
        pick = one_hot(slot_positions([lengths_ref[base + s, j] for j in range(IMAGES)]))
        rows_here = dot(pick, tok[span, :])
        packed[span, :] = rows_here.astype(BF16)
        unit, _ = row_stats(rows_here)
        normed[span, :] = (unit * ln_gain_ref[...].reshape(1, width)).astype(BF16)
        grads_here = dot(pick, cot[span, :])
        grow[span, :] = grads_here.astype(BF16)
        grad_sum = grad_sum + jnp.sum(grads_here, axis=0, keepdims=True)
    small_ref[pl.ds(7, 1), pl.ds(0, width)] = grad_sum
    for part in range(groups):
        flip(normed, flipped, part)
    cost(6.0)

    def add_fed(f):
        for part in range(groups):
            lanes = lanes_of(part)
            up = dot(hid[f % 2][...], w_out[f][:, lanes])
            fed[:, lanes] = up if f == 0 else fed[:, lanes] + up

    def add_gnorm(source, target, first):
        for part in range(groups):
            lanes = lanes_of(part)
            down = dot(source[...], target[lanes, :], 1, 1)
            gnorm[:, lanes] = down if first else gnorm[:, lanes] + down

    b_in = b_in_ref[...].reshape(1, hidden_width)
    for f in range(chunks):
        slot = f % 2
        loads["in", f].wait()
        loads["out", f].wait()
        for c in range(groups):
            place = f * width + c * GROUP
            lanes = lanes_of(c)
            pre = dot(normed[...], w_in[f][:, lanes]) + b_in[:, place : place + GROUP]
            back = dot(grow[...], w_out[f][lanes, :], 1, 1)
            if f > 0 and c == 0:
                add_fed(f - 1)
            if f > 0 and c == 1:
                add_gnorm(gpre[1 - slot], w_in[f - 1], f == 1)
            if c > 0:
                flip(hid[slot], turned, c - 1)
            hidden, grad_pre = gelu_pair(pre, back)
            hid[slot][:, lanes] = hidden.astype(BF16)
            gpre[slot][:, lanes] = grad_pre.astype(BF16)
            point(2.9 if f > 0 and c < 2 else 1.2)
        flip(hid[slot], turned, groups - 1)
        sums = dot(flipped[...], gpre[slot][...])
        cost(2.2)
        emit(sums[:width], f, XY)
        small_ref[pl.ds(f, 1), pl.ds(0, width)] = sums[width : width + 1]
        point(0.0)
        cost(1.9)
        emit(dot(turned[...], grow[...]), (f,), YX[:2])
        point(0.0)
        if f == 1:
            load_chunk(3)
        if f == 2:
            load_qkv(0)
            load_qkv(1)
        if f == 3:
            load_qkv(2)
            load("wo", w_o_hbm, w_o)

    add_fed(chunks - 1)
    hid_odd[...] = (fed[...] + b_out_ref[...].reshape(1, width)).astype(BF16)
    point(1.9)

    same_head = (
        lax.broadcasted_iota(jnp.int32, (GROUP, GROUP), 0) // HEAD
        == lax.broadcasted_iota(jnp.int32, (GROUP, GROUP), 1) // HEAD
    )
    average = jnp.where(same_head, 1.0 / HEAD, 0.0).astype(BF16)
    q_gain = jnp.concatenate([q_gain_ref[...].reshape(1, HEAD)] * (GROUP // HEAD), axis=1)
    k_gain = jnp.concatenate([k_gain_ref[...].reshape(1, HEAD)] * (GROUP // HEAD), axis=1)
    b_qkv = b_qkv_ref[...].reshape(1, 3 * width)
    lane = lax.broadcasted_iota(jnp.int32, (1, KEYS), 1)
    first_head = jnp.where(lane < HEAD, 1.0, 0.0).astype(BF16)
    second_head = jnp.where(lane < HEAD, 0.0, 1.0).astype(BF16)

    def head_mean(values, split):
        high = values.astype(BF16)
        mean = dot(high, average)
        if split:
            mean = mean + dot((values - high.astype(F32)).astype(BF16), average)
        return mean

    def head_norm(raw):
        centered = raw - head_mean(raw, True)
        inverse = lax.rsqrt(head_mean(centered * centered, False) + EPS)
        return centered * inverse, inverse

    def two_heads(block):
        return jnp.concatenate([block * first_head, block * second_head], axis=0)

    def side_by_side(block):
        return jnp.concatenate([block[:SLOT], block[SLOT:]], axis=1)

    ks[pl.ds(rows, KEYS - SLOT), :] = jnp.zeros((KEYS - SLOT, GROUP), BF16)
    vs[pl.ds(rows, KEYS - SLOT), :] = jnp.zeros((KEYS - SLOT, GROUP), BF16)

    for hg in range(groups):
        gproj = gprojs[hg]
        bias_q, bias_k, bias_v = (
            b_qkv[:, t * width + hg * GROUP : t * width + (hg + 1) * GROUP] for t in range(3)
        )
        loads["qkv", hg, 0].wait()
        raw = dot(normed[...], w_qkv[hg][:, pl.ds(0, GROUP)]) + bias_q
        unit, inverse = head_norm(raw)
        nq[...] = unit
        rq[...] = inverse
        qs[...] = (unit * q_gain).astype(BF16) * SCALE
        point(1.5)
        loads["qkv", hg, 1].wait()
        raw = dot(normed[...], w_qkv[hg][:, pl.ds(GROUP, GROUP)]) + bias_k
        unit, inverse = head_norm(raw)
        nk[...] = unit
        rk[...] = inverse
        ks[pl.ds(0, rows), :] = (unit * k_gain).astype(BF16)
        point(1.5)
        loads["qkv", hg, 2].wait()
        if hg == 0:
            loads["wo"].wait()
        raw = dot(normed[...], w_qkv[hg][:, pl.ds(2 * GROUP, GROUP)]) + bias_v
        vs[pl.ds(0, rows), :] = raw.astype(BF16)
        gm[...] = dot(grow[...], w_o[pl.ds(hg * GROUP, GROUP), :], 1, 1).astype(BF16)
        point(1.5)

        def one_image(image):
            start = image * SLOT
            span = pl.ds(start, SLOT)
            window = pl.ds(start, KEYS)
            seen = lane < lengths_ref[base + image // IMAGES, image % IMAGES]
            for pair in range(GROUP // KEYS):
                lanes = pl.ds(pair * KEYS, KEYS)
                query = two_heads(qs[span, lanes])
                grad = two_heads(gm[span, lanes])
                key, value = ks[window, lanes], vs[window, lanes]
                weight = jnp.where(seen, jnp.exp(dot(query, key, 1, 1)), 0.0)
                probs = weight / jnp.sum(weight, axis=1, keepdims=True)
                grad_probs = dot(grad, value, 1, 1)
                inner = jnp.sum(probs * grad_probs, axis=1, keepdims=True)
                grad_scores = (probs * (grad_probs - inner)).astype(BF16)
                probs_low = probs.astype(BF16)
                mixed[span, pl.ds(hg * GROUP + pair * KEYS, KEYS)] = dot(
                    side_by_side(probs_low), two_heads(value)
                ).astype(BF16)
                dq[span, lanes] = dot(side_by_side(grad_scores), two_heads(key)) * SCALE
                dk[span, lanes] = dot(grad_scores, query, 0, 0)[:SLOT]
                gproj[span, pl.ds(2 * GROUP + pair * KEYS, KEYS)] = dot(probs_low, grad, 0, 0)[
                    :SLOT
                ].astype(BF16)

        for image in range(0, images, 2):
            one_image(image)
            one_image(image + 1)
            point(1.3)
        if hg == groups - 1:
            for part in range(groups):
                flip(mixed, turned, part)
            cost(2.2)
            emit(dot(turned[...], grow[...]), chunks + groups, XY)
            point(0.0)

        gain_sums = []
        for side, (grad_ref, unit_ref, inverse_ref, gain) in enumerate(
            ((dq, nq, rq, q_gain), (dk, nk, rk, k_gain))
        ):
            grad, unit = grad_ref[...], unit_ref[...]
            gain_sums.append(jnp.sum(grad * unit, axis=0, keepdims=True))
            grad = grad * gain
            back = grad - head_mean(grad, True) - unit * head_mean(grad * unit, False)
            gproj[:, pl.ds(side * GROUP, GROUP)] = (back * inverse_ref[...]).astype(BF16)
            point(0.8)
        for side in range(2):
            small_ref[pl.ds(3 + side, 1), pl.ds(width, GROUP)] += gain_sums[side]
        sums = dot(flipped[...], gproj[...])
        cost(1.9)
        emit(sums[:width], chunks + hg, (YX, XY, YX)[hg])
        small_ref[pl.ds(4 + hg, 1), pl.ds(0, width)] = sums[width : width + 1]
        point(0.0)

    add_gnorm(gpre_odd, w_in[chunks - 1], False)
    point(1.7)
    for hg in range(groups):
        add_gnorm(gprojs[hg], w_qkv[hg], False)
        if hg == 0:
            load("tok again", tokens_hbm, hid_even)
        if hg == 1:
            load("cot again", cot_hbm, gpre_even)
        point(1.7)
    ln_gain = ln_gain_ref[...].reshape(1, width)
    b_o = b_o_ref[...].reshape(1, width)
    gain_grad = jnp.zeros((1, width), F32)
    for s in range(seqs):
        span = pl.ds(s * SEQ, SEQ)
        unit, inverse = row_stats(packed[span, :].astype(F32))
        grad = gnorm[span, :]
        gain_grad = gain_grad + jnp.sum(grad * unit, axis=0, keepdims=True)
        grad = grad * ln_gain
        back = grad - jnp.mean(grad, axis=1, keepdims=True)
        back = (back - unit * jnp.mean(grad * unit, axis=1, keepdims=True)) * inverse
        normed[span, :] = (grow[span, :].astype(F32) + back).astype(BF16)
    for t in range(width // GROUP):
        small_ref[pl.ds(t, 1), pl.ds(width, GROUP)] = gain_grad[:, t * GROUP : (t + 1) * GROUP]
    if wired:
        net.start_small()
    point(1.5)
    finals = []
    loads["tok again"].wait()
    loads["cot again"].wait()

    def hand_over(source, target):
        copy = pltpu.make_async_copy(source, target, done_sem.at[len(finals)])
        copy.start()
        finals.append(copy)

    for s in range(seqs):
        span = pl.ds(s * SEQ, SEQ)
        place = position_slots([lengths_ref[base + s, j] for j in range(IMAGES)])
        put = one_hot(place)
        padding = jnp.where(place < 0, 1.0, 0.0)
        attended = (dot(mixed[span, :], w_o[...]) + b_o).astype(BF16).astype(F32)
        result = packed[span, :].astype(F32) + (attended + hid_odd[span, :].astype(F32))
        result = dot(put, result.astype(BF16)) + padding * hid_even[span, :].astype(F32)
        hid_even[span, :] = result.astype(BF16)
        hand_over(hid_even.at[span], output_hbm.at[span])
        point(1.2)
        grads = dot(put, normed[span, :]) + padding * gpre_even[span, :].astype(F32)
        gpre_even[span, :] = grads.astype(BF16)
        hand_over(gpre_even.at[span], grad_tokens_hbm.at[span])
        point(0.8)
    if wired:
        net.drain()
        hand_over(net.fin, pieces_hbm)
    else:
        parking.finish()
    hand_over(small_ref, small_hbm)
    for copy in finals:
        copy.wait()


def split_lanes(block, groups):
    width = block.shape[1] // 3
    return jnp.concatenate(
        [
            block[:, hg * width + t * GROUP : hg * width + (t + 1) * GROUP]
            for t in range(3)
            for hg in range(groups)
        ],
        axis=1,
    )


def fold_heads(gains):
    return sum(gains[:, h * HEAD : (h + 1) * HEAD] for h in range(GROUP // HEAD))


def small_parts(small, chunks, groups, width):
    b_in = jnp.concatenate([small[f : f + 1, :width] for f in range(chunks)], axis=1)
    b_qkv = jnp.concatenate([small[4 + hg : 5 + hg, :width] for hg in range(groups)], axis=1)
    ln = jnp.concatenate([small[t : t + 1, width:] for t in range(width // GROUP)], axis=1)
    gains = [fold_heads(small[3 + side : 4 + side, width:]) for side in range(2)]
    return ln, split_lanes(b_qkv, groups), gains[0], gains[1], small[7:8, :width], b_in


def finish_kernel(
    rows_hbm, grads_hbm, fin_hbm, small_hbm, output_hbm, grad_tokens_hbm, g_ln, g_qkv, g_b_qkv,
    g_q, g_k, g_o, g_b_o, g_in, g_b_in, g_out, g_b_out, held, fin, small, sem,
):
    comes = [
        pltpu.make_async_copy(source, target, sem.at[0, i])
        for i, (source, target) in enumerate(
            ((rows_hbm, held.at[0]), (grads_hbm, held.at[1]), (fin_hbm, fin), (small_hbm, small))
        )
    ]
    goes = [
        pltpu.make_async_copy(held.at[i], target, sem.at[1, i])
        for i, target in enumerate((output_hbm, grad_tokens_hbm))
    ]
    for copy in comes:
        copy.start()
    width = g_o.shape[1]
    chunks, groups = g_in.shape[1] // width, width // GROUP
    for come, go in zip(comes, goes):
        come.wait()
        go.start()
    for come in comes[2:]:
        come.wait()

    def whole(shard):
        return jnp.concatenate([fin[side, shard].astype(F32) for side in range(2)], axis=1)

    for f in range(chunks):
        g_in[:, f * width : (f + 1) * width] = whole(f)
    qkv = jnp.concatenate([whole(chunks + hg) for hg in range(groups)], axis=1)
    g_qkv[...] = split_lanes(qkv, groups)
    g_o[...] = whole(chunks + groups)
    for j in range(4):
        g_out[j * BLOCK : (j + 1) * BLOCK, :] = whole(chunks + groups + 1 + j)
    ln, b_qkv, q, k, b_out, b_in = small_parts(small[...], chunks, groups, width)
    for ref, value in (
        (g_ln, ln), (g_b_qkv, b_qkv), (g_q, q), (g_k, k), (g_b_o, b_out), (g_b_in, b_in), (g_b_out, b_out)
    ):
        ref[...] = value.reshape(value.shape[1])
    for copy in goes:
        copy.wait()


def local(n_dp, tokens, lengths, cotangent, ln_gain, w_qkv, b_qkv, q_gain, k_gain, w_o, b_o, w_in, b_in, w_out, b_out):
    rows, width = tokens.shape
    hidden_width = w_in.shape[1]
    chunks = hidden_width // width
    groups = width // GROUP
    seqs = rows // SEQ
    shards = chunks + groups + 1
    everyone = shards + chunks
    wired = n_dp * BLOCK == width and n_dp == 4 * chunks
    half = width // 2
    extra = KEYS - SLOT
    anywhere = pl.BlockSpec(memory_space=pl.ANY)
    vmem = pl.BlockSpec(memory_space=pltpu.VMEM)
    smem = pl.BlockSpec(memory_space=pltpu.SMEM)
    wide = lambda *shape: pltpu.VMEM(shape, F32)
    slim = lambda *shape: pltpu.VMEM(shape, BF16)
    flags = lambda *shape: pltpu.SemaphoreType.DMA(shape)
    low = lambda *shape: jax.ShapeDtypeStruct(shape, BF16)
    full = lambda *shape: jax.ShapeDtypeStruct(shape, F32)
    small_shape = (8, width + GROUP)

    if wired:
        out_piece = low(2, shards + 4, BLOCK, half)
        flights = 6 * shards + 3 * chunks + 3 + 5
        others = [
            slim(SLOTS, 2, 16, BLOCK, half), slim(RING, 16, BLOCK, half),
            slim(everyone, 8, BLOCK, half), slim(everyone, 4, BLOCK, half),
            slim(shards, 2, BLOCK, half), slim(shards, 1, BLOCK, half), slim(4, 4, BLOCK, half),
            slim(2, 4, BLOCK, half), slim(1, 4, BLOCK, half), slim(2, shards + 4, BLOCK, half),
            wide(5, *small_shape), flags(flights), flags(flights),
        ]
        settings = dict(collective_id=0, has_side_effects=True)
    else:
        out_piece = low(everyone, width, width)
        others = [slim(2, width, width), flags(2)]
        settings = {}
    output, grad_tokens, pieces, small = pl.pallas_call(
        functools.partial(layer_kernel, wired),
        out_shape=(low(rows, width), low(rows, width), out_piece, full(*small_shape)),
        in_specs=[
            smem, anywhere, anywhere, vmem, anywhere, vmem, vmem, vmem, anywhere, vmem, anywhere,
            vmem, anywhere, vmem,
        ],
        out_specs=(anywhere,) * 4,
        scratch_shapes=[slim(6, width, width)]
        + [slim(rows, width)] * 9
        + [
            slim(width + 16, rows), slim(width, rows), wide(rows, width), wide(rows, width),
            slim(rows, GROUP), slim(rows + extra, GROUP), slim(rows + extra, GROUP),
            slim(rows, GROUP),
        ]
        + [wide(rows, GROUP)] * 3
        + [wide(*small_shape), flags(5 + 2 * chunks + 3 * groups), flags(2 * seqs + 2)]
        + others,
        compiler_params=pltpu.CompilerParams(vmem_limit_bytes=62 << 20, **settings),
    )(
        lengths, tokens, cotangent, ln_gain, w_qkv, b_qkv, q_gain, k_gain, w_o, b_o, w_in, b_in,
        w_out, b_out,
    )

    if wired:
        return pl.pallas_call(
            finish_kernel,
            out_shape=(
                low(rows, width), low(rows, width), full(width), full(BLOCK, 3 * width),
                full(3 * width), full(HEAD), full(HEAD), full(BLOCK, width), full(width),
                full(BLOCK, hidden_width), full(hidden_width), full(4 * BLOCK, width), full(width),
            ),
            in_specs=[anywhere] * 4,
            out_specs=(anywhere, anywhere) + (vmem,) * 11,
            scratch_shapes=[
                slim(2, rows, width), slim(2, shards + 4, BLOCK, half), wide(*small_shape),
                flags(2, 4),
            ],
        )(output, grad_tokens, pieces, small)

    def scatter(block, dim):
        part = lax.psum_scatter(block, "dp", scatter_dimension=dim, tiled=True)
        return lax.psum(part, "branch").astype(F32)

    grad_out = scatter(pieces[shards:].reshape(hidden_width, width), 0)
    reduced = scatter(pieces[:shards], 1)
    grad_in = jnp.concatenate([reduced[f] for f in range(chunks)], axis=1)
    qkv = jnp.concatenate([reduced[chunks + hg] for hg in range(groups)], axis=1)
    small = lax.psum(small, ("dp", "branch"))
    ln, g_b_qkv, g_q, g_k, g_b_out, g_b_in = (
        part[0] for part in small_parts(small, chunks, groups, width)
    )
    return (
        output, grad_tokens, ln, split_lanes(qkv, groups), g_b_qkv, g_q, g_k,
        reduced[chunks + groups], g_b_out, grad_in, g_b_in, grad_out, g_b_out,
    )


def solution(mesh):
    rows, split, whole = P(("dp", "branch"), None), P("dp", None), P()
    return jax.shard_map(
        functools.partial(local, mesh.shape["dp"]),
        mesh=mesh,
        in_specs=(rows, split, rows) + (whole,) * 11,
        out_specs=(
            rows, rows, whole, split, whole, whole, whole, split, whole, split, whole, split, whole,
        ),
        check_vma=False,
    )
```

```python
import functools
import math

import jax
import jax.numpy as jnp
from jax import lax
from jax.experimental import pallas as pl
from jax.experimental.pallas import tpu as pltpu
from jax.sharding import PartitionSpec as P

HEAD = 64
SEQ = 448
IMAGES = 4
SLOT = SEQ // IMAGES
KEYS = 128
GROUP = 256
EPS = 1e-06
SCALE = 0.125
F32 = jnp.float32
BF16 = jnp.bfloat16
GELU_A = math.sqrt(2.0 / math.pi)
GELU_B = 0.044715


def dot(left, right, left_dim=1, right_dim=0):
    return lax.dot_general(
        left, right, (((left_dim,), (right_dim,)), ((), ())), preferred_element_type=F32
    )


def slot_positions(lens):
    row = lax.broadcasted_iota(jnp.int32, (SEQ, 1), 0)
    held = jnp.full((SEQ, 1), -1, jnp.int32)
    start = jnp.int32(0)
    for image in range(IMAGES):
        place = row - SLOT * image
        held = jnp.where((place >= 0) & (place < lens[image]), place + start, held)
        start = start + lens[image]
    return held


def position_slots(lens):
    row = lax.broadcasted_iota(jnp.int32, (SEQ, 1), 0)
    held = jnp.full((SEQ, 1), -1, jnp.int32)
    start = jnp.int32(0)
    for image in range(IMAGES):
        place = row - start
        held = jnp.where((place >= 0) & (place < lens[image]), place + SLOT * image, held)
        start = start + lens[image]
    return held


def one_hot(index):
    lanes = lax.broadcasted_iota(jnp.int32, (SEQ, SEQ), 1)
    return jnp.where(lanes == index, 1.0, 0.0).astype(BF16)


def row_stats(values):
    centered = values - jnp.mean(values, axis=1, keepdims=True)
    spread = jnp.mean(centered * centered, axis=1, keepdims=True)
    inverse = lax.rsqrt(spread + EPS)
    return centered * inverse, inverse


def gelu_pair(pre, grad):
    square = pre * pre
    bent = jnp.tanh(pre * (GELU_A + (GELU_A * GELU_B) * square))
    half = 0.5 * pre
    up = 1.0 + bent
    hidden = half * up
    slope = half * (GELU_A + (3.0 * GELU_A * GELU_B) * square)
    return hidden, (up * (0.5 + (1.0 - bent) * slope)) * grad


MESH = pl.DeviceIdType.MESH
BLOCK = 48
SLOTS = 2
RING = 8
XY, YX = ("x", "y", "z0", "z1"), ("y", "x", "z0", "z1")
ZX, ZY = ("z0", "z1", "x", "y"), ("z0", "z1", "y", "x")
RATES = {"core": 400e3, "x": 38e3, "y": 38e3, "z0": 38e3, "z1": 19e3}
LATENCY = 2.5


class Piece:
    def __init__(self, index, shard, axes, lanes):
        self.index, self.shard, self.axes, self.lanes = index, shard, axes, lanes
        self.stage, self.copy, self.eta = 0, None, 0.0

    def cut(self, ref):
        return ref.at[:, :, self.lanes]


class Small:
    def __init__(self):
        self.stage, self.copy, self.eta = 0, None, 0.0


class Exchange:
    def __init__(self, refs, chunks):
        (self.both, self.inbox, self.in1, self.in2, self.in3, self.in4, self.osum, self.oin3,
         self.oin4, self.fin, self.small, self.small_in, self.send_sem, self.recv_sem) = refs
        self.chunks = chunks
        self.dp, self.core = lax.axis_index("dp"), lax.axis_index("branch")
        self.bits = {
            "x": lax.rem(self.dp, 2),
            "y": lax.rem(self.dp // 2, 2),
            "z0": lax.rem(self.dp // 4, 2),
            "z1": lax.rem(self.dp // 8, 2),
        }
        self.far = {
            axis: (self.dp + step - 2 * step * self.bits[axis], self.core)
            for axis, step in (("x", 1), ("y", 2), ("z0", 4), ("z1", 8))
        }
        self.far["core"] = (self.dp, 1 - self.core)
        self.items, self.opened = [], 0
        self.flights, self.merged, self.now, self.free = 0, 0, 0.0, {}

    def greet(self):
        barrier = pltpu.get_barrier_semaphore()
        for device in self.far.values():
            pl.semaphore_signal(barrier, inc=1, device_id=device, device_id_type=MESH)
        pl.semaphore_wait(barrier, len(self.far))

    def send(self, item, source, target, axis):
        copy = pltpu.make_async_remote_copy(
            src_ref=source, dst_ref=target, send_sem=self.send_sem.at[self.flights],
            recv_sem=self.recv_sem.at[self.flights], device_id=self.far[axis], device_id_type=MESH,
        )
        self.flights += 1
        copy.start()
        link = axis[0]
        size = source.dtype.itemsize * math.prod(source.shape)
        self.free[link] = max(self.free.get(link, 0.0), self.now) + size / RATES[axis]
        item.copy, item.eta = copy, self.free[link] + LATENCY

    def open(self):
        index = self.opened
        for behind, stage in ((SLOTS, 1), (RING - SLOTS, 2)):
            while any(
                item.index == index - behind and item.stage < stage
                for item in self.items
                if isinstance(item, Piece)
            ):
                self.advance(min(self.under_way(), key=lambda item: item.eta))
        self.opened += 1
        return index

    def put(self, index, value, lane, axes):
        half = value.shape[1] // 2
        for side, role in ((0, self.core), (1, 1 - self.core)):
            target = self.both.at[index % SLOTS, role, :, :, pl.ds(lane, half)]
            put_blocks(value, target, side, axes)

    def start(self, index, shard, axes, lane, width):
        piece = Piece(index, shard, axes, pl.ds(lane, width))
        self.send(
            piece, piece.cut(self.both.at[index % SLOTS, 1]), piece.cut(self.inbox.at[index % RING]),
            "core",
        )
        self.items.append(piece)

    def halve(self, piece, held, held_at, arrived, count, axis, target):
        near = self.bits[axis] * count
        away = (1 - self.bits[axis]) * count
        span = pl.ds(away, count)
        arrived[span] = arrived[span] + held[pl.ds(held_at + away, count)]
        self.send(piece, arrived.at[span], target, axis)
        span = pl.ds(near, count)
        arrived[span] = arrived[span] + held[pl.ds(held_at + near, count)]

    def advance(self, piece):
        piece.copy.wait()
        self.now = max(self.now, piece.eta)
        piece.copy = None
        if isinstance(piece, Small):
            self.advance_small(piece)
            return
        k, shard, axes, cut = piece.index, piece.shard, piece.axes, piece.cut
        whole = isinstance(shard, int)
        in0, in1, in2 = cut(self.inbox.at[k % RING]), cut(self.in1.at[k]), cut(self.in2.at[k])
        if whole:
            in3, in4 = cut(self.in3.at[shard]), cut(self.in4.at[shard])
        if piece.stage == 0:
            self.halve(piece, cut(self.both.at[k % SLOTS, 0]), 0, in0, 8, axes[0], in1)
        elif piece.stage == 1:
            self.halve(piece, in0, self.bits[axes[0]] * 8, in1, 4, axes[1], in2)
        elif piece.stage == 2 and whole:
            self.halve(piece, in1, self.bits[axes[1]] * 4, in2, 2, axes[2], in3)
        elif piece.stage == 2:
            place = shard[0] % 2 * 2 + shard[0] // 2
            self.osum[place] = in2[...] + in1[pl.ds(self.bits[axes[1]] * 4, 4)]
            self.merged += 1
            if self.merged < self.chunks:
                piece.stage = 5
            else:
                far = pl.ds((1 - self.bits["z0"]) * 2, 2)
                self.send(piece, self.osum.at[far], self.oin3, "z0")
        elif piece.stage == 3 and whole:
            self.halve(piece, in2, self.bits[axes[2]] * 2, in3, 1, axes[3], in4)
        elif piece.stage == 3:
            self.halve(piece, self.osum, self.bits["z0"] * 2, self.oin3, 1, "z1", self.oin4)
        elif piece.stage == 4:
            if whole:
                final = self.fin.at[self.core, pl.ds(shard, 1), :, piece.lanes]
                final[...] = in4[...] + in3[pl.ds(self.bits[axes[3]], 1)]
            else:
                final = self.fin.at[self.core, pl.ds(self.fin.shape[1] - 4, 4)]
                final[...] = self.oin4[0] + self.oin3[self.bits["z1"]]
            self.send(piece, final, final, "core")
        piece.stage += 1

    def start_small(self):
        item = Small()
        self.send(item, self.small, self.small_in.at[0], "core")
        self.items.append(item)

    def advance_small(self, item):
        self.small[...] = self.small[...] + self.small_in[item.stage]
        item.stage += 1
        if item.stage < 5:
            axis = ("core", "x", "y", "z0", "z1")[item.stage]
            self.send(item, self.small, self.small_in.at[item.stage], axis)

    def under_way(self):
        return [item for item in self.items if item.copy is not None]

    def progress(self, cost):
        self.now += cost
        while True:
            due = [item for item in self.under_way() if item.eta <= self.now]
            if not due:
                return
            self.advance(min(due, key=lambda item: item.eta))

    def drain(self):
        while self.under_way():
            self.advance(min(self.under_way(), key=lambda item: item.eta))


def put_blocks(value, target, side, axes):
    half = value.shape[1] // 2
    for block in range(16):
        place = block
        if axes is not None and len(axes) == 4:
            bit = dict(x=block % 2, y=block // 2 % 2, z0=block // 4 % 2, z1=block // 8)
            place = sum(bit[axis] << (3 - i) for i, axis in enumerate(axes))
        target[place] = value[
            BLOCK * block : BLOCK * (block + 1), half * side : half * (side + 1)
        ].astype(BF16)


def make_flip():
    eye = jnp.where(
        lax.broadcasted_iota(jnp.int32, (GROUP, GROUP), 0)
        == lax.broadcasted_iota(jnp.int32, (GROUP, GROUP), 1),
        1.0,
        0.0,
    ).astype(BF16)

    def flip(source, target):
        for part in range(source.shape[1] // GROUP):
            lanes = pl.ds(part * GROUP, GROUP)
            target[lanes, :] = dot(eye, source[:, lanes], 1, 1).astype(BF16)

    return flip


class Parking:
    def __init__(self, stage, target, sem):
        self.stage, self.target, self.sem = stage, target, sem
        self.sent = []

    def put(self, value, index):
        slot = len(self.sent) % 2
        if len(self.sent) >= 2:
            self.sent[-2].wait()
        self.stage[slot] = value.astype(BF16)
        copy = pltpu.make_async_copy(self.stage.at[slot], self.target.at[index], self.sem.at[slot])
        copy.start()
        self.sent.append(copy)

    def finish(self):
        for copy in self.sent[-2:]:
            copy.wait()


def layer_kernel(
    wired,
    lengths_ref, tokens_hbm, cot_hbm, ln_gain_ref, w_qkv_hbm, b_qkv_ref, q_gain_ref, k_gain_ref,
    w_o_hbm, b_o_ref, w_in_hbm, b_in_ref, w_out_hbm, b_out_ref,
    output_hbm, grad_tokens_hbm, pieces_hbm, small_hbm,
    weights, tok, cot, packed, grow, normed, hid_even, gpre_even, hid_odd, gpre_odd,
    flipped, turned, fed, gnorm, qs, ks, vs, gm, rk, dq, dk, small_ref,
    load_sem, done_sem, *refs,
):
    rows, width = tok.shape
    hidden_width = w_in_hbm.shape[1]
    chunks = hidden_width // width
    groups = width // GROUP
    seqs = rows // SEQ
    images = seqs * IMAGES
    base = lax.axis_index("branch") * seqs
    assert chunks == 4 and groups == 3
    hid, gpre = (hid_even, hid_odd), (gpre_even, gpre_odd)
    mixed, gprojs = tok, (hid_even, gpre_even, cot)
    w_in = [weights.at[f % 3] for f in range(chunks)]
    w_out = [weights.at[3 + f % 3] for f in range(chunks)]
    w_qkv, w_o = [weights.at[1], weights.at[4], weights.at[2]], weights.at[5]
    nq, rq, nk = (fed.at[:, pl.ds(part * GROUP, GROUP)] for part in range(3))
    loads = {}

    def load(name, source, target):
        copy = pltpu.make_async_copy(source, target, load_sem.at[len(loads)])
        copy.start()
        loads[name] = copy

    def load_chunk(f):
        cols = pl.ds(f * width, width)
        load(("in", f), w_in_hbm.at[:, cols], w_in[f])
        load(("out", f), w_out_hbm.at[cols, :], w_out[f])

    def load_qkv(hg):
        for t in range(3):
            load(
                ("qkv", hg, t),
                w_qkv_hbm.at[:, pl.ds(t * width + hg * GROUP, GROUP)],
                w_qkv[hg].at[:, pl.ds(t * GROUP, GROUP)],
            )

    load("tok", tokens_hbm, tok)
    load("cot", cot_hbm, cot)
    for f in range(3):
        load_chunk(f)
    small_ref[...] = jnp.zeros_like(small_ref)
    net, parking = None, None
    if wired:
        net = Exchange(refs[:10] + (small_ref,) + refs[10:], chunks)
        net.greet()
    else:
        parking = Parking(refs[0], pieces_hbm, refs[1])

    def emit(value, shard, axes):
        if wired:
            index = net.open()
            net.put(index, value, 0, axes)
            net.start(index, shard, axes, 0, width // 2)
        else:
            parking.put(value, shard if isinstance(shard, int) else chunks + groups + 1 + shard[0])

    def point(cost):
        if wired:
            net.progress(cost)

    def cost(amount):
        if wired:
            net.now += amount

    def lanes_of(part):
        return pl.ds(part * GROUP, GROUP)

    ones_row = jnp.where(lax.broadcasted_iota(jnp.int32, (16, rows), 0) == 0, 1.0, 0.0)
    flipped[pl.ds(width, 16), :] = ones_row.astype(BF16)
    eye = jnp.where(
        lax.broadcasted_iota(jnp.int32, (GROUP, GROUP), 0)
        == lax.broadcasted_iota(jnp.int32, (GROUP, GROUP), 1),
        1.0,
        0.0,
    ).astype(BF16)

    def flip(source, target, part):
        target[lanes_of(part), :] = dot(eye, source[:, lanes_of(part)], 1, 1).astype(BF16)

    loads["tok"].wait()
    loads["cot"].wait()
    grad_sum = jnp.zeros((1, width), F32)
    for s in range(seqs):
        span = pl.ds(s * SEQ, SEQ)
        pick = one_hot(slot_positions([lengths_ref[base + s, j] for j in range(IMAGES)]))
        rows_here = dot(pick, tok[span, :])
        packed[span, :] = rows_here.astype(BF16)
        unit, _ = row_stats(rows_here)
        normed[span, :] = (unit * ln_gain_ref[...].reshape(1, width)).astype(BF16)
        grads_here = dot(pick, cot[span, :])
        grow[span, :] = grads_here.astype(BF16)
        grad_sum = grad_sum + jnp.sum(grads_here, axis=0, keepdims=True)
    small_ref[pl.ds(7, 1), pl.ds(0, width)] = grad_sum
    for part in range(groups):
        flip(normed, flipped, part)
    cost(6.0)

    def add_fed(f):
        for part in range(groups):
            lanes = lanes_of(part)
            up = dot(hid[f % 2][...], w_out[f][:, lanes])
            fed[:, lanes] = up if f == 0 else fed[:, lanes] + up

    def add_gnorm(source, target, first):
        for part in range(groups):
            lanes = lanes_of(part)
            down = dot(source[...], target[lanes, :], 1, 1)
            gnorm[:, lanes] = down if first else gnorm[:, lanes] + down

    b_in = b_in_ref[...].reshape(1, hidden_width)
    for f in range(chunks):
        slot = f % 2
        loads["in", f].wait()
        loads["out", f].wait()
        for c in range(groups):
            place = f * width + c * GROUP
            lanes = lanes_of(c)
            pre = dot(normed[...], w_in[f][:, lanes]) + b_in[:, place : place + GROUP]
            back = dot(grow[...], w_out[f][lanes, :], 1, 1)
            if f > 0 and c == 0:
                add_fed(f - 1)
            if f > 0 and c == 1:
                add_gnorm(gpre[1 - slot], w_in[f - 1], f == 1)
            if c > 0:
                flip(hid[slot], turned, c - 1)
            hidden, grad_pre = gelu_pair(pre, back)
            hid[slot][:, lanes] = hidden.astype(BF16)
            gpre[slot][:, lanes] = grad_pre.astype(BF16)
            point(2.9 if f > 0 and c < 2 else 1.2)
        flip(hid[slot], turned, groups - 1)
        sums = dot(flipped[...], gpre[slot][...])
        cost(2.2)
        emit(sums[:width], f, XY)
        small_ref[pl.ds(f, 1), pl.ds(0, width)] = sums[width : width + 1]
        point(0.0)
        cost(1.9)
        emit(dot(turned[...], grow[...]), (f,), YX[:2])
        point(0.0)
        if f == 1:
            load_chunk(3)
        if f == 2:
            load_qkv(0)
            load_qkv(1)
        if f == 3:
            load_qkv(2)
            load("wo", w_o_hbm, w_o)

    add_fed(chunks - 1)
    hid_odd[...] = (fed[...] + b_out_ref[...].reshape(1, width)).astype(BF16)
    point(1.9)

    same_head = (
        lax.broadcasted_iota(jnp.int32, (GROUP, GROUP), 0) // HEAD
        == lax.broadcasted_iota(jnp.int32, (GROUP, GROUP), 1) // HEAD
    )
    average = jnp.where(same_head, 1.0 / HEAD, 0.0).astype(BF16)
    q_gain = jnp.concatenate([q_gain_ref[...].reshape(1, HEAD)] * (GROUP // HEAD), axis=1)
    k_gain = jnp.concatenate([k_gain_ref[...].reshape(1, HEAD)] * (GROUP // HEAD), axis=1)
    b_qkv = b_qkv_ref[...].reshape(1, 3 * width)
    lane = lax.broadcasted_iota(jnp.int32, (1, KEYS), 1)
    pair_lane = jnp.concatenate([lane, lane], axis=1)
    first_head = jnp.where(lane < HEAD, 1.0, 0.0).astype(BF16)
    second_head = jnp.where(lane < HEAD, 0.0, 1.0).astype(BF16)

    def head_mean(values, split):
        high = values.astype(BF16)
        mean = dot(high, average)
        if split:
            mean = mean + dot((values - high.astype(F32)).astype(BF16), average)
        return mean

    def head_norm(raw):
        centered = raw - head_mean(raw, True)
        inverse = lax.rsqrt(head_mean(centered * centered, False) + EPS)
        return centered * inverse, inverse

    def two_heads(block):
        return jnp.concatenate([block * first_head, block * second_head], axis=0)

    def stacked(block):
        return jnp.concatenate([block[:, :KEYS], block[:, KEYS:]], axis=0)

    def invert(total):
        guess = pl.reciprocal(total, approx=True)
        return guess * (2.0 - total * guess)

    def over_heads(block, change):
        parts = []
        for head in range(2):
            part = block[:, head * KEYS : (head + 1) * KEYS]
            total = change(jnp.sum(part, axis=1, keepdims=True))
            parts.append(jnp.broadcast_to(total, part.shape))
        return jnp.concatenate(parts, axis=1)

    ks[pl.ds(rows, KEYS - SLOT), :] = jnp.zeros((KEYS - SLOT, GROUP), BF16)
    vs[pl.ds(rows, KEYS - SLOT), :] = jnp.zeros((KEYS - SLOT, GROUP), BF16)

    for hg in range(groups):
        gproj = gprojs[hg]
        bias_q, bias_k, bias_v = (
            b_qkv[:, t * width + hg * GROUP : t * width + (hg + 1) * GROUP] for t in range(3)
        )
        for t in range(3):
            loads["qkv", hg, t].wait()
        if hg == 0:
            loads["wo"].wait()
        raw = dot(normed[...], w_qkv[hg][:, lanes_of(0)]) + bias_q
        unit, inverse = head_norm(raw)
        nq[...] = unit
        rq[...] = inverse
        qs[...] = (unit * q_gain).astype(BF16) * SCALE
        raw = dot(normed[...], w_qkv[hg][:, lanes_of(1)]) + bias_k
        unit, inverse = head_norm(raw)
        nk[...] = unit
        rk[...] = inverse
        ks[pl.ds(0, rows), :] = (unit * k_gain).astype(BF16)
        raw = dot(normed[...], w_qkv[hg][:, lanes_of(2)]) + bias_v
        vs[pl.ds(0, rows), :] = raw.astype(BF16)
        gm[...] = dot(grow[...], w_o[lanes_of(hg), :], 1, 1).astype(BF16)
        point(4.5)

        def one_image(image):
            start = image * SLOT
            span = pl.ds(start, SLOT)
            window = pl.ds(start, KEYS)
            seen = pair_lane < lengths_ref[base + image // IMAGES, image % IMAGES]
            for pair in range(GROUP // KEYS):
                lanes = pl.ds(pair * KEYS, KEYS)
                query, grad = qs[span, lanes], gm[span, lanes]
                keys, values = two_heads(ks[window, lanes]), two_heads(vs[window, lanes])
                weight = jnp.where(seen, jnp.exp(dot(query, keys, 1, 1)), 0.0)
                probs = weight * over_heads(weight, invert)
                grad_probs = dot(grad, values, 1, 1)
                inner = over_heads(probs * grad_probs, lambda total: total)
                grad_scores = (probs * (grad_probs - inner)).astype(BF16)
                probs_low = probs.astype(BF16)
                mixed[span, pl.ds(hg * GROUP + pair * KEYS, KEYS)] = dot(probs_low, values).astype(
                    BF16
                )
                dq[span, lanes] = dot(grad_scores, keys) * SCALE
                dk[span, lanes] = dot(stacked(grad_scores), two_heads(query), 0, 0)[:SLOT]
                gproj[span, pl.ds(2 * GROUP + pair * KEYS, KEYS)] = dot(
                    stacked(probs_low), two_heads(grad), 0, 0
                )[:SLOT].astype(BF16)

        for image in range(0, images, 2):
            one_image(image)
            one_image(image + 1)
            point(1.3)
        if hg == groups - 1:
            for part in range(groups):
                flip(mixed, turned, part)
            cost(2.2)
            emit(dot(turned[...], grow[...]), chunks + groups, XY)
            point(0.0)

        axes = (YX, XY, YX)[hg]
        last = hg == groups - 1
        index = net.open() if wired else None
        parts = {}

        def part_grad(t, part_axes):
            sums = dot(flipped[...], gproj[:, lanes_of(t)])
            small_ref[pl.ds(4 + hg, 1), lanes_of(t)] = sums[width : width + 1]
            if wired:
                net.put(index, sums[:width], t * KEYS, part_axes)
                if last:
                    net.start(index, chunks + hg, part_axes, t * KEYS, KEYS)
            else:
                parts[t] = sums[:width]

        def norm_back(side, grad_ref, unit_ref, inverse_ref, gain):
            grad, unit = grad_ref[...], unit_ref[...]
            gain_sum = jnp.sum(grad * unit, axis=0, keepdims=True)
            small_ref[pl.ds(3 + side, 1), pl.ds(width, GROUP)] += gain_sum
            grad = grad * gain
            back = grad - head_mean(grad, False) - unit * head_mean(grad * unit, False)
            gproj[:, lanes_of(side)] = (back * inverse_ref[...]).astype(BF16)

        cost(0.7)
        part_grad(2, YX if last else axes)
        norm_back(0, dq, nq, rq, q_gain)
        cost(1.5)
        if last:
            point(0.0)
        part_grad(0, YX if last else axes)
        norm_back(1, dk, nk, rk, k_gain)
        cost(1.5)
        if last:
            point(0.0)
        part_grad(1, XY if last else axes)
        if not wired:
            parking.put(jnp.concatenate([parts[t] for t in range(3)], axis=1), chunks + hg)
        elif not last:
            net.start(index, chunks + hg, axes, 0, width // 2)
        point(0.0)

    add_gnorm(gpre_odd, w_in[chunks - 1], False)
    point(1.7)
    for hg in range(groups):
        add_gnorm(gprojs[hg], w_qkv[hg], False)
        if hg == 0:
            load("tok again", tokens_hbm, hid_even)
        if hg == 1:
            load("cot again", cot_hbm, gpre_even)
        point(1.7)
    ln_gain = ln_gain_ref[...].reshape(1, width)
    b_o = b_o_ref[...].reshape(1, width)
    gain_grad = jnp.zeros((1, width), F32)
    for s in range(seqs):
        span = pl.ds(s * SEQ, SEQ)
        unit, inverse = row_stats(packed[span, :].astype(F32))
        grad = gnorm[span, :]
        gain_grad = gain_grad + jnp.sum(grad * unit, axis=0, keepdims=True)
        grad = grad * ln_gain
        back = grad - jnp.mean(grad, axis=1, keepdims=True)
        back = (back - unit * jnp.mean(grad * unit, axis=1, keepdims=True)) * inverse
        normed[span, :] = (grow[span, :].astype(F32) + back).astype(BF16)
    for t in range(width // GROUP):
        small_ref[pl.ds(t, 1), pl.ds(width, GROUP)] = gain_grad[:, t * GROUP : (t + 1) * GROUP]
    if wired:
        net.start_small()
    point(1.5)
    finals = []
    loads["tok again"].wait()
    loads["cot again"].wait()

    def hand_over(source, target):
        copy = pltpu.make_async_copy(source, target, done_sem.at[len(finals)])
        copy.start()
        finals.append(copy)

    for s in range(seqs):
        span = pl.ds(s * SEQ, SEQ)
        place = position_slots([lengths_ref[base + s, j] for j in range(IMAGES)])
        put = one_hot(place)
        padding = jnp.where(place < 0, 1.0, 0.0)
        attended = (dot(mixed[span, :], w_o[...]) + b_o).astype(BF16).astype(F32)
        result = packed[span, :].astype(F32) + (attended + hid_odd[span, :].astype(F32))
        result = dot(put, result.astype(BF16)) + padding * hid_even[span, :].astype(F32)
        hid_even[span, :] = result.astype(BF16)
        hand_over(hid_even.at[span], output_hbm.at[span])
        point(1.2)
        grads = dot(put, normed[span, :]) + padding * gpre_even[span, :].astype(F32)
        gpre_even[span, :] = grads.astype(BF16)
        hand_over(gpre_even.at[span], grad_tokens_hbm.at[span])
        point(0.8)
    if wired:
        net.drain()
        hand_over(net.fin, pieces_hbm)
    else:
        parking.finish()
    hand_over(small_ref, small_hbm)
    for copy in finals:
        copy.wait()


def split_lanes(block, groups):
    width = block.shape[1] // 3
    return jnp.concatenate(
        [
            block[:, hg * width + t * GROUP : hg * width + (t + 1) * GROUP]
            for t in range(3)
            for hg in range(groups)
        ],
        axis=1,
    )


def fold_heads(gains):
    return sum(gains[:, h * HEAD : (h + 1) * HEAD] for h in range(GROUP // HEAD))


def small_parts(small, chunks, groups, width):
    b_in = jnp.concatenate([small[f : f + 1, :width] for f in range(chunks)], axis=1)
    b_qkv = jnp.concatenate([small[4 + hg : 5 + hg, :width] for hg in range(groups)], axis=1)
    ln = jnp.concatenate([small[t : t + 1, width:] for t in range(width // GROUP)], axis=1)
    gains = [fold_heads(small[3 + side : 4 + side, width:]) for side in range(2)]
    return ln, split_lanes(b_qkv, groups), gains[0], gains[1], small[7:8, :width], b_in


def finish_kernel(
    rows_hbm, grads_hbm, fin_hbm, small_hbm, output_hbm, grad_tokens_hbm, g_ln, g_qkv_hbm, g_b_qkv,
    g_q, g_k, g_o_hbm, g_b_o, g_in_hbm, g_b_in, g_out_hbm, g_b_out, held, fin, small, g_qkv, g_o, g_in,
    g_out, sem,
):
    comes = [
        pltpu.make_async_copy(source, target, sem.at[0, i])
        for i, (source, target) in enumerate(
            ((fin_hbm, fin), (small_hbm, small), (rows_hbm, held.at[0]), (grads_hbm, held.at[1]))
        )
    ]
    goes = [
        pltpu.make_async_copy(source, target, sem.at[1, i])
        for i, (source, target) in enumerate(
            (
                (held.at[0], output_hbm), (held.at[1], grad_tokens_hbm), (g_in, g_in_hbm),
                (g_qkv, g_qkv_hbm), (g_out, g_out_hbm), (g_o, g_o_hbm),
            )
        )
    ]
    for copy in comes:
        copy.start()
    width = g_o.shape[1]
    chunks, groups = g_in.shape[1] // width, width // GROUP

    def whole(shard, lane, size):
        return jnp.concatenate(
            [fin[side, shard, :, lane : lane + size].astype(F32) for side in range(2)], axis=1
        )

    comes[0].wait()
    for f in range(chunks):
        g_in[:, f * width : (f + 1) * width] = whole(f, 0, width // 2)
    goes[2].start()
    for hg in range(groups):
        for t in range(3):
            place = t * width + hg * GROUP
            g_qkv[:, place : place + GROUP] = whole(chunks + hg, t * KEYS, KEYS)
    goes[3].start()
    for i in range(2):
        comes[2 + i].wait()
        goes[i].start()
    for j in range(4):
        g_out[j * BLOCK : (j + 1) * BLOCK, :] = whole(chunks + groups + 1 + j, 0, width // 2)
    goes[4].start()
    g_o[...] = whole(chunks + groups, 0, width // 2)
    goes[5].start()
    comes[1].wait()
    ln, b_qkv, q, k, b_out, b_in = small_parts(small[...], chunks, groups, width)
    for ref, value in (
        (g_ln, ln), (g_b_qkv, b_qkv), (g_q, q), (g_k, k), (g_b_o, b_out), (g_b_in, b_in), (g_b_out, b_out)
    ):
        ref[...] = value.reshape(value.shape[1])
    for copy in goes:
        copy.wait()


def local(n_dp, tokens, lengths, cotangent, ln_gain, w_qkv, b_qkv, q_gain, k_gain, w_o, b_o, w_in, b_in, w_out, b_out):
    rows, width = tokens.shape
    hidden_width = w_in.shape[1]
    chunks = hidden_width // width
    groups = width // GROUP
    seqs = rows // SEQ
    shards = chunks + groups + 1
    everyone = shards + chunks
    wired = n_dp * BLOCK == width and n_dp == 4 * chunks
    half = width // 2
    extra = KEYS - SLOT
    anywhere = pl.BlockSpec(memory_space=pl.ANY)
    vmem = pl.BlockSpec(memory_space=pltpu.VMEM)
    smem = pl.BlockSpec(memory_space=pltpu.SMEM)
    wide = lambda *shape: pltpu.VMEM(shape, F32)
    slim = lambda *shape: pltpu.VMEM(shape, BF16)
    flags = lambda *shape: pltpu.SemaphoreType.DMA(shape)
    low = lambda *shape: jax.ShapeDtypeStruct(shape, BF16)
    full = lambda *shape: jax.ShapeDtypeStruct(shape, F32)
    small_shape = (8, width + GROUP)

    if wired:
        out_piece = low(2, shards + 4, BLOCK, half)
        flights = 6 * (shards + 2) + 3 * chunks + 3 + 5
        others = [
            slim(SLOTS, 2, 16, BLOCK, half), slim(RING, 16, BLOCK, half),
            slim(everyone, 8, BLOCK, half), slim(everyone, 4, BLOCK, half),
            slim(shards, 2, BLOCK, half), slim(shards, 1, BLOCK, half), slim(4, 4, BLOCK, half),
            slim(2, 4, BLOCK, half), slim(1, 4, BLOCK, half), slim(2, shards + 4, BLOCK, half),
            wide(5, *small_shape), flags(flights), flags(flights),
        ]
        settings = dict(collective_id=0, has_side_effects=True)
    else:
        out_piece = low(everyone, width, width)
        others = [slim(2, width, width), flags(2)]
        settings = {}
    output, grad_tokens, pieces, small = pl.pallas_call(
        functools.partial(layer_kernel, wired),
        out_shape=(low(rows, width), low(rows, width), out_piece, full(*small_shape)),
        in_specs=[
            smem, anywhere, anywhere, vmem, anywhere, vmem, vmem, vmem, anywhere, vmem, anywhere,
            vmem, anywhere, vmem,
        ],
        out_specs=(anywhere,) * 4,
        scratch_shapes=[slim(6, width, width)]
        + [slim(rows, width)] * 9
        + [
            slim(width + 16, rows), slim(width, rows), wide(rows, width), wide(rows, width),
            slim(rows, GROUP), slim(rows + extra, GROUP), slim(rows + extra, GROUP),
            slim(rows, GROUP),
        ]
        + [wide(rows, GROUP)] * 3
        + [wide(*small_shape), flags(5 + 2 * chunks + 3 * groups), flags(2 * seqs + 2)]
        + others,
        compiler_params=pltpu.CompilerParams(vmem_limit_bytes=62 << 20, **settings),
    )(
        lengths, tokens, cotangent, ln_gain, w_qkv, b_qkv, q_gain, k_gain, w_o, b_o, w_in, b_in,
        w_out, b_out,
    )

    if wired:
        return pl.pallas_call(
            finish_kernel,
            out_shape=(
                low(rows, width), low(rows, width), full(width), full(BLOCK, 3 * width),
                full(3 * width), full(HEAD), full(HEAD), full(BLOCK, width), full(width),
                full(BLOCK, hidden_width), full(hidden_width), full(4 * BLOCK, width), full(width),
            ),
            in_specs=[anywhere] * 4,
            out_specs=(
                anywhere, anywhere, vmem, anywhere, vmem, vmem, vmem, anywhere, vmem, anywhere, vmem,
                anywhere, vmem,
            ),
            scratch_shapes=[
                slim(2, rows, width), slim(2, shards + 4, BLOCK, half), wide(*small_shape),
                wide(BLOCK, 3 * width), wide(BLOCK, width), wide(BLOCK, hidden_width),
                wide(4 * BLOCK, width), flags(2, 6),
            ],
        )(output, grad_tokens, pieces, small)

    def scatter(block, dim):
        part = lax.psum_scatter(block, "dp", scatter_dimension=dim, tiled=True)
        return lax.psum(part, "branch").astype(F32)

    grad_out = scatter(pieces[shards:].reshape(hidden_width, width), 0)
    reduced = scatter(pieces[:shards], 1)
    grad_in = jnp.concatenate([reduced[f] for f in range(chunks)], axis=1)
    qkv = jnp.concatenate([reduced[chunks + hg] for hg in range(groups)], axis=1)
    small = lax.psum(small, ("dp", "branch"))
    ln, g_b_qkv, g_q, g_k, g_b_out, g_b_in = (
        part[0] for part in small_parts(small, chunks, groups, width)
    )
    return (
        output, grad_tokens, ln, split_lanes(qkv, groups), g_b_qkv, g_q, g_k,
        reduced[chunks + groups], g_b_out, grad_in, g_b_in, grad_out, g_b_out,
    )


def solution(mesh):
    rows, split, whole = P(("dp", "branch"), None), P("dp", None), P()
    return jax.shard_map(
        functools.partial(local, mesh.shape["dp"]),
        mesh=mesh,
        in_specs=(rows, split, rows) + (whole,) * 11,
        out_specs=(
            rows, rows, whole, split, whole, whole, whole, split, whole, split, whole, split, whole,
        ),
        check_vma=False,
    )
```

```python
import functools
import math

import jax
import jax.numpy as jnp
from jax import lax
from jax.experimental import pallas as pl
from jax.experimental.pallas import tpu as pltpu
from jax.sharding import PartitionSpec as P

HEAD = 64
SEQ = 448
IMAGES = 4
SLOT = SEQ // IMAGES
KEYS = 128
GROUP = 256
EPS = 1e-06
SCALE = 0.125
F32 = jnp.float32
BF16 = jnp.bfloat16
GELU_A = math.sqrt(2.0 / math.pi)
GELU_B = 0.044715


def dot(left, right, left_dim=1, right_dim=0):
    return lax.dot_general(
        left, right, (((left_dim,), (right_dim,)), ((), ())), preferred_element_type=F32
    )


def slot_positions(lens):
    row = lax.broadcasted_iota(jnp.int32, (SEQ, 1), 0)
    held = jnp.full((SEQ, 1), -1, jnp.int32)
    start = jnp.int32(0)
    for image in range(IMAGES):
        place = row - SLOT * image
        held = jnp.where((place >= 0) & (place < lens[image]), place + start, held)
        start = start + lens[image]
    return held


def position_slots(lens):
    row = lax.broadcasted_iota(jnp.int32, (SEQ, 1), 0)
    held = jnp.full((SEQ, 1), -1, jnp.int32)
    start = jnp.int32(0)
    for image in range(IMAGES):
        place = row - start
        held = jnp.where((place >= 0) & (place < lens[image]), place + SLOT * image, held)
        start = start + lens[image]
    return held


def one_hot(index):
    lanes = lax.broadcasted_iota(jnp.int32, (SEQ, SEQ), 1)
    return jnp.where(lanes == index, 1.0, 0.0).astype(BF16)


def row_stats(values):
    centered = values - jnp.mean(values, axis=1, keepdims=True)
    spread = jnp.mean(centered * centered, axis=1, keepdims=True)
    inverse = lax.rsqrt(spread + EPS)
    return centered * inverse, inverse


def gelu_pair(pre, grad):
    square = pre * pre
    bent = jnp.tanh(pre * (GELU_A + (GELU_A * GELU_B) * square))
    half = 0.5 * pre
    up = 1.0 + bent
    hidden = half * up
    slope = half * (GELU_A + (3.0 * GELU_A * GELU_B) * square)
    return hidden, (up * (0.5 + (1.0 - bent) * slope)) * grad


MESH = pl.DeviceIdType.MESH
BLOCK = 48
SLOTS = 2
RING = 8
XY, YX = ("x", "y", "z0", "z1"), ("y", "x", "z0", "z1")
ZX, ZY = ("z0", "z1", "x", "y"), ("z0", "z1", "y", "x")
RATES = {"core": 400e3, "x": 42e3, "y": 42e3, "z0": 42e3, "z1": 21e3}
LATENCY = 2.0


class Piece:
    def __init__(self, index, shard, axes, lanes):
        self.index, self.shard, self.axes, self.lanes = index, shard, axes, lanes
        self.stage, self.copy, self.eta = 0, None, 0.0

    def cut(self, ref):
        return ref.at[:, :, self.lanes]


class Small:
    def __init__(self):
        self.stage, self.copy, self.eta = 0, None, 0.0


class Exchange:
    def __init__(self, refs, chunks):
        (self.both, self.inbox, self.in1, self.in2, self.in3, self.in4, self.osum, self.oin3,
         self.oin4, self.fin, self.small, self.small_in, self.send_sem, self.recv_sem) = refs
        self.chunks = chunks
        self.dp, self.core = lax.axis_index("dp"), lax.axis_index("branch")
        self.bits = {
            "x": lax.rem(self.dp, 2),
            "y": lax.rem(self.dp // 2, 2),
            "z0": lax.rem(self.dp // 4, 2),
            "z1": lax.rem(self.dp // 8, 2),
        }
        self.far = {
            axis: (self.dp + step - 2 * step * self.bits[axis], self.core)
            for axis, step in (("x", 1), ("y", 2), ("z0", 4), ("z1", 8))
        }
        self.far["core"] = (self.dp, 1 - self.core)
        self.items, self.opened = [], 0
        self.flights, self.merged, self.now, self.free = 0, 0, 0.0, {}

    def greet(self):
        barrier = pltpu.get_barrier_semaphore()
        for device in self.far.values():
            pl.semaphore_signal(barrier, inc=1, device_id=device, device_id_type=MESH)
        pl.semaphore_wait(barrier, len(self.far))

    def send(self, item, source, target, axis):
        copy = pltpu.make_async_remote_copy(
            src_ref=source, dst_ref=target, send_sem=self.send_sem.at[self.flights],
            recv_sem=self.recv_sem.at[self.flights], device_id=self.far[axis], device_id_type=MESH,
        )
        self.flights += 1
        copy.start()
        link = axis[0]
        size = source.dtype.itemsize * math.prod(source.shape)
        self.free[link] = max(self.free.get(link, 0.0), self.now) + size / RATES[axis]
        item.copy, item.eta = copy, self.free[link] + LATENCY

    def open(self):
        index = self.opened
        for behind, stage in ((SLOTS, 1), (RING - SLOTS, 2)):
            while any(
                item.index == index - behind and item.stage < stage
                for item in self.items
                if isinstance(item, Piece)
            ):
                self.advance(min(self.under_way(), key=lambda item: item.eta))
        self.opened += 1
        return index

    def put(self, index, value, lane, axes):
        half = value.shape[1] // 2
        for side, role in ((0, self.core), (1, 1 - self.core)):
            target = self.both.at[index % SLOTS, role, :, :, pl.ds(lane, half)]
            put_blocks(value, target, side, axes)

    def start(self, index, shard, axes, lane, width):
        piece = Piece(index, shard, axes, pl.ds(lane, width))
        self.send(
            piece, piece.cut(self.both.at[index % SLOTS, 1]), piece.cut(self.inbox.at[index % RING]),
            "core",
        )
        self.items.append(piece)

    def halve(self, piece, held, held_at, arrived, count, axis, target):
        near = self.bits[axis] * count
        away = (1 - self.bits[axis]) * count
        span = pl.ds(away, count)
        arrived[span] = arrived[span] + held[pl.ds(held_at + away, count)]
        self.send(piece, arrived.at[span], target, axis)
        span = pl.ds(near, count)
        arrived[span] = arrived[span] + held[pl.ds(held_at + near, count)]

    def advance(self, piece):
        piece.copy.wait()
        self.now = max(self.now, piece.eta)
        piece.copy = None
        if isinstance(piece, Small):
            self.advance_small(piece)
            return
        k, shard, axes, cut = piece.index, piece.shard, piece.axes, piece.cut
        whole = isinstance(shard, int)
        in0, in1, in2 = cut(self.inbox.at[k % RING]), cut(self.in1.at[k]), cut(self.in2.at[k])
        if whole:
            in3, in4 = cut(self.in3.at[shard]), cut(self.in4.at[shard])
        if piece.stage == 0:
            self.halve(piece, cut(self.both.at[k % SLOTS, 0]), 0, in0, 8, axes[0], in1)
        elif piece.stage == 1:
            self.halve(piece, in0, self.bits[axes[0]] * 8, in1, 4, axes[1], in2)
        elif piece.stage == 2 and whole:
            self.halve(piece, in1, self.bits[axes[1]] * 4, in2, 2, axes[2], in3)
        elif piece.stage == 2:
            place = shard[0] % 2 * 2 + shard[0] // 2
            self.osum[place] = in2[...] + in1[pl.ds(self.bits[axes[1]] * 4, 4)]
            self.merged += 1
            if self.merged < self.chunks:
                piece.stage = 5
            else:
                far = pl.ds((1 - self.bits["z0"]) * 2, 2)
                self.send(piece, self.osum.at[far], self.oin3, "z0")
        elif piece.stage == 3 and whole:
            self.halve(piece, in2, self.bits[axes[2]] * 2, in3, 1, axes[3], in4)
        elif piece.stage == 3:
            self.halve(piece, self.osum, self.bits["z0"] * 2, self.oin3, 1, "z1", self.oin4)
        elif piece.stage == 4:
            if whole:
                final = self.fin.at[self.core, pl.ds(shard, 1), :, piece.lanes]
                final[...] = in4[...] + in3[pl.ds(self.bits[axes[3]], 1)]
            else:
                final = self.fin.at[self.core, pl.ds(self.fin.shape[1] - 4, 4)]
                final[...] = self.oin4[0] + self.oin3[self.bits["z1"]]
            self.send(piece, final, final, "core")
        piece.stage += 1

    def start_small(self):
        item = Small()
        self.send(item, self.small, self.small_in.at[0], "core")
        self.items.append(item)

    def advance_small(self, item):
        self.small[...] = self.small[...] + self.small_in[item.stage]
        item.stage += 1
        if item.stage < 5:
            axis = ("core", "x", "y", "z0", "z1")[item.stage]
            self.send(item, self.small, self.small_in.at[item.stage], axis)

    def under_way(self):
        return [item for item in self.items if item.copy is not None]

    def progress(self, cost):
        self.now += cost
        while True:
            due = [item for item in self.under_way() if item.eta <= self.now]
            if not due:
                return
            self.advance(min(due, key=lambda item: item.eta))

    def drain(self):
        while self.under_way():
            self.advance(min(self.under_way(), key=lambda item: item.eta))


def put_blocks(value, target, side, axes):
    half = value.shape[1] // 2
    for block in range(16):
        place = block
        if axes is not None and len(axes) == 4:
            bit = dict(x=block % 2, y=block // 2 % 2, z0=block // 4 % 2, z1=block // 8)
            place = sum(bit[axis] << (3 - i) for i, axis in enumerate(axes))
        target[place] = value[
            BLOCK * block : BLOCK * (block + 1), half * side : half * (side + 1)
        ].astype(BF16)


def make_flip():
    eye = jnp.where(
        lax.broadcasted_iota(jnp.int32, (GROUP, GROUP), 0)
        == lax.broadcasted_iota(jnp.int32, (GROUP, GROUP), 1),
        1.0,
        0.0,
    ).astype(BF16)

    def flip(source, target):
        for part in range(source.shape[1] // GROUP):
            lanes = pl.ds(part * GROUP, GROUP)
            target[lanes, :] = dot(eye, source[:, lanes], 1, 1).astype(BF16)

    return flip


class Parking:
    def __init__(self, stage, target, sem):
        self.stage, self.target, self.sem = stage, target, sem
        self.sent = []

    def put(self, value, index):
        slot = len(self.sent) % 2
        if len(self.sent) >= 2:
            self.sent[-2].wait()
        self.stage[slot] = value.astype(BF16)
        copy = pltpu.make_async_copy(self.stage.at[slot], self.target.at[index], self.sem.at[slot])
        copy.start()
        self.sent.append(copy)

    def finish(self):
        for copy in self.sent[-2:]:
            copy.wait()


def layer_kernel(
    wired,
    lengths_ref, tokens_hbm, cot_hbm, ln_gain_ref, w_qkv_hbm, b_qkv_ref, q_gain_ref, k_gain_ref,
    w_o_hbm, b_o_ref, w_in_hbm, b_in_ref, w_out_hbm, b_out_ref,
    output_hbm, grad_tokens_hbm, pieces_hbm, small_hbm,
    weights, tok, cot, packed, grow, normed, hid_even, gpre_even, hid_odd, gpre_odd,
    flipped, turned, fed, gnorm, qs, ks, vs, gm, rk, dq, dk, small_ref,
    load_sem, done_sem, *refs,
):
    rows, width = tok.shape
    hidden_width = w_in_hbm.shape[1]
    chunks = hidden_width // width
    groups = width // GROUP
    seqs = rows // SEQ
    images = seqs * IMAGES
    base = lax.axis_index("branch") * seqs
    assert chunks == 4 and groups == 3
    hid, gpre = (hid_even, hid_odd), (gpre_even, gpre_odd)
    mixed, gprojs = tok, (hid_even, gpre_even, cot)
    w_in = [weights.at[f % 3] for f in range(chunks)]
    w_out = [weights.at[3 + f % 3] for f in range(chunks)]
    w_qkv, w_o = [weights.at[1], weights.at[4], weights.at[2]], weights.at[5]
    nq, rq, nk = (fed.at[:, pl.ds(part * GROUP, GROUP)] for part in range(3))
    loads = {}

    def load(name, source, target):
        copy = pltpu.make_async_copy(source, target, load_sem.at[len(loads)])
        copy.start()
        loads[name] = copy

    def load_chunk(f):
        cols = pl.ds(f * width, width)
        load(("in", f), w_in_hbm.at[:, cols], w_in[f])
        load(("out", f), w_out_hbm.at[cols, :], w_out[f])

    def load_qkv(hg):
        for t in range(3):
            load(
                ("qkv", hg, t),
                w_qkv_hbm.at[:, pl.ds(t * width + hg * GROUP, GROUP)],
                w_qkv[hg].at[:, pl.ds(t * GROUP, GROUP)],
            )

    load("tok", tokens_hbm, tok)
    load("cot", cot_hbm, cot)
    for f in range(3):
        load_chunk(f)
    small_ref[...] = jnp.zeros_like(small_ref)
    net, parking = None, None
    if wired:
        net = Exchange(refs[:10] + (small_ref,) + refs[10:], chunks)
        net.greet()
    else:
        parking = Parking(refs[0], pieces_hbm, refs[1])

    def emit(value, shard, axes):
        if wired:
            index = net.open()
            net.put(index, value, 0, axes)
            net.start(index, shard, axes, 0, width // 2)
        else:
            parking.put(value, shard if isinstance(shard, int) else chunks + groups + 1 + shard[0])

    def point(cost):
        if wired:
            net.progress(cost)

    def cost(amount):
        if wired:
            net.now += amount

    def lanes_of(part):
        return pl.ds(part * GROUP, GROUP)

    ones_row = jnp.where(lax.broadcasted_iota(jnp.int32, (16, rows), 0) == 0, 1.0, 0.0)
    flipped[pl.ds(width, 16), :] = ones_row.astype(BF16)
    eye = jnp.where(
        lax.broadcasted_iota(jnp.int32, (GROUP, GROUP), 0)
        == lax.broadcasted_iota(jnp.int32, (GROUP, GROUP), 1),
        1.0,
        0.0,
    ).astype(BF16)

    def flip(source, target, part):
        target[lanes_of(part), :] = dot(eye, source[:, lanes_of(part)], 1, 1).astype(BF16)

    loads["tok"].wait()
    loads["cot"].wait()
    grad_sum = jnp.zeros((1, width), F32)
    for s in range(seqs):
        span = pl.ds(s * SEQ, SEQ)
        pick = one_hot(slot_positions([lengths_ref[base + s, j] for j in range(IMAGES)]))
        rows_here = dot(pick, tok[span, :])
        packed[span, :] = rows_here.astype(BF16)
        unit, _ = row_stats(rows_here)
        normed[span, :] = (unit * ln_gain_ref[...].reshape(1, width)).astype(BF16)
        grads_here = dot(pick, cot[span, :])
        grow[span, :] = grads_here.astype(BF16)
        grad_sum = grad_sum + jnp.sum(grads_here, axis=0, keepdims=True)
    small_ref[pl.ds(7, 1), pl.ds(0, width)] = grad_sum
    for part in range(groups):
        flip(normed, flipped, part)
    cost(6.0)

    def add_fed(f):
        for part in range(groups):
            lanes = lanes_of(part)
            up = dot(hid[f % 2][...], w_out[f][:, lanes])
            fed[:, lanes] = up if f == 0 else fed[:, lanes] + up

    def add_gnorm(source, target, first):
        for part in range(groups):
            lanes = lanes_of(part)
            down = dot(source[...], target[lanes, :], 1, 1)
            gnorm[:, lanes] = down if first else gnorm[:, lanes] + down

    b_in = b_in_ref[...].reshape(1, hidden_width)
    ready = None

    def activate():
        f, c, pre, back = ready
        hidden, grad_pre = gelu_pair(pre, back)
        hid[f % 2][:, lanes_of(c)] = hidden.astype(BF16)
        gpre[f % 2][:, lanes_of(c)] = grad_pre.astype(BF16)

    def send_w_in(f):
        sums = dot(flipped[...], gpre[f % 2][...])
        cost(2.2)
        emit(sums[:width], f, XY)
        small_ref[pl.ds(f, 1), pl.ds(0, width)] = sums[width : width + 1]
        point(0.0)

    def send_w_out(f):
        cost(1.9)
        emit(dot(turned[...], grow[...]), (f,), YX[:2])
        point(0.0)

    for f in range(chunks):
        loads["in", f].wait()
        loads["out", f].wait()
        for c in range(groups):
            place = f * width + c * GROUP
            lanes = lanes_of(c)
            pre = dot(normed[...], w_in[f][:, lanes]) + b_in[:, place : place + GROUP]
            back = dot(grow[...], w_out[f][lanes, :], 1, 1)
            if ready is not None:
                activate()
            ready = (f, c, pre, back)
            if f > 0 and c == 0:
                for part in range(groups):
                    flip(hid[1 - f % 2], turned, part)
            if f > 0 and c == 2:
                add_fed(f - 1)
                add_gnorm(gpre[1 - f % 2], w_in[f - 1], f == 1)
            point((1.7, 1.2, 4.6)[c] if f > 0 else 1.2)
            if f > 0 and c == 0:
                send_w_in(f - 1)
            if f > 0 and c == 1:
                send_w_out(f - 1)
        if f == 1:
            load_chunk(3)
        if f == 2:
            load_qkv(0)
            load_qkv(1)
        if f == 3:
            load_qkv(2)
            load("wo", w_o_hbm, w_o)
    activate()
    for part in range(groups):
        flip(hid_odd, turned, part)
    send_w_in(chunks - 1)
    send_w_out(chunks - 1)

    add_fed(chunks - 1)
    hid_odd[...] = (fed[...] + b_out_ref[...].reshape(1, width)).astype(BF16)
    point(1.9)

    same_head = (
        lax.broadcasted_iota(jnp.int32, (GROUP, GROUP), 0) // HEAD
        == lax.broadcasted_iota(jnp.int32, (GROUP, GROUP), 1) // HEAD
    )
    average = jnp.where(same_head, 1.0 / HEAD, 0.0).astype(BF16)
    q_gain = jnp.concatenate([q_gain_ref[...].reshape(1, HEAD)] * (GROUP // HEAD), axis=1)
    k_gain = jnp.concatenate([k_gain_ref[...].reshape(1, HEAD)] * (GROUP // HEAD), axis=1)
    b_qkv = b_qkv_ref[...].reshape(1, 3 * width)
    lane = lax.broadcasted_iota(jnp.int32, (1, KEYS), 1)
    pair_lane = jnp.concatenate([lane, lane], axis=1)
    first_head = jnp.where(lane < HEAD, 1.0, 0.0).astype(BF16)
    second_head = jnp.where(lane < HEAD, 0.0, 1.0).astype(BF16)

    def head_mean(values, split):
        high = values.astype(BF16)
        mean = dot(high, average)
        if split:
            mean = mean + dot((values - high.astype(F32)).astype(BF16), average)
        return mean

    def head_norm(raw):
        centered = raw - head_mean(raw, True)
        inverse = lax.rsqrt(head_mean(centered * centered, False) + EPS)
        return centered * inverse, inverse

    def two_heads(block):
        return jnp.concatenate([block * first_head, block * second_head], axis=0)

    def stacked(block):
        return jnp.concatenate([block[:, :KEYS], block[:, KEYS:]], axis=0)

    def invert(total):
        guess = pl.reciprocal(total, approx=True)
        return guess * (2.0 - total * guess)

    def over_heads(block, change):
        parts = []
        for head in range(2):
            part = block[:, head * KEYS : (head + 1) * KEYS]
            total = change(jnp.sum(part, axis=1, keepdims=True))
            parts.append(jnp.broadcast_to(total, part.shape))
        return jnp.concatenate(parts, axis=1)

    ks[pl.ds(rows, KEYS - SLOT), :] = jnp.zeros((KEYS - SLOT, GROUP), BF16)
    vs[pl.ds(rows, KEYS - SLOT), :] = jnp.zeros((KEYS - SLOT, GROUP), BF16)

    for hg in range(groups):
        gproj = gprojs[hg]
        bias_q, bias_k, bias_v = (
            b_qkv[:, t * width + hg * GROUP : t * width + (hg + 1) * GROUP] for t in range(3)
        )
        for t in range(3):
            loads["qkv", hg, t].wait()
        if hg == 0:
            loads["wo"].wait()
        raw = dot(normed[...], w_qkv[hg][:, lanes_of(0)]) + bias_q
        unit, inverse = head_norm(raw)
        nq[...] = unit
        rq[...] = inverse
        qs[...] = (unit * q_gain).astype(BF16) * SCALE
        raw = dot(normed[...], w_qkv[hg][:, lanes_of(1)]) + bias_k
        unit, inverse = head_norm(raw)
        nk[...] = unit
        rk[...] = inverse
        ks[pl.ds(0, rows), :] = (unit * k_gain).astype(BF16)
        raw = dot(normed[...], w_qkv[hg][:, lanes_of(2)]) + bias_v
        vs[pl.ds(0, rows), :] = raw.astype(BF16)
        gm[...] = dot(grow[...], w_o[lanes_of(hg), :], 1, 1).astype(BF16)
        point(4.5)

        def one_image(image):
            start = image * SLOT
            span = pl.ds(start, SLOT)
            window = pl.ds(start, KEYS)
            seen = pair_lane < lengths_ref[base + image // IMAGES, image % IMAGES]
            for pair in range(GROUP // KEYS):
                lanes = pl.ds(pair * KEYS, KEYS)
                query, grad = qs[span, lanes], gm[span, lanes]
                keys, values = two_heads(ks[window, lanes]), two_heads(vs[window, lanes])
                weight = jnp.where(seen, jnp.exp(dot(query, keys, 1, 1)), 0.0)
                probs = weight * over_heads(weight, invert)
                grad_probs = dot(grad, values, 1, 1)
                inner = over_heads(probs * grad_probs, lambda total: total)
                grad_scores = (probs * (grad_probs - inner)).astype(BF16)
                probs_low = probs.astype(BF16)
                mixed[span, pl.ds(hg * GROUP + pair * KEYS, KEYS)] = dot(probs_low, values).astype(
                    BF16
                )
                dq[span, lanes] = dot(grad_scores, keys) * SCALE
                dk[span, lanes] = dot(stacked(grad_scores), two_heads(query), 0, 0)[:SLOT]
                gproj[span, pl.ds(2 * GROUP + pair * KEYS, KEYS)] = dot(
                    stacked(probs_low), two_heads(grad), 0, 0
                )[:SLOT].astype(BF16)

        for image in range(0, images, 2):
            one_image(image)
            one_image(image + 1)
            point(1.3)
        if hg == groups - 1:
            for part in range(groups):
                flip(mixed, turned, part)
            if wired:
                index = net.open()
                for lane, size, part_axes in ((0, KEYS, XY), (KEYS, 2 * KEYS, YX)):
                    sums = dot(turned[...], grow[:, pl.ds(2 * lane, 2 * size)])
                    net.put(index, sums, lane, part_axes)
                    cost(1.1)
                    net.start(index, chunks + groups, part_axes, lane, size)
                point(0.0)
            else:
                parking.put(dot(turned[...], grow[...]), chunks + groups)

        axes = (YX, XY, YX)[hg]
        last = hg == groups - 1
        index = net.open() if wired else None
        parts = {}

        def part_grad(t, part_axes):
            sums = dot(flipped[...], gproj[:, lanes_of(t)])
            small_ref[pl.ds(4 + hg, 1), lanes_of(t)] = sums[width : width + 1]
            if wired:
                net.put(index, sums[:width], t * KEYS, part_axes)
                if last:
                    net.start(index, chunks + hg, part_axes, t * KEYS, KEYS)
            else:
                parts[t] = sums[:width]

        def norm_back(side, grad_ref, unit_ref, inverse_ref, gain):
            grad, unit = grad_ref[...], unit_ref[...]
            gain_sum = jnp.sum(grad * unit, axis=0, keepdims=True)
            small_ref[pl.ds(3 + side, 1), pl.ds(width, GROUP)] += gain_sum
            grad = grad * gain
            back = grad - head_mean(grad, False) - unit * head_mean(grad * unit, False)
            gproj[:, lanes_of(side)] = (back * inverse_ref[...]).astype(BF16)

        cost(0.7)
        part_grad(2, ZX if last else axes)
        norm_back(0, dq, nq, rq, q_gain)
        cost(1.5)
        if last:
            point(0.0)
        part_grad(0, XY if last else axes)
        norm_back(1, dk, nk, rk, k_gain)
        cost(1.5)
        if last:
            point(0.0)
        part_grad(1, YX if last else axes)
        if not wired:
            parking.put(jnp.concatenate([parts[t] for t in range(3)], axis=1), chunks + hg)
        elif not last:
            net.start(index, chunks + hg, axes, 0, width // 2)
        point(0.0)

    add_gnorm(gpre_odd, w_in[chunks - 1], False)
    point(1.7)
    for hg in range(groups):
        add_gnorm(gprojs[hg], w_qkv[hg], False)
        if hg == 0:
            load("tok again", tokens_hbm, hid_even)
        if hg == 1:
            load("cot again", cot_hbm, gpre_even)
        point(1.7)
    ln_gain = ln_gain_ref[...].reshape(1, width)
    b_o = b_o_ref[...].reshape(1, width)
    gain_grad = jnp.zeros((1, width), F32)
    for s in range(seqs):
        span = pl.ds(s * SEQ, SEQ)
        unit, inverse = row_stats(packed[span, :].astype(F32))
        grad = gnorm[span, :]
        gain_grad = gain_grad + jnp.sum(grad * unit, axis=0, keepdims=True)
        grad = grad * ln_gain
        back = grad - jnp.mean(grad, axis=1, keepdims=True)
        back = (back - unit * jnp.mean(grad * unit, axis=1, keepdims=True)) * inverse
        normed[span, :] = (grow[span, :].astype(F32) + back).astype(BF16)
    for t in range(width // GROUP):
        small_ref[pl.ds(t, 1), pl.ds(width, GROUP)] = gain_grad[:, t * GROUP : (t + 1) * GROUP]
    if wired:
        net.start_small()
    point(1.5)
    finals = []
    loads["tok again"].wait()
    loads["cot again"].wait()

    def hand_over(source, target):
        copy = pltpu.make_async_copy(source, target, done_sem.at[len(finals)])
        copy.start()
        finals.append(copy)

    for s in range(seqs):
        span = pl.ds(s * SEQ, SEQ)
        place = position_slots([lengths_ref[base + s, j] for j in range(IMAGES)])
        put = one_hot(place)
        padding = jnp.where(place < 0, 1.0, 0.0)
        attended = (dot(mixed[span, :], w_o[...]) + b_o).astype(BF16).astype(F32)
        result = packed[span, :].astype(F32) + (attended + hid_odd[span, :].astype(F32))
        result = dot(put, result.astype(BF16)) + padding * hid_even[span, :].astype(F32)
        hid_even[span, :] = result.astype(BF16)
        hand_over(hid_even.at[span], output_hbm.at[span])
        point(1.2)
        grads = dot(put, normed[span, :]) + padding * gpre_even[span, :].astype(F32)
        gpre_even[span, :] = grads.astype(BF16)
        hand_over(gpre_even.at[span], grad_tokens_hbm.at[span])
        point(0.8)
    if wired:
        net.drain()
        hand_over(net.fin, pieces_hbm)
    else:
        parking.finish()
    hand_over(small_ref, small_hbm)
    for copy in finals:
        copy.wait()


def split_lanes(block, groups):
    width = block.shape[1] // 3
    return jnp.concatenate(
        [
            block[:, hg * width + t * GROUP : hg * width + (t + 1) * GROUP]
            for t in range(3)
            for hg in range(groups)
        ],
        axis=1,
    )


def fold_heads(gains):
    return sum(gains[:, h * HEAD : (h + 1) * HEAD] for h in range(GROUP // HEAD))


def small_parts(small, chunks, groups, width):
    b_in = jnp.concatenate([small[f : f + 1, :width] for f in range(chunks)], axis=1)
    b_qkv = jnp.concatenate([small[4 + hg : 5 + hg, :width] for hg in range(groups)], axis=1)
    ln = jnp.concatenate([small[t : t + 1, width:] for t in range(width // GROUP)], axis=1)
    gains = [fold_heads(small[3 + side : 4 + side, width:]) for side in range(2)]
    return ln, split_lanes(b_qkv, groups), gains[0], gains[1], small[7:8, :width], b_in


def finish_kernel(
    rows_hbm, grads_hbm, fin_hbm, small_hbm, output_hbm, grad_tokens_hbm, g_ln, g_qkv_hbm, g_b_qkv,
    g_q, g_k, g_o_hbm, g_b_o, g_in_hbm, g_b_in, g_out_hbm, g_b_out, held, fin, small, g_qkv, g_o, g_in,
    g_out, sem,
):
    comes = [
        pltpu.make_async_copy(source, target, sem.at[0, i])
        for i, (source, target) in enumerate(
            ((fin_hbm, fin), (small_hbm, small), (rows_hbm, held.at[0]), (grads_hbm, held.at[1]))
        )
    ]
    goes = [
        pltpu.make_async_copy(source, target, sem.at[1, i])
        for i, (source, target) in enumerate(
            (
                (held.at[0], output_hbm), (held.at[1], grad_tokens_hbm), (g_in, g_in_hbm),
                (g_qkv, g_qkv_hbm), (g_out, g_out_hbm), (g_o, g_o_hbm),
            )
        )
    ]
    for copy in comes:
        copy.start()
    width = g_o.shape[1]
    chunks, groups = g_in.shape[1] // width, width // GROUP

    def whole(shard, lane, size):
        return jnp.concatenate(
            [fin[side, shard, :, lane : lane + size].astype(F32) for side in range(2)], axis=1
        )

    comes[0].wait()
    for f in range(chunks):
        g_in[:, f * width : (f + 1) * width] = whole(f, 0, width // 2)
    goes[2].start()
    for hg in range(groups):
        for t in range(3):
            place = t * width + hg * GROUP
            g_qkv[:, place : place + GROUP] = whole(chunks + hg, t * KEYS, KEYS)
    goes[3].start()
    for i in range(2):
        comes[2 + i].wait()
        goes[i].start()
    for j in range(4):
        g_out[j * BLOCK : (j + 1) * BLOCK, :] = whole(chunks + groups + 1 + j, 0, width // 2)
    goes[4].start()
    g_o[:, :GROUP] = whole(chunks + groups, 0, KEYS)
    g_o[:, GROUP:] = whole(chunks + groups, KEYS, 2 * KEYS)
    goes[5].start()
    comes[1].wait()
    ln, b_qkv, q, k, b_out, b_in = small_parts(small[...], chunks, groups, width)
    for ref, value in (
        (g_ln, ln), (g_b_qkv, b_qkv), (g_q, q), (g_k, k), (g_b_o, b_out), (g_b_in, b_in), (g_b_out, b_out)
    ):
        ref[...] = value.reshape(value.shape[1])
    for copy in goes:
        copy.wait()


def local(n_dp, tokens, lengths, cotangent, ln_gain, w_qkv, b_qkv, q_gain, k_gain, w_o, b_o, w_in, b_in, w_out, b_out):
    rows, width = tokens.shape
    hidden_width = w_in.shape[1]
    chunks = hidden_width // width
    groups = width // GROUP
    seqs = rows // SEQ
    shards = chunks + groups + 1
    everyone = shards + chunks
    wired = n_dp * BLOCK == width and n_dp == 4 * chunks
    half = width // 2
    extra = KEYS - SLOT
    anywhere = pl.BlockSpec(memory_space=pl.ANY)
    vmem = pl.BlockSpec(memory_space=pltpu.VMEM)
    smem = pl.BlockSpec(memory_space=pltpu.SMEM)
    wide = lambda *shape: pltpu.VMEM(shape, F32)
    slim = lambda *shape: pltpu.VMEM(shape, BF16)
    flags = lambda *shape: pltpu.SemaphoreType.DMA(shape)
    low = lambda *shape: jax.ShapeDtypeStruct(shape, BF16)
    full = lambda *shape: jax.ShapeDtypeStruct(shape, F32)
    small_shape = (8, width + GROUP)

    if wired:
        out_piece = low(2, shards + 4, BLOCK, half)
        flights = 6 * (shards + 3) + 3 * chunks + 3 + 5
        others = [
            slim(SLOTS, 2, 16, BLOCK, half), slim(RING, 16, BLOCK, half),
            slim(everyone, 8, BLOCK, half), slim(everyone, 4, BLOCK, half),
            slim(shards, 2, BLOCK, half), slim(shards, 1, BLOCK, half), slim(4, 4, BLOCK, half),
            slim(2, 4, BLOCK, half), slim(1, 4, BLOCK, half), slim(2, shards + 4, BLOCK, half),
            wide(5, *small_shape), flags(flights), flags(flights),
        ]
        settings = dict(collective_id=0, has_side_effects=True)
    else:
        out_piece = low(everyone, width, width)
        others = [slim(2, width, width), flags(2)]
        settings = {}
    output, grad_tokens, pieces, small = pl.pallas_call(
        functools.partial(layer_kernel, wired),
        out_shape=(low(rows, width), low(rows, width), out_piece, full(*small_shape)),
        in_specs=[
            smem, anywhere, anywhere, vmem, anywhere, vmem, vmem, vmem, anywhere, vmem, anywhere,
            vmem, anywhere, vmem,
        ],
        out_specs=(anywhere,) * 4,
        scratch_shapes=[slim(6, width, width)]
        + [slim(rows, width)] * 9
        + [
            slim(width + 16, rows), slim(width, rows), wide(rows, width), wide(rows, width),
            slim(rows, GROUP), slim(rows + extra, GROUP), slim(rows + extra, GROUP),
            slim(rows, GROUP),
        ]
        + [wide(rows, GROUP)] * 3
        + [wide(*small_shape), flags(5 + 2 * chunks + 3 * groups), flags(2 * seqs + 2)]
        + others,
        compiler_params=pltpu.CompilerParams(vmem_limit_bytes=62 << 20, **settings),
    )(
        lengths, tokens, cotangent, ln_gain, w_qkv, b_qkv, q_gain, k_gain, w_o, b_o, w_in, b_in,
        w_out, b_out,
    )

    if wired:
        return pl.pallas_call(
            finish_kernel,
            out_shape=(
                low(rows, width), low(rows, width), full(width), full(BLOCK, 3 * width),
                full(3 * width), full(HEAD), full(HEAD), full(BLOCK, width), full(width),
                full(BLOCK, hidden_width), full(hidden_width), full(4 * BLOCK, width), full(width),
            ),
            in_specs=[anywhere] * 4,
            out_specs=(
                anywhere, anywhere, vmem, anywhere, vmem, vmem, vmem, anywhere, vmem, anywhere, vmem,
                anywhere, vmem,
            ),
            scratch_shapes=[
                slim(2, rows, width), slim(2, shards + 4, BLOCK, half), wide(*small_shape),
                wide(BLOCK, 3 * width), wide(BLOCK, width), wide(BLOCK, hidden_width),
                wide(4 * BLOCK, width), flags(2, 6),
            ],
        )(output, grad_tokens, pieces, small)

    def scatter(block, dim):
        part = lax.psum_scatter(block, "dp", scatter_dimension=dim, tiled=True)
        return lax.psum(part, "branch").astype(F32)

    grad_out = scatter(pieces[shards:].reshape(hidden_width, width), 0)
    reduced = scatter(pieces[:shards], 1)
    grad_in = jnp.concatenate([reduced[f] for f in range(chunks)], axis=1)
    qkv = jnp.concatenate([reduced[chunks + hg] for hg in range(groups)], axis=1)
    small = lax.psum(small, ("dp", "branch"))
    ln, g_b_qkv, g_q, g_k, g_b_out, g_b_in = (
        part[0] for part in small_parts(small, chunks, groups, width)
    )
    return (
        output, grad_tokens, ln, split_lanes(qkv, groups), g_b_qkv, g_q, g_k,
        reduced[chunks + groups], g_b_out, grad_in, g_b_in, grad_out, g_b_out,
    )


def solution(mesh):
    rows, split, whole = P(("dp", "branch"), None), P("dp", None), P()
    return jax.shard_map(
        functools.partial(local, mesh.shape["dp"]),
        mesh=mesh,
        in_specs=(rows, split, rows) + (whole,) * 11,
        out_specs=(
            rows, rows, whole, split, whole, whole, whole, split, whole, split, whole, split, whole,
        ),
        check_vma=False,
    )
```

```python
import functools
import math

import jax
import jax.numpy as jnp
from jax import lax
from jax.experimental import pallas as pl
from jax.experimental.pallas import tpu as pltpu
from jax.sharding import PartitionSpec as P

HEAD = 64
SEQ = 448
IMAGES = 4
SLOT = SEQ // IMAGES
LEAST = 32
KEYS = 128
GROUP = 256
EPS = 1e-06
SCALE = 0.125
F32 = jnp.float32
BF16 = jnp.bfloat16
GELU_A = math.sqrt(2.0 / math.pi)
GELU_B = 0.044715


def dot(left, right, left_dim=1, right_dim=0):
    return lax.dot_general(
        left, right, (((left_dim,), (right_dim,)), ((), ())), preferred_element_type=F32
    )


def image_rows(block, lens, image):
    row = lax.broadcasted_iota(jnp.int32, (SLOT, 1), 0)
    if image == 0:
        return jnp.where(row < lens[0], block[:SLOT].astype(F32), 0.0)
    first, end = LEAST * image, SLOT * (image + 1)
    start = sum(lens[1:image], lens[0])
    lane = lax.broadcasted_iota(jnp.int32, (SLOT, end - first), 1) + first
    hit = (lane - row == start) & (row < lens[image])
    return dot(jnp.where(hit, 1.0, 0.0).astype(BF16), block[first:end])


def position_slots(lens):
    row = lax.broadcasted_iota(jnp.int32, (SEQ, 1), 0)
    held = jnp.full((SEQ, 1), -1, jnp.int32)
    start = jnp.int32(0)
    for image in range(IMAGES):
        place = row - start
        held = jnp.where((place >= 0) & (place < lens[image]), place + SLOT * image, held)
        start = start + lens[image]
    return held


def put_back(place, block):
    parts = []
    for i in range(IMAGES):
        lane = lax.broadcasted_iota(jnp.int32, (SLOT, SEQ - SLOT * i), 1) + SLOT * i
        hit = lane == place[SLOT * i : SLOT * (i + 1)]
        parts.append(dot(jnp.where(hit, 1.0, 0.0).astype(BF16), block[SLOT * i :]))
    return jnp.concatenate(parts, axis=0)


def row_stats(values):
    centered = values - jnp.mean(values, axis=1, keepdims=True)
    spread = jnp.mean(centered * centered, axis=1, keepdims=True)
    inverse = lax.rsqrt(spread + EPS)
    return centered * inverse, inverse


def gelu_pair(pre, grad):
    square = pre * pre
    bent = jnp.tanh(pre * (GELU_A + (GELU_A * GELU_B) * square))
    half = 0.5 * pre
    up = 1.0 + bent
    hidden = half * up
    slope = half * (GELU_A + (3.0 * GELU_A * GELU_B) * square)
    return hidden, (up * (0.5 + (1.0 - bent) * slope)) * grad


MESH = pl.DeviceIdType.MESH
BLOCK = 48
SLOTS = 2
RING = 8
XY, YX = ("x", "y", "z0", "z1"), ("y", "x", "z0", "z1")
ZX, ZY = ("z0", "z1", "x", "y"), ("z0", "z1", "y", "x")
RATES = {"core": 400e3, "x": 42e3, "y": 42e3, "z0": 42e3, "z1": 21e3}
LATENCY = 2.0


class Piece:
    def __init__(self, index, shard, axes, lanes):
        self.index, self.shard, self.axes, self.lanes = index, shard, axes, lanes
        self.stage, self.copy, self.eta = 0, None, 0.0

    def cut(self, ref):
        return ref.at[:, :, self.lanes]


class Small:
    def __init__(self):
        self.stage, self.copy, self.eta = 0, None, 0.0


class Exchange:
    def __init__(self, refs, chunks):
        (self.both, self.inbox, self.in1, self.in2, self.in3, self.in4, self.osum, self.oin3,
         self.oin4, self.fin, self.small, self.small_in, self.send_sem, self.recv_sem) = refs
        self.chunks = chunks
        self.dp, self.core = lax.axis_index("dp"), lax.axis_index("branch")
        self.bits = {
            "x": lax.rem(self.dp, 2),
            "y": lax.rem(self.dp // 2, 2),
            "z0": lax.rem(self.dp // 4, 2),
            "z1": lax.rem(self.dp // 8, 2),
        }
        self.far = {
            axis: (self.dp + step - 2 * step * self.bits[axis], self.core)
            for axis, step in (("x", 1), ("y", 2), ("z0", 4), ("z1", 8))
        }
        self.far["core"] = (self.dp, 1 - self.core)
        self.far["core x"] = (self.far["x"][0], 1 - self.core)
        self.far["y z0"] = (self.far["y"][0] + self.far["z0"][0] - self.dp, self.core)
        self.bits["core"] = self.core
        self.items, self.opened = [], 0
        self.flights, self.merged, self.now, self.free = 0, 0, 0.0, {}

    def greet(self):
        barrier = pltpu.get_barrier_semaphore()
        for device in self.far.values():
            pl.semaphore_signal(barrier, inc=1, device_id=device, device_id_type=MESH)

    def meet(self):
        pl.semaphore_wait(pltpu.get_barrier_semaphore(), len(self.far))

    def send(self, item, source, target, axis):
        copy = pltpu.make_async_remote_copy(
            src_ref=source, dst_ref=target, send_sem=self.send_sem.at[self.flights],
            recv_sem=self.recv_sem.at[self.flights], device_id=self.far[axis], device_id_type=MESH,
        )
        self.flights += 1
        copy.start()
        link, axis = axis[0], axis.split()[0]
        size = source.dtype.itemsize * math.prod(source.shape)
        self.free[link] = max(self.free.get(link, 0.0), self.now) + size / RATES[axis]
        item.copy, item.eta = copy, self.free[link] + LATENCY

    def open(self):
        index = self.opened
        for behind, stage in ((SLOTS, 1), (RING - SLOTS, 2)):
            while any(
                item.index == index - behind and item.stage < stage
                for item in self.items
                if isinstance(item, Piece)
            ):
                self.advance(min(self.under_way(), key=lambda item: item.eta))
        self.opened += 1
        return index

    def put(self, index, value, lane, axes):
        half = value.shape[1] // 2
        for side, role in ((0, self.core), (1, 1 - self.core)):
            target = self.both.at[index % SLOTS, role, :, :, pl.ds(lane, half)]
            put_blocks(value, target, side, axes)

    def start(self, index, shard, axes, lane, width):
        piece = Piece(index, shard, axes, pl.ds(lane, width))
        self.send(
            piece, piece.cut(self.both.at[index % SLOTS, 1]), piece.cut(self.inbox.at[index % RING]),
            "core",
        )
        self.items.append(piece)

    def halve(self, piece, held, held_at, arrived, count, axis, target):
        near = self.bits[axis] * count
        away = (1 - self.bits[axis]) * count
        span = pl.ds(away, count)
        arrived[span] = arrived[span] + held[pl.ds(held_at + away, count)]
        self.send(piece, arrived.at[span], target, axis)
        span = pl.ds(near, count)
        arrived[span] = arrived[span] + held[pl.ds(held_at + near, count)]

    def advance(self, piece):
        for copy in piece.copy if isinstance(piece.copy, list) else [piece.copy]:
            copy.wait()
        self.now = max(self.now, piece.eta)
        piece.copy = None
        if isinstance(piece, Small):
            self.advance_small(piece)
            return
        k, shard, axes, cut = piece.index, piece.shard, piece.axes, piece.cut
        whole = isinstance(shard, int)
        in0, in1, in2 = cut(self.inbox.at[k % RING]), cut(self.in1.at[k]), cut(self.in2.at[k])
        if whole:
            in3, in4 = cut(self.in3.at[shard]), cut(self.in4.at[shard])
        if piece.stage == 0:
            self.halve(piece, cut(self.both.at[k % SLOTS, 0]), 0, in0, 8, axes[0], in1)
        elif piece.stage == 1:
            self.halve(piece, in0, self.bits[axes[0]] * 8, in1, 4, axes[1], in2)
        elif piece.stage == 2 and whole:
            self.halve(piece, in1, self.bits[axes[1]] * 4, in2, 2, axes[2], in3)
        elif piece.stage == 2:
            place = shard[0] % 2 * 2 + shard[0] // 2
            self.osum[place] = in2[...] + in1[pl.ds(self.bits[axes[1]] * 4, 4)]
            self.merged += 1
            if self.merged < self.chunks:
                piece.stage = 5
            else:
                far = pl.ds((1 - self.bits["z0"]) * 2, 2)
                self.send(piece, self.osum.at[far], self.oin3, "z0")
        elif piece.stage == 3 and whole:
            self.halve(piece, in2, self.bits[axes[2]] * 2, in3, 1, axes[3], in4)
        elif piece.stage == 3:
            self.halve(piece, self.osum, self.bits["z0"] * 2, self.oin3, 1, "z1", self.oin4)
        elif piece.stage == 4:
            if whole:
                final = self.fin.at[self.core, pl.ds(shard, 1), :, piece.lanes]
                final[...] = in4[...] + in3[pl.ds(self.bits[axes[3]], 1)]
            else:
                final = self.fin.at[self.core, pl.ds(self.fin.shape[1] - 4, 4)]
                final[...] = self.oin4[0] + self.oin3[self.bits["z1"]]
            self.send(piece, final, final, "core")
        piece.stage += 1

    def send_small(self, item):
        axes = (("core", "x"), ("y", "z0"), ("z1",))[item.stage]
        me = sum(self.bits[axis] << i for i, axis in enumerate(axes))
        self.small_in[item.stage, me] = self.small[...]
        copies = []
        for axis in axes + ((" ".join(axes),) if len(axes) > 1 else ()):
            source = self.small_in.at[item.stage, me]
            self.send(item, source, source, axis)
            copies.append(item.copy)
        item.copy, item.eta = copies, self.now + LATENCY

    def start_small(self):
        item = Small()
        self.send_small(item)
        self.items.append(item)

    def advance_small(self, item):
        parts = [self.small_in[item.stage, i] for i in range(4 if item.stage < 2 else 2)]
        while len(parts) > 1:
            parts = [parts[i] + parts[i + 1] for i in range(0, len(parts), 2)]
        self.small[...] = parts[0]
        item.stage += 1
        if item.stage < 3:
            self.send_small(item)

    def under_way(self):
        return [item for item in self.items if item.copy is not None]

    def progress(self, cost):
        self.now += cost
        while True:
            due = [item for item in self.under_way() if item.eta <= self.now]
            if not due:
                return
            self.advance(min(due, key=lambda item: item.eta))

    def drain(self):
        while self.under_way():
            self.advance(min(self.under_way(), key=lambda item: item.eta))


def put_blocks(value, target, side, axes):
    half = value.shape[1] // 2
    for block in range(16):
        place = block
        if axes is not None and len(axes) == 4:
            bit = dict(x=block % 2, y=block // 2 % 2, z0=block // 4 % 2, z1=block // 8)
            place = sum(bit[axis] << (3 - i) for i, axis in enumerate(axes))
        target[place] = value[
            BLOCK * block : BLOCK * (block + 1), half * side : half * (side + 1)
        ].astype(BF16)


def make_flip():
    eye = jnp.where(
        lax.broadcasted_iota(jnp.int32, (GROUP, GROUP), 0)
        == lax.broadcasted_iota(jnp.int32, (GROUP, GROUP), 1),
        1.0,
        0.0,
    ).astype(BF16)

    def flip(source, target):
        for part in range(source.shape[1] // GROUP):
            lanes = pl.ds(part * GROUP, GROUP)
            target[lanes, :] = dot(eye, source[:, lanes], 1, 1).astype(BF16)

    return flip


class Parking:
    def __init__(self, stage, target, sem):
        self.stage, self.target, self.sem = stage, target, sem
        self.sent = []

    def put(self, value, index):
        slot = len(self.sent) % 2
        if len(self.sent) >= 2:
            self.sent[-2].wait()
        self.stage[slot] = value.astype(BF16)
        copy = pltpu.make_async_copy(self.stage.at[slot], self.target.at[index], self.sem.at[slot])
        copy.start()
        self.sent.append(copy)

    def finish(self):
        for copy in self.sent[-2:]:
            copy.wait()


def layer_kernel(
    wired,
    lengths_ref, tokens_hbm, cot_hbm, ln_gain_ref, w_qkv_hbm, b_qkv_ref, q_gain_ref, k_gain_ref,
    w_o_hbm, b_o_ref, w_in_hbm, b_in_ref, w_out_hbm, b_out_ref,
    output_hbm, grad_tokens_hbm, pieces_hbm, small_hbm,
    weights, tok, cot, packed, grow, normed, hid_even, gpre_even, hid_odd, gpre_odd,
    flipped, turned, fed, gnorm, qs, ks, vs, gm, rk, dq, dk, small_ref,
    load_sem, done_sem, *refs,
):
    rows, width = tok.shape
    hidden_width = w_in_hbm.shape[1]
    chunks = hidden_width // width
    groups = width // GROUP
    seqs = rows // SEQ
    images = seqs * IMAGES
    base = lax.axis_index("branch") * seqs
    assert chunks == 4 and groups == 3
    hid, gpre = (hid_even, hid_odd), (gpre_even, gpre_odd)
    mixed, gprojs = tok, (hid_even, gpre_even, cot)
    w_in = [weights.at[f % 3] for f in range(chunks)]
    w_out = [weights.at[3 + f % 3] for f in range(chunks)]
    w_qkv, w_o = [weights.at[1], weights.at[4], weights.at[2]], weights.at[5]
    nq, rq, nk = (fed.at[:, pl.ds(part * GROUP, GROUP)] for part in range(3))
    loads = {}

    def load(name, source, target):
        copy = pltpu.make_async_copy(source, target, load_sem.at[len(loads)])
        copy.start()
        loads[name] = copy

    def load_chunk(f):
        cols = pl.ds(f * width, width)
        load(("in", f), w_in_hbm.at[:, cols], w_in[f])
        load(("out", f), w_out_hbm.at[cols, :], w_out[f])

    def load_qkv(hg):
        for t in range(3):
            load(
                ("qkv", hg, t),
                w_qkv_hbm.at[:, pl.ds(t * width + hg * GROUP, GROUP)],
                w_qkv[hg].at[:, pl.ds(t * GROUP, GROUP)],
            )

    load("tok", tokens_hbm, tok)
    load("cot", cot_hbm, cot)
    for f in range(3):
        load_chunk(f)
    small_ref[...] = jnp.zeros_like(small_ref)
    net, parking = None, None
    if wired:
        net = Exchange(refs[:10] + (small_ref,) + refs[10:], chunks)
        net.greet()
    else:
        parking = Parking(refs[0], pieces_hbm, refs[1])

    def emit(value, shard, axes):
        if wired:
            index = net.open()
            net.put(index, value, 0, axes)
            net.start(index, shard, axes, 0, width // 2)
        else:
            parking.put(value, shard if isinstance(shard, int) else chunks + groups + 1 + shard[0])

    def point(cost):
        if wired:
            net.progress(cost)

    def cost(amount):
        if wired:
            net.now += amount

    def lanes_of(part):
        return pl.ds(part * GROUP, GROUP)

    ones_row = jnp.where(lax.broadcasted_iota(jnp.int32, (16, rows), 0) == 0, 1.0, 0.0)
    flipped[pl.ds(width, 16), :] = ones_row.astype(BF16)
    eye = jnp.where(
        lax.broadcasted_iota(jnp.int32, (GROUP, GROUP), 0)
        == lax.broadcasted_iota(jnp.int32, (GROUP, GROUP), 1),
        1.0,
        0.0,
    ).astype(BF16)

    def flip(source, target, part):
        target[lanes_of(part), :] = dot(eye, source[:, lanes_of(part)], 1, 1).astype(BF16)

    loads["tok"].wait()
    loads["cot"].wait()
    grad_sum = jnp.zeros((1, width), F32)
    for s in range(seqs):
        lens = [lengths_ref[base + s, j] for j in range(IMAGES)]
        for image in range(IMAGES):
            span = pl.ds(s * SEQ + image * SLOT, SLOT)
            sequence = pl.ds(s * SEQ, SEQ)
            rows_here = image_rows(tok[sequence, :], lens, image)
            packed[span, :] = rows_here.astype(BF16)
            unit, _ = row_stats(rows_here)
            normed[span, :] = (unit * ln_gain_ref[...].reshape(1, width)).astype(BF16)
            grads_here = image_rows(cot[sequence, :], lens, image)
            grow[span, :] = grads_here.astype(BF16)
            grad_sum = grad_sum + jnp.sum(grads_here, axis=0, keepdims=True)
    small_ref[pl.ds(7, 1), pl.ds(0, width)] = grad_sum
    for part in range(groups):
        flip(normed, flipped, part)
    cost(6.0)

    def add_fed(f):
        for part in range(groups):
            lanes = lanes_of(part)
            up = dot(hid[f % 2][...], w_out[f][:, lanes])
            fed[:, lanes] = up if f == 0 else fed[:, lanes] + up

    def add_gnorm(source, target, first, step=None):
        for part in range(groups):
            lanes = lanes_of(part)
            down = dot(source[...], target[lanes, :], 1, 1)
            gnorm[:, lanes] = down if first else gnorm[:, lanes] + down
            if step is not None:
                point(step)

    if wired:
        net.meet()
    b_in = b_in_ref[...].reshape(1, hidden_width)
    ready = None

    def activate():
        f, c, pre, back = ready
        place = f * width + c * GROUP
        hidden, grad_pre = gelu_pair(pre + b_in[:, place : place + GROUP], back)
        hid[f % 2][:, lanes_of(c)] = hidden.astype(BF16)
        gpre[f % 2][:, lanes_of(c)] = grad_pre.astype(BF16)

    def send_w_in(f):
        sums = dot(flipped[...], gpre[f % 2][...])
        cost(2.2)
        emit(sums[:width], f, XY)
        small_ref[pl.ds(f, 1), pl.ds(0, width)] = sums[width : width + 1]
        point(0.0)

    def send_w_out(f):
        cost(1.9)
        emit(dot(turned[...], grow[...]), (f,), YX[:2])
        point(0.0)

    for f in range(chunks):
        loads["in", f].wait()
        loads["out", f].wait()
        for c in range(groups):
            lanes = lanes_of(c)
            pre = dot(normed[...], w_in[f][:, lanes])
            back = dot(grow[...], w_out[f][lanes, :], 1, 1)
            if ready is not None:
                activate()
            ready = (f, c, pre, back)
            if f > 0 and c == 0:
                for part in range(groups):
                    flip(hid[1 - f % 2], turned, part)
            if f > 0 and c == 2:
                add_fed(f - 1)
                add_gnorm(gpre[1 - f % 2], w_in[f - 1], f == 1)
            point((1.7, 1.2, 4.6)[c] if f > 0 else 1.2)
            if f > 0 and c == 0:
                send_w_in(f - 1)
            if f > 0 and c == 1:
                send_w_out(f - 1)
        if f == 1:
            load_chunk(3)
        if f == 2:
            load_qkv(0)
            load_qkv(1)
        if f == 3:
            load_qkv(2)
            load("wo", w_o_hbm, w_o)
    activate()
    for part in range(groups):
        flip(hid_odd, turned, part)
    send_w_in(chunks - 1)
    send_w_out(chunks - 1)

    add_fed(chunks - 1)
    hid_odd[...] = (fed[...] + b_out_ref[...].reshape(1, width)).astype(BF16)
    point(1.9)

    same_head = (
        lax.broadcasted_iota(jnp.int32, (GROUP, GROUP), 0) // HEAD
        == lax.broadcasted_iota(jnp.int32, (GROUP, GROUP), 1) // HEAD
    )
    average = jnp.where(same_head, 1.0 / HEAD, 0.0).astype(BF16)
    q_gain = jnp.concatenate([q_gain_ref[...].reshape(1, HEAD)] * (GROUP // HEAD), axis=1)
    k_gain = jnp.concatenate([k_gain_ref[...].reshape(1, HEAD)] * (GROUP // HEAD), axis=1)
    b_qkv = b_qkv_ref[...].reshape(1, 3 * width)
    lane = lax.broadcasted_iota(jnp.int32, (1, KEYS), 1)
    pair_lane = jnp.concatenate([lane, lane], axis=1)
    first_head = jnp.where(lane < HEAD, 1.0, 0.0).astype(BF16)
    second_head = jnp.where(lane < HEAD, 0.0, 1.0).astype(BF16)

    def head_mean(values, split):
        high = values.astype(BF16)
        mean = dot(high, average)
        if split:
            mean = mean + dot((values - high.astype(F32)).astype(BF16), average)
        return mean

    def head_norm(raw):
        centered = raw - head_mean(raw, True)
        inverse = lax.rsqrt(head_mean(centered * centered, False) + EPS)
        return centered * inverse, inverse

    def two_heads(block):
        return jnp.concatenate([block * first_head, block * second_head], axis=0)

    def stacked(block):
        return jnp.concatenate([block[:, :KEYS], block[:, KEYS:]], axis=0)

    def invert(total):
        guess = pl.reciprocal(total, approx=True)
        return guess * (2.0 - total * guess)

    def over_heads(block, change):
        parts = []
        for head in range(2):
            part = block[:, head * KEYS : (head + 1) * KEYS]
            total = change(jnp.sum(part, axis=1, keepdims=True))
            parts.append(jnp.broadcast_to(total, part.shape))
        return jnp.concatenate(parts, axis=1)

    ks[pl.ds(rows, KEYS - SLOT), :] = jnp.zeros((KEYS - SLOT, GROUP), BF16)
    vs[pl.ds(rows, KEYS - SLOT), :] = jnp.zeros((KEYS - SLOT, GROUP), BF16)

    for hg in range(groups):
        gproj = gprojs[hg]
        bias_q, bias_k, bias_v = (
            b_qkv[:, t * width + hg * GROUP : t * width + (hg + 1) * GROUP] for t in range(3)
        )
        for t in range(3):
            loads["qkv", hg, t].wait()
        if hg == 0:
            loads["wo"].wait()
        raw = dot(normed[...], w_qkv[hg][:, lanes_of(0)]) + bias_q
        unit, inverse = head_norm(raw)
        nq[...] = unit
        rq[...] = inverse
        qs[...] = (unit * q_gain).astype(BF16) * SCALE
        raw = dot(normed[...], w_qkv[hg][:, lanes_of(1)]) + bias_k
        unit, inverse = head_norm(raw)
        nk[...] = unit
        rk[...] = inverse
        ks[pl.ds(0, rows), :] = (unit * k_gain).astype(BF16)
        raw = dot(normed[...], w_qkv[hg][:, lanes_of(2)]) + bias_v
        vs[pl.ds(0, rows), :] = raw.astype(BF16)
        gm[...] = dot(grow[...], w_o[lanes_of(hg), :], 1, 1).astype(BF16)
        point(4.5)

        def one_image(image):
            start = image * SLOT
            span = pl.ds(start, SLOT)
            window = pl.ds(start, KEYS)
            seen = pair_lane < lengths_ref[base + image // IMAGES, image % IMAGES]
            for pair in range(GROUP // KEYS):
                lanes = pl.ds(pair * KEYS, KEYS)
                query, grad = qs[span, lanes], gm[span, lanes]
                keys, values = two_heads(ks[window, lanes]), two_heads(vs[window, lanes])
                weight = jnp.where(seen, jnp.exp(dot(query, keys, 1, 1)), 0.0)
                probs = weight * over_heads(weight, invert)
                grad_probs = dot(grad, values, 1, 1)
                inner = over_heads(probs * grad_probs, lambda total: total)
                grad_scores = (probs * (grad_probs - inner)).astype(BF16)
                probs_low = probs.astype(BF16)
                mixed[span, pl.ds(hg * GROUP + pair * KEYS, KEYS)] = dot(probs_low, values).astype(
                    BF16
                )
                dq[span, lanes] = dot(grad_scores, keys) * SCALE
                dk[span, lanes] = dot(stacked(grad_scores), two_heads(query), 0, 0)[:SLOT]
                gproj[span, pl.ds(2 * GROUP + pair * KEYS, KEYS)] = dot(
                    stacked(probs_low), two_heads(grad), 0, 0
                )[:SLOT].astype(BF16)

        for image in range(0, images, 2):
            one_image(image)
            one_image(image + 1)
            point(1.3)
        if hg == groups - 1:
            for part in range(groups):
                flip(mixed, turned, part)
            if wired:
                index = net.open()
                for lane, size, part_axes in ((0, KEYS, XY), (KEYS, 2 * KEYS, YX)):
                    sums = dot(turned[...], grow[:, pl.ds(2 * lane, 2 * size)])
                    net.put(index, sums, lane, part_axes)
                    cost(1.1)
                    net.start(index, chunks + groups, part_axes, lane, size)
                point(0.0)
            else:
                parking.put(dot(turned[...], grow[...]), chunks + groups)

        axes = (YX, XY, YX)[hg]
        last = hg == groups - 1
        index = net.open() if wired else None
        parts = {}

        def part_grad(t, part_axes):
            sums = dot(flipped[...], gproj[:, lanes_of(t)])
            small_ref[pl.ds(4 + hg, 1), lanes_of(t)] = sums[width : width + 1]
            if wired:
                net.put(index, sums[:width], t * KEYS, part_axes)
                if last:
                    net.start(index, chunks + hg, part_axes, t * KEYS, KEYS)
            else:
                parts[t] = sums[:width]

        def norm_back(side, grad_ref, unit_ref, inverse_ref, gain):
            grad, unit = grad_ref[...], unit_ref[...]
            gain_sum = jnp.sum(grad * unit, axis=0, keepdims=True)
            small_ref[pl.ds(3 + side, 1), pl.ds(width, GROUP)] += gain_sum
            grad = grad * gain
            back = grad - head_mean(grad, False) - unit * head_mean(grad * unit, False)
            gproj[:, lanes_of(side)] = (back * inverse_ref[...]).astype(BF16)

        cost(0.7)
        part_grad(2, ZX if last else axes)
        norm_back(0, dq, nq, rq, q_gain)
        cost(1.5)
        if last:
            point(0.0)
        part_grad(0, XY if last else axes)
        norm_back(1, dk, nk, rk, k_gain)
        cost(1.5)
        if last:
            point(0.0)
        part_grad(1, YX if last else axes)
        if not wired:
            parking.put(jnp.concatenate([parts[t] for t in range(3)], axis=1), chunks + hg)
        elif not last:
            net.start(index, chunks + hg, axes, 0, width // 2)
        point(0.0)

    add_gnorm(gpre_odd, w_in[chunks - 1], False, 0.5)
    for hg in range(groups):
        add_gnorm(gprojs[hg], w_qkv[hg], False, 0.5)
        if hg == 0:
            load("tok again", tokens_hbm, hid_even)
        if hg == 1:
            load("cot again", cot_hbm, gpre_even)
    ln_gain = ln_gain_ref[...].reshape(1, width)
    b_o = b_o_ref[...].reshape(1, width)
    gain_grad = jnp.zeros((1, width), F32)
    for s in range(seqs):
        span = pl.ds(s * SEQ, SEQ)
        unit, inverse = row_stats(packed[span, :].astype(F32))
        grad = gnorm[span, :]
        gain_grad = gain_grad + jnp.sum(grad * unit, axis=0, keepdims=True)
        grad = grad * ln_gain
        back = grad - jnp.mean(grad, axis=1, keepdims=True)
        back = (back - unit * jnp.mean(grad * unit, axis=1, keepdims=True)) * inverse
        normed[span, :] = (grow[span, :].astype(F32) + back).astype(BF16)
        point(0.6)
    for t in range(width // GROUP):
        small_ref[pl.ds(t, 1), pl.ds(width, GROUP)] = gain_grad[:, t * GROUP : (t + 1) * GROUP]
    if wired:
        net.start_small()
    finals = []
    loads["tok again"].wait()
    loads["cot again"].wait()

    def hand_over(source, target):
        copy = pltpu.make_async_copy(source, target, done_sem.at[len(finals)])
        copy.start()
        finals.append(copy)

    for s in range(seqs):
        span = pl.ds(s * SEQ, SEQ)
        place = position_slots([lengths_ref[base + s, j] for j in range(IMAGES)])
        padding = jnp.where(place < 0, 1.0, 0.0)
        attended = (dot(mixed[span, :], w_o[...]) + b_o).astype(BF16).astype(F32)
        point(0.4)
        result = packed[span, :].astype(F32) + (attended + hid_odd[span, :].astype(F32))
        result = put_back(place, result.astype(BF16)) + padding * hid_even[span, :].astype(F32)
        hid_even[span, :] = result.astype(BF16)
        hand_over(hid_even.at[span], output_hbm.at[span])
        point(0.6)
        grads = put_back(place, normed[span, :]) + padding * gpre_even[span, :].astype(F32)
        gpre_even[span, :] = grads.astype(BF16)
        hand_over(gpre_even.at[span], grad_tokens_hbm.at[span])
        point(0.6)
    if wired:
        net.drain()
        hand_over(net.fin, pieces_hbm)
    else:
        parking.finish()
    hand_over(small_ref, small_hbm)
    for copy in finals:
        copy.wait()


def split_lanes(block, groups):
    width = block.shape[1] // 3
    return jnp.concatenate(
        [
            block[:, hg * width + t * GROUP : hg * width + (t + 1) * GROUP]
            for t in range(3)
            for hg in range(groups)
        ],
        axis=1,
    )


def fold_heads(gains):
    return sum(gains[:, h * HEAD : (h + 1) * HEAD] for h in range(GROUP // HEAD))


def small_parts(small, chunks, groups, width):
    b_in = jnp.concatenate([small[f : f + 1, :width] for f in range(chunks)], axis=1)
    b_qkv = jnp.concatenate([small[4 + hg : 5 + hg, :width] for hg in range(groups)], axis=1)
    ln = jnp.concatenate([small[t : t + 1, width:] for t in range(width // GROUP)], axis=1)
    gains = [fold_heads(small[3 + side : 4 + side, width:]) for side in range(2)]
    return ln, split_lanes(b_qkv, groups), gains[0], gains[1], small[7:8, :width], b_in


def finish_kernel(
    rows_hbm, grads_hbm, fin_hbm, small_hbm, output_hbm, grad_tokens_hbm, g_ln, g_qkv_hbm, g_b_qkv,
    g_q, g_k, g_o_hbm, g_b_o, g_in_hbm, g_b_in, g_out_hbm, g_b_out, held, fin, small, g_qkv, g_o, g_in,
    g_out, sem,
):
    comes = [
        pltpu.make_async_copy(source, target, sem.at[0, i])
        for i, (source, target) in enumerate(
            ((fin_hbm, fin), (small_hbm, small), (rows_hbm, held.at[0]), (grads_hbm, held.at[1]))
        )
    ]
    goes = [
        pltpu.make_async_copy(source, target, sem.at[1, i])
        for i, (source, target) in enumerate(
            (
                (held.at[0], output_hbm), (held.at[1], grad_tokens_hbm), (g_in, g_in_hbm),
                (g_qkv, g_qkv_hbm), (g_out, g_out_hbm), (g_o, g_o_hbm),
            )
        )
    ]
    for copy in comes:
        copy.start()
    width = g_o.shape[1]
    chunks, groups = g_in.shape[1] // width, width // GROUP

    def whole(shard, lane, size):
        return jnp.concatenate(
            [fin[side, shard, :, lane : lane + size].astype(F32) for side in range(2)], axis=1
        )

    comes[0].wait()
    for f in range(chunks):
        g_in[:, f * width : (f + 1) * width] = whole(f, 0, width // 2)
    goes[2].start()
    for hg in range(groups):
        for t in range(3):
            place = t * width + hg * GROUP
            g_qkv[:, place : place + GROUP] = whole(chunks + hg, t * KEYS, KEYS)
    goes[3].start()
    for i in range(2):
        comes[2 + i].wait()
        goes[i].start()
    for j in range(4):
        g_out[j * BLOCK : (j + 1) * BLOCK, :] = whole(chunks + groups + 1 + j, 0, width // 2)
    goes[4].start()
    g_o[:, :GROUP] = whole(chunks + groups, 0, KEYS)
    g_o[:, GROUP:] = whole(chunks + groups, KEYS, 2 * KEYS)
    goes[5].start()
    comes[1].wait()
    ln, b_qkv, q, k, b_out, b_in = small_parts(small[...], chunks, groups, width)
    for ref, value in (
        (g_ln, ln), (g_b_qkv, b_qkv), (g_q, q), (g_k, k), (g_b_o, b_out), (g_b_in, b_in), (g_b_out, b_out)
    ):
        ref[...] = value.reshape(value.shape[1])
    for copy in goes:
        copy.wait()


def local(n_dp, tokens, lengths, cotangent, ln_gain, w_qkv, b_qkv, q_gain, k_gain, w_o, b_o, w_in, b_in, w_out, b_out):
    rows, width = tokens.shape
    hidden_width = w_in.shape[1]
    chunks = hidden_width // width
    groups = width // GROUP
    seqs = rows // SEQ
    shards = chunks + groups + 1
    everyone = shards + chunks
    wired = n_dp * BLOCK == width and n_dp == 4 * chunks
    half = width // 2
    extra = KEYS - SLOT
    anywhere = pl.BlockSpec(memory_space=pl.ANY)
    vmem = pl.BlockSpec(memory_space=pltpu.VMEM)
    smem = pl.BlockSpec(memory_space=pltpu.SMEM)
    wide = lambda *shape: pltpu.VMEM(shape, F32)
    slim = lambda *shape: pltpu.VMEM(shape, BF16)
    flags = lambda *shape: pltpu.SemaphoreType.DMA(shape)
    low = lambda *shape: jax.ShapeDtypeStruct(shape, BF16)
    full = lambda *shape: jax.ShapeDtypeStruct(shape, F32)
    small_shape = (8, width + GROUP)

    if wired:
        out_piece = low(2, shards + 4, BLOCK, half)
        flights = 6 * (shards + 3) + 3 * chunks + 3 + 7
        others = [
            slim(SLOTS, 2, 16, BLOCK, half), slim(RING, 16, BLOCK, half),
            slim(everyone, 8, BLOCK, half), slim(everyone, 4, BLOCK, half),
            slim(shards, 2, BLOCK, half), slim(shards, 1, BLOCK, half), slim(4, 4, BLOCK, half),
            slim(2, 4, BLOCK, half), slim(1, 4, BLOCK, half), slim(2, shards + 4, BLOCK, half),
            wide(3, 4, *small_shape), flags(flights), flags(flights),
        ]
        settings = dict(collective_id=0, has_side_effects=True)
    else:
        out_piece = low(everyone, width, width)
        others = [slim(2, width, width), flags(2)]
        settings = {}
    output, grad_tokens, pieces, small = pl.pallas_call(
        functools.partial(layer_kernel, wired),
        out_shape=(low(rows, width), low(rows, width), out_piece, full(*small_shape)),
        in_specs=[
            smem, anywhere, anywhere, vmem, anywhere, vmem, vmem, vmem, anywhere, vmem, anywhere,
            vmem, anywhere, vmem,
        ],
        out_specs=(anywhere,) * 4,
        scratch_shapes=[slim(6, width, width)]
        + [slim(rows, width)] * 9
        + [
            slim(width + 16, rows), slim(width, rows), wide(rows, width), wide(rows, width),
            slim(rows, GROUP), slim(rows + extra, GROUP), slim(rows + extra, GROUP),
            slim(rows, GROUP),
        ]
        + [wide(rows, GROUP)] * 3
        + [wide(*small_shape), flags(5 + 2 * chunks + 3 * groups), flags(2 * seqs + 2)]
        + others,
        compiler_params=pltpu.CompilerParams(vmem_limit_bytes=62 << 20, **settings),
    )(
        lengths, tokens, cotangent, ln_gain, w_qkv, b_qkv, q_gain, k_gain, w_o, b_o, w_in, b_in,
        w_out, b_out,
    )

    if wired:
        return pl.pallas_call(
            finish_kernel,
            out_shape=(
                low(rows, width), low(rows, width), full(width), full(BLOCK, 3 * width),
                full(3 * width), full(HEAD), full(HEAD), full(BLOCK, width), full(width),
                full(BLOCK, hidden_width), full(hidden_width), full(4 * BLOCK, width), full(width),
            ),
            in_specs=[anywhere] * 4,
            out_specs=(
                anywhere, anywhere, vmem, anywhere, vmem, vmem, vmem, anywhere, vmem, anywhere, vmem,
                anywhere, vmem,
            ),
            scratch_shapes=[
                slim(2, rows, width), slim(2, shards + 4, BLOCK, half), wide(*small_shape),
                wide(BLOCK, 3 * width), wide(BLOCK, width), wide(BLOCK, hidden_width),
                wide(4 * BLOCK, width), flags(2, 6),
            ],
        )(output, grad_tokens, pieces, small)

    def scatter(block, dim):
        part = lax.psum_scatter(block, "dp", scatter_dimension=dim, tiled=True)
        return lax.psum(part, "branch").astype(F32)

    grad_out = scatter(pieces[shards:].reshape(hidden_width, width), 0)
    reduced = scatter(pieces[:shards], 1)
    grad_in = jnp.concatenate([reduced[f] for f in range(chunks)], axis=1)
    qkv = jnp.concatenate([reduced[chunks + hg] for hg in range(groups)], axis=1)
    small = lax.psum(small, ("dp", "branch"))
    ln, g_b_qkv, g_q, g_k, g_b_out, g_b_in = (
        part[0] for part in small_parts(small, chunks, groups, width)
    )
    return (
        output, grad_tokens, ln, split_lanes(qkv, groups), g_b_qkv, g_q, g_k,
        reduced[chunks + groups], g_b_out, grad_in, g_b_in, grad_out, g_b_out,
    )


def solution(mesh):
    rows, split, whole = P(("dp", "branch"), None), P("dp", None), P()
    return jax.shard_map(
        functools.partial(local, mesh.shape["dp"]),
        mesh=mesh,
        in_specs=(rows, split, rows) + (whole,) * 11,
        out_specs=(
            rows, rows, whole, split, whole, whole, whole, split, whole, split, whole, split, whole,
        ),
        check_vma=False,
    )
```

```python
import functools
import math

import jax
import jax.numpy as jnp
from jax import lax
from jax.experimental import pallas as pl
from jax.experimental.pallas import tpu as pltpu
from jax.sharding import PartitionSpec as P

HEAD = 64
SEQ = 448
IMAGES = 4
SLOT = SEQ // IMAGES
KEYS = 128
GROUP = 256
EPS = 1e-06
SCALE = 0.125
F32 = jnp.float32
BF16 = jnp.bfloat16
GELU_A = math.sqrt(2.0 / math.pi)
GELU_B = 0.044715


def dot(left, right, left_dim=1, right_dim=0):
    return lax.dot_general(
        left, right, (((left_dim,), (right_dim,)), ((), ())), preferred_element_type=F32
    )


def slot_positions(lens):
    row = lax.broadcasted_iota(jnp.int32, (SEQ, 1), 0)
    held = jnp.full((SEQ, 1), -1, jnp.int32)
    start = jnp.int32(0)
    for image in range(IMAGES):
        place = row - SLOT * image
        held = jnp.where((place >= 0) & (place < lens[image]), place + start, held)
        start = start + lens[image]
    return held


def position_slots(lens):
    row = lax.broadcasted_iota(jnp.int32, (SEQ, 1), 0)
    held = jnp.full((SEQ, 1), -1, jnp.int32)
    start = jnp.int32(0)
    for image in range(IMAGES):
        place = row - start
        held = jnp.where((place >= 0) & (place < lens[image]), place + SLOT * image, held)
        start = start + lens[image]
    return held


def one_hot(index):
    lanes = lax.broadcasted_iota(jnp.int32, (SEQ, SEQ), 1)
    return jnp.where(lanes == index, 1.0, 0.0).astype(BF16)


def row_stats(values):
    centered = values - jnp.mean(values, axis=1, keepdims=True)
    spread = jnp.mean(centered * centered, axis=1, keepdims=True)
    inverse = lax.rsqrt(spread + EPS)
    return centered * inverse, inverse


def gelu_pair(pre, grad):
    square = pre * pre
    bent = jnp.tanh(pre * (GELU_A + (GELU_A * GELU_B) * square))
    half = 0.5 * pre
    up = 1.0 + bent
    hidden = half * up
    slope = half * (GELU_A + (3.0 * GELU_A * GELU_B) * square)
    return hidden, (up * (0.5 + (1.0 - bent) * slope)) * grad


MESH = pl.DeviceIdType.MESH
BLOCK = 48
SLOTS = 2
RING = 6
XY, YX = ("x", "y", "z0", "z1"), ("y", "x", "z0", "z1")
ZX, ZY = ("z0", "z1", "x", "y"), ("z0", "z1", "y", "x")
RATES = {"core": 400e3, "x": 42e3, "y": 42e3, "z0": 42e3, "z1": 21e3}
LATENCY = 2.0
LATE_PACE, LATE_LATENCY = 0.8, 3.0


class Piece:
    def __init__(self, index, shard, axes, lanes):
        self.index, self.shard, self.axes, self.lanes = index, shard, axes, lanes
        self.stage, self.copy, self.eta = 0, None, 0.0

    def cut(self, ref):
        return ref.at[:, :, self.lanes]


class Small:
    def __init__(self):
        self.stage, self.copy, self.eta = 0, None, 0.0


class Exchange:
    def __init__(self, refs, chunks):
        (self.both, self.inbox, self.in1, self.in2, self.in3, self.in4, self.osum, self.oin3,
         self.oin4, self.fin, self.small, self.small_in, self.send_sem, self.recv_sem) = refs
        self.chunks = chunks
        self.dp, self.core = lax.axis_index("dp"), lax.axis_index("branch")
        self.bits = {
            "x": lax.rem(self.dp, 2),
            "y": lax.rem(self.dp // 2, 2),
            "z0": lax.rem(self.dp // 4, 2),
            "z1": lax.rem(self.dp // 8, 2),
        }
        self.far = {
            axis: (self.dp + step - 2 * step * self.bits[axis], self.core)
            for axis, step in (("x", 1), ("y", 2), ("z0", 4), ("z1", 8))
        }
        self.far["core"] = (self.dp, 1 - self.core)
        self.far["core x"] = (self.far["x"][0], 1 - self.core)
        self.far["y z0"] = (self.far["y"][0] + self.far["z0"][0] - self.dp, self.core)
        self.bits["core"] = self.core
        self.items, self.opened = [], 0
        self.pace, self.latency = 1.0, LATENCY
        self.flights, self.merged, self.now, self.free = 0, 0, 0.0, {}

    def greet(self):
        barrier = pltpu.get_barrier_semaphore()
        for device in self.far.values():
            pl.semaphore_signal(barrier, inc=1, device_id=device, device_id_type=MESH)

    def meet(self):
        pl.semaphore_wait(pltpu.get_barrier_semaphore(), len(self.far))

    def send(self, item, source, target, axis):
        copy = pltpu.make_async_remote_copy(
            src_ref=source, dst_ref=target, send_sem=self.send_sem.at[self.flights],
            recv_sem=self.recv_sem.at[self.flights], device_id=self.far[axis], device_id_type=MESH,
        )
        self.flights += 1
        copy.start()
        link, axis = axis[0], axis.split()[0]
        size = source.dtype.itemsize * math.prod(source.shape)
        rate = RATES[axis] * (self.pace if axis != "core" else 1.0)
        self.free[link] = max(self.free.get(link, 0.0), self.now) + size / rate
        item.copy, item.eta = copy, self.free[link] + self.latency

    def open(self):
        index = self.opened
        for behind, stage in ((SLOTS, 1), (RING - SLOTS, 2)):
            while any(
                item.index == index - behind and item.stage < stage
                for item in self.items
                if isinstance(item, Piece)
            ):
                self.advance(min(self.under_way(), key=lambda item: item.eta))
        self.opened += 1
        return index

    def put(self, index, value, lane, axes):
        half = value.shape[1] // 2
        for side, role in ((0, self.core), (1, 1 - self.core)):
            target = self.both.at[index % SLOTS, role, :, :, pl.ds(lane, half)]
            put_blocks(value, target, side, axes)

    def start(self, index, shard, axes, lane, width):
        piece = Piece(index, shard, axes, pl.ds(lane, width))
        self.send(
            piece, piece.cut(self.both.at[index % SLOTS, 1]), piece.cut(self.inbox.at[index % RING]),
            "core",
        )
        self.items.append(piece)

    def halve(self, piece, held, held_at, arrived, count, axis, target):
        near = self.bits[axis] * count
        away = (1 - self.bits[axis]) * count
        span = pl.ds(away, count)
        arrived[span] = arrived[span] + held[pl.ds(held_at + away, count)]
        self.send(piece, arrived.at[span], target, axis)
        span = pl.ds(near, count)
        arrived[span] = arrived[span] + held[pl.ds(held_at + near, count)]

    def advance(self, piece):
        for copy in piece.copy if isinstance(piece.copy, list) else [piece.copy]:
            copy.wait()
        self.now = max(self.now, piece.eta)
        piece.copy = None
        if isinstance(piece, Small):
            self.advance_small(piece)
            return
        k, shard, axes, cut = piece.index, piece.shard, piece.axes, piece.cut
        whole = isinstance(shard, int)
        in0, in1, in2 = cut(self.inbox.at[k % RING]), cut(self.in1.at[k]), cut(self.in2.at[k])
        if whole:
            in3, in4 = cut(self.in3.at[shard]), cut(self.in4.at[shard])
        if piece.stage == 0:
            self.halve(piece, cut(self.both.at[k % SLOTS, 0]), 0, in0, 8, axes[0], in1)
        elif piece.stage == 1:
            self.halve(piece, in0, self.bits[axes[0]] * 8, in1, 4, axes[1], in2)
        elif piece.stage == 2 and whole:
            self.halve(piece, in1, self.bits[axes[1]] * 4, in2, 2, axes[2], in3)
        elif piece.stage == 2:
            place = shard[0] % 2 * 2 + shard[0] // 2
            self.osum[place] = in2[...] + in1[pl.ds(self.bits[axes[1]] * 4, 4)]
            self.merged += 1
            if self.merged < self.chunks:
                piece.stage = 5
            else:
                far = pl.ds((1 - self.bits["z0"]) * 2, 2)
                self.send(piece, self.osum.at[far], self.oin3, "z0")
        elif piece.stage == 3 and whole:
            self.halve(piece, in2, self.bits[axes[2]] * 2, in3, 1, axes[3], in4)
        elif piece.stage == 3:
            self.halve(piece, self.osum, self.bits["z0"] * 2, self.oin3, 1, "z1", self.oin4)
        elif piece.stage == 4:
            if whole:
                final = self.fin.at[self.core, pl.ds(shard, 1), :, piece.lanes]
                final[...] = in4[...] + in3[pl.ds(self.bits[axes[3]], 1)]
            else:
                final = self.fin.at[self.core, pl.ds(self.fin.shape[1] - 4, 4)]
                final[...] = self.oin4[0] + self.oin3[self.bits["z1"]]
            self.send(piece, final, final, "core")
        piece.stage += 1

    def send_small(self, item):
        axes = (("core", "x"), ("y", "z0"), ("z1",))[item.stage]
        me = sum(self.bits[axis] << i for i, axis in enumerate(axes))
        self.small_in[item.stage, me] = self.small[...]
        copies = []
        for axis in axes + ((" ".join(axes),) if len(axes) > 1 else ()):
            source = self.small_in.at[item.stage, me]
            self.send(item, source, source, axis)
            copies.append(item.copy)
        item.copy, item.eta = copies, self.now + self.latency

    def start_small(self):
        item = Small()
        self.send_small(item)
        self.items.append(item)

    def advance_small(self, item):
        parts = [self.small_in[item.stage, i] for i in range(4 if item.stage < 2 else 2)]
        while len(parts) > 1:
            parts = [parts[i] + parts[i + 1] for i in range(0, len(parts), 2)]
        self.small[...] = parts[0]
        item.stage += 1
        if item.stage < 3:
            self.send_small(item)

    def under_way(self):
        return [item for item in self.items if item.copy is not None]

    def progress(self, cost):
        self.now += cost
        while True:
            due = [item for item in self.under_way() if item.eta <= self.now]
            if not due:
                return
            self.advance(min(due, key=lambda item: item.eta))

    def drain(self):
        while self.under_way():
            self.advance(min(self.under_way(), key=lambda item: item.eta))


def put_blocks(value, target, side, axes):
    half = value.shape[1] // 2
    for block in range(16):
        place = block
        if axes is not None and len(axes) == 4:
            bit = dict(x=block % 2, y=block // 2 % 2, z0=block // 4 % 2, z1=block // 8)
            place = sum(bit[axis] << (3 - i) for i, axis in enumerate(axes))
        target[place] = value[
            BLOCK * block : BLOCK * (block + 1), half * side : half * (side + 1)
        ].astype(BF16)


def make_flip():
    eye = jnp.where(
        lax.broadcasted_iota(jnp.int32, (GROUP, GROUP), 0)
        == lax.broadcasted_iota(jnp.int32, (GROUP, GROUP), 1),
        1.0,
        0.0,
    ).astype(BF16)

    def flip(source, target):
        for part in range(source.shape[1] // GROUP):
            lanes = pl.ds(part * GROUP, GROUP)
            target[lanes, :] = dot(eye, source[:, lanes], 1, 1).astype(BF16)

    return flip


class Parking:
    def __init__(self, stage, target, sem):
        self.stage, self.target, self.sem = stage, target, sem
        self.sent = []

    def put(self, value, index):
        slot = len(self.sent) % 2
        if len(self.sent) >= 2:
            self.sent[-2].wait()
        self.stage[slot] = value.astype(BF16)
        copy = pltpu.make_async_copy(self.stage.at[slot], self.target.at[index], self.sem.at[slot])
        copy.start()
        self.sent.append(copy)

    def finish(self):
        for copy in self.sent[-2:]:
            copy.wait()


def layer_kernel(
    wired,
    lengths_ref, tokens_hbm, cot_hbm, ln_gain_ref, w_qkv_hbm, b_qkv_ref, q_gain_ref, k_gain_ref,
    w_o_hbm, b_o_ref, w_in_hbm, b_in_ref, w_out_hbm, b_out_ref,
    output_hbm, grad_tokens_hbm, pieces_hbm, small_hbm,
    weights, tok, cot, packed, grow, normed, hid_even, hid_odd, gpre_0, gpre_1, gpre_2, gpre_3, spare,
    flipped, turned, fed, gnorm, qs, ks, vs, gm, small_ref,
    load_sem, done_sem, *refs,
):
    rows, width = tok.shape
    hidden_width = w_in_hbm.shape[1]
    chunks = hidden_width // width
    groups = width // GROUP
    seqs = rows // SEQ
    images = seqs * IMAGES
    base = lax.axis_index("branch") * seqs
    assert chunks == 4 and groups == 3
    hid, gpre = (hid_even, hid_odd), (gpre_0, gpre_1, gpre_2, gpre_3)
    mixed, gprojs = tok, (hid_even, spare, cot)
    w_in = [weights.at[f] for f in range(chunks)]
    w_out = [weights.at[4 + f % 3] for f in range(chunks)]
    w_qkv, w_o = [weights.at[5], weights.at[6], weights.at[4]], weights.at[7]
    nq, rq, nk = (fed.at[:, pl.ds(part * GROUP, GROUP)] for part in range(3))
    rk, dq, dk = (gnorm.at[:, pl.ds(part * GROUP, GROUP)] for part in range(3))
    loads = {}

    def load(name, source, target):
        copy = pltpu.make_async_copy(source, target, load_sem.at[len(loads)])
        copy.start()
        loads[name] = copy

    def load_chunk(f):
        cols = pl.ds(f * width, width)
        load(("out", f), w_out_hbm.at[cols, :], w_out[f])
        load(("in", f), w_in_hbm.at[:, cols], w_in[f])

    def load_qkv(hg):
        for t in range(3):
            load(
                ("qkv", hg, t),
                w_qkv_hbm.at[:, pl.ds(t * width + hg * GROUP, GROUP)],
                w_qkv[hg].at[:, pl.ds(t * GROUP, GROUP)],
            )

    load("tok", tokens_hbm, tok)
    load("cot", cot_hbm, cot)
    for f in range(3):
        load_chunk(f)
    load("wo", w_o_hbm, w_o)
    small_ref[...] = jnp.zeros_like(small_ref)
    net, parking = None, None
    if wired:
        net = Exchange(refs[:10] + (small_ref,) + refs[10:], chunks)
        net.greet()
    else:
        parking = Parking(refs[0], pieces_hbm, refs[1])

    def emit(value, shard, axes):
        if wired:
            index = net.open()
            net.put(index, value, 0, axes)
            net.start(index, shard, axes, 0, width // 2)
        else:
            parking.put(value, shard if isinstance(shard, int) else chunks + groups + 1 + shard[0])

    def point(cost):
        if wired:
            net.progress(cost)

    def cost(amount):
        if wired:
            net.now += amount

    def lanes_of(part):
        return pl.ds(part * GROUP, GROUP)

    ones_row = jnp.where(lax.broadcasted_iota(jnp.int32, (16, rows), 0) == 0, 1.0, 0.0)
    flipped[pl.ds(width, 16), :] = ones_row.astype(BF16)
    eye = jnp.where(
        lax.broadcasted_iota(jnp.int32, (GROUP, GROUP), 0)
        == lax.broadcasted_iota(jnp.int32, (GROUP, GROUP), 1),
        1.0,
        0.0,
    ).astype(BF16)

    def flip(source, target, part):
        target[lanes_of(part), :] = dot(eye, source[:, lanes_of(part)], 1, 1).astype(BF16)

    loads["tok"].wait()
    loads["cot"].wait()
    grad_sum = jnp.zeros((1, width), F32)
    for s in range(seqs):
        span = pl.ds(s * SEQ, SEQ)
        pick = one_hot(slot_positions([lengths_ref[base + s, j] for j in range(IMAGES)]))
        rows_here = dot(pick, tok[span, :])
        packed[span, :] = rows_here.astype(BF16)
        unit, _ = row_stats(rows_here)
        normed[span, :] = (unit * ln_gain_ref[...].reshape(1, width)).astype(BF16)
        grads_here = dot(pick, cot[span, :])
        grow[span, :] = grads_here.astype(BF16)
        grad_sum = grad_sum + jnp.sum(grads_here, axis=0, keepdims=True)
    small_ref[pl.ds(7, 1), pl.ds(0, width)] = grad_sum
    for part in range(groups):
        flip(normed, flipped, part)
    cost(6.0)

    def add_fed(f):
        for part in range(groups):
            lanes = lanes_of(part)
            up = dot(hid[f % 2][...], w_out[f][:, lanes])
            fed[:, lanes] = up if f == 0 else fed[:, lanes] + up

    if wired:
        net.meet()
    b_in = b_in_ref[...].reshape(1, hidden_width)
    ready = None

    def activate():
        f, c, pre, back = ready
        hidden, grad_pre = gelu_pair(pre, back)
        hid[f % 2][:, lanes_of(c)] = hidden.astype(BF16)
        gpre[f][:, lanes_of(c)] = grad_pre.astype(BF16)

    def send_w_in(f):
        sums = dot(flipped[...], gpre[f][...])
        cost(2.2)
        emit(sums[:width], f, XY)
        small_ref[pl.ds(f, 1), pl.ds(0, width)] = sums[width : width + 1]
        point(0.0)

    def send_w_out(f):
        cost(1.9)
        emit(dot(turned[...], grow[...]), (f,), YX[:2])
        point(0.0)

    for f in range(chunks):
        loads["in", f].wait()
        loads["out", f].wait()
        for c in range(groups):
            place = f * width + c * GROUP
            lanes = lanes_of(c)
            pre = dot(normed[...], w_in[f][:, lanes]) + b_in[:, place : place + GROUP]
            back = dot(grow[...], w_out[f][lanes, :], 1, 1)
            if ready is not None:
                activate()
            ready = (f, c, pre, back)
            if f > 0 and c == 0:
                for part in range(groups):
                    flip(hid[1 - f % 2], turned, part)
            if f > 0 and c == 2:
                add_fed(f - 1)
            point((1.7, 1.2, 2.9)[c] if f > 0 else 1.2)
            if f > 0 and c == 0:
                send_w_in(f - 1)
            if f > 0 and c == 1:
                send_w_out(f - 1)
        if f == 1:
            load_chunk(3)
        if f == 2:
            load_qkv(0)
        if f == 3:
            load_qkv(1)
    activate()
    for part in range(groups):
        flip(hid_odd, turned, part)
    send_w_in(chunks - 1)
    send_w_out(chunks - 1)

    add_fed(chunks - 1)
    load_qkv(2)
    hid_odd[...] = (fed[...] + b_out_ref[...].reshape(1, width)).astype(BF16)
    point(1.9)

    same_head = (
        lax.broadcasted_iota(jnp.int32, (GROUP, GROUP), 0) // HEAD
        == lax.broadcasted_iota(jnp.int32, (GROUP, GROUP), 1) // HEAD
    )
    average = jnp.where(same_head, 1.0 / HEAD, 0.0).astype(BF16)
    q_gain = jnp.concatenate([q_gain_ref[...].reshape(1, HEAD)] * (GROUP // HEAD), axis=1)
    k_gain = jnp.concatenate([k_gain_ref[...].reshape(1, HEAD)] * (GROUP // HEAD), axis=1)
    b_qkv = b_qkv_ref[...].reshape(1, 3 * width)
    lane = lax.broadcasted_iota(jnp.int32, (1, KEYS), 1)
    pair_lane = jnp.concatenate([lane, lane], axis=1)
    first_head = jnp.where(lane < HEAD, 1.0, 0.0).astype(BF16)
    second_head = jnp.where(lane < HEAD, 0.0, 1.0).astype(BF16)

    def head_mean(values, split):
        high = values.astype(BF16)
        mean = dot(high, average)
        if split:
            mean = mean + dot((values - high.astype(F32)).astype(BF16), average)
        return mean

    def head_norm(raw):
        centered = raw - head_mean(raw, True)
        inverse = lax.rsqrt(head_mean(centered * centered, False) + EPS)
        return centered * inverse, inverse

    def two_heads(block):
        return jnp.concatenate([block * first_head, block * second_head], axis=0)

    def stacked(block):
        return jnp.concatenate([block[:, :KEYS], block[:, KEYS:]], axis=0)

    def invert(total):
        guess = pl.reciprocal(total, approx=True)
        return guess * (2.0 - total * guess)

    def over_heads(block, change):
        parts = []
        for head in range(2):
            part = block[:, head * KEYS : (head + 1) * KEYS]
            total = change(jnp.sum(part, axis=1, keepdims=True))
            parts.append(jnp.broadcast_to(total, part.shape))
        return jnp.concatenate(parts, axis=1)

    ks[pl.ds(rows, KEYS - SLOT), :] = jnp.zeros((KEYS - SLOT, GROUP), BF16)
    vs[pl.ds(rows, KEYS - SLOT), :] = jnp.zeros((KEYS - SLOT, GROUP), BF16)

    for hg in range(groups):
        gproj = gprojs[hg]
        bias_q, bias_k, bias_v = (
            b_qkv[:, t * width + hg * GROUP : t * width + (hg + 1) * GROUP] for t in range(3)
        )
        for t in range(3):
            loads["qkv", hg, t].wait()
        if hg == 0:
            loads["wo"].wait()
        if wired and hg == groups - 1:
            net.pace, net.latency = LATE_PACE, LATE_LATENCY
        raw = dot(normed[...], w_qkv[hg][:, lanes_of(0)]) + bias_q
        unit, inverse = head_norm(raw)
        nq[...] = unit
        rq[...] = inverse
        qs[...] = (unit * q_gain).astype(BF16) * SCALE
        raw = dot(normed[...], w_qkv[hg][:, lanes_of(1)]) + bias_k
        unit, inverse = head_norm(raw)
        nk[...] = unit
        rk[...] = inverse
        ks[pl.ds(0, rows), :] = (unit * k_gain).astype(BF16)
        raw = dot(normed[...], w_qkv[hg][:, lanes_of(2)]) + bias_v
        vs[pl.ds(0, rows), :] = raw.astype(BF16)
        gm[...] = dot(grow[...], w_o[lanes_of(hg), :], 1, 1).astype(BF16)
        point(4.5)

        def one_image(image):
            start = image * SLOT
            span = pl.ds(start, SLOT)
            window = pl.ds(start, KEYS)
            seen = pair_lane < lengths_ref[base + image // IMAGES, image % IMAGES]
            for pair in range(GROUP // KEYS):
                lanes = pl.ds(pair * KEYS, KEYS)
                query, grad = qs[span, lanes], gm[span, lanes]
                keys, values = two_heads(ks[window, lanes]), two_heads(vs[window, lanes])
                weight = jnp.where(seen, jnp.exp(dot(query, keys, 1, 1)), 0.0)
                probs = weight * over_heads(weight, invert)
                grad_probs = dot(grad, values, 1, 1)
                inner = over_heads(probs * grad_probs, lambda total: total)
                grad_scores = (probs * (grad_probs - inner)).astype(BF16)
                probs_low = probs.astype(BF16)
                mixed[span, pl.ds(hg * GROUP + pair * KEYS, KEYS)] = dot(probs_low, values).astype(
                    BF16
                )
                dq[span, lanes] = dot(grad_scores, keys) * SCALE
                dk[span, lanes] = dot(stacked(grad_scores), two_heads(query), 0, 0)[:SLOT]
                gproj[span, pl.ds(2 * GROUP + pair * KEYS, KEYS)] = dot(
                    stacked(probs_low), two_heads(grad), 0, 0
                )[:SLOT].astype(BF16)

        for image in range(0, images, 2):
            one_image(image)
            one_image(image + 1)
            point(1.3)
        if hg == groups - 1:
            for part in range(groups):
                flip(mixed, turned, part)
            if wired:
                index = net.open()
                for lane, size, part_axes in ((0, KEYS, XY), (KEYS, 2 * KEYS, YX)):
                    sums = dot(turned[...], grow[:, pl.ds(2 * lane, 2 * size)])
                    net.put(index, sums, lane, part_axes)
                    cost(1.1)
                    net.start(index, chunks + groups, part_axes, lane, size)
                point(0.0)
            else:
                parking.put(dot(turned[...], grow[...]), chunks + groups)

        axes = (YX, XY, YX)[hg]
        last = hg == groups - 1
        index = net.open() if wired else None
        parts = {}

        def part_grad(t, part_axes):
            sums = dot(flipped[...], gproj[:, lanes_of(t)])
            small_ref[pl.ds(4 + hg, 1), lanes_of(t)] = sums[width : width + 1]
            if wired:
                net.put(index, sums[:width], t * KEYS, part_axes)
                if last:
                    net.start(index, chunks + hg, part_axes, t * KEYS, KEYS)
            else:
                parts[t] = sums[:width]

        def norm_back(side, grad_ref, unit_ref, inverse_ref, gain):
            grad, unit = grad_ref[...], unit_ref[...]
            gain_sum = jnp.sum(grad * unit, axis=0, keepdims=True)
            small_ref[pl.ds(3 + side, 1), pl.ds(width, GROUP)] += gain_sum
            grad = grad * gain
            back = grad - head_mean(grad, False) - unit * head_mean(grad * unit, False)
            gproj[:, lanes_of(side)] = (back * inverse_ref[...]).astype(BF16)

        cost(0.7)
        part_grad(2, ZX if last else axes)
        norm_back(0, dq, nq, rq, q_gain)
        cost(1.5)
        if last:
            point(0.0)
        part_grad(0, XY if last else axes)
        norm_back(1, dk, nk, rk, k_gain)
        cost(1.5)
        if last:
            point(0.0)
        part_grad(1, YX if last else axes)
        if not wired:
            parking.put(jnp.concatenate([parts[t] for t in range(3)], axis=1), chunks + hg)
        elif not last:
            net.start(index, chunks + hg, axes, 0, width // 2)
        point(0.0)

    for part in range(groups):
        lanes = lanes_of(part)
        total = None
        for source, target in list(zip(gpre, w_in)) + list(zip(gprojs, w_qkv)):
            down = dot(source[...], target[lanes, :], 1, 1)
            total = down if total is None else total + down
            point(0.55)
        gnorm[:, lanes] = total
    load("tok again", tokens_hbm, hid_even)
    load("cot again", cot_hbm, gpre_0)
    ln_gain = ln_gain_ref[...].reshape(1, width)
    b_o = b_o_ref[...].reshape(1, width)
    gain_grad = jnp.zeros((1, width), F32)
    for s in range(seqs):
        span = pl.ds(s * SEQ, SEQ)
        unit, inverse = row_stats(packed[span, :].astype(F32))
        grad = gnorm[span, :]
        gain_grad = gain_grad + jnp.sum(grad * unit, axis=0, keepdims=True)
        grad = grad * ln_gain
        back = grad - jnp.mean(grad, axis=1, keepdims=True)
        back = (back - unit * jnp.mean(grad * unit, axis=1, keepdims=True)) * inverse
        normed[span, :] = (grow[span, :].astype(F32) + back).astype(BF16)
    for t in range(width // GROUP):
        small_ref[pl.ds(t, 1), pl.ds(width, GROUP)] = gain_grad[:, t * GROUP : (t + 1) * GROUP]
    if wired:
        net.start_small()
    point(1.5)
    finals = []
    loads["tok again"].wait()
    loads["cot again"].wait()

    def hand_over(source, target):
        copy = pltpu.make_async_copy(source, target, done_sem.at[len(finals)])
        copy.start()
        finals.append(copy)

    for s in range(seqs):
        span = pl.ds(s * SEQ, SEQ)
        place = position_slots([lengths_ref[base + s, j] for j in range(IMAGES)])
        put = one_hot(place)
        padding = jnp.where(place < 0, 1.0, 0.0)
        attended = (dot(mixed[span, :], w_o[...]) + b_o).astype(BF16).astype(F32)
        result = packed[span, :].astype(F32) + (attended + hid_odd[span, :].astype(F32))
        result = dot(put, result.astype(BF16)) + padding * hid_even[span, :].astype(F32)
        hid_even[span, :] = result.astype(BF16)
        hand_over(hid_even.at[span], output_hbm.at[span])
        point(1.2)
        grads = dot(put, normed[span, :]) + padding * gpre_0[span, :].astype(F32)
        gpre_0[span, :] = grads.astype(BF16)
        hand_over(gpre_0.at[span], grad_tokens_hbm.at[span])
        point(0.8)
    if wired:
        net.drain()
        hand_over(net.fin, pieces_hbm)
    else:
        parking.finish()
    hand_over(small_ref, small_hbm)
    for copy in finals:
        copy.wait()


def split_lanes(block, groups):
    width = block.shape[1] // 3
    return jnp.concatenate(
        [
            block[:, hg * width + t * GROUP : hg * width + (t + 1) * GROUP]
            for t in range(3)
            for hg in range(groups)
        ],
        axis=1,
    )


def fold_heads(gains):
    return sum(gains[:, h * HEAD : (h + 1) * HEAD] for h in range(GROUP // HEAD))


def small_parts(small, chunks, groups, width):
    b_in = jnp.concatenate([small[f : f + 1, :width] for f in range(chunks)], axis=1)
    b_qkv = jnp.concatenate([small[4 + hg : 5 + hg, :width] for hg in range(groups)], axis=1)
    ln = jnp.concatenate([small[t : t + 1, width:] for t in range(width // GROUP)], axis=1)
    gains = [fold_heads(small[3 + side : 4 + side, width:]) for side in range(2)]
    return ln, split_lanes(b_qkv, groups), gains[0], gains[1], small[7:8, :width], b_in


def finish_kernel(
    rows_hbm, grads_hbm, fin_hbm, small_hbm, output_hbm, grad_tokens_hbm, g_ln, g_qkv_hbm, g_b_qkv,
    g_q, g_k, g_o_hbm, g_b_o, g_in_hbm, g_b_in, g_out_hbm, g_b_out, held, fin, small, g_qkv, g_o, g_in,
    g_out, sem,
):
    comes = [
        pltpu.make_async_copy(source, target, sem.at[0, i])
        for i, (source, target) in enumerate(
            ((fin_hbm, fin), (small_hbm, small), (rows_hbm, held.at[0]), (grads_hbm, held.at[1]))
        )
    ]
    goes = [
        pltpu.make_async_copy(source, target, sem.at[1, i])
        for i, (source, target) in enumerate(
            (
                (held.at[0], output_hbm), (held.at[1], grad_tokens_hbm), (g_in, g_in_hbm),
                (g_qkv, g_qkv_hbm), (g_out, g_out_hbm), (g_o, g_o_hbm),
            )
        )
    ]
    for copy in comes:
        copy.start()
    width = g_o.shape[1]
    chunks, groups = g_in.shape[1] // width, width // GROUP

    def whole(shard, lane, size):
        return jnp.concatenate(
            [fin[side, shard, :, lane : lane + size].astype(F32) for side in range(2)], axis=1
        )

    comes[0].wait()
    for f in range(chunks):
        g_in[:, f * width : (f + 1) * width] = whole(f, 0, width // 2)
    goes[2].start()
    for hg in range(groups):
        for t in range(3):
            place = t * width + hg * GROUP
            g_qkv[:, place : place + GROUP] = whole(chunks + hg, t * KEYS, KEYS)
    goes[3].start()
    for i in range(2):
        comes[2 + i].wait()
        goes[i].start()
    for j in range(4):
        g_out[j * BLOCK : (j + 1) * BLOCK, :] = whole(chunks + groups + 1 + j, 0, width // 2)
    goes[4].start()
    g_o[:, :GROUP] = whole(chunks + groups, 0, KEYS)
    g_o[:, GROUP:] = whole(chunks + groups, KEYS, 2 * KEYS)
    goes[5].start()
    comes[1].wait()
    ln, b_qkv, q, k, b_out, b_in = small_parts(small[...], chunks, groups, width)
    for ref, value in (
        (g_ln, ln), (g_b_qkv, b_qkv), (g_q, q), (g_k, k), (g_b_o, b_out), (g_b_in, b_in), (g_b_out, b_out)
    ):
        ref[...] = value.reshape(value.shape[1])
    for copy in goes:
        copy.wait()


def local(n_dp, tokens, lengths, cotangent, ln_gain, w_qkv, b_qkv, q_gain, k_gain, w_o, b_o, w_in, b_in, w_out, b_out):
    rows, width = tokens.shape
    hidden_width = w_in.shape[1]
    chunks = hidden_width // width
    groups = width // GROUP
    seqs = rows // SEQ
    shards = chunks + groups + 1
    everyone = shards + chunks
    wired = n_dp * BLOCK == width and n_dp == 4 * chunks
    half = width // 2
    extra = KEYS - SLOT
    anywhere = pl.BlockSpec(memory_space=pl.ANY)
    vmem = pl.BlockSpec(memory_space=pltpu.VMEM)
    smem = pl.BlockSpec(memory_space=pltpu.SMEM)
    wide = lambda *shape: pltpu.VMEM(shape, F32)
    slim = lambda *shape: pltpu.VMEM(shape, BF16)
    flags = lambda *shape: pltpu.SemaphoreType.DMA(shape)
    low = lambda *shape: jax.ShapeDtypeStruct(shape, BF16)
    full = lambda *shape: jax.ShapeDtypeStruct(shape, F32)
    small_shape = (8, width + GROUP)

    if wired:
        out_piece = low(2, shards + 4, BLOCK, half)
        flights = 6 * (shards + 3) + 3 * chunks + 3 + 7
        others = [
            slim(SLOTS, 2, 16, BLOCK, half), slim(RING, 16, BLOCK, half),
            slim(everyone, 8, BLOCK, half), slim(everyone, 4, BLOCK, half),
            slim(shards, 2, BLOCK, half), slim(shards, 1, BLOCK, half), slim(4, 4, BLOCK, half),
            slim(2, 4, BLOCK, half), slim(1, 4, BLOCK, half), slim(2, shards + 4, BLOCK, half),
            wide(3, 4, *small_shape), flags(flights), flags(flights),
        ]
        settings = dict(collective_id=0, has_side_effects=True)
    else:
        out_piece = low(everyone, width, width)
        others = [slim(2, width, width), flags(2)]
        settings = {}
    output, grad_tokens, pieces, small = pl.pallas_call(
        functools.partial(layer_kernel, wired),
        out_shape=(low(rows, width), low(rows, width), out_piece, full(*small_shape)),
        in_specs=[
            smem, anywhere, anywhere, vmem, anywhere, vmem, vmem, vmem, anywhere, vmem, anywhere,
            vmem, anywhere, vmem,
        ],
        out_specs=(anywhere,) * 4,
        scratch_shapes=[slim(8, width, width)]
        + [slim(rows, width)] * 12
        + [
            slim(width + 16, rows), slim(width, rows), wide(rows, width), wide(rows, width),
            slim(rows, GROUP), slim(rows + extra, GROUP), slim(rows + extra, GROUP),
            slim(rows, GROUP),
        ]
        + [wide(*small_shape), flags(5 + 2 * chunks + 3 * groups), flags(2 * seqs + 2)]
        + others,
        compiler_params=pltpu.CompilerParams(vmem_limit_bytes=62 << 20, **settings),
    )(
        lengths, tokens, cotangent, ln_gain, w_qkv, b_qkv, q_gain, k_gain, w_o, b_o, w_in, b_in,
        w_out, b_out,
    )

    if wired:
        return pl.pallas_call(
            finish_kernel,
            out_shape=(
                low(rows, width), low(rows, width), full(width), full(BLOCK, 3 * width),
                full(3 * width), full(HEAD), full(HEAD), full(BLOCK, width), full(width),
                full(BLOCK, hidden_width), full(hidden_width), full(4 * BLOCK, width), full(width),
            ),
            in_specs=[anywhere] * 4,
            out_specs=(
                anywhere, anywhere, vmem, anywhere, vmem, vmem, vmem, anywhere, vmem, anywhere, vmem,
                anywhere, vmem,
            ),
            scratch_shapes=[
                slim(2, rows, width), slim(2, shards + 4, BLOCK, half), wide(*small_shape),
                wide(BLOCK, 3 * width), wide(BLOCK, width), wide(BLOCK, hidden_width),
                wide(4 * BLOCK, width), flags(2, 6),
            ],
        )(output, grad_tokens, pieces, small)

    def scatter(block, dim):
        part = lax.psum_scatter(block, "dp", scatter_dimension=dim, tiled=True)
        return lax.psum(part, "branch").astype(F32)

    grad_out = scatter(pieces[shards:].reshape(hidden_width, width), 0)
    reduced = scatter(pieces[:shards], 1)
    grad_in = jnp.concatenate([reduced[f] for f in range(chunks)], axis=1)
    qkv = jnp.concatenate([reduced[chunks + hg] for hg in range(groups)], axis=1)
    small = lax.psum(small, ("dp", "branch"))
    ln, g_b_qkv, g_q, g_k, g_b_out, g_b_in = (
        part[0] for part in small_parts(small, chunks, groups, width)
    )
    return (
        output, grad_tokens, ln, split_lanes(qkv, groups), g_b_qkv, g_q, g_k,
        reduced[chunks + groups], g_b_out, grad_in, g_b_in, grad_out, g_b_out,
    )


def solution(mesh):
    rows, split, whole = P(("dp", "branch"), None), P("dp", None), P()
    return jax.shard_map(
        functools.partial(local, mesh.shape["dp"]),
        mesh=mesh,
        in_specs=(rows, split, rows) + (whole,) * 11,
        out_specs=(
            rows, rows, whole, split, whole, whole, whole, split, whole, split, whole, split, whole,
        ),
        check_vma=False,
    )
```

```python
import functools
import math

import jax
import jax.numpy as jnp
from jax import lax
from jax.experimental import pallas as pl
from jax.experimental.pallas import tpu as pltpu
from jax.sharding import PartitionSpec as P

HEAD = 64
SEQ = 448
IMAGES = 4
SLOT = SEQ // IMAGES
KEYS = 128
GROUP = 256
EPS = 1e-06
SCALE = 0.125
F32 = jnp.float32
BF16 = jnp.bfloat16
GELU_A = math.sqrt(2.0 / math.pi)
GELU_B = 0.044715


def dot(left, right, left_dim=1, right_dim=0):
    return lax.dot_general(
        left, right, (((left_dim,), (right_dim,)), ((), ())), preferred_element_type=F32
    )


def slot_positions(lens):
    row = lax.broadcasted_iota(jnp.int32, (SEQ, 1), 0)
    held = jnp.full((SEQ, 1), -1, jnp.int32)
    start = jnp.int32(0)
    for image in range(IMAGES):
        place = row - SLOT * image
        held = jnp.where((place >= 0) & (place < lens[image]), place + start, held)
        start = start + lens[image]
    return held


def position_slots(lens):
    row = lax.broadcasted_iota(jnp.int32, (SEQ, 1), 0)
    held = jnp.full((SEQ, 1), -1, jnp.int32)
    start = jnp.int32(0)
    for image in range(IMAGES):
        place = row - start
        held = jnp.where((place >= 0) & (place < lens[image]), place + SLOT * image, held)
        start = start + lens[image]
    return held


def one_hot(index):
    lanes = lax.broadcasted_iota(jnp.int32, (SEQ, SEQ), 1)
    return jnp.where(lanes == index, 1.0, 0.0).astype(BF16)


def row_stats(values):
    centered = values - jnp.mean(values, axis=1, keepdims=True)
    spread = jnp.mean(centered * centered, axis=1, keepdims=True)
    inverse = lax.rsqrt(spread + EPS)
    return centered * inverse, inverse


def gelu_pair(pre, grad):
    square = pre * pre
    bent = jnp.tanh(pre * (GELU_A + (GELU_A * GELU_B) * square))
    half = 0.5 * pre
    up = 1.0 + bent
    hidden = half * up
    slope = half * (GELU_A + (3.0 * GELU_A * GELU_B) * square)
    return hidden, (up * (0.5 + (1.0 - bent) * slope)) * grad


MESH = pl.DeviceIdType.MESH
BLOCK = 48
SLOTS = 2
RING = 6
XY, YX = ("x", "y", "z0", "z1"), ("y", "x", "z0", "z1")
ZX, ZY = ("z0", "z1", "x", "y"), ("z0", "z1", "y", "x")
RATES = {"core": 400e3, "x": 42e3, "y": 42e3, "z0": 42e3, "z1": 21e3}
LATENCY = 2.0
LATE_PACE, LATE_LATENCY = 0.8, 3.0


class Piece:
    def __init__(self, index, shard, axes, lanes):
        self.index, self.shard, self.axes, self.lanes = index, shard, axes, lanes
        self.stage, self.copy, self.eta = 0, None, 0.0

    def cut(self, ref):
        return ref.at[:, :, self.lanes]


class Small:
    def __init__(self):
        self.stage, self.copy, self.eta = 0, None, 0.0


class Exchange:
    def __init__(self, refs, chunks):
        (self.both, self.inbox, self.in1, self.in2, self.in3, self.in4, self.osum, self.oin3,
         self.oin4, self.fin, self.small, self.small_in, self.send_sem, self.recv_sem) = refs
        self.chunks = chunks
        self.dp, self.core = lax.axis_index("dp"), lax.axis_index("branch")
        self.bits = {
            "x": lax.rem(self.dp, 2),
            "y": lax.rem(self.dp // 2, 2),
            "z0": lax.rem(self.dp // 4, 2),
            "z1": lax.rem(self.dp // 8, 2),
        }
        self.far = {
            axis: (self.dp + step - 2 * step * self.bits[axis], self.core)
            for axis, step in (("x", 1), ("y", 2), ("z0", 4), ("z1", 8))
        }
        self.far["core"] = (self.dp, 1 - self.core)
        self.items, self.opened = [], 0
        self.pace, self.latency = 1.0, LATENCY
        self.flights, self.merged, self.now, self.free = 0, 0, 0.0, {}

    def greet(self):
        barrier = pltpu.get_barrier_semaphore()
        for device in self.far.values():
            pl.semaphore_signal(barrier, inc=1, device_id=device, device_id_type=MESH)

    def meet(self):
        pl.semaphore_wait(pltpu.get_barrier_semaphore(), len(self.far))

    def send(self, item, source, target, axis):
        copy = pltpu.make_async_remote_copy(
            src_ref=source, dst_ref=target, send_sem=self.send_sem.at[self.flights],
            recv_sem=self.recv_sem.at[self.flights], device_id=self.far[axis], device_id_type=MESH,
        )
        self.flights += 1
        copy.start()
        link = axis[0]
        size = source.dtype.itemsize * math.prod(source.shape)
        rate = RATES[axis] * (self.pace if axis != "core" else 1.0)
        self.free[link] = max(self.free.get(link, 0.0), self.now) + size / rate
        item.copy, item.eta = copy, self.free[link] + self.latency

    def open(self):
        index = self.opened
        for behind, stage in ((SLOTS, 1), (RING - SLOTS, 2)):
            while any(
                item.index == index - behind and item.stage < stage
                for item in self.items
                if isinstance(item, Piece)
            ):
                self.advance(min(self.under_way(), key=lambda item: item.eta))
        self.opened += 1
        return index

    def put(self, index, value, lane, axes):
        half = value.shape[1] // 2
        for side, role in ((0, self.core), (1, 1 - self.core)):
            target = self.both.at[index % SLOTS, role, :, :, pl.ds(lane, half)]
            put_blocks(value, target, side, axes)

    def start(self, index, shard, axes, lane, width):
        piece = Piece(index, shard, axes, pl.ds(lane, width))
        self.send(
            piece, piece.cut(self.both.at[index % SLOTS, 1]), piece.cut(self.inbox.at[index % RING]),
            "core",
        )
        self.items.append(piece)

    def halve(self, piece, held, held_at, arrived, count, axis, target):
        near = self.bits[axis] * count
        away = (1 - self.bits[axis]) * count
        span = pl.ds(away, count)
        arrived[span] = arrived[span] + held[pl.ds(held_at + away, count)]
        self.send(piece, arrived.at[span], target, axis)
        span = pl.ds(near, count)
        arrived[span] = arrived[span] + held[pl.ds(held_at + near, count)]

    def advance(self, piece):
        piece.copy.wait()
        self.now = max(self.now, piece.eta)
        piece.copy = None
        if isinstance(piece, Small):
            self.advance_small(piece)
            return
        k, shard, axes, cut = piece.index, piece.shard, piece.axes, piece.cut
        whole = isinstance(shard, int)
        in0, in1, in2 = cut(self.inbox.at[k % RING]), cut(self.in1.at[k]), cut(self.in2.at[k])
        if whole:
            in3, in4 = cut(self.in3.at[shard]), cut(self.in4.at[shard])
        if piece.stage == 0:
            self.halve(piece, cut(self.both.at[k % SLOTS, 0]), 0, in0, 8, axes[0], in1)
        elif piece.stage == 1:
            self.halve(piece, in0, self.bits[axes[0]] * 8, in1, 4, axes[1], in2)
        elif piece.stage == 2 and whole:
            self.halve(piece, in1, self.bits[axes[1]] * 4, in2, 2, axes[2], in3)
        elif piece.stage == 2:
            place = shard[0] % 2 * 2 + shard[0] // 2
            self.osum[place] = in2[...] + in1[pl.ds(self.bits[axes[1]] * 4, 4)]
            self.merged += 1
            if self.merged < self.chunks:
                piece.stage = 5
            else:
                far = pl.ds((1 - self.bits["z0"]) * 2, 2)
                self.send(piece, self.osum.at[far], self.oin3, "z0")
        elif piece.stage == 3 and whole:
            self.halve(piece, in2, self.bits[axes[2]] * 2, in3, 1, axes[3], in4)
        elif piece.stage == 3:
            self.halve(piece, self.osum, self.bits["z0"] * 2, self.oin3, 1, "z1", self.oin4)
        elif piece.stage == 4:
            if whole:
                final = self.fin.at[self.core, pl.ds(shard, 1), :, piece.lanes]
                final[...] = in4[...] + in3[pl.ds(self.bits[axes[3]], 1)]
            else:
                final = self.fin.at[self.core, pl.ds(self.fin.shape[1] - 4, 4)]
                final[...] = self.oin4[0] + self.oin3[self.bits["z1"]]
            self.send(piece, final, final, "core")
        piece.stage += 1

    def start_small(self):
        item = Small()
        self.send(item, self.small, self.small_in.at[0], "core")
        self.items.append(item)

    def advance_small(self, item):
        self.small[...] = self.small[...] + self.small_in[item.stage]
        item.stage += 1
        if item.stage < 5:
            axis = ("core", "x", "y", "z0", "z1")[item.stage]
            self.send(item, self.small, self.small_in.at[item.stage], axis)

    def under_way(self):
        return [item for item in self.items if item.copy is not None]

    def progress(self, cost):
        self.now += cost
        while True:
            due = [item for item in self.under_way() if item.eta <= self.now]
            if not due:
                return
            self.advance(min(due, key=lambda item: item.eta))

    def drain(self):
        while self.under_way():
            self.advance(min(self.under_way(), key=lambda item: item.eta))


def put_blocks(value, target, side, axes):
    half = value.shape[1] // 2
    for block in range(16):
        place = block
        if axes is not None and len(axes) == 4:
            bit = dict(x=block % 2, y=block // 2 % 2, z0=block // 4 % 2, z1=block // 8)
            place = sum(bit[axis] << (3 - i) for i, axis in enumerate(axes))
        target[place] = value[
            BLOCK * block : BLOCK * (block + 1), half * side : half * (side + 1)
        ].astype(BF16)


def make_flip():
    eye = jnp.where(
        lax.broadcasted_iota(jnp.int32, (GROUP, GROUP), 0)
        == lax.broadcasted_iota(jnp.int32, (GROUP, GROUP), 1),
        1.0,
        0.0,
    ).astype(BF16)

    def flip(source, target):
        for part in range(source.shape[1] // GROUP):
            lanes = pl.ds(part * GROUP, GROUP)
            target[lanes, :] = dot(eye, source[:, lanes], 1, 1).astype(BF16)

    return flip


class Parking:
    def __init__(self, stage, target, sem):
        self.stage, self.target, self.sem = stage, target, sem
        self.sent = []

    def put(self, value, index):
        slot = len(self.sent) % 2
        if len(self.sent) >= 2:
            self.sent[-2].wait()
        self.stage[slot] = value.astype(BF16)
        copy = pltpu.make_async_copy(self.stage.at[slot], self.target.at[index], self.sem.at[slot])
        copy.start()
        self.sent.append(copy)

    def finish(self):
        for copy in self.sent[-2:]:
            copy.wait()


def layer_kernel(
    wired,
    lengths_ref, tokens_hbm, cot_hbm, ln_gain_ref, w_qkv_hbm, b_qkv_ref, q_gain_ref, k_gain_ref,
    w_o_hbm, b_o_ref, w_in_hbm, b_in_ref, w_out_hbm, b_out_ref,
    output_hbm, grad_tokens_hbm, pieces_hbm, small_hbm,
    weights, tok, cot, packed, grow, normed, hid_even, hid_odd, gpre_0, gpre_1, gpre_2, gpre_3, spare,
    flipped, turned, fed, gnorm, qs, ks, vs, gm, small_ref,
    load_sem, done_sem, *refs,
):
    rows, width = tok.shape
    hidden_width = w_in_hbm.shape[1]
    chunks = hidden_width // width
    groups = width // GROUP
    seqs = rows // SEQ
    images = seqs * IMAGES
    base = lax.axis_index("branch") * seqs
    assert chunks == 4 and groups == 3
    hid, gpre = (hid_even, hid_odd), (gpre_0, gpre_1, gpre_2, gpre_3)
    mixed, gprojs = tok, (hid_even, spare, cot)
    w_in = [weights.at[f] for f in range(chunks)]
    w_out = [weights.at[4 + f % 3] for f in range(chunks)]
    w_qkv, w_o = [weights.at[5], weights.at[6], weights.at[4]], weights.at[7]
    nq, rq, nk = (fed.at[:, pl.ds(part * GROUP, GROUP)] for part in range(3))
    rk, dq, dk = (gnorm.at[:, pl.ds(part * GROUP, GROUP)] for part in range(3))
    loads = {}

    def load(name, source, target):
        copy = pltpu.make_async_copy(source, target, load_sem.at[len(loads)])
        copy.start()
        loads[name] = copy

    def load_chunk(f):
        cols = pl.ds(f * width, width)
        load(("out", f), w_out_hbm.at[cols, :], w_out[f])
        load(("in", f), w_in_hbm.at[:, cols], w_in[f])

    def load_qkv(hg):
        for t in range(3):
            load(
                ("qkv", hg, t),
                w_qkv_hbm.at[:, pl.ds(t * width + hg * GROUP, GROUP)],
                w_qkv[hg].at[:, pl.ds(t * GROUP, GROUP)],
            )

    load("tok", tokens_hbm, tok)
    load("cot", cot_hbm, cot)
    for f in range(3):
        load_chunk(f)
    load("wo", w_o_hbm, w_o)
    small_ref[...] = jnp.zeros_like(small_ref)
    net, parking = None, None
    if wired:
        net = Exchange(refs[:10] + (small_ref,) + refs[10:], chunks)
        net.greet()
    else:
        parking = Parking(refs[0], pieces_hbm, refs[1])

    def emit(value, shard, axes):
        if wired:
            index = net.open()
            net.put(index, value, 0, axes)
            net.start(index, shard, axes, 0, width // 2)
        else:
            parking.put(value, shard if isinstance(shard, int) else chunks + groups + 1 + shard[0])

    def point(cost):
        if wired:
            net.progress(cost)

    def cost(amount):
        if wired:
            net.now += amount

    def lanes_of(part):
        return pl.ds(part * GROUP, GROUP)

    ones_row = jnp.where(lax.broadcasted_iota(jnp.int32, (16, rows), 0) == 0, 1.0, 0.0)
    flipped[pl.ds(width, 16), :] = ones_row.astype(BF16)
    eye = jnp.where(
        lax.broadcasted_iota(jnp.int32, (GROUP, GROUP), 0)
        == lax.broadcasted_iota(jnp.int32, (GROUP, GROUP), 1),
        1.0,
        0.0,
    ).astype(BF16)

    def flip(source, target, part):
        target[lanes_of(part), :] = dot(eye, source[:, lanes_of(part)], 1, 1).astype(BF16)

    loads["tok"].wait()
    loads["cot"].wait()
    grad_sum = jnp.zeros((1, width), F32)
    for s in range(seqs):
        span = pl.ds(s * SEQ, SEQ)
        pick = one_hot(slot_positions([lengths_ref[base + s, j] for j in range(IMAGES)]))
        rows_here = dot(pick, tok[span, :])
        packed[span, :] = rows_here.astype(BF16)
        unit, _ = row_stats(rows_here)
        normed[span, :] = (unit * ln_gain_ref[...].reshape(1, width)).astype(BF16)
        grads_here = dot(pick, cot[span, :])
        grow[span, :] = grads_here.astype(BF16)
        grad_sum = grad_sum + jnp.sum(grads_here, axis=0, keepdims=True)
    small_ref[pl.ds(7, 1), pl.ds(0, width)] = grad_sum
    for part in range(groups):
        flip(normed, flipped, part)
    cost(6.0)

    def add_fed(f):
        for part in range(groups):
            lanes = lanes_of(part)
            up = dot(hid[f % 2][...], w_out[f][:, lanes])
            fed[:, lanes] = up if f == 0 else fed[:, lanes] + up

    if wired:
        net.meet()
    b_in = b_in_ref[...].reshape(1, hidden_width)
    ready = None

    def activate():
        f, c, pre, back = ready
        hidden, grad_pre = gelu_pair(pre, back)
        hid[f % 2][:, lanes_of(c)] = hidden.astype(BF16)
        gpre[f][:, lanes_of(c)] = grad_pre.astype(BF16)

    def send_w_in(f):
        sums = dot(flipped[...], gpre[f][...])
        cost(2.2)
        emit(sums[:width], f, XY)
        small_ref[pl.ds(f, 1), pl.ds(0, width)] = sums[width : width + 1]
        point(0.0)

    def send_w_out(f):
        cost(1.9)
        emit(dot(turned[...], grow[...]), (f,), YX[:2])
        point(0.0)

    for f in range(chunks):
        loads["in", f].wait()
        loads["out", f].wait()
        for c in range(groups):
            place = f * width + c * GROUP
            lanes = lanes_of(c)
            pre = dot(normed[...], w_in[f][:, lanes]) + b_in[:, place : place + GROUP]
            back = dot(grow[...], w_out[f][lanes, :], 1, 1)
            if ready is not None:
                activate()
            ready = (f, c, pre, back)
            if f > 0 and c == 0:
                for part in range(groups):
                    flip(hid[1 - f % 2], turned, part)
            if f > 0 and c == 2:
                add_fed(f - 1)
            point((1.7, 1.2, 2.9)[c] if f > 0 else 1.2)
            if f > 0 and c == 0:
                send_w_in(f - 1)
            if f > 0 and c == 1:
                send_w_out(f - 1)
        if f == 1:
            load_chunk(3)
        if f == 2:
            load_qkv(0)
        if f == 3:
            load_qkv(1)
    activate()
    for part in range(groups):
        flip(hid_odd, turned, part)
    send_w_in(chunks - 1)
    send_w_out(chunks - 1)

    add_fed(chunks - 1)
    load_qkv(2)
    hid_odd[...] = (fed[...] + b_out_ref[...].reshape(1, width)).astype(BF16)
    point(1.9)

    same_head = (
        lax.broadcasted_iota(jnp.int32, (GROUP, GROUP), 0) // HEAD
        == lax.broadcasted_iota(jnp.int32, (GROUP, GROUP), 1) // HEAD
    )
    average = jnp.where(same_head, 1.0 / HEAD, 0.0).astype(BF16)
    q_gain = jnp.concatenate([q_gain_ref[...].reshape(1, HEAD)] * (GROUP // HEAD), axis=1)
    k_gain = jnp.concatenate([k_gain_ref[...].reshape(1, HEAD)] * (GROUP // HEAD), axis=1)
    b_qkv = b_qkv_ref[...].reshape(1, 3 * width)
    lane = lax.broadcasted_iota(jnp.int32, (1, KEYS), 1)
    pair_lane = jnp.concatenate([lane, lane], axis=1)
    first_head = jnp.where(lane < HEAD, 1.0, 0.0).astype(BF16)
    second_head = jnp.where(lane < HEAD, 0.0, 1.0).astype(BF16)

    def head_mean(values, split):
        high = values.astype(BF16)
        mean = dot(high, average)
        if split:
            mean = mean + dot((values - high.astype(F32)).astype(BF16), average)
        return mean

    def head_norm(raw):
        centered = raw - head_mean(raw, True)
        inverse = lax.rsqrt(head_mean(centered * centered, False) + EPS)
        return centered * inverse, inverse

    def two_heads(block):
        return jnp.concatenate([block * first_head, block * second_head], axis=0)

    def stacked(block):
        return jnp.concatenate([block[:, :KEYS], block[:, KEYS:]], axis=0)

    def invert(total):
        guess = pl.reciprocal(total, approx=True)
        return guess * (2.0 - total * guess)

    def over_heads(block, change):
        parts = []
        for head in range(2):
            part = block[:, head * KEYS : (head + 1) * KEYS]
            total = change(jnp.sum(part, axis=1, keepdims=True))
            parts.append(jnp.broadcast_to(total, part.shape))
        return jnp.concatenate(parts, axis=1)

    ks[pl.ds(rows, KEYS - SLOT), :] = jnp.zeros((KEYS - SLOT, GROUP), BF16)
    vs[pl.ds(rows, KEYS - SLOT), :] = jnp.zeros((KEYS - SLOT, GROUP), BF16)

    for hg in range(groups):
        gproj = gprojs[hg]
        bias_q, bias_k, bias_v = (
            b_qkv[:, t * width + hg * GROUP : t * width + (hg + 1) * GROUP] for t in range(3)
        )
        for t in range(3):
            loads["qkv", hg, t].wait()
        if hg == 0:
            loads["wo"].wait()
        if wired and hg == groups - 1:
            net.pace, net.latency = LATE_PACE, LATE_LATENCY
        raw = dot(normed[...], w_qkv[hg][:, lanes_of(0)]) + bias_q
        unit, inverse = head_norm(raw)
        nq[...] = unit
        rq[...] = inverse
        qs[...] = (unit * q_gain).astype(BF16) * SCALE
        raw = dot(normed[...], w_qkv[hg][:, lanes_of(1)]) + bias_k
        unit, inverse = head_norm(raw)
        nk[...] = unit
        rk[...] = inverse
        ks[pl.ds(0, rows), :] = (unit * k_gain).astype(BF16)
        raw = dot(normed[...], w_qkv[hg][:, lanes_of(2)]) + bias_v
        vs[pl.ds(0, rows), :] = raw.astype(BF16)
        gm[...] = dot(grow[...], w_o[lanes_of(hg), :], 1, 1).astype(BF16)
        point(4.5)

        def one_image(image):
            start = image * SLOT
            span = pl.ds(start, SLOT)
            window = pl.ds(start, KEYS)
            seen = pair_lane < lengths_ref[base + image // IMAGES, image % IMAGES]
            for pair in range(GROUP // KEYS):
                lanes = pl.ds(pair * KEYS, KEYS)
                query, grad = qs[span, lanes], gm[span, lanes]
                keys, values = two_heads(ks[window, lanes]), two_heads(vs[window, lanes])
                weight = jnp.where(seen, jnp.exp(dot(query, keys, 1, 1)), 0.0)
                probs = weight * over_heads(weight, invert)
                grad_probs = dot(grad, values, 1, 1)
                inner = over_heads(probs * grad_probs, lambda total: total)
                grad_scores = (probs * (grad_probs - inner)).astype(BF16)
                probs_low = probs.astype(BF16)
                mixed[span, pl.ds(hg * GROUP + pair * KEYS, KEYS)] = dot(probs_low, values).astype(
                    BF16
                )
                dq[span, lanes] = dot(grad_scores, keys) * SCALE
                dk[span, lanes] = dot(stacked(grad_scores), two_heads(query), 0, 0)[:SLOT]
                gproj[span, pl.ds(2 * GROUP + pair * KEYS, KEYS)] = dot(
                    stacked(probs_low), two_heads(grad), 0, 0
                )[:SLOT].astype(BF16)

        for image in range(0, images, 2):
            one_image(image)
            one_image(image + 1)
            point(1.3)
        if hg == groups - 1:
            for part in range(groups):
                flip(mixed, turned, part)
            if wired:
                index = net.open()
                for lane, size, part_axes in ((0, KEYS, XY), (KEYS, 2 * KEYS, YX)):
                    sums = dot(turned[...], grow[:, pl.ds(2 * lane, 2 * size)])
                    net.put(index, sums, lane, part_axes)
                    cost(1.1)
                    net.start(index, chunks + groups, part_axes, lane, size)
                point(0.0)
            else:
                parking.put(dot(turned[...], grow[...]), chunks + groups)

        axes = (YX, XY, YX)[hg]
        last = hg == groups - 1
        index = net.open() if wired else None
        parts = {}

        def part_grad(t, part_axes):
            sums = dot(flipped[...], gproj[:, lanes_of(t)])
            small_ref[pl.ds(4 + hg, 1), lanes_of(t)] = sums[width : width + 1]
            if wired:
                net.put(index, sums[:width], t * KEYS, part_axes)
                if last:
                    net.start(index, chunks + hg, part_axes, t * KEYS, KEYS)
            else:
                parts[t] = sums[:width]

        def norm_back(side, grad_ref, unit_ref, inverse_ref, gain):
            grad, unit = grad_ref[...], unit_ref[...]
            gain_sum = jnp.sum(grad * unit, axis=0, keepdims=True)
            small_ref[pl.ds(3 + side, 1), pl.ds(width, GROUP)] += gain_sum
            grad = grad * gain
            back = grad - head_mean(grad, False) - unit * head_mean(grad * unit, False)
            gproj[:, lanes_of(side)] = (back * inverse_ref[...]).astype(BF16)

        cost(0.7)
        part_grad(2, ZX if last else axes)
        norm_back(0, dq, nq, rq, q_gain)
        cost(1.5)
        if last:
            point(0.0)
        part_grad(0, XY if last else axes)
        norm_back(1, dk, nk, rk, k_gain)
        cost(1.5)
        if last:
            point(0.0)
        part_grad(1, YX if last else axes)
        if not wired:
            parking.put(jnp.concatenate([parts[t] for t in range(3)], axis=1), chunks + hg)
        elif not last:
            net.start(index, chunks + hg, axes, 0, width // 2)
        point(0.0)

    for part in range(groups):
        lanes = lanes_of(part)
        total = None
        for i, (source, target) in enumerate(list(zip(gpre, w_in)) + list(zip(gprojs, w_qkv))):
            down = dot(source[...], target[lanes, :], 1, 1)
            total = down if total is None else total + down
            if i == 3:
                point(2.0)
        gnorm[:, lanes] = total
        point(1.5)
    load("tok again", tokens_hbm, hid_even)
    load("cot again", cot_hbm, gpre_0)
    ln_gain = ln_gain_ref[...].reshape(1, width)
    b_o = b_o_ref[...].reshape(1, width)
    gain_grad = jnp.zeros((1, width), F32)
    for s in range(seqs):
        span = pl.ds(s * SEQ, SEQ)
        unit, inverse = row_stats(packed[span, :].astype(F32))
        grad = gnorm[span, :]
        gain_grad = gain_grad + jnp.sum(grad * unit, axis=0, keepdims=True)
        grad = grad * ln_gain
        back = grad - jnp.mean(grad, axis=1, keepdims=True)
        back = (back - unit * jnp.mean(grad * unit, axis=1, keepdims=True)) * inverse
        normed[span, :] = (grow[span, :].astype(F32) + back).astype(BF16)
    for t in range(width // GROUP):
        small_ref[pl.ds(t, 1), pl.ds(width, GROUP)] = gain_grad[:, t * GROUP : (t + 1) * GROUP]
    if wired:
        net.start_small()
    point(1.5)
    finals = []
    loads["tok again"].wait()
    loads["cot again"].wait()

    def hand_over(source, target):
        copy = pltpu.make_async_copy(source, target, done_sem.at[len(finals)])
        copy.start()
        finals.append(copy)

    for s in range(seqs):
        span = pl.ds(s * SEQ, SEQ)
        place = position_slots([lengths_ref[base + s, j] for j in range(IMAGES)])
        put = one_hot(place)
        padding = jnp.where(place < 0, 1.0, 0.0)
        attended = (dot(mixed[span, :], w_o[...]) + b_o).astype(BF16).astype(F32)
        result = packed[span, :].astype(F32) + (attended + hid_odd[span, :].astype(F32))
        result = dot(put, result.astype(BF16)) + padding * hid_even[span, :].astype(F32)
        hid_even[span, :] = result.astype(BF16)
        hand_over(hid_even.at[span], output_hbm.at[span])
        point(1.2)
        grads = dot(put, normed[span, :]) + padding * gpre_0[span, :].astype(F32)
        gpre_0[span, :] = grads.astype(BF16)
        hand_over(gpre_0.at[span], grad_tokens_hbm.at[span])
        point(0.8)
    if wired:
        net.drain()
        hand_over(net.fin, pieces_hbm)
    else:
        parking.finish()
    hand_over(small_ref, small_hbm)
    for copy in finals:
        copy.wait()


def split_lanes(block, groups):
    width = block.shape[1] // 3
    return jnp.concatenate(
        [
            block[:, hg * width + t * GROUP : hg * width + (t + 1) * GROUP]
            for t in range(3)
            for hg in range(groups)
        ],
        axis=1,
    )


def fold_heads(gains):
    return sum(gains[:, h * HEAD : (h + 1) * HEAD] for h in range(GROUP // HEAD))


def small_parts(small, chunks, groups, width):
    b_in = jnp.concatenate([small[f : f + 1, :width] for f in range(chunks)], axis=1)
    b_qkv = jnp.concatenate([small[4 + hg : 5 + hg, :width] for hg in range(groups)], axis=1)
    ln = jnp.concatenate([small[t : t + 1, width:] for t in range(width // GROUP)], axis=1)
    gains = [fold_heads(small[3 + side : 4 + side, width:]) for side in range(2)]
    return ln, split_lanes(b_qkv, groups), gains[0], gains[1], small[7:8, :width], b_in


def finish_kernel(
    rows_hbm, grads_hbm, fin_hbm, small_hbm, output_hbm, grad_tokens_hbm, g_ln, g_qkv_hbm, g_b_qkv,
    g_q, g_k, g_o_hbm, g_b_o, g_in_hbm, g_b_in, g_out_hbm, g_b_out, held, fin, small, g_qkv, g_o, g_in,
    g_out, sem,
):
    comes = [
        pltpu.make_async_copy(source, target, sem.at[0, i])
        for i, (source, target) in enumerate(
            ((fin_hbm, fin), (small_hbm, small), (rows_hbm, held.at[0]), (grads_hbm, held.at[1]))
        )
    ]
    goes = [
        pltpu.make_async_copy(source, target, sem.at[1, i])
        for i, (source, target) in enumerate(
            (
                (held.at[0], output_hbm), (held.at[1], grad_tokens_hbm), (g_in, g_in_hbm),
                (g_qkv, g_qkv_hbm), (g_out, g_out_hbm), (g_o, g_o_hbm),
            )
        )
    ]
    for copy in comes:
        copy.start()
    width = g_o.shape[1]
    chunks, groups = g_in.shape[1] // width, width // GROUP

    def whole(shard, lane, size):
        return jnp.concatenate(
            [fin[side, shard, :, lane : lane + size].astype(F32) for side in range(2)], axis=1
        )

    comes[0].wait()
    for f in range(chunks):
        g_in[:, f * width : (f + 1) * width] = whole(f, 0, width // 2)
    goes[2].start()
    for hg in range(groups):
        for t in range(3):
            place = t * width + hg * GROUP
            g_qkv[:, place : place + GROUP] = whole(chunks + hg, t * KEYS, KEYS)
    goes[3].start()
    for i in range(2):
        comes[2 + i].wait()
        goes[i].start()
    for j in range(4):
        g_out[j * BLOCK : (j + 1) * BLOCK, :] = whole(chunks + groups + 1 + j, 0, width // 2)
    goes[4].start()
    g_o[:, :GROUP] = whole(chunks + groups, 0, KEYS)
    g_o[:, GROUP:] = whole(chunks + groups, KEYS, 2 * KEYS)
    goes[5].start()
    comes[1].wait()
    ln, b_qkv, q, k, b_out, b_in = small_parts(small[...], chunks, groups, width)
    for ref, value in (
        (g_ln, ln), (g_b_qkv, b_qkv), (g_q, q), (g_k, k), (g_b_o, b_out), (g_b_in, b_in), (g_b_out, b_out)
    ):
        ref[...] = value.reshape(value.shape[1])
    for copy in goes:
        copy.wait()


def local(n_dp, tokens, lengths, cotangent, ln_gain, w_qkv, b_qkv, q_gain, k_gain, w_o, b_o, w_in, b_in, w_out, b_out):
    rows, width = tokens.shape
    hidden_width = w_in.shape[1]
    chunks = hidden_width // width
    groups = width // GROUP
    seqs = rows // SEQ
    shards = chunks + groups + 1
    everyone = shards + chunks
    wired = n_dp * BLOCK == width and n_dp == 4 * chunks
    half = width // 2
    extra = KEYS - SLOT
    anywhere = pl.BlockSpec(memory_space=pl.ANY)
    vmem = pl.BlockSpec(memory_space=pltpu.VMEM)
    smem = pl.BlockSpec(memory_space=pltpu.SMEM)
    wide = lambda *shape: pltpu.VMEM(shape, F32)
    slim = lambda *shape: pltpu.VMEM(shape, BF16)
    flags = lambda *shape: pltpu.SemaphoreType.DMA(shape)
    low = lambda *shape: jax.ShapeDtypeStruct(shape, BF16)
    full = lambda *shape: jax.ShapeDtypeStruct(shape, F32)
    small_shape = (8, width + GROUP)

    if wired:
        out_piece = low(2, shards + 4, BLOCK, half)
        flights = 6 * (shards + 3) + 3 * chunks + 3 + 5
        others = [
            slim(SLOTS, 2, 16, BLOCK, half), slim(RING, 16, BLOCK, half),
            slim(everyone, 8, BLOCK, half), slim(everyone, 4, BLOCK, half),
            slim(shards, 2, BLOCK, half), slim(shards, 1, BLOCK, half), slim(4, 4, BLOCK, half),
            slim(2, 4, BLOCK, half), slim(1, 4, BLOCK, half), slim(2, shards + 4, BLOCK, half),
            wide(5, *small_shape), flags(flights), flags(flights),
        ]
        settings = dict(collective_id=0, has_side_effects=True)
    else:
        out_piece = low(everyone, width, width)
        others = [slim(2, width, width), flags(2)]
        settings = {}
    output, grad_tokens, pieces, small = pl.pallas_call(
        functools.partial(layer_kernel, wired),
        out_shape=(low(rows, width), low(rows, width), out_piece, full(*small_shape)),
        in_specs=[
            smem, anywhere, anywhere, vmem, anywhere, vmem, vmem, vmem, anywhere, vmem, anywhere,
            vmem, anywhere, vmem,
        ],
        out_specs=(anywhere,) * 4,
        scratch_shapes=[slim(8, width, width)]
        + [slim(rows, width)] * 12
        + [
            slim(width + 16, rows), slim(width, rows), wide(rows, width), wide(rows, width),
            slim(rows, GROUP), slim(rows + extra, GROUP), slim(rows + extra, GROUP),
            slim(rows, GROUP),
        ]
        + [wide(*small_shape), flags(5 + 2 * chunks + 3 * groups), flags(2 * seqs + 2)]
        + others,
        compiler_params=pltpu.CompilerParams(vmem_limit_bytes=62 << 20, **settings),
    )(
        lengths, tokens, cotangent, ln_gain, w_qkv, b_qkv, q_gain, k_gain, w_o, b_o, w_in, b_in,
        w_out, b_out,
    )

    if wired:
        return pl.pallas_call(
            finish_kernel,
            out_shape=(
                low(rows, width), low(rows, width), full(width), full(BLOCK, 3 * width),
                full(3 * width), full(HEAD), full(HEAD), full(BLOCK, width), full(width),
                full(BLOCK, hidden_width), full(hidden_width), full(4 * BLOCK, width), full(width),
            ),
            in_specs=[anywhere] * 4,
            out_specs=(
                anywhere, anywhere, vmem, anywhere, vmem, vmem, vmem, anywhere, vmem, anywhere, vmem,
                anywhere, vmem,
            ),
            scratch_shapes=[
                slim(2, rows, width), slim(2, shards + 4, BLOCK, half), wide(*small_shape),
                wide(BLOCK, 3 * width), wide(BLOCK, width), wide(BLOCK, hidden_width),
                wide(4 * BLOCK, width), flags(2, 6),
            ],
        )(output, grad_tokens, pieces, small)

    def scatter(block, dim):
        part = lax.psum_scatter(block, "dp", scatter_dimension=dim, tiled=True)
        return lax.psum(part, "branch").astype(F32)

    grad_out = scatter(pieces[shards:].reshape(hidden_width, width), 0)
    reduced = scatter(pieces[:shards], 1)
    grad_in = jnp.concatenate([reduced[f] for f in range(chunks)], axis=1)
    qkv = jnp.concatenate([reduced[chunks + hg] for hg in range(groups)], axis=1)
    small = lax.psum(small, ("dp", "branch"))
    ln, g_b_qkv, g_q, g_k, g_b_out, g_b_in = (
        part[0] for part in small_parts(small, chunks, groups, width)
    )
    return (
        output, grad_tokens, ln, split_lanes(qkv, groups), g_b_qkv, g_q, g_k,
        reduced[chunks + groups], g_b_out, grad_in, g_b_in, grad_out, g_b_out,
    )


def solution(mesh):
    rows, split, whole = P(("dp", "branch"), None), P("dp", None), P()
    return jax.shard_map(
        functools.partial(local, mesh.shape["dp"]),
        mesh=mesh,
        in_specs=(rows, split, rows) + (whole,) * 11,
        out_specs=(
            rows, rows, whole, split, whole, whole, whole, split, whole, split, whole, split, whole,
        ),
        check_vma=False,
    )
```

```python
import functools
import math

import jax
import jax.numpy as jnp
from jax import lax
from jax.experimental import pallas as pl
from jax.experimental.pallas import tpu as pltpu
from jax.sharding import PartitionSpec as P

HEAD = 64
SEQ = 448
IMAGES = 4
SLOT = SEQ // IMAGES
KEYS = 128
GROUP = 256
EPS = 1e-06
SCALE = 0.125
F32 = jnp.float32
BF16 = jnp.bfloat16
GELU_A = math.sqrt(2.0 / math.pi)
GELU_B = 0.044715


def dot(left, right, left_dim=1, right_dim=0):
    return lax.dot_general(
        left, right, (((left_dim,), (right_dim,)), ((), ())), preferred_element_type=F32
    )


def slot_positions(lens):
    row = lax.broadcasted_iota(jnp.int32, (SEQ, 1), 0)
    held = jnp.full((SEQ, 1), -1, jnp.int32)
    start = jnp.int32(0)
    for image in range(IMAGES):
        place = row - SLOT * image
        held = jnp.where((place >= 0) & (place < lens[image]), place + start, held)
        start = start + lens[image]
    return held


def position_slots(lens):
    row = lax.broadcasted_iota(jnp.int32, (SEQ, 1), 0)
    held = jnp.full((SEQ, 1), -1, jnp.int32)
    start = jnp.int32(0)
    for image in range(IMAGES):
        place = row - start
        held = jnp.where((place >= 0) & (place < lens[image]), place + SLOT * image, held)
        start = start + lens[image]
    return held


def one_hot(index):
    lanes = lax.broadcasted_iota(jnp.int32, (SEQ, SEQ), 1)
    return jnp.where(lanes == index, 1.0, 0.0).astype(BF16)


def row_stats(values):
    centered = values - jnp.mean(values, axis=1, keepdims=True)
    spread = jnp.mean(centered * centered, axis=1, keepdims=True)
    inverse = lax.rsqrt(spread + EPS)
    return centered * inverse, inverse


def gelu_pair(pre, grad):
    square = pre * pre
    up = 0.5 * jnp.tanh(pre * (GELU_A + (GELU_A * GELU_B) * square)) + 0.5
    hidden = pre * up
    slope = 2.0 * GELU_A + (6.0 * GELU_A * GELU_B) * square
    return hidden, (up + (hidden * (1.0 - up)) * slope) * grad


MESH = pl.DeviceIdType.MESH
BLOCK = 48
SLOTS = 2
RING = 8
XY, YX = ("x", "y", "z0", "z1"), ("y", "x", "z0", "z1")
ZX, ZY = ("z0", "z1", "x", "y"), ("z0", "z1", "y", "x")
RATES = {"core": 400e3, "x": 42e3, "y": 42e3, "z0": 42e3, "z1": 21e3}
LATENCY = 2.0


class Piece:
    def __init__(self, index, shard, axes, lanes):
        self.index, self.shard, self.axes, self.lanes = index, shard, axes, lanes
        self.stage, self.copy, self.eta = 0, None, 0.0

    def cut(self, ref):
        return ref.at[:, :, self.lanes]


class Small:
    def __init__(self):
        self.stage, self.copy, self.eta = 0, None, 0.0


class Exchange:
    def __init__(self, refs, chunks):
        (self.both, self.inbox, self.in1, self.in2, self.in3, self.in4, self.osum, self.oin3,
         self.oin4, self.fin, self.small, self.small_in, self.send_sem, self.recv_sem) = refs
        self.chunks = chunks
        self.dp, self.core = lax.axis_index("dp"), lax.axis_index("branch")
        self.bits = {
            "x": lax.rem(self.dp, 2),
            "y": lax.rem(self.dp // 2, 2),
            "z0": lax.rem(self.dp // 4, 2),
            "z1": lax.rem(self.dp // 8, 2),
        }
        self.far = {
            axis: (self.dp + step - 2 * step * self.bits[axis], self.core)
            for axis, step in (("x", 1), ("y", 2), ("z0", 4), ("z1", 8))
        }
        self.far["core"] = (self.dp, 1 - self.core)
        self.items, self.opened = [], 0
        self.flights, self.merged, self.now, self.free = 0, 0, 0.0, {}

    def greet(self):
        barrier = pltpu.get_barrier_semaphore()
        for device in self.far.values():
            pl.semaphore_signal(barrier, inc=1, device_id=device, device_id_type=MESH)
        pl.semaphore_wait(barrier, len(self.far))

    def send(self, item, source, target, axis):
        copy = pltpu.make_async_remote_copy(
            src_ref=source, dst_ref=target, send_sem=self.send_sem.at[self.flights],
            recv_sem=self.recv_sem.at[self.flights], device_id=self.far[axis], device_id_type=MESH,
        )
        self.flights += 1
        copy.start()
        link = axis[0]
        size = source.dtype.itemsize * math.prod(source.shape)
        self.free[link] = max(self.free.get(link, 0.0), self.now) + size / RATES[axis]
        item.copy, item.eta = copy, self.free[link] + LATENCY

    def open(self):
        index = self.opened
        for behind, stage in ((SLOTS, 1), (RING - SLOTS, 2)):
            while any(
                item.index == index - behind and item.stage < stage
                for item in self.items
                if isinstance(item, Piece)
            ):
                self.advance(min(self.under_way(), key=lambda item: item.eta))
        self.opened += 1
        return index

    def put(self, index, value, lane, axes):
        half = value.shape[1] // 2
        for side, role in ((0, self.core), (1, 1 - self.core)):
            target = self.both.at[index % SLOTS, role, :, :, pl.ds(lane, half)]
            put_blocks(value, target, side, axes)

    def start(self, index, shard, axes, lane, width):
        piece = Piece(index, shard, axes, pl.ds(lane, width))
        self.send(
            piece, piece.cut(self.both.at[index % SLOTS, 1]), piece.cut(self.inbox.at[index % RING]),
            "core",
        )
        self.items.append(piece)

    def halve(self, piece, held, held_at, arrived, count, axis, target):
        near = self.bits[axis] * count
        away = (1 - self.bits[axis]) * count
        span = pl.ds(away, count)
        arrived[span] = arrived[span] + held[pl.ds(held_at + away, count)]
        self.send(piece, arrived.at[span], target, axis)
        span = pl.ds(near, count)
        arrived[span] = arrived[span] + held[pl.ds(held_at + near, count)]

    def advance(self, piece):
        piece.copy.wait()
        self.now = max(self.now, piece.eta)
        piece.copy = None
        if isinstance(piece, Small):
            self.advance_small(piece)
            return
        k, shard, axes, cut = piece.index, piece.shard, piece.axes, piece.cut
        whole = isinstance(shard, int)
        in0, in1, in2 = cut(self.inbox.at[k % RING]), cut(self.in1.at[k]), cut(self.in2.at[k])
        if whole:
            in3, in4 = cut(self.in3.at[shard]), cut(self.in4.at[shard])
        if piece.stage == 0:
            self.halve(piece, cut(self.both.at[k % SLOTS, 0]), 0, in0, 8, axes[0], in1)
        elif piece.stage == 1:
            self.halve(piece, in0, self.bits[axes[0]] * 8, in1, 4, axes[1], in2)
        elif piece.stage == 2 and whole:
            self.halve(piece, in1, self.bits[axes[1]] * 4, in2, 2, axes[2], in3)
        elif piece.stage == 2:
            place = shard[0] % 2 * 2 + shard[0] // 2
            self.osum[place] = in2[...] + in1[pl.ds(self.bits[axes[1]] * 4, 4)]
            self.merged += 1
            if self.merged < self.chunks:
                piece.stage = 5
            else:
                far = pl.ds((1 - self.bits["z0"]) * 2, 2)
                self.send(piece, self.osum.at[far], self.oin3, "z0")
        elif piece.stage == 3 and whole:
            self.halve(piece, in2, self.bits[axes[2]] * 2, in3, 1, axes[3], in4)
        elif piece.stage == 3:
            self.halve(piece, self.osum, self.bits["z0"] * 2, self.oin3, 1, "z1", self.oin4)
        elif piece.stage == 4:
            if whole:
                final = self.fin.at[self.core, pl.ds(shard, 1), :, piece.lanes]
                final[...] = in4[...] + in3[pl.ds(self.bits[axes[3]], 1)]
            else:
                final = self.fin.at[self.core, pl.ds(self.fin.shape[1] - 4, 4)]
                final[...] = self.oin4[0] + self.oin3[self.bits["z1"]]
            self.send(piece, final, final, "core")
        piece.stage += 1

    def start_small(self):
        item = Small()
        self.send(item, self.small, self.small_in.at[0], "core")
        self.items.append(item)

    def advance_small(self, item):
        self.small[...] = self.small[...] + self.small_in[item.stage]
        item.stage += 1
        if item.stage < 5:
            axis = ("core", "x", "y", "z0", "z1")[item.stage]
            self.send(item, self.small, self.small_in.at[item.stage], axis)

    def under_way(self):
        return [item for item in self.items if item.copy is not None]

    def progress(self, cost):
        self.now += cost
        while True:
            due = [item for item in self.under_way() if item.eta <= self.now]
            if not due:
                return
            self.advance(min(due, key=lambda item: item.eta))

    def drain(self):
        while self.under_way():
            self.advance(min(self.under_way(), key=lambda item: item.eta))


def put_blocks(value, target, side, axes):
    half = value.shape[1] // 2
    for block in range(16):
        place = block
        if axes is not None and len(axes) == 4:
            bit = dict(x=block % 2, y=block // 2 % 2, z0=block // 4 % 2, z1=block // 8)
            place = sum(bit[axis] << (3 - i) for i, axis in enumerate(axes))
        target[place] = value[
            BLOCK * block : BLOCK * (block + 1), half * side : half * (side + 1)
        ].astype(BF16)


def make_flip():
    eye = jnp.where(
        lax.broadcasted_iota(jnp.int32, (GROUP, GROUP), 0)
        == lax.broadcasted_iota(jnp.int32, (GROUP, GROUP), 1),
        1.0,
        0.0,
    ).astype(BF16)

    def flip(source, target):
        for part in range(source.shape[1] // GROUP):
            lanes = pl.ds(part * GROUP, GROUP)
            target[lanes, :] = dot(eye, source[:, lanes], 1, 1).astype(BF16)

    return flip


class Parking:
    def __init__(self, stage, target, sem):
        self.stage, self.target, self.sem = stage, target, sem
        self.sent = []

    def put(self, value, index):
        slot = len(self.sent) % 2
        if len(self.sent) >= 2:
            self.sent[-2].wait()
        self.stage[slot] = value.astype(BF16)
        copy = pltpu.make_async_copy(self.stage.at[slot], self.target.at[index], self.sem.at[slot])
        copy.start()
        self.sent.append(copy)

    def finish(self):
        for copy in self.sent[-2:]:
            copy.wait()


def layer_kernel(
    wired,
    lengths_ref, tokens_hbm, cot_hbm, ln_gain_ref, w_qkv_hbm, b_qkv_ref, q_gain_ref, k_gain_ref,
    w_o_hbm, b_o_ref, w_in_hbm, b_in_ref, w_out_hbm, b_out_ref,
    output_hbm, grad_tokens_hbm, pieces_hbm, small_hbm,
    weights, tok, cot, packed, grow, normed, hid_even, gpre_even, hid_odd, gpre_odd,
    flipped, turned, fed, gnorm, qs, ks, vs, gm, rk, dq, dk, small_ref,
    load_sem, done_sem, *refs,
):
    rows, width = tok.shape
    hidden_width = w_in_hbm.shape[1]
    chunks = hidden_width // width
    groups = width // GROUP
    seqs = rows // SEQ
    images = seqs * IMAGES
    base = lax.axis_index("branch") * seqs
    assert chunks == 4 and groups == 3
    hid, gpre = (hid_even, hid_odd), (gpre_even, gpre_odd)
    mixed, gprojs = tok, (hid_even, gpre_even, cot)
    w_in = [weights.at[f % 3] for f in range(chunks)]
    w_out = [weights.at[3 + f % 3] for f in range(chunks)]
    w_qkv, w_o = [weights.at[1], weights.at[4], weights.at[2]], weights.at[5]
    nq, rq, nk = (fed.at[:, pl.ds(part * GROUP, GROUP)] for part in range(3))
    loads = {}

    def load(name, source, target):
        copy = pltpu.make_async_copy(source, target, load_sem.at[len(loads)])
        copy.start()
        loads[name] = copy

    def load_chunk(f):
        cols = pl.ds(f * width, width)
        load(("in", f), w_in_hbm.at[:, cols], w_in[f])
        load(("out", f), w_out_hbm.at[cols, :], w_out[f])

    def load_qkv(hg):
        for t in range(3):
            load(
                ("qkv", hg, t),
                w_qkv_hbm.at[:, pl.ds(t * width + hg * GROUP, GROUP)],
                w_qkv[hg].at[:, pl.ds(t * GROUP, GROUP)],
            )

    load("tok", tokens_hbm, tok)
    load("cot", cot_hbm, cot)
    for f in range(3):
        load_chunk(f)
    small_ref[...] = jnp.zeros_like(small_ref)
    net, parking = None, None
    if wired:
        net = Exchange(refs[:10] + (small_ref,) + refs[10:], chunks)
        net.greet()
    else:
        parking = Parking(refs[0], pieces_hbm, refs[1])

    def emit(value, shard, axes):
        if wired:
            index = net.open()
            net.put(index, value, 0, axes)
            net.start(index, shard, axes, 0, width // 2)
        else:
            parking.put(value, shard if isinstance(shard, int) else chunks + groups + 1 + shard[0])

    def point(cost):
        if wired:
            net.progress(cost)

    def cost(amount):
        if wired:
            net.now += amount

    def lanes_of(part):
        return pl.ds(part * GROUP, GROUP)

    ones_row = jnp.where(lax.broadcasted_iota(jnp.int32, (16, rows), 0) == 0, 1.0, 0.0)
    flipped[pl.ds(width, 16), :] = ones_row.astype(BF16)
    eye = jnp.where(
        lax.broadcasted_iota(jnp.int32, (GROUP, GROUP), 0)
        == lax.broadcasted_iota(jnp.int32, (GROUP, GROUP), 1),
        1.0,
        0.0,
    ).astype(BF16)

    def flip(source, target, part):
        target[lanes_of(part), :] = dot(eye, source[:, lanes_of(part)], 1, 1).astype(BF16)

    for name in ("tok", "cot", ("in", 0), ("out", 0)):
        loads[name].wait()
    grad_sum = jnp.zeros((1, width), F32)
    for s in range(seqs):
        span = pl.ds(s * SEQ, SEQ)
        pick = one_hot(slot_positions([lengths_ref[base + s, j] for j in range(IMAGES)]))
        rows_here = dot(pick, tok[span, :])
        packed[span, :] = rows_here.astype(BF16)
        unit, _ = row_stats(rows_here)
        normed[span, :] = (unit * ln_gain_ref[...].reshape(1, width)).astype(BF16)
        grads_here = dot(pick, cot[span, :])
        grow[span, :] = grads_here.astype(BF16)
        grad_sum = grad_sum + jnp.sum(grads_here, axis=0, keepdims=True)
    small_ref[pl.ds(7, 1), pl.ds(0, width)] = grad_sum
    for part in range(groups):
        flip(normed, flipped, part)
    cost(6.0)

    def add_fed(f):
        for part in range(groups):
            lanes = lanes_of(part)
            up = dot(hid[f % 2][...], w_out[f][:, lanes])
            fed[:, lanes] = up if f == 0 else fed[:, lanes] + up

    def add_gnorm(source, target, first):
        for part in range(groups):
            lanes = lanes_of(part)
            down = dot(source[...], target[lanes, :], 1, 1)
            gnorm[:, lanes] = down if first else gnorm[:, lanes] + down

    b_in = b_in_ref[...].reshape(1, hidden_width)
    ready = None

    def activate():
        f, c, pre, back = ready
        hidden, grad_pre = gelu_pair(pre, back)
        hid[f % 2][:, lanes_of(c)] = hidden.astype(BF16)
        gpre[f % 2][:, lanes_of(c)] = grad_pre.astype(BF16)

    def send_w_in(f):
        sums = dot(flipped[...], gpre[f % 2][...])
        cost(2.2)
        emit(sums[:width], f, XY)
        small_ref[pl.ds(f, 1), pl.ds(0, width)] = sums[width : width + 1]
        point(0.0)

    def send_w_out(f):
        cost(1.9)
        emit(dot(turned[...], grow[...]), (f,), YX[:2])
        point(0.0)

    for f in range(chunks):
        if f > 0:
            loads["in", f].wait()
            loads["out", f].wait()
        for c in range(groups):
            place = f * width + c * GROUP
            lanes = lanes_of(c)
            pre = dot(normed[...], w_in[f][:, lanes]) + b_in[:, place : place + GROUP]
            back = dot(grow[...], w_out[f][lanes, :], 1, 1)
            if ready is not None:
                activate()
            ready = (f, c, pre, back)
            if f > 0 and c == 0:
                for part in range(groups):
                    flip(hid[1 - f % 2], turned, part)
            if f > 0 and c == 2:
                add_fed(f - 1)
                add_gnorm(gpre[1 - f % 2], w_in[f - 1], f == 1)
            point((1.7, 1.2, 4.6)[c] if f > 0 else 1.2)
            if f > 0 and c == 0:
                send_w_in(f - 1)
            if f > 0 and c == 1:
                send_w_out(f - 1)
        if f == 1:
            load_chunk(3)
        if f == 2:
            load_qkv(0)
            load_qkv(1)
        if f == 3:
            load_qkv(2)
            load("wo", w_o_hbm, w_o)
    activate()
    for part in range(groups):
        flip(hid_odd, turned, part)
    send_w_in(chunks - 1)
    send_w_out(chunks - 1)

    add_fed(chunks - 1)
    hid_odd[...] = (fed[...] + b_out_ref[...].reshape(1, width)).astype(BF16)
    point(1.9)

    same_head = (
        lax.broadcasted_iota(jnp.int32, (GROUP, GROUP), 0) // HEAD
        == lax.broadcasted_iota(jnp.int32, (GROUP, GROUP), 1) // HEAD
    )
    average = jnp.where(same_head, 1.0 / HEAD, 0.0).astype(BF16)
    q_gain = jnp.concatenate([q_gain_ref[...].reshape(1, HEAD)] * (GROUP // HEAD), axis=1)
    k_gain = jnp.concatenate([k_gain_ref[...].reshape(1, HEAD)] * (GROUP // HEAD), axis=1)
    b_qkv = b_qkv_ref[...].reshape(1, 3 * width)
    lane = lax.broadcasted_iota(jnp.int32, (1, KEYS), 1)
    pair_lane = jnp.concatenate([lane, lane], axis=1)
    first_head = jnp.where(lane < HEAD, 1.0, 0.0).astype(BF16)
    second_head = jnp.where(lane < HEAD, 0.0, 1.0).astype(BF16)

    def head_mean(values, split):
        high = values.astype(BF16)
        mean = dot(high, average)
        if split:
            mean = mean + dot((values - high.astype(F32)).astype(BF16), average)
        return mean

    def head_norm(raw):
        centered = raw - head_mean(raw, True)
        inverse = lax.rsqrt(head_mean(centered * centered, False) + EPS)
        return centered * inverse, inverse

    def two_heads(block):
        return jnp.concatenate([block * first_head, block * second_head], axis=0)

    def stacked(block):
        return jnp.concatenate([block[:, :KEYS], block[:, KEYS:]], axis=0)

    def invert(total):
        guess = pl.reciprocal(total, approx=True)
        return guess * (2.0 - total * guess)

    def over_heads(block, change):
        parts = []
        for head in range(2):
            part = block[:, head * KEYS : (head + 1) * KEYS]
            total = change(jnp.sum(part, axis=1, keepdims=True))
            parts.append(jnp.broadcast_to(total, part.shape))
        return jnp.concatenate(parts, axis=1)

    ks[pl.ds(rows, KEYS - SLOT), :] = jnp.zeros((KEYS - SLOT, GROUP), BF16)
    vs[pl.ds(rows, KEYS - SLOT), :] = jnp.zeros((KEYS - SLOT, GROUP), BF16)

    for hg in range(groups):
        gproj = gprojs[hg]
        bias_q, bias_k, bias_v = (
            b_qkv[:, t * width + hg * GROUP : t * width + (hg + 1) * GROUP] for t in range(3)
        )
        for t in range(3):
            loads["qkv", hg, t].wait()
        if hg == 0:
            loads["wo"].wait()
        raw = dot(normed[...], w_qkv[hg][:, lanes_of(0)]) + bias_q
        unit, inverse = head_norm(raw)
        nq[...] = unit
        rq[...] = inverse
        qs[...] = (unit * q_gain).astype(BF16) * SCALE
        raw = dot(normed[...], w_qkv[hg][:, lanes_of(1)]) + bias_k
        unit, inverse = head_norm(raw)
        nk[...] = unit
        rk[...] = inverse
        ks[pl.ds(0, rows), :] = (unit * k_gain).astype(BF16)
        raw = dot(normed[...], w_qkv[hg][:, lanes_of(2)]) + bias_v
        vs[pl.ds(0, rows), :] = raw.astype(BF16)
        gm[...] = dot(grow[...], w_o[lanes_of(hg), :], 1, 1).astype(BF16)
        point(4.5)

        def one_image(image):
            start = image * SLOT
            span = pl.ds(start, SLOT)
            window = pl.ds(start, KEYS)
            seen = pair_lane < lengths_ref[base + image // IMAGES, image % IMAGES]
            for pair in range(GROUP // KEYS):
                lanes = pl.ds(pair * KEYS, KEYS)
                query, grad = qs[span, lanes], gm[span, lanes]
                keys, values = two_heads(ks[window, lanes]), two_heads(vs[window, lanes])
                weight = jnp.where(seen, jnp.exp(dot(query, keys, 1, 1)), 0.0)
                probs = weight * over_heads(weight, invert)
                grad_probs = dot(grad, values, 1, 1)
                inner = over_heads(probs * grad_probs, lambda total: total)
                grad_scores = (probs * (grad_probs - inner)).astype(BF16)
                probs_low = probs.astype(BF16)
                mixed[span, pl.ds(hg * GROUP + pair * KEYS, KEYS)] = dot(probs_low, values).astype(
                    BF16
                )
                dq[span, lanes] = dot(grad_scores, keys) * SCALE
                dk[span, lanes] = dot(stacked(grad_scores), two_heads(query), 0, 0)[:SLOT]
                gproj[span, pl.ds(2 * GROUP + pair * KEYS, KEYS)] = dot(
                    stacked(probs_low), two_heads(grad), 0, 0
                )[:SLOT].astype(BF16)

        for image in range(images):
            one_image(image)
            if image % 4 == 3:
                point(2.6)
        if hg == groups - 1:
            for part in range(groups):
                flip(mixed, turned, part)
            if wired:
                index = net.open()
                for lane, size, part_axes in ((0, KEYS, XY), (KEYS, 2 * KEYS, YX)):
                    sums = dot(turned[...], grow[:, pl.ds(2 * lane, 2 * size)])
                    net.put(index, sums, lane, part_axes)
                    cost(1.1)
                    net.start(index, chunks + groups, part_axes, lane, size)
                point(0.0)
            else:
                parking.put(dot(turned[...], grow[...]), chunks + groups)

        axes = (XY, YX, YX)[hg]
        last = hg == groups - 1
        index = net.open() if wired else None
        parts = {}

        def part_grad(t, part_axes):
            sums = dot(flipped[...], gproj[:, lanes_of(t)])
            small_ref[pl.ds(4 + hg, 1), lanes_of(t)] = sums[width : width + 1]
            if wired:
                net.put(index, sums[:width], t * KEYS, part_axes)
                if last:
                    net.start(index, chunks + hg, part_axes, t * KEYS, KEYS)
            else:
                parts[t] = sums[:width]

        def norm_back(side, grad_ref, unit_ref, inverse_ref, gain):
            grad, unit = grad_ref[...], unit_ref[...]
            gain_sum = jnp.sum(grad * unit, axis=0, keepdims=True)
            small_ref[pl.ds(3 + side, 1), pl.ds(width, GROUP)] += gain_sum
            grad = grad * gain
            back = grad - head_mean(grad, False) - unit * head_mean(grad * unit, False)
            gproj[:, lanes_of(side)] = (back * inverse_ref[...]).astype(BF16)

        cost(0.7)
        part_grad(2, ZX if last else axes)
        norm_back(0, dq, nq, rq, q_gain)
        cost(1.5)
        if last:
            point(0.0)
        part_grad(0, XY if last else axes)
        norm_back(1, dk, nk, rk, k_gain)
        cost(1.5)
        if last:
            point(0.0)
        part_grad(1, YX if last else axes)
        if not wired:
            parking.put(jnp.concatenate([parts[t] for t in range(3)], axis=1), chunks + hg)
        elif not last:
            net.start(index, chunks + hg, axes, 0, width // 2)
        point(0.0)

    add_gnorm(gpre_odd, w_in[chunks - 1], False)
    point(1.7)
    for hg in range(groups):
        add_gnorm(gprojs[hg], w_qkv[hg], False)
        if hg == 0:
            load("tok again", tokens_hbm, hid_even)
        if hg == 1:
            load("cot again", cot_hbm, gpre_even)
        point(1.7)
    ln_gain = ln_gain_ref[...].reshape(1, width)
    b_o = b_o_ref[...].reshape(1, width)
    gain_grad = jnp.zeros((1, width), F32)
    for s in range(seqs):
        span = pl.ds(s * SEQ, SEQ)
        unit, inverse = row_stats(packed[span, :].astype(F32))
        grad = gnorm[span, :]
        gain_grad = gain_grad + jnp.sum(grad * unit, axis=0, keepdims=True)
        grad = grad * ln_gain
        back = grad - jnp.mean(grad, axis=1, keepdims=True)
        back = (back - unit * jnp.mean(grad * unit, axis=1, keepdims=True)) * inverse
        normed[span, :] = (grow[span, :].astype(F32) + back).astype(BF16)
    for t in range(width // GROUP):
        small_ref[pl.ds(t, 1), pl.ds(width, GROUP)] = gain_grad[:, t * GROUP : (t + 1) * GROUP]
    if wired:
        net.start_small()
    point(1.5)
    finals = []
    loads["tok again"].wait()
    loads["cot again"].wait()

    def hand_over(source, target):
        copy = pltpu.make_async_copy(source, target, done_sem.at[len(finals)])
        copy.start()
        finals.append(copy)

    for s in range(seqs):
        span = pl.ds(s * SEQ, SEQ)
        place = position_slots([lengths_ref[base + s, j] for j in range(IMAGES)])
        put = one_hot(place)
        padding = jnp.where(place < 0, 1.0, 0.0)
        attended = (dot(mixed[span, :], w_o[...]) + b_o).astype(BF16).astype(F32)
        result = packed[span, :].astype(F32) + (attended + hid_odd[span, :].astype(F32))
        result = dot(put, result.astype(BF16)) + padding * hid_even[span, :].astype(F32)
        hid_even[span, :] = result.astype(BF16)
        hand_over(hid_even.at[span], output_hbm.at[span])
        point(1.2)
        grads = dot(put, normed[span, :]) + padding * gpre_even[span, :].astype(F32)
        gpre_even[span, :] = grads.astype(BF16)
        hand_over(gpre_even.at[span], grad_tokens_hbm.at[span])
        point(0.8)
    if wired:
        net.drain()
        hand_over(net.fin, pieces_hbm)
    else:
        parking.finish()
    hand_over(small_ref, small_hbm)
    for copy in finals:
        copy.wait()


def split_lanes(block, groups):
    width = block.shape[1] // 3
    return jnp.concatenate(
        [
            block[:, hg * width + t * GROUP : hg * width + (t + 1) * GROUP]
            for t in range(3)
            for hg in range(groups)
        ],
        axis=1,
    )


def fold_heads(gains):
    return sum(gains[:, h * HEAD : (h + 1) * HEAD] for h in range(GROUP // HEAD))


def small_parts(small, chunks, groups, width):
    b_in = jnp.concatenate([small[f : f + 1, :width] for f in range(chunks)], axis=1)
    b_qkv = jnp.concatenate([small[4 + hg : 5 + hg, :width] for hg in range(groups)], axis=1)
    ln = jnp.concatenate([small[t : t + 1, width:] for t in range(width // GROUP)], axis=1)
    gains = [fold_heads(small[3 + side : 4 + side, width:]) for side in range(2)]
    return ln, split_lanes(b_qkv, groups), gains[0], gains[1], small[7:8, :width], b_in


def finish_kernel(
    rows_hbm, grads_hbm, fin_hbm, small_hbm, output_hbm, grad_tokens_hbm, g_ln, g_qkv_hbm, g_b_qkv,
    g_q, g_k, g_o_hbm, g_b_o, g_in_hbm, g_b_in, g_out_hbm, g_b_out, held, fin, small, g_qkv, g_o, g_in,
    g_out, sem,
):
    comes = [
        pltpu.make_async_copy(source, target, sem.at[0, i])
        for i, (source, target) in enumerate(
            ((fin_hbm, fin), (small_hbm, small), (rows_hbm, held.at[0]), (grads_hbm, held.at[1]))
        )
    ]
    goes = [
        pltpu.make_async_copy(source, target, sem.at[1, i])
        for i, (source, target) in enumerate(
            (
                (held.at[0], output_hbm), (held.at[1], grad_tokens_hbm), (g_in, g_in_hbm),
                (g_qkv, g_qkv_hbm), (g_out, g_out_hbm), (g_o, g_o_hbm),
            )
        )
    ]
    for copy in comes:
        copy.start()
    width = g_o.shape[1]
    chunks, groups = g_in.shape[1] // width, width // GROUP

    def whole(shard, lane, size):
        return jnp.concatenate(
            [fin[side, shard, :, lane : lane + size].astype(F32) for side in range(2)], axis=1
        )

    comes[0].wait()
    for f in range(chunks):
        g_in[:, f * width : (f + 1) * width] = whole(f, 0, width // 2)
    goes[2].start()
    for hg in range(groups):
        for t in range(3):
            place = t * width + hg * GROUP
            g_qkv[:, place : place + GROUP] = whole(chunks + hg, t * KEYS, KEYS)
    goes[3].start()
    for i in range(2):
        comes[2 + i].wait()
        goes[i].start()
    for j in range(4):
        g_out[j * BLOCK : (j + 1) * BLOCK, :] = whole(chunks + groups + 1 + j, 0, width // 2)
    goes[4].start()
    g_o[:, :GROUP] = whole(chunks + groups, 0, KEYS)
    g_o[:, GROUP:] = whole(chunks + groups, KEYS, 2 * KEYS)
    goes[5].start()
    comes[1].wait()
    ln, b_qkv, q, k, b_out, b_in = small_parts(small[...], chunks, groups, width)
    for ref, value in (
        (g_ln, ln), (g_b_qkv, b_qkv), (g_q, q), (g_k, k), (g_b_o, b_out), (g_b_in, b_in), (g_b_out, b_out)
    ):
        ref[...] = value.reshape(value.shape[1])
    for copy in goes:
        copy.wait()


def local(n_dp, tokens, lengths, cotangent, ln_gain, w_qkv, b_qkv, q_gain, k_gain, w_o, b_o, w_in, b_in, w_out, b_out):
    rows, width = tokens.shape
    hidden_width = w_in.shape[1]
    chunks = hidden_width // width
    groups = width // GROUP
    seqs = rows // SEQ
    shards = chunks + groups + 1
    everyone = shards + chunks
    wired = n_dp * BLOCK == width and n_dp == 4 * chunks
    half = width // 2
    extra = KEYS - SLOT
    anywhere = pl.BlockSpec(memory_space=pl.ANY)
    vmem = pl.BlockSpec(memory_space=pltpu.VMEM)
    smem = pl.BlockSpec(memory_space=pltpu.SMEM)
    wide = lambda *shape: pltpu.VMEM(shape, F32)
    slim = lambda *shape: pltpu.VMEM(shape, BF16)
    flags = lambda *shape: pltpu.SemaphoreType.DMA(shape)
    low = lambda *shape: jax.ShapeDtypeStruct(shape, BF16)
    full = lambda *shape: jax.ShapeDtypeStruct(shape, F32)
    small_shape = (8, width + GROUP)

    if wired:
        out_piece = low(2, shards + 4, BLOCK, half)
        flights = 6 * (shards + 3) + 3 * chunks + 3 + 5
        others = [
            slim(SLOTS, 2, 16, BLOCK, half), slim(RING, 16, BLOCK, half),
            slim(everyone, 8, BLOCK, half), slim(everyone, 4, BLOCK, half),
            slim(shards, 2, BLOCK, half), slim(shards, 1, BLOCK, half), slim(4, 4, BLOCK, half),
            slim(2, 4, BLOCK, half), slim(1, 4, BLOCK, half), slim(2, shards + 4, BLOCK, half),
            wide(5, *small_shape), flags(flights), flags(flights),
        ]
        settings = dict(collective_id=0, has_side_effects=True)
    else:
        out_piece = low(everyone, width, width)
        others = [slim(2, width, width), flags(2)]
        settings = {}
    output, grad_tokens, pieces, small = pl.pallas_call(
        functools.partial(layer_kernel, wired),
        out_shape=(low(rows, width), low(rows, width), out_piece, full(*small_shape)),
        in_specs=[
            smem, anywhere, anywhere, vmem, anywhere, vmem, vmem, vmem, anywhere, vmem, anywhere,
            vmem, anywhere, vmem,
        ],
        out_specs=(anywhere,) * 4,
        scratch_shapes=[slim(6, width, width)]
        + [slim(rows, width)] * 9
        + [
            slim(width + 16, rows), slim(width, rows), wide(rows, width), wide(rows, width),
            slim(rows, GROUP), slim(rows + extra, GROUP), slim(rows + extra, GROUP),
            slim(rows, GROUP),
        ]
        + [wide(rows, GROUP)] * 3
        + [wide(*small_shape), flags(5 + 2 * chunks + 3 * groups), flags(2 * seqs + 2)]
        + others,
        compiler_params=pltpu.CompilerParams(vmem_limit_bytes=62 << 20, **settings),
    )(
        lengths, tokens, cotangent, ln_gain, w_qkv, b_qkv, q_gain, k_gain, w_o, b_o, w_in, b_in,
        w_out, b_out,
    )

    if wired:
        return pl.pallas_call(
            finish_kernel,
            out_shape=(
                low(rows, width), low(rows, width), full(width), full(BLOCK, 3 * width),
                full(3 * width), full(HEAD), full(HEAD), full(BLOCK, width), full(width),
                full(BLOCK, hidden_width), full(hidden_width), full(4 * BLOCK, width), full(width),
            ),
            in_specs=[anywhere] * 4,
            out_specs=(
                anywhere, anywhere, vmem, anywhere, vmem, vmem, vmem, anywhere, vmem, anywhere, vmem,
                anywhere, vmem,
            ),
            scratch_shapes=[
                slim(2, rows, width), slim(2, shards + 4, BLOCK, half), wide(*small_shape),
                wide(BLOCK, 3 * width), wide(BLOCK, width), wide(BLOCK, hidden_width),
                wide(4 * BLOCK, width), flags(2, 6),
            ],
        )(output, grad_tokens, pieces, small)

    def scatter(block, dim):
        part = lax.psum_scatter(block, "dp", scatter_dimension=dim, tiled=True)
        return lax.psum(part, "branch").astype(F32)

    grad_out = scatter(pieces[shards:].reshape(hidden_width, width), 0)
    reduced = scatter(pieces[:shards], 1)
    grad_in = jnp.concatenate([reduced[f] for f in range(chunks)], axis=1)
    qkv = jnp.concatenate([reduced[chunks + hg] for hg in range(groups)], axis=1)
    small = lax.psum(small, ("dp", "branch"))
    ln, g_b_qkv, g_q, g_k, g_b_out, g_b_in = (
        part[0] for part in small_parts(small, chunks, groups, width)
    )
    return (
        output, grad_tokens, ln, split_lanes(qkv, groups), g_b_qkv, g_q, g_k,
        reduced[chunks + groups], g_b_out, grad_in, g_b_in, grad_out, g_b_out,
    )


def solution(mesh):
    rows, split, whole = P(("dp", "branch"), None), P("dp", None), P()
    return jax.shard_map(
        functools.partial(local, mesh.shape["dp"]),
        mesh=mesh,
        in_specs=(rows, split, rows) + (whole,) * 11,
        out_specs=(
            rows, rows, whole, split, whole, whole, whole, split, whole, split, whole, split, whole,
        ),
        check_vma=False,
    )
```

```python
import functools
import math

import jax
import jax.numpy as jnp
from jax import lax
from jax.experimental import pallas as pl
from jax.experimental.pallas import tpu as pltpu
from jax.sharding import PartitionSpec as P

HEAD = 64
SEQ = 448
IMAGES = 4
SLOT = SEQ // IMAGES
KEYS = 128
GROUP = 256
EPS = 1e-06
SCALE = 0.125
F32 = jnp.float32
BF16 = jnp.bfloat16
GELU_A = math.sqrt(2.0 / math.pi)
GELU_B = 0.044715


def dot(left, right, left_dim=1, right_dim=0):
    return lax.dot_general(
        left, right, (((left_dim,), (right_dim,)), ((), ())), preferred_element_type=F32
    )


def slot_positions(lens):
    row = lax.broadcasted_iota(jnp.int32, (SEQ, 1), 0)
    held = jnp.full((SEQ, 1), -1, jnp.int32)
    start = jnp.int32(0)
    for image in range(IMAGES):
        place = row - SLOT * image
        held = jnp.where((place >= 0) & (place < lens[image]), place + start, held)
        start = start + lens[image]
    return held


def position_slots(lens):
    row = lax.broadcasted_iota(jnp.int32, (SEQ, 1), 0)
    held = jnp.full((SEQ, 1), -1, jnp.int32)
    start = jnp.int32(0)
    for image in range(IMAGES):
        place = row - start
        held = jnp.where((place >= 0) & (place < lens[image]), place + SLOT * image, held)
        start = start + lens[image]
    return held


def one_hot(index):
    lanes = lax.broadcasted_iota(jnp.int32, (SEQ, SEQ), 1)
    return jnp.where(lanes == index, 1.0, 0.0).astype(BF16)


def row_stats(values):
    centered = values - jnp.mean(values, axis=1, keepdims=True)
    spread = jnp.mean(centered * centered, axis=1, keepdims=True)
    inverse = lax.rsqrt(spread + EPS)
    return centered * inverse, inverse


def gelu_pair(pre, grad):
    square = pre * pre
    up = 0.5 * jnp.tanh(pre * (GELU_A + (GELU_A * GELU_B) * square)) + 0.5
    hidden = pre * up
    slope = 2.0 * GELU_A + (6.0 * GELU_A * GELU_B) * square
    return hidden, (up + (hidden * (1.0 - up)) * slope) * grad


MESH = pl.DeviceIdType.MESH
BLOCK = 48
SLOTS = 2
RING = 8
XY, YX = ("x", "y", "z0", "z1"), ("y", "x", "z0", "z1")
ZX, ZY = ("z0", "z1", "x", "y"), ("z0", "z1", "y", "x")
RATES = {"core": 400e3, "x": 42e3, "y": 42e3, "z0": 42e3, "z1": 21e3}
LATENCY = 2.0


class Piece:
    def __init__(self, index, shard, axes, lanes):
        self.index, self.shard, self.axes, self.lanes = index, shard, axes, lanes
        self.stage, self.copy, self.eta = 0, None, 0.0

    def cut(self, ref):
        return ref.at[:, :, self.lanes]


class Small:
    def __init__(self):
        self.stage, self.copy, self.eta = 0, None, 0.0


class Exchange:
    def __init__(self, refs, chunks):
        (self.both, self.inbox, self.in1, self.in2, self.in3, self.in4, self.osum, self.oin3,
         self.oin4, self.fin, self.small, self.small_in, self.send_sem, self.recv_sem) = refs
        self.chunks = chunks
        self.dp, self.core = lax.axis_index("dp"), lax.axis_index("branch")
        self.bits = {
            "x": lax.rem(self.dp, 2),
            "y": lax.rem(self.dp // 2, 2),
            "z0": lax.rem(self.dp // 4, 2),
            "z1": lax.rem(self.dp // 8, 2),
        }
        self.far = {
            axis: (self.dp + step - 2 * step * self.bits[axis], self.core)
            for axis, step in (("x", 1), ("y", 2), ("z0", 4), ("z1", 8))
        }
        self.far["core"] = (self.dp, 1 - self.core)
        self.items, self.opened = [], 0
        self.flights, self.merged, self.now, self.free = 0, 0, 0.0, {}

    def greet(self):
        barrier = pltpu.get_barrier_semaphore()
        for device in self.far.values():
            pl.semaphore_signal(barrier, inc=1, device_id=device, device_id_type=MESH)
        pl.semaphore_wait(barrier, len(self.far))

    def send(self, item, source, target, axis):
        copy = pltpu.make_async_remote_copy(
            src_ref=source, dst_ref=target, send_sem=self.send_sem.at[self.flights],
            recv_sem=self.recv_sem.at[self.flights], device_id=self.far[axis], device_id_type=MESH,
        )
        self.flights += 1
        copy.start()
        link = axis[0]
        size = source.dtype.itemsize * math.prod(source.shape)
        self.free[link] = max(self.free.get(link, 0.0), self.now) + size / RATES[axis]
        item.copy, item.eta = copy, self.free[link] + LATENCY

    def open(self):
        index = self.opened
        for behind, stage in ((SLOTS, 1), (RING - SLOTS, 2)):
            while any(
                item.index == index - behind and item.stage < stage
                for item in self.items
                if isinstance(item, Piece)
            ):
                self.advance(min(self.under_way(), key=lambda item: item.eta))
        self.opened += 1
        return index

    def put(self, index, value, lane, axes):
        half = value.shape[1] // 2
        for side, role in ((0, self.core), (1, 1 - self.core)):
            target = self.both.at[index % SLOTS, role, :, :, pl.ds(lane, half)]
            put_blocks(value, target, side, axes)

    def start(self, index, shard, axes, lane, width):
        piece = Piece(index, shard, axes, pl.ds(lane, width))
        self.send(
            piece, piece.cut(self.both.at[index % SLOTS, 1]), piece.cut(self.inbox.at[index % RING]),
            "core",
        )
        self.items.append(piece)

    def halve(self, piece, held, held_at, arrived, count, axis, target):
        near = self.bits[axis] * count
        away = (1 - self.bits[axis]) * count
        span = pl.ds(away, count)
        arrived[span] = arrived[span] + held[pl.ds(held_at + away, count)]
        self.send(piece, arrived.at[span], target, axis)
        span = pl.ds(near, count)
        arrived[span] = arrived[span] + held[pl.ds(held_at + near, count)]

    def advance(self, piece):
        piece.copy.wait()
        self.now = max(self.now, piece.eta)
        piece.copy = None
        if isinstance(piece, Small):
            self.advance_small(piece)
            return
        k, shard, axes, cut = piece.index, piece.shard, piece.axes, piece.cut
        whole = isinstance(shard, int)
        in0, in1, in2 = cut(self.inbox.at[k % RING]), cut(self.in1.at[k]), cut(self.in2.at[k])
        if whole:
            in3, in4 = cut(self.in3.at[shard]), cut(self.in4.at[shard])
        if piece.stage == 0:
            self.halve(piece, cut(self.both.at[k % SLOTS, 0]), 0, in0, 8, axes[0], in1)
        elif piece.stage == 1:
            self.halve(piece, in0, self.bits[axes[0]] * 8, in1, 4, axes[1], in2)
        elif piece.stage == 2 and whole:
            self.halve(piece, in1, self.bits[axes[1]] * 4, in2, 2, axes[2], in3)
        elif piece.stage == 2:
            place = shard[0] % 2 * 2 + shard[0] // 2
            self.osum[place] = in2[...] + in1[pl.ds(self.bits[axes[1]] * 4, 4)]
            self.merged += 1
            if self.merged < self.chunks:
                piece.stage = 5
            else:
                far = pl.ds((1 - self.bits["z0"]) * 2, 2)
                self.send(piece, self.osum.at[far], self.oin3, "z0")
        elif piece.stage == 3 and whole:
            self.halve(piece, in2, self.bits[axes[2]] * 2, in3, 1, axes[3], in4)
        elif piece.stage == 3:
            self.halve(piece, self.osum, self.bits["z0"] * 2, self.oin3, 1, "z1", self.oin4)
        elif piece.stage == 4:
            if whole:
                final = self.fin.at[self.core, pl.ds(shard, 1), :, piece.lanes]
                final[...] = in4[...] + in3[pl.ds(self.bits[axes[3]], 1)]
            else:
                final = self.fin.at[self.core, pl.ds(self.fin.shape[1] - 4, 4)]
                final[...] = self.oin4[0] + self.oin3[self.bits["z1"]]
            self.send(piece, final, final, "core")
        piece.stage += 1

    def start_small(self):
        item = Small()
        self.send(item, self.small, self.small_in.at[0], "core")
        self.items.append(item)

    def advance_small(self, item):
        self.small[...] = self.small[...] + self.small_in[item.stage]
        item.stage += 1
        if item.stage < 5:
            axis = ("core", "x", "y", "z0", "z1")[item.stage]
            self.send(item, self.small, self.small_in.at[item.stage], axis)

    def under_way(self):
        return [item for item in self.items if item.copy is not None]

    def progress(self, cost):
        self.now += cost
        while True:
            due = [item for item in self.under_way() if item.eta <= self.now]
            if not due:
                return
            self.advance(min(due, key=lambda item: item.eta))

    def drain(self):
        while self.under_way():
            self.advance(min(self.under_way(), key=lambda item: item.eta))


def put_blocks(value, target, side, axes):
    half = value.shape[1] // 2
    for block in range(16):
        place = block
        if axes is not None and len(axes) == 4:
            bit = dict(x=block % 2, y=block // 2 % 2, z0=block // 4 % 2, z1=block // 8)
            place = sum(bit[axis] << (3 - i) for i, axis in enumerate(axes))
        target[place] = value[
            BLOCK * block : BLOCK * (block + 1), half * side : half * (side + 1)
        ].astype(BF16)


def make_flip():
    eye = jnp.where(
        lax.broadcasted_iota(jnp.int32, (GROUP, GROUP), 0)
        == lax.broadcasted_iota(jnp.int32, (GROUP, GROUP), 1),
        1.0,
        0.0,
    ).astype(BF16)

    def flip(source, target):
        for part in range(source.shape[1] // GROUP):
            lanes = pl.ds(part * GROUP, GROUP)
            target[lanes, :] = dot(eye, source[:, lanes], 1, 1).astype(BF16)

    return flip


class Parking:
    def __init__(self, stage, target, sem):
        self.stage, self.target, self.sem = stage, target, sem
        self.sent = []

    def put(self, value, index):
        slot = len(self.sent) % 2
        if len(self.sent) >= 2:
            self.sent[-2].wait()
        self.stage[slot] = value.astype(BF16)
        copy = pltpu.make_async_copy(self.stage.at[slot], self.target.at[index], self.sem.at[slot])
        copy.start()
        self.sent.append(copy)

    def finish(self):
        for copy in self.sent[-2:]:
            copy.wait()


def layer_kernel(
    wired,
    lengths_ref, tokens_hbm, cot_hbm, ln_gain_ref, w_qkv_hbm, b_qkv_ref, q_gain_ref, k_gain_ref,
    w_o_hbm, b_o_ref, w_in_hbm, b_in_ref, w_out_hbm, b_out_ref,
    output_hbm, grad_tokens_hbm, pieces_hbm, small_hbm,
    weights, tok, cot, packed, grow, normed, hid_even, gpre_even, hid_odd, gpre_odd,
    flipped, turned, fed, gnorm, qs, ks, vs, gm, rk, dq, dk, small_ref,
    load_sem, done_sem, *refs,
):
    rows, width = tok.shape
    hidden_width = w_in_hbm.shape[1]
    chunks = hidden_width // width
    groups = width // GROUP
    seqs = rows // SEQ
    images = seqs * IMAGES
    base = lax.axis_index("branch") * seqs
    assert chunks == 4 and groups == 3
    hid, gpre = (hid_even, hid_odd), (gpre_even, gpre_odd)
    mixed, gprojs = tok, (hid_even, gpre_even, cot)
    w_in = [weights.at[f % 3] for f in range(chunks)]
    w_out = [weights.at[3 + f % 3] for f in range(chunks)]
    w_qkv, w_o = [weights.at[1], weights.at[4], weights.at[2]], weights.at[5]
    nq, rq, nk = (fed.at[:, pl.ds(part * GROUP, GROUP)] for part in range(3))
    loads = {}

    def load(name, source, target):
        copy = pltpu.make_async_copy(source, target, load_sem.at[len(loads)])
        copy.start()
        loads[name] = copy

    def load_chunk(f):
        cols = pl.ds(f * width, width)
        load(("in", f), w_in_hbm.at[:, cols], w_in[f])
        load(("out", f), w_out_hbm.at[cols, :], w_out[f])

    def load_qkv(hg):
        for t in range(3):
            load(
                ("qkv", hg, t),
                w_qkv_hbm.at[:, pl.ds(t * width + hg * GROUP, GROUP)],
                w_qkv[hg].at[:, pl.ds(t * GROUP, GROUP)],
            )

    load("tok", tokens_hbm, tok)
    load("cot", cot_hbm, cot)
    for f in range(3):
        load_chunk(f)
    small_ref[...] = jnp.zeros_like(small_ref)
    net, parking = None, None
    if wired:
        net = Exchange(refs[:10] + (small_ref,) + refs[10:], chunks)
        net.greet()
    else:
        parking = Parking(refs[0], pieces_hbm, refs[1])

    def emit(value, shard, axes):
        if wired:
            index = net.open()
            net.put(index, value, 0, axes)
            net.start(index, shard, axes, 0, width // 2)
        else:
            parking.put(value, shard if isinstance(shard, int) else chunks + groups + 1 + shard[0])

    def point(cost):
        if wired:
            net.progress(cost)

    def cost(amount):
        if wired:
            net.now += amount

    def lanes_of(part):
        return pl.ds(part * GROUP, GROUP)

    ones_row = jnp.where(lax.broadcasted_iota(jnp.int32, (16, rows), 0) == 0, 1.0, 0.0)
    flipped[pl.ds(width, 16), :] = ones_row.astype(BF16)
    eye = jnp.where(
        lax.broadcasted_iota(jnp.int32, (GROUP, GROUP), 0)
        == lax.broadcasted_iota(jnp.int32, (GROUP, GROUP), 1),
        1.0,
        0.0,
    ).astype(BF16)

    def flip(source, target, part):
        target[lanes_of(part), :] = dot(eye, source[:, lanes_of(part)], 1, 1).astype(BF16)

    for name in ("tok", "cot", ("in", 0), ("out", 0)):
        loads[name].wait()
    grad_sum = jnp.zeros((1, width), F32)
    for s in range(seqs):
        span = pl.ds(s * SEQ, SEQ)
        pick = one_hot(slot_positions([lengths_ref[base + s, j] for j in range(IMAGES)]))
        rows_here = dot(pick, tok[span, :])
        packed[span, :] = rows_here.astype(BF16)
        unit, _ = row_stats(rows_here)
        normed[span, :] = (unit * ln_gain_ref[...].reshape(1, width)).astype(BF16)
        grads_here = dot(pick, cot[span, :])
        grow[span, :] = grads_here.astype(BF16)
        grad_sum = grad_sum + jnp.sum(grads_here, axis=0, keepdims=True)
    small_ref[pl.ds(7, 1), pl.ds(0, width)] = grad_sum
    for part in range(groups):
        flip(normed, flipped, part)
    cost(6.0)

    def add_fed(f):
        up = dot(hid[f % 2][...], w_out[f][...])
        fed[...] = up if f == 0 else fed[...] + up

    def add_gnorm(source, target, first):
        down = dot(source[...], target[...], 1, 1)
        gnorm[...] = down if first else gnorm[...] + down

    b_in = b_in_ref[...].reshape(1, hidden_width)
    ready = None

    def activate():
        f, span, pre, back = ready
        hidden, grad_pre = gelu_pair(pre, back)
        hid[f % 2][span, :] = hidden.astype(BF16)
        gpre[f % 2][span, :] = grad_pre.astype(BF16)

    def send_w_in(f):
        sums = dot(flipped[...], gpre[f % 2][...])
        cost(2.2)
        emit(sums[:width], f, XY)
        small_ref[pl.ds(f, 1), pl.ds(0, width)] = sums[width : width + 1]
        point(0.0)

    def send_w_out(f):
        cost(1.9)
        emit(dot(turned[...], grow[...]), (f,), YX[:2])
        point(0.0)

    for f in range(chunks):
        if f > 0:
            loads["in", f].wait()
            loads["out", f].wait()
        for half in range(2):
            span = pl.ds(half * (rows // 2), rows // 2)
            pre = dot(normed[span, :], w_in[f][...]) + b_in[:, f * width : (f + 1) * width]
            back = dot(grow[span, :], w_out[f][...], 1, 1)
            if ready is not None:
                activate()
            ready = (f, span, pre, back)
            if f > 0 and half == 0:
                for part in range(groups):
                    flip(hid[1 - f % 2], turned, part)
            point(2.3 if f > 0 and half == 0 else 1.7)
            if f > 0 and half == 0:
                send_w_in(f - 1)
            if f > 0 and half == 1:
                send_w_out(f - 1)
                add_fed(f - 1)
                add_gnorm(gpre[1 - f % 2], w_in[f - 1], f == 1)
                point(3.4)
        if f == 1:
            load_chunk(3)
        if f == 2:
            load_qkv(0)
            load_qkv(1)
        if f == 3:
            load_qkv(2)
            load("wo", w_o_hbm, w_o)
    activate()
    for part in range(groups):
        flip(hid_odd, turned, part)
    send_w_in(chunks - 1)
    send_w_out(chunks - 1)

    add_fed(chunks - 1)
    hid_odd[...] = (fed[...] + b_out_ref[...].reshape(1, width)).astype(BF16)
    point(1.9)

    same_head = (
        lax.broadcasted_iota(jnp.int32, (GROUP, GROUP), 0) // HEAD
        == lax.broadcasted_iota(jnp.int32, (GROUP, GROUP), 1) // HEAD
    )
    average = jnp.where(same_head, 1.0 / HEAD, 0.0).astype(BF16)
    q_gain = jnp.concatenate([q_gain_ref[...].reshape(1, HEAD)] * (GROUP // HEAD), axis=1)
    k_gain = jnp.concatenate([k_gain_ref[...].reshape(1, HEAD)] * (GROUP // HEAD), axis=1)
    b_qkv = b_qkv_ref[...].reshape(1, 3 * width)
    lane = lax.broadcasted_iota(jnp.int32, (1, KEYS), 1)
    pair_lane = jnp.concatenate([lane, lane], axis=1)
    first_head = jnp.where(lane < HEAD, 1.0, 0.0).astype(BF16)
    second_head = jnp.where(lane < HEAD, 0.0, 1.0).astype(BF16)

    def head_mean(values, split):
        high = values.astype(BF16)
        mean = dot(high, average)
        if split:
            mean = mean + dot((values - high.astype(F32)).astype(BF16), average)
        return mean

    def head_norm(raw):
        centered = raw - head_mean(raw, True)
        inverse = lax.rsqrt(head_mean(centered * centered, False) + EPS)
        return centered * inverse, inverse

    def two_heads(block):
        return jnp.concatenate([block * first_head, block * second_head], axis=0)

    def stacked(block):
        return jnp.concatenate([block[:, :KEYS], block[:, KEYS:]], axis=0)

    def invert(total):
        guess = pl.reciprocal(total, approx=True)
        return guess * (2.0 - total * guess)

    def over_heads(block, change):
        parts = []
        for head in range(2):
            part = block[:, head * KEYS : (head + 1) * KEYS]
            total = change(jnp.sum(part, axis=1, keepdims=True))
            parts.append(jnp.broadcast_to(total, part.shape))
        return jnp.concatenate(parts, axis=1)

    ks[pl.ds(rows, KEYS - SLOT), :] = jnp.zeros((KEYS - SLOT, GROUP), BF16)
    vs[pl.ds(rows, KEYS - SLOT), :] = jnp.zeros((KEYS - SLOT, GROUP), BF16)

    for hg in range(groups):
        gproj = gprojs[hg]
        bias_q, bias_k, bias_v = (
            b_qkv[:, t * width + hg * GROUP : t * width + (hg + 1) * GROUP] for t in range(3)
        )
        for t in range(3):
            loads["qkv", hg, t].wait()
        if hg == 0:
            loads["wo"].wait()
        raw = dot(normed[...], w_qkv[hg][...])
        unit, inverse = head_norm(raw[:, :GROUP] + bias_q)
        nq[...] = unit
        rq[...] = inverse
        qs[...] = (unit * q_gain).astype(BF16) * SCALE
        unit, inverse = head_norm(raw[:, GROUP : 2 * GROUP] + bias_k)
        nk[...] = unit
        rk[...] = inverse
        ks[pl.ds(0, rows), :] = (unit * k_gain).astype(BF16)
        vs[pl.ds(0, rows), :] = (raw[:, 2 * GROUP :] + bias_v).astype(BF16)
        gm[...] = dot(grow[...], w_o[lanes_of(hg), :], 1, 1).astype(BF16)
        point(4.5)

        def one_image(image):
            start = image * SLOT
            span = pl.ds(start, SLOT)
            window = pl.ds(start, KEYS)
            seen = pair_lane < lengths_ref[base + image // IMAGES, image % IMAGES]
            for pair in range(GROUP // KEYS):
                lanes = pl.ds(pair * KEYS, KEYS)
                query, grad = qs[span, lanes], gm[span, lanes]
                keys, values = two_heads(ks[window, lanes]), two_heads(vs[window, lanes])
                weight = jnp.where(seen, jnp.exp(dot(query, keys, 1, 1)), 0.0)
                probs = weight * over_heads(weight, invert)
                grad_probs = dot(grad, values, 1, 1)
                inner = over_heads(probs * grad_probs, lambda total: total)
                grad_scores = (probs * (grad_probs - inner)).astype(BF16)
                probs_low = probs.astype(BF16)
                mixed[span, pl.ds(hg * GROUP + pair * KEYS, KEYS)] = dot(probs_low, values).astype(
                    BF16
                )
                dq[span, lanes] = dot(grad_scores, keys) * SCALE
                dk[span, lanes] = dot(stacked(grad_scores), two_heads(query), 0, 0)[:SLOT]
                gproj[span, pl.ds(2 * GROUP + pair * KEYS, KEYS)] = dot(
                    stacked(probs_low), two_heads(grad), 0, 0
                )[:SLOT].astype(BF16)

        for image in range(images):
            one_image(image)
            if image % 4 == 3:
                point(2.6)
        if hg == groups - 1:
            for part in range(groups):
                flip(mixed, turned, part)
            if wired:
                index = net.open()
                for lane, size, part_axes in ((0, KEYS, XY), (KEYS, 2 * KEYS, YX)):
                    sums = dot(turned[...], grow[:, pl.ds(2 * lane, 2 * size)])
                    net.put(index, sums, lane, part_axes)
                    cost(1.1)
                    net.start(index, chunks + groups, part_axes, lane, size)
                point(0.0)
            else:
                parking.put(dot(turned[...], grow[...]), chunks + groups)

        axes = (XY, YX, YX)[hg]
        last = hg == groups - 1
        index = net.open() if wired else None
        parts = {}

        def part_grad(t, part_axes):
            sums = dot(flipped[...], gproj[:, lanes_of(t)])
            small_ref[pl.ds(4 + hg, 1), lanes_of(t)] = sums[width : width + 1]
            if wired:
                net.put(index, sums[:width], t * KEYS, part_axes)
                if last:
                    net.start(index, chunks + hg, part_axes, t * KEYS, KEYS)
            else:
                parts[t] = sums[:width]

        def norm_back(side, grad_ref, unit_ref, inverse_ref, gain):
            grad, unit = grad_ref[...], unit_ref[...]
            gain_sum = jnp.sum(grad * unit, axis=0, keepdims=True)
            small_ref[pl.ds(3 + side, 1), pl.ds(width, GROUP)] += gain_sum
            grad = grad * gain
            back = grad - head_mean(grad, False) - unit * head_mean(grad * unit, False)
            gproj[:, lanes_of(side)] = (back * inverse_ref[...]).astype(BF16)

        cost(0.7)
        part_grad(2, ZX if last else axes)
        norm_back(0, dq, nq, rq, q_gain)
        cost(1.5)
        if last:
            point(0.0)
        part_grad(0, XY if last else axes)
        norm_back(1, dk, nk, rk, k_gain)
        cost(1.5)
        if last:
            point(0.0)
        part_grad(1, YX if last else axes)
        if not wired:
            parking.put(jnp.concatenate([parts[t] for t in range(3)], axis=1), chunks + hg)
        elif not last:
            net.start(index, chunks + hg, axes, 0, width // 2)
        point(0.0)

    add_gnorm(gpre_odd, w_in[chunks - 1], False)
    point(1.7)
    for hg in range(groups):
        add_gnorm(gprojs[hg], w_qkv[hg], False)
        if hg == 0:
            load("tok again", tokens_hbm, hid_even)
        if hg == 1:
            load("cot again", cot_hbm, gpre_even)
        point(1.7)
    ln_gain = ln_gain_ref[...].reshape(1, width)
    b_o = b_o_ref[...].reshape(1, width)
    gain_grad = jnp.zeros((1, width), F32)
    for s in range(seqs):
        span = pl.ds(s * SEQ, SEQ)
        unit, inverse = row_stats(packed[span, :].astype(F32))
        grad = gnorm[span, :]
        gain_grad = gain_grad + jnp.sum(grad * unit, axis=0, keepdims=True)
        grad = grad * ln_gain
        back = grad - jnp.mean(grad, axis=1, keepdims=True)
        back = (back - unit * jnp.mean(grad * unit, axis=1, keepdims=True)) * inverse
        normed[span, :] = (grow[span, :].astype(F32) + back).astype(BF16)
    for t in range(width // GROUP):
        small_ref[pl.ds(t, 1), pl.ds(width, GROUP)] = gain_grad[:, t * GROUP : (t + 1) * GROUP]
    if wired:
        net.start_small()
    point(1.5)
    finals = []
    loads["tok again"].wait()
    loads["cot again"].wait()

    def hand_over(source, target):
        copy = pltpu.make_async_copy(source, target, done_sem.at[len(finals)])
        copy.start()
        finals.append(copy)

    for s in range(seqs):
        span = pl.ds(s * SEQ, SEQ)
        place = position_slots([lengths_ref[base + s, j] for j in range(IMAGES)])
        put = one_hot(place)
        padding = jnp.where(place < 0, 1.0, 0.0)
        attended = (dot(mixed[span, :], w_o[...]) + b_o).astype(BF16).astype(F32)
        result = packed[span, :].astype(F32) + (attended + hid_odd[span, :].astype(F32))
        result = dot(put, result.astype(BF16)) + padding * hid_even[span, :].astype(F32)
        hid_even[span, :] = result.astype(BF16)
        hand_over(hid_even.at[span], output_hbm.at[span])
        point(1.2)
        grads = dot(put, normed[span, :]) + padding * gpre_even[span, :].astype(F32)
        gpre_even[span, :] = grads.astype(BF16)
        hand_over(gpre_even.at[span], grad_tokens_hbm.at[span])
        point(0.8)
    if wired:
        net.drain()
        hand_over(net.fin, pieces_hbm)
    else:
        parking.finish()
    hand_over(small_ref, small_hbm)
    for copy in finals:
        copy.wait()


def split_lanes(block, groups):
    width = block.shape[1] // 3
    return jnp.concatenate(
        [
            block[:, hg * width + t * GROUP : hg * width + (t + 1) * GROUP]
            for t in range(3)
            for hg in range(groups)
        ],
        axis=1,
    )


def fold_heads(gains):
    return sum(gains[:, h * HEAD : (h + 1) * HEAD] for h in range(GROUP // HEAD))


def small_parts(small, chunks, groups, width):
    b_in = jnp.concatenate([small[f : f + 1, :width] for f in range(chunks)], axis=1)
    b_qkv = jnp.concatenate([small[4 + hg : 5 + hg, :width] for hg in range(groups)], axis=1)
    ln = jnp.concatenate([small[t : t + 1, width:] for t in range(width // GROUP)], axis=1)
    gains = [fold_heads(small[3 + side : 4 + side, width:]) for side in range(2)]
    return ln, split_lanes(b_qkv, groups), gains[0], gains[1], small[7:8, :width], b_in


def finish_kernel(
    rows_hbm, grads_hbm, fin_hbm, small_hbm, output_hbm, grad_tokens_hbm, g_ln, g_qkv_hbm, g_b_qkv,
    g_q, g_k, g_o_hbm, g_b_o, g_in_hbm, g_b_in, g_out_hbm, g_b_out, held, fin, small, g_qkv, g_o, g_in,
    g_out, sem,
):
    comes = [
        pltpu.make_async_copy(source, target, sem.at[0, i])
        for i, (source, target) in enumerate(
            ((fin_hbm, fin), (small_hbm, small), (rows_hbm, held.at[0]), (grads_hbm, held.at[1]))
        )
    ]
    goes = [
        pltpu.make_async_copy(source, target, sem.at[1, i])
        for i, (source, target) in enumerate(
            (
                (held.at[0], output_hbm), (held.at[1], grad_tokens_hbm), (g_in, g_in_hbm),
                (g_qkv, g_qkv_hbm), (g_out, g_out_hbm), (g_o, g_o_hbm),
            )
        )
    ]
    for copy in comes:
        copy.start()
    width = g_o.shape[1]
    chunks, groups = g_in.shape[1] // width, width // GROUP

    def whole(shard, lane, size):
        return jnp.concatenate(
            [fin[side, shard, :, lane : lane + size].astype(F32) for side in range(2)], axis=1
        )

    comes[0].wait()
    for f in range(chunks):
        g_in[:, f * width : (f + 1) * width] = whole(f, 0, width // 2)
    goes[2].start()
    for hg in range(groups):
        for t in range(3):
            place = t * width + hg * GROUP
            g_qkv[:, place : place + GROUP] = whole(chunks + hg, t * KEYS, KEYS)
    goes[3].start()
    for i in range(2):
        comes[2 + i].wait()
        goes[i].start()
    for j in range(4):
        g_out[j * BLOCK : (j + 1) * BLOCK, :] = whole(chunks + groups + 1 + j, 0, width // 2)
    goes[4].start()
    g_o[:, :GROUP] = whole(chunks + groups, 0, KEYS)
    g_o[:, GROUP:] = whole(chunks + groups, KEYS, 2 * KEYS)
    goes[5].start()
    comes[1].wait()
    ln, b_qkv, q, k, b_out, b_in = small_parts(small[...], chunks, groups, width)
    for ref, value in (
        (g_ln, ln), (g_b_qkv, b_qkv), (g_q, q), (g_k, k), (g_b_o, b_out), (g_b_in, b_in), (g_b_out, b_out)
    ):
        ref[...] = value.reshape(value.shape[1])
    for copy in goes:
        copy.wait()


def local(n_dp, tokens, lengths, cotangent, ln_gain, w_qkv, b_qkv, q_gain, k_gain, w_o, b_o, w_in, b_in, w_out, b_out):
    rows, width = tokens.shape
    hidden_width = w_in.shape[1]
    chunks = hidden_width // width
    groups = width // GROUP
    seqs = rows // SEQ
    shards = chunks + groups + 1
    everyone = shards + chunks
    wired = n_dp * BLOCK == width and n_dp == 4 * chunks
    half = width // 2
    extra = KEYS - SLOT
    anywhere = pl.BlockSpec(memory_space=pl.ANY)
    vmem = pl.BlockSpec(memory_space=pltpu.VMEM)
    smem = pl.BlockSpec(memory_space=pltpu.SMEM)
    wide = lambda *shape: pltpu.VMEM(shape, F32)
    slim = lambda *shape: pltpu.VMEM(shape, BF16)
    flags = lambda *shape: pltpu.SemaphoreType.DMA(shape)
    low = lambda *shape: jax.ShapeDtypeStruct(shape, BF16)
    full = lambda *shape: jax.ShapeDtypeStruct(shape, F32)
    small_shape = (8, width + GROUP)

    if wired:
        out_piece = low(2, shards + 4, BLOCK, half)
        flights = 6 * (shards + 3) + 3 * chunks + 3 + 5
        others = [
            slim(SLOTS, 2, 16, BLOCK, half), slim(RING, 16, BLOCK, half),
            slim(everyone, 8, BLOCK, half), slim(everyone, 4, BLOCK, half),
            slim(shards, 2, BLOCK, half), slim(shards, 1, BLOCK, half), slim(4, 4, BLOCK, half),
            slim(2, 4, BLOCK, half), slim(1, 4, BLOCK, half), slim(2, shards + 4, BLOCK, half),
            wide(5, *small_shape), flags(flights), flags(flights),
        ]
        settings = dict(collective_id=0, has_side_effects=True)
    else:
        out_piece = low(everyone, width, width)
        others = [slim(2, width, width), flags(2)]
        settings = {}
    output, grad_tokens, pieces, small = pl.pallas_call(
        functools.partial(layer_kernel, wired),
        out_shape=(low(rows, width), low(rows, width), out_piece, full(*small_shape)),
        in_specs=[
            smem, anywhere, anywhere, vmem, anywhere, vmem, vmem, vmem, anywhere, vmem, anywhere,
            vmem, anywhere, vmem,
        ],
        out_specs=(anywhere,) * 4,
        scratch_shapes=[slim(6, width, width)]
        + [slim(rows, width)] * 9
        + [
            slim(width + 16, rows), slim(width, rows), wide(rows, width), wide(rows, width),
            slim(rows, GROUP), slim(rows + extra, GROUP), slim(rows + extra, GROUP),
            slim(rows, GROUP),
        ]
        + [wide(rows, GROUP)] * 3
        + [wide(*small_shape), flags(5 + 2 * chunks + 3 * groups), flags(2 * seqs + 2)]
        + others,
        compiler_params=pltpu.CompilerParams(vmem_limit_bytes=62 << 20, **settings),
    )(
        lengths, tokens, cotangent, ln_gain, w_qkv, b_qkv, q_gain, k_gain, w_o, b_o, w_in, b_in,
        w_out, b_out,
    )

    if wired:
        return pl.pallas_call(
            finish_kernel,
            out_shape=(
                low(rows, width), low(rows, width), full(width), full(BLOCK, 3 * width),
                full(3 * width), full(HEAD), full(HEAD), full(BLOCK, width), full(width),
                full(BLOCK, hidden_width), full(hidden_width), full(4 * BLOCK, width), full(width),
            ),
            in_specs=[anywhere] * 4,
            out_specs=(
                anywhere, anywhere, vmem, anywhere, vmem, vmem, vmem, anywhere, vmem, anywhere, vmem,
                anywhere, vmem,
            ),
            scratch_shapes=[
                slim(2, rows, width), slim(2, shards + 4, BLOCK, half), wide(*small_shape),
                wide(BLOCK, 3 * width), wide(BLOCK, width), wide(BLOCK, hidden_width),
                wide(4 * BLOCK, width), flags(2, 6),
            ],
        )(output, grad_tokens, pieces, small)

    def scatter(block, dim):
        part = lax.psum_scatter(block, "dp", scatter_dimension=dim, tiled=True)
        return lax.psum(part, "branch").astype(F32)

    grad_out = scatter(pieces[shards:].reshape(hidden_width, width), 0)
    reduced = scatter(pieces[:shards], 1)
    grad_in = jnp.concatenate([reduced[f] for f in range(chunks)], axis=1)
    qkv = jnp.concatenate([reduced[chunks + hg] for hg in range(groups)], axis=1)
    small = lax.psum(small, ("dp", "branch"))
    ln, g_b_qkv, g_q, g_k, g_b_out, g_b_in = (
        part[0] for part in small_parts(small, chunks, groups, width)
    )
    return (
        output, grad_tokens, ln, split_lanes(qkv, groups), g_b_qkv, g_q, g_k,
        reduced[chunks + groups], g_b_out, grad_in, g_b_in, grad_out, g_b_out,
    )


def solution(mesh):
    rows, split, whole = P(("dp", "branch"), None), P("dp", None), P()
    return jax.shard_map(
        functools.partial(local, mesh.shape["dp"]),
        mesh=mesh,
        in_specs=(rows, split, rows) + (whole,) * 11,
        out_specs=(
            rows, rows, whole, split, whole, whole, whole, split, whole, split, whole, split, whole,
        ),
        check_vma=False,
    )
```

```python
import functools
import math

import jax
import jax.numpy as jnp
from jax import lax
from jax.experimental import pallas as pl
from jax.experimental.pallas import tpu as pltpu
from jax.sharding import PartitionSpec as P

HEAD = 64
SEQ = 448
IMAGES = 4
SLOT = SEQ // IMAGES
KEYS = 128
GROUP = 256
EPS = 1e-06
SCALE = 0.125
F32 = jnp.float32
BF16 = jnp.bfloat16
GELU_A = math.sqrt(2.0 / math.pi)
GELU_B = 0.044715


def dot(left, right, left_dim=1, right_dim=0):
    return lax.dot_general(
        left, right, (((left_dim,), (right_dim,)), ((), ())), preferred_element_type=F32
    )


def slot_positions(lens):
    row = lax.broadcasted_iota(jnp.int32, (SEQ, 1), 0)
    held = jnp.full((SEQ, 1), -1, jnp.int32)
    start = jnp.int32(0)
    for image in range(IMAGES):
        place = row - SLOT * image
        held = jnp.where((place >= 0) & (place < lens[image]), place + start, held)
        start = start + lens[image]
    return held


def position_slots(lens):
    row = lax.broadcasted_iota(jnp.int32, (SEQ, 1), 0)
    held = jnp.full((SEQ, 1), -1, jnp.int32)
    start = jnp.int32(0)
    for image in range(IMAGES):
        place = row - start
        held = jnp.where((place >= 0) & (place < lens[image]), place + SLOT * image, held)
        start = start + lens[image]
    return held


def one_hot(index):
    lanes = lax.broadcasted_iota(jnp.int32, (SEQ, SEQ), 1)
    return jnp.where(lanes == index, 1.0, 0.0).astype(BF16)


def row_stats(values):
    centered = values - jnp.mean(values, axis=1, keepdims=True)
    spread = jnp.mean(centered * centered, axis=1, keepdims=True)
    inverse = lax.rsqrt(spread + EPS)
    return centered * inverse, inverse


def gelu_pair(pre, grad):
    square = pre * pre
    up = 0.5 * jnp.tanh(pre * (GELU_A + (GELU_A * GELU_B) * square)) + 0.5
    hidden = pre * up
    slope = 2.0 * GELU_A + (6.0 * GELU_A * GELU_B) * square
    return hidden, (up + (hidden * (1.0 - up)) * slope) * grad


MESH = pl.DeviceIdType.MESH
BLOCK = 48
SLOTS = 2
RING = 8
XY, YX = ("x", "y", "z0", "z1"), ("y", "x", "z0", "z1")
ZX, ZY = ("z0", "z1", "x", "y"), ("z0", "z1", "y", "x")
RATES = {"core": 400e3, "x": 42e3, "y": 42e3, "z0": 42e3, "z1": 21e3}
LATENCY, SMALL_LATENCY = 2.0, 1.0


class Piece:
    def __init__(self, index, shard, axes, lanes):
        self.index, self.shard, self.axes, self.lanes = index, shard, axes, lanes
        self.stage, self.copy, self.eta = 0, None, 0.0

    def cut(self, ref):
        return ref.at[:, :, self.lanes]


class Small:
    def __init__(self):
        self.stage, self.copy, self.eta = 0, None, 0.0


class Exchange:
    def __init__(self, refs, chunks):
        (self.both, self.inbox, self.in1, self.in2, self.in3, self.in4, self.osum, self.oin3,
         self.oin4, self.fin, self.small, self.small_in, self.send_sem, self.recv_sem) = refs
        self.chunks = chunks
        self.dp, self.core = lax.axis_index("dp"), lax.axis_index("branch")
        self.bits = {
            "x": lax.rem(self.dp, 2),
            "y": lax.rem(self.dp // 2, 2),
            "z0": lax.rem(self.dp // 4, 2),
            "z1": lax.rem(self.dp // 8, 2),
        }
        self.far = {
            axis: (self.dp + step - 2 * step * self.bits[axis], self.core)
            for axis, step in (("x", 1), ("y", 2), ("z0", 4), ("z1", 8))
        }
        self.far["core"] = (self.dp, 1 - self.core)
        self.items, self.opened = [], 0
        self.flights, self.merged, self.now, self.free = 0, 0, 0.0, {}

    def greet(self):
        barrier = pltpu.get_barrier_semaphore()
        for device in self.far.values():
            pl.semaphore_signal(barrier, inc=1, device_id=device, device_id_type=MESH)
        pl.semaphore_wait(barrier, len(self.far))

    def send(self, item, source, target, axis):
        copy = pltpu.make_async_remote_copy(
            src_ref=source, dst_ref=target, send_sem=self.send_sem.at[self.flights],
            recv_sem=self.recv_sem.at[self.flights], device_id=self.far[axis], device_id_type=MESH,
        )
        self.flights += 1
        copy.start()
        link = axis[0]
        size = source.dtype.itemsize * math.prod(source.shape)
        self.free[link] = max(self.free.get(link, 0.0), self.now) + size / RATES[axis]
        item.copy, item.eta = copy, self.free[link] + LATENCY
        if isinstance(item, Small):
            item.eta = self.now + SMALL_LATENCY

    def open(self):
        index = self.opened
        for behind, stage in ((SLOTS, 1), (RING - SLOTS, 2)):
            while any(
                item.index == index - behind and item.stage < stage
                for item in self.items
                if isinstance(item, Piece)
            ):
                self.advance(min(self.under_way(), key=lambda item: item.eta))
        self.opened += 1
        return index

    def put(self, index, value, lane, axes):
        half = value.shape[1] // 2
        for side, role in ((0, self.core), (1, 1 - self.core)):
            target = self.both.at[index % SLOTS, role, :, :, pl.ds(lane, half)]
            put_blocks(value, target, side, axes)

    def start(self, index, shard, axes, lane, width):
        piece = Piece(index, shard, axes, pl.ds(lane, width))
        self.send(
            piece, piece.cut(self.both.at[index % SLOTS, 1]), piece.cut(self.inbox.at[index % RING]),
            "core",
        )
        self.items.append(piece)

    def halve(self, piece, held, held_at, arrived, count, axis, target):
        near = self.bits[axis] * count
        away = (1 - self.bits[axis]) * count
        span = pl.ds(away, count)
        arrived[span] = arrived[span] + held[pl.ds(held_at + away, count)]
        self.send(piece, arrived.at[span], target, axis)
        span = pl.ds(near, count)
        arrived[span] = arrived[span] + held[pl.ds(held_at + near, count)]

    def advance(self, piece):
        piece.copy.wait()
        self.now = max(self.now, piece.eta)
        piece.copy = None
        if isinstance(piece, Small):
            self.advance_small(piece)
            return
        k, shard, axes, cut = piece.index, piece.shard, piece.axes, piece.cut
        whole = isinstance(shard, int)
        in0, in1, in2 = cut(self.inbox.at[k % RING]), cut(self.in1.at[k]), cut(self.in2.at[k])
        if whole:
            in3, in4 = cut(self.in3.at[shard]), cut(self.in4.at[shard])
        if piece.stage == 0:
            self.halve(piece, cut(self.both.at[k % SLOTS, 0]), 0, in0, 8, axes[0], in1)
        elif piece.stage == 1:
            self.halve(piece, in0, self.bits[axes[0]] * 8, in1, 4, axes[1], in2)
        elif piece.stage == 2 and whole:
            self.halve(piece, in1, self.bits[axes[1]] * 4, in2, 2, axes[2], in3)
        elif piece.stage == 2:
            place = shard[0] % 2 * 2 + shard[0] // 2
            self.osum[place] = in2[...] + in1[pl.ds(self.bits[axes[1]] * 4, 4)]
            self.merged += 1
            if self.merged < self.chunks:
                piece.stage = 5
            else:
                far = pl.ds((1 - self.bits["z0"]) * 2, 2)
                self.send(piece, self.osum.at[far], self.oin3, "z0")
        elif piece.stage == 3 and whole:
            self.halve(piece, in2, self.bits[axes[2]] * 2, in3, 1, axes[3], in4)
        elif piece.stage == 3:
            self.halve(piece, self.osum, self.bits["z0"] * 2, self.oin3, 1, "z1", self.oin4)
        elif piece.stage == 4:
            if whole:
                final = self.fin.at[self.core, pl.ds(shard, 1), :, piece.lanes]
                final[...] = in4[...] + in3[pl.ds(self.bits[axes[3]], 1)]
            else:
                final = self.fin.at[self.core, pl.ds(self.fin.shape[1] - 4, 4)]
                final[...] = self.oin4[0] + self.oin3[self.bits["z1"]]
            self.send(piece, final, final, "core")
        piece.stage += 1

    def start_small(self):
        item = Small()
        self.send(item, self.small, self.small_in.at[0], "core")
        self.items.append(item)

    def advance_small(self, item):
        self.small[...] = self.small[...] + self.small_in[item.stage]
        item.stage += 1
        if item.stage < 5:
            axis = ("core", "x", "y", "z0", "z1")[item.stage]
            self.send(item, self.small, self.small_in.at[item.stage], axis)

    def under_way(self):
        return [item for item in self.items if item.copy is not None]

    def progress(self, cost):
        self.now += cost
        while True:
            due = [item for item in self.under_way() if item.eta <= self.now]
            if not due:
                return
            self.advance(min(due, key=lambda item: item.eta))

    def drain(self):
        while self.under_way():
            self.advance(min(self.under_way(), key=lambda item: item.eta))


def put_blocks(value, target, side, axes):
    half = value.shape[1] // 2
    for block in range(16):
        place = block
        if axes is not None and len(axes) == 4:
            bit = dict(x=block % 2, y=block // 2 % 2, z0=block // 4 % 2, z1=block // 8)
            place = sum(bit[axis] << (3 - i) for i, axis in enumerate(axes))
        target[place] = value[
            BLOCK * block : BLOCK * (block + 1), half * side : half * (side + 1)
        ].astype(BF16)


def make_flip():
    eye = jnp.where(
        lax.broadcasted_iota(jnp.int32, (GROUP, GROUP), 0)
        == lax.broadcasted_iota(jnp.int32, (GROUP, GROUP), 1),
        1.0,
        0.0,
    ).astype(BF16)

    def flip(source, target):
        for part in range(source.shape[1] // GROUP):
            lanes = pl.ds(part * GROUP, GROUP)
            target[lanes, :] = dot(eye, source[:, lanes], 1, 1).astype(BF16)

    return flip


class Parking:
    def __init__(self, stage, target, sem):
        self.stage, self.target, self.sem = stage, target, sem
        self.sent = []

    def put(self, value, index):
        slot = len(self.sent) % 2
        if len(self.sent) >= 2:
            self.sent[-2].wait()
        self.stage[slot] = value.astype(BF16)
        copy = pltpu.make_async_copy(self.stage.at[slot], self.target.at[index], self.sem.at[slot])
        copy.start()
        self.sent.append(copy)

    def finish(self):
        for copy in self.sent[-2:]:
            copy.wait()


def layer_kernel(
    wired,
    lengths_ref, tokens_hbm, cot_hbm, ln_gain_ref, w_qkv_hbm, b_qkv_ref, q_gain_ref, k_gain_ref,
    w_o_hbm, b_o_ref, w_in_hbm, b_in_ref, w_out_hbm, b_out_ref,
    output_hbm, grad_tokens_hbm, pieces_hbm, small_hbm,
    weights, tok, cot, packed, grow, normed, hid_even, gpre_even, hid_odd, gpre_odd,
    flipped, turned, fed, gnorm, qs, ks, vs, gm, rk, dq, dk, small_ref,
    load_sem, done_sem, *refs,
):
    rows, width = tok.shape
    hidden_width = w_in_hbm.shape[1]
    chunks = hidden_width // width
    groups = width // GROUP
    seqs = rows // SEQ
    images = seqs * IMAGES
    base = lax.axis_index("branch") * seqs
    assert chunks == 4 and groups == 3
    hid, gpre = (hid_even, hid_odd), (gpre_even, gpre_odd)
    mixed, gprojs = tok, (hid_even, gpre_even, cot)
    w_in = [weights.at[f % 3] for f in range(chunks)]
    w_out = [weights.at[3 + f % 3] for f in range(chunks)]
    w_qkv, w_o = [weights.at[1], weights.at[4], weights.at[2]], weights.at[5]
    nq, rq, nk = (fed.at[:, pl.ds(part * GROUP, GROUP)] for part in range(3))
    loads = {}

    def load(name, source, target):
        copy = pltpu.make_async_copy(source, target, load_sem.at[len(loads)])
        copy.start()
        loads[name] = copy

    def load_chunk(f):
        cols = pl.ds(f * width, width)
        load(("in", f), w_in_hbm.at[:, cols], w_in[f])
        load(("out", f), w_out_hbm.at[cols, :], w_out[f])

    def load_qkv(hg):
        for t in range(3):
            load(
                ("qkv", hg, t),
                w_qkv_hbm.at[:, pl.ds(t * width + hg * GROUP, GROUP)],
                w_qkv[hg].at[:, pl.ds(t * GROUP, GROUP)],
            )

    load("tok", tokens_hbm, tok)
    load("cot", cot_hbm, cot)
    for f in range(3):
        load_chunk(f)
    small_ref[...] = jnp.zeros_like(small_ref)
    net, parking = None, None
    if wired:
        net = Exchange(refs[:10] + (small_ref,) + refs[10:], chunks)
        net.greet()
    else:
        parking = Parking(refs[0], pieces_hbm, refs[1])

    def emit(value, shard, axes):
        if wired:
            index = net.open()
            net.put(index, value, 0, axes)
            net.start(index, shard, axes, 0, width // 2)
        else:
            parking.put(value, shard if isinstance(shard, int) else chunks + groups + 1 + shard[0])

    def point(cost):
        if wired:
            net.progress(cost)

    def cost(amount):
        if wired:
            net.now += amount

    def lanes_of(part):
        return pl.ds(part * GROUP, GROUP)

    ones_row = jnp.where(lax.broadcasted_iota(jnp.int32, (16, rows), 0) == 0, 1.0, 0.0)
    flipped[pl.ds(width, 16), :] = ones_row.astype(BF16)
    eye = jnp.where(
        lax.broadcasted_iota(jnp.int32, (GROUP, GROUP), 0)
        == lax.broadcasted_iota(jnp.int32, (GROUP, GROUP), 1),
        1.0,
        0.0,
    ).astype(BF16)

    def flip(source, target, part):
        target[lanes_of(part), :] = dot(eye, source[:, lanes_of(part)], 1, 1).astype(BF16)

    for name in ("tok", "cot", ("in", 0), ("out", 0)):
        loads[name].wait()
    grad_sum = jnp.zeros((1, width), F32)
    for s in range(seqs):
        span = pl.ds(s * SEQ, SEQ)
        pick = one_hot(slot_positions([lengths_ref[base + s, j] for j in range(IMAGES)]))
        rows_here = dot(pick, tok[span, :])
        packed[span, :] = rows_here.astype(BF16)
        unit, _ = row_stats(rows_here)
        normed[span, :] = (unit * ln_gain_ref[...].reshape(1, width)).astype(BF16)
        grads_here = dot(pick, cot[span, :])
        grow[span, :] = grads_here.astype(BF16)
        grad_sum = grad_sum + jnp.sum(grads_here, axis=0, keepdims=True)
    small_ref[pl.ds(7, 1), pl.ds(0, width)] = grad_sum
    for part in range(groups):
        flip(normed, flipped, part)
    cost(6.0)

    def add_fed(f):
        for part in range(groups):
            lanes = lanes_of(part)
            up = dot(hid[f % 2][...], w_out[f][:, lanes])
            fed[:, lanes] = up if f == 0 else fed[:, lanes] + up

    def add_gnorm(source, target, first):
        for part in range(groups):
            lanes = lanes_of(part)
            down = dot(source[...], target[lanes, :], 1, 1)
            gnorm[:, lanes] = down if first else gnorm[:, lanes] + down

    b_in = b_in_ref[...].reshape(1, hidden_width)
    ready = None

    def activate():
        f, c, pre, back = ready
        hidden, grad_pre = gelu_pair(pre, back)
        hid[f % 2][:, lanes_of(c)] = hidden.astype(BF16)
        gpre[f % 2][:, lanes_of(c)] = grad_pre.astype(BF16)

    def send_w_in(f):
        sums = dot(flipped[...], gpre[f % 2][...])
        cost(2.2)
        emit(sums[:width], f, XY)
        small_ref[pl.ds(f, 1), pl.ds(0, width)] = sums[width : width + 1]
        point(0.0)

    def send_w_out(f):
        cost(1.9)
        emit(dot(turned[...], grow[...]), (f,), YX[:2])
        point(0.0)

    for f in range(chunks):
        if f > 0:
            loads["in", f].wait()
            loads["out", f].wait()
        for c in range(groups):
            place = f * width + c * GROUP
            lanes = lanes_of(c)
            pre = dot(normed[...], w_in[f][:, lanes]) + b_in[:, place : place + GROUP]
            back = dot(grow[...], w_out[f][lanes, :], 1, 1)
            if ready is not None:
                activate()
            ready = (f, c, pre, back)
            if f > 0 and c == 0:
                for part in range(groups):
                    flip(hid[1 - f % 2], turned, part)
            if f > 0 and c == 2:
                add_fed(f - 1)
                add_gnorm(gpre[1 - f % 2], w_in[f - 1], f == 1)
            point((1.7, 1.2, 4.6)[c] if f > 0 else 1.2)
            if f > 0 and c == 0:
                send_w_in(f - 1)
            if f > 0 and c == 1:
                send_w_out(f - 1)
        if f == 1:
            load_chunk(3)
        if f == 2:
            load_qkv(0)
            load_qkv(1)
        if f == 3:
            load_qkv(2)
            load("wo", w_o_hbm, w_o)
    activate()
    for part in range(groups):
        flip(hid_odd, turned, part)
    send_w_in(chunks - 1)
    send_w_out(chunks - 1)

    add_fed(chunks - 1)
    hid_odd[...] = (fed[...] + b_out_ref[...].reshape(1, width)).astype(BF16)
    point(1.9)

    same_head = (
        lax.broadcasted_iota(jnp.int32, (GROUP, GROUP), 0) // HEAD
        == lax.broadcasted_iota(jnp.int32, (GROUP, GROUP), 1) // HEAD
    )
    average = jnp.where(same_head, 1.0 / HEAD, 0.0).astype(BF16)
    q_gain = jnp.concatenate([q_gain_ref[...].reshape(1, HEAD)] * (GROUP // HEAD), axis=1)
    k_gain = jnp.concatenate([k_gain_ref[...].reshape(1, HEAD)] * (GROUP // HEAD), axis=1)
    b_qkv = b_qkv_ref[...].reshape(1, 3 * width)
    lane = lax.broadcasted_iota(jnp.int32, (1, KEYS), 1)
    pair_lane = jnp.concatenate([lane, lane], axis=1)
    first_head = jnp.where(lane < HEAD, 1.0, 0.0).astype(BF16)
    second_head = jnp.where(lane < HEAD, 0.0, 1.0).astype(BF16)

    def head_mean(values, split):
        high = values.astype(BF16)
        mean = dot(high, average)
        if split:
            mean = mean + dot((values - high.astype(F32)).astype(BF16), average)
        return mean

    def head_norm(raw):
        centered = raw - head_mean(raw, True)
        inverse = lax.rsqrt(head_mean(centered * centered, False) + EPS)
        return centered * inverse, inverse

    def two_heads(block):
        return jnp.concatenate([block * first_head, block * second_head], axis=0)

    def stacked(block):
        return jnp.concatenate([block[:, :KEYS], block[:, KEYS:]], axis=0)

    def invert(total):
        guess = pl.reciprocal(total, approx=True)
        return guess * (2.0 - total * guess)

    def over_heads(block, change):
        parts = []
        for head in range(2):
            part = block[:, head * KEYS : (head + 1) * KEYS]
            total = change(jnp.sum(part, axis=1, keepdims=True))
            parts.append(jnp.broadcast_to(total, part.shape))
        return jnp.concatenate(parts, axis=1)

    ks[pl.ds(rows, KEYS - SLOT), :] = jnp.zeros((KEYS - SLOT, GROUP), BF16)
    vs[pl.ds(rows, KEYS - SLOT), :] = jnp.zeros((KEYS - SLOT, GROUP), BF16)

    for hg in range(groups):
        gproj = gprojs[hg]
        bias_q, bias_k, bias_v = (
            b_qkv[:, t * width + hg * GROUP : t * width + (hg + 1) * GROUP] for t in range(3)
        )
        for t in range(3):
            loads["qkv", hg, t].wait()
        if hg == 0:
            loads["wo"].wait()
        raw = dot(normed[...], w_qkv[hg][:, lanes_of(0)]) + bias_q
        unit, inverse = head_norm(raw)
        nq[...] = unit
        rq[...] = inverse
        qs[...] = (unit * q_gain).astype(BF16) * SCALE
        raw = dot(normed[...], w_qkv[hg][:, lanes_of(1)]) + bias_k
        unit, inverse = head_norm(raw)
        nk[...] = unit
        rk[...] = inverse
        ks[pl.ds(0, rows), :] = (unit * k_gain).astype(BF16)
        raw = dot(normed[...], w_qkv[hg][:, lanes_of(2)]) + bias_v
        vs[pl.ds(0, rows), :] = raw.astype(BF16)
        gm[...] = dot(grow[...], w_o[lanes_of(hg), :], 1, 1).astype(BF16)
        point(4.5)

        def one_image(image):
            start = image * SLOT
            span = pl.ds(start, SLOT)
            window = pl.ds(start, KEYS)
            seen = pair_lane < lengths_ref[base + image // IMAGES, image % IMAGES]
            for pair in range(GROUP // KEYS):
                lanes = pl.ds(pair * KEYS, KEYS)
                query, grad = qs[span, lanes], gm[span, lanes]
                keys, values = two_heads(ks[window, lanes]), two_heads(vs[window, lanes])
                weight = jnp.where(seen, jnp.exp(dot(query, keys, 1, 1)), 0.0)
                probs = weight * over_heads(weight, invert)
                grad_probs = dot(grad, values, 1, 1)
                inner = over_heads(probs * grad_probs, lambda total: total)
                grad_scores = (probs * (grad_probs - inner)).astype(BF16)
                probs_low = probs.astype(BF16)
                mixed[span, pl.ds(hg * GROUP + pair * KEYS, KEYS)] = dot(probs_low, values).astype(
                    BF16
                )
                dq[span, lanes] = dot(grad_scores, keys) * SCALE
                dk[span, lanes] = dot(stacked(grad_scores), two_heads(query), 0, 0)[:SLOT]
                gproj[span, pl.ds(2 * GROUP + pair * KEYS, KEYS)] = dot(
                    stacked(probs_low), two_heads(grad), 0, 0
                )[:SLOT].astype(BF16)

        for image in range(images):
            one_image(image)
            if image % 4 == 3:
                point(2.6)
        if hg == groups - 1:
            for part in range(groups):
                flip(mixed, turned, part)
            if wired:
                index = net.open()
                for lane, size, part_axes in ((0, KEYS, XY), (KEYS, 2 * KEYS, YX)):
                    sums = dot(turned[...], grow[:, pl.ds(2 * lane, 2 * size)])
                    net.put(index, sums, lane, part_axes)
                    cost(1.1)
                    net.start(index, chunks + groups, part_axes, lane, size)
                point(0.0)
            else:
                parking.put(dot(turned[...], grow[...]), chunks + groups)

        axes = (XY, YX, YX)[hg]
        last = hg == groups - 1
        index = net.open() if wired else None
        parts = {}

        def part_grad(t, part_axes):
            sums = dot(flipped[...], gproj[:, lanes_of(t)])
            small_ref[pl.ds(4 + hg, 1), lanes_of(t)] = sums[width : width + 1]
            if wired:
                net.put(index, sums[:width], t * KEYS, part_axes)
                if last:
                    net.start(index, chunks + hg, part_axes, t * KEYS, KEYS)
            else:
                parts[t] = sums[:width]

        def norm_back(side, grad_ref, unit_ref, inverse_ref, gain):
            grad, unit = grad_ref[...], unit_ref[...]
            gain_sum = jnp.sum(grad * unit, axis=0, keepdims=True)
            small_ref[pl.ds(3 + side, 1), pl.ds(width, GROUP)] += gain_sum
            grad = grad * gain
            back = grad - head_mean(grad, False) - unit * head_mean(grad * unit, False)
            gproj[:, lanes_of(side)] = (back * inverse_ref[...]).astype(BF16)

        cost(0.7)
        part_grad(2, ZX if last else axes)
        norm_back(0, dq, nq, rq, q_gain)
        cost(1.5)
        if last:
            point(0.0)
        part_grad(0, XY if last else axes)
        norm_back(1, dk, nk, rk, k_gain)
        cost(1.5)
        if last:
            point(0.0)
        part_grad(1, YX if last else axes)
        if not wired:
            parking.put(jnp.concatenate([parts[t] for t in range(3)], axis=1), chunks + hg)
        elif not last:
            net.start(index, chunks + hg, axes, 0, width // 2)
        point(0.0)

    add_gnorm(gpre_odd, w_in[chunks - 1], False)
    point(1.7)
    for hg in range(groups):
        add_gnorm(gprojs[hg], w_qkv[hg], False)
        if hg == 0:
            load("tok again", tokens_hbm, hid_even)
        if hg == 1:
            load("cot again", cot_hbm, gpre_even)
        point(1.7)
    ln_gain = ln_gain_ref[...].reshape(1, width)
    b_o = b_o_ref[...].reshape(1, width)
    gain_grad = jnp.zeros((1, width), F32)
    spans = [pl.ds(s * SEQ, SEQ) for s in range(seqs)]
    stats = [row_stats(packed[span, :].astype(F32)) for span in spans]
    for span, (unit, _) in zip(spans, stats):
        gain_grad = gain_grad + jnp.sum(gnorm[span, :] * unit, axis=0, keepdims=True)
    for t in range(width // GROUP):
        small_ref[pl.ds(t, 1), pl.ds(width, GROUP)] = gain_grad[:, t * GROUP : (t + 1) * GROUP]
    if wired:
        net.start_small()
    point(0.0)
    for span, (unit, inverse) in zip(spans, stats):
        grad = gnorm[span, :] * ln_gain
        back = grad - jnp.mean(grad, axis=1, keepdims=True)
        back = (back - unit * jnp.mean(grad * unit, axis=1, keepdims=True)) * inverse
        normed[span, :] = (grow[span, :].astype(F32) + back).astype(BF16)
        point(0.7)
    finals = []
    loads["tok again"].wait()
    loads["cot again"].wait()

    def hand_over(source, target):
        copy = pltpu.make_async_copy(source, target, done_sem.at[len(finals)])
        copy.start()
        finals.append(copy)

    for s in range(seqs):
        span = pl.ds(s * SEQ, SEQ)
        place = position_slots([lengths_ref[base + s, j] for j in range(IMAGES)])
        put = one_hot(place)
        padding = jnp.where(place < 0, 1.0, 0.0)
        attended = (dot(mixed[span, :], w_o[...]) + b_o).astype(BF16).astype(F32)
        point(0.5)
        result = packed[span, :].astype(F32) + (attended + hid_odd[span, :].astype(F32))
        result = dot(put, result.astype(BF16)) + padding * hid_even[span, :].astype(F32)
        hid_even[span, :] = result.astype(BF16)
        hand_over(hid_even.at[span], output_hbm.at[span])
        point(0.7)
        grads = dot(put, normed[span, :]) + padding * gpre_even[span, :].astype(F32)
        gpre_even[span, :] = grads.astype(BF16)
        hand_over(gpre_even.at[span], grad_tokens_hbm.at[span])
        point(0.8)
    if wired:
        net.drain()
        hand_over(net.fin, pieces_hbm)
    else:
        parking.finish()
    hand_over(small_ref, small_hbm)
    for copy in finals:
        copy.wait()


def split_lanes(block, groups):
    width = block.shape[1] // 3
    return jnp.concatenate(
        [
            block[:, hg * width + t * GROUP : hg * width + (t + 1) * GROUP]
            for t in range(3)
            for hg in range(groups)
        ],
        axis=1,
    )


def fold_heads(gains):
    return sum(gains[:, h * HEAD : (h + 1) * HEAD] for h in range(GROUP // HEAD))


def small_parts(small, chunks, groups, width):
    b_in = jnp.concatenate([small[f : f + 1, :width] for f in range(chunks)], axis=1)
    b_qkv = jnp.concatenate([small[4 + hg : 5 + hg, :width] for hg in range(groups)], axis=1)
    ln = jnp.concatenate([small[t : t + 1, width:] for t in range(width // GROUP)], axis=1)
    gains = [fold_heads(small[3 + side : 4 + side, width:]) for side in range(2)]
    return ln, split_lanes(b_qkv, groups), gains[0], gains[1], small[7:8, :width], b_in


def finish_kernel(
    rows_hbm, grads_hbm, fin_hbm, small_hbm, output_hbm, grad_tokens_hbm, g_ln, g_qkv_hbm, g_b_qkv,
    g_q, g_k, g_o_hbm, g_b_o, g_in_hbm, g_b_in, g_out_hbm, g_b_out, held, fin, small, g_qkv, g_o, g_in,
    g_out, sem,
):
    comes = [
        pltpu.make_async_copy(source, target, sem.at[0, i])
        for i, (source, target) in enumerate(
            ((fin_hbm, fin), (small_hbm, small), (rows_hbm, held.at[0]), (grads_hbm, held.at[1]))
        )
    ]
    goes = [
        pltpu.make_async_copy(source, target, sem.at[1, i])
        for i, (source, target) in enumerate(
            (
                (held.at[0], output_hbm), (held.at[1], grad_tokens_hbm), (g_in, g_in_hbm),
                (g_qkv, g_qkv_hbm), (g_out, g_out_hbm), (g_o, g_o_hbm),
            )
        )
    ]
    for copy in comes:
        copy.start()
    width = g_o.shape[1]
    chunks, groups = g_in.shape[1] // width, width // GROUP

    def whole(shard, lane, size):
        return jnp.concatenate(
            [fin[side, shard, :, lane : lane + size].astype(F32) for side in range(2)], axis=1
        )

    comes[0].wait()
    for f in range(chunks):
        g_in[:, f * width : (f + 1) * width] = whole(f, 0, width // 2)
    goes[2].start()
    for hg in range(groups):
        for t in range(3):
            place = t * width + hg * GROUP
            g_qkv[:, place : place + GROUP] = whole(chunks + hg, t * KEYS, KEYS)
    goes[3].start()
    for i in range(2):
        comes[2 + i].wait()
        goes[i].start()
    for j in range(4):
        g_out[j * BLOCK : (j + 1) * BLOCK, :] = whole(chunks + groups + 1 + j, 0, width // 2)
    goes[4].start()
    g_o[:, :GROUP] = whole(chunks + groups, 0, KEYS)
    g_o[:, GROUP:] = whole(chunks + groups, KEYS, 2 * KEYS)
    goes[5].start()
    comes[1].wait()
    ln, b_qkv, q, k, b_out, b_in = small_parts(small[...], chunks, groups, width)
    for ref, value in (
        (g_ln, ln), (g_b_qkv, b_qkv), (g_q, q), (g_k, k), (g_b_o, b_out), (g_b_in, b_in), (g_b_out, b_out)
    ):
        ref[...] = value.reshape(value.shape[1])
    for copy in goes:
        copy.wait()


def local(n_dp, tokens, lengths, cotangent, ln_gain, w_qkv, b_qkv, q_gain, k_gain, w_o, b_o, w_in, b_in, w_out, b_out):
    rows, width = tokens.shape
    hidden_width = w_in.shape[1]
    chunks = hidden_width // width
    groups = width // GROUP
    seqs = rows // SEQ
    shards = chunks + groups + 1
    everyone = shards + chunks
    wired = n_dp * BLOCK == width and n_dp == 4 * chunks
    half = width // 2
    extra = KEYS - SLOT
    anywhere = pl.BlockSpec(memory_space=pl.ANY)
    vmem = pl.BlockSpec(memory_space=pltpu.VMEM)
    smem = pl.BlockSpec(memory_space=pltpu.SMEM)
    wide = lambda *shape: pltpu.VMEM(shape, F32)
    slim = lambda *shape: pltpu.VMEM(shape, BF16)
    flags = lambda *shape: pltpu.SemaphoreType.DMA(shape)
    low = lambda *shape: jax.ShapeDtypeStruct(shape, BF16)
    full = lambda *shape: jax.ShapeDtypeStruct(shape, F32)
    small_shape = (8, width + GROUP)

    if wired:
        out_piece = low(2, shards + 4, BLOCK, half)
        flights = 6 * (shards + 3) + 3 * chunks + 3 + 5
        others = [
            slim(SLOTS, 2, 16, BLOCK, half), slim(RING, 16, BLOCK, half),
            slim(everyone, 8, BLOCK, half), slim(everyone, 4, BLOCK, half),
            slim(shards, 2, BLOCK, half), slim(shards, 1, BLOCK, half), slim(4, 4, BLOCK, half),
            slim(2, 4, BLOCK, half), slim(1, 4, BLOCK, half), slim(2, shards + 4, BLOCK, half),
            wide(5, *small_shape), flags(flights), flags(flights),
        ]
        settings = dict(collective_id=0, has_side_effects=True)
    else:
        out_piece = low(everyone, width, width)
        others = [slim(2, width, width), flags(2)]
        settings = {}
    output, grad_tokens, pieces, small = pl.pallas_call(
        functools.partial(layer_kernel, wired),
        out_shape=(low(rows, width), low(rows, width), out_piece, full(*small_shape)),
        in_specs=[
            smem, anywhere, anywhere, vmem, anywhere, vmem, vmem, vmem, anywhere, vmem, anywhere,
            vmem, anywhere, vmem,
        ],
        out_specs=(anywhere,) * 4,
        scratch_shapes=[slim(6, width, width)]
        + [slim(rows, width)] * 9
        + [
            slim(width + 16, rows), slim(width, rows), wide(rows, width), wide(rows, width),
            slim(rows, GROUP), slim(rows + extra, GROUP), slim(rows + extra, GROUP),
            slim(rows, GROUP),
        ]
        + [wide(rows, GROUP)] * 3
        + [wide(*small_shape), flags(5 + 2 * chunks + 3 * groups), flags(2 * seqs + 2)]
        + others,
        compiler_params=pltpu.CompilerParams(vmem_limit_bytes=62 << 20, **settings),
    )(
        lengths, tokens, cotangent, ln_gain, w_qkv, b_qkv, q_gain, k_gain, w_o, b_o, w_in, b_in,
        w_out, b_out,
    )

    if wired:
        return pl.pallas_call(
            finish_kernel,
            out_shape=(
                low(rows, width), low(rows, width), full(width), full(BLOCK, 3 * width),
                full(3 * width), full(HEAD), full(HEAD), full(BLOCK, width), full(width),
                full(BLOCK, hidden_width), full(hidden_width), full(4 * BLOCK, width), full(width),
            ),
            in_specs=[anywhere] * 4,
            out_specs=(
                anywhere, anywhere, vmem, anywhere, vmem, vmem, vmem, anywhere, vmem, anywhere, vmem,
                anywhere, vmem,
            ),
            scratch_shapes=[
                slim(2, rows, width), slim(2, shards + 4, BLOCK, half), wide(*small_shape),
                wide(BLOCK, 3 * width), wide(BLOCK, width), wide(BLOCK, hidden_width),
                wide(4 * BLOCK, width), flags(2, 6),
            ],
        )(output, grad_tokens, pieces, small)

    def scatter(block, dim):
        part = lax.psum_scatter(block, "dp", scatter_dimension=dim, tiled=True)
        return lax.psum(part, "branch").astype(F32)

    grad_out = scatter(pieces[shards:].reshape(hidden_width, width), 0)
    reduced = scatter(pieces[:shards], 1)
    grad_in = jnp.concatenate([reduced[f] for f in range(chunks)], axis=1)
    qkv = jnp.concatenate([reduced[chunks + hg] for hg in range(groups)], axis=1)
    small = lax.psum(small, ("dp", "branch"))
    ln, g_b_qkv, g_q, g_k, g_b_out, g_b_in = (
        part[0] for part in small_parts(small, chunks, groups, width)
    )
    return (
        output, grad_tokens, ln, split_lanes(qkv, groups), g_b_qkv, g_q, g_k,
        reduced[chunks + groups], g_b_out, grad_in, g_b_in, grad_out, g_b_out,
    )


def solution(mesh):
    rows, split, whole = P(("dp", "branch"), None), P("dp", None), P()
    return jax.shard_map(
        functools.partial(local, mesh.shape["dp"]),
        mesh=mesh,
        in_specs=(rows, split, rows) + (whole,) * 11,
        out_specs=(
            rows, rows, whole, split, whole, whole, whole, split, whole, split, whole, split, whole,
        ),
        check_vma=False,
    )
```

```python
import functools
import math

import jax
import jax.numpy as jnp
from jax import lax
from jax.experimental import pallas as pl
from jax.experimental.pallas import tpu as pltpu
from jax.sharding import PartitionSpec as P

HEAD = 64
SEQ = 448
IMAGES = 4
SLOT = SEQ // IMAGES
LEAST = 32
KEYS = 128
GROUP = 256
EPS = 1e-06
SCALE = 0.125
F32 = jnp.float32
BF16 = jnp.bfloat16
GELU_A = math.sqrt(2.0 / math.pi)
GELU_B = 0.044715


def dot(left, right, left_dim=1, right_dim=0):
    return lax.dot_general(
        left, right, (((left_dim,), (right_dim,)), ((), ())), preferred_element_type=F32
    )


def slot_positions(lens):
    row = lax.broadcasted_iota(jnp.int32, (SEQ, 1), 0)
    held = jnp.full((SEQ, 1), -1, jnp.int32)
    start = jnp.int32(0)
    for image in range(IMAGES):
        place = row - SLOT * image
        held = jnp.where((place >= 0) & (place < lens[image]), place + start, held)
        start = start + lens[image]
    return held


def position_slots(lens):
    row = lax.broadcasted_iota(jnp.int32, (SEQ, 1), 0)
    held = jnp.full((SEQ, 1), -1, jnp.int32)
    start = jnp.int32(0)
    for image in range(IMAGES):
        place = row - start
        held = jnp.where((place >= 0) & (place < lens[image]), place + SLOT * image, held)
        start = start + lens[image]
    return held


def one_hot(index, first=0, size=SEQ):
    lanes = lax.broadcasted_iota(jnp.int32, (index.shape[0], size), 1) + first
    return jnp.where(lanes == index, 1.0, 0.0).astype(BF16)


def pick_rows(held, block):
    parts = []
    for image in range(0, IMAGES, 2):
        first, end = LEAST * image, SLOT * (image + 2)
        pick = one_hot(held[SLOT * image : end], first, end - first)
        parts.append(dot(pick, block[first:end]))
    return jnp.concatenate(parts, axis=0)


def row_stats(values):
    centered = values - jnp.mean(values, axis=1, keepdims=True)
    spread = jnp.mean(centered * centered, axis=1, keepdims=True)
    inverse = lax.rsqrt(spread + EPS)
    return centered * inverse, inverse


def gelu_pair(pre, grad):
    square = pre * pre
    up = 0.5 * jnp.tanh(pre * (GELU_A + (GELU_A * GELU_B) * square)) + 0.5
    hidden = pre * up
    slope = 2.0 * GELU_A + (6.0 * GELU_A * GELU_B) * square
    return hidden, (up + (hidden * (1.0 - up)) * slope) * grad


MESH = pl.DeviceIdType.MESH
BLOCK = 48
SLOTS = 2
RING = 8
XY, YX = ("x", "y", "z0", "z1"), ("y", "x", "z0", "z1")
ZX, ZY = ("z0", "z1", "x", "y"), ("z0", "z1", "y", "x")
RATES = {"core": 400e3, "x": 42e3, "y": 42e3, "z0": 42e3, "z1": 21e3}
LATENCY = 2.0


class Piece:
    def __init__(self, index, shard, axes, lanes):
        self.index, self.shard, self.axes, self.lanes = index, shard, axes, lanes
        self.stage, self.copy, self.eta = 0, None, 0.0

    def cut(self, ref):
        return ref.at[:, :, self.lanes]


class Small:
    def __init__(self):
        self.stage, self.copy, self.eta = 0, None, 0.0


class Exchange:
    def __init__(self, refs, chunks):
        (self.both, self.inbox, self.in1, self.in2, self.in3, self.in4, self.osum, self.oin3,
         self.oin4, self.fin, self.small, self.small_in, self.send_sem, self.recv_sem) = refs
        self.chunks = chunks
        self.dp, self.core = lax.axis_index("dp"), lax.axis_index("branch")
        self.bits = {
            "x": lax.rem(self.dp, 2),
            "y": lax.rem(self.dp // 2, 2),
            "z0": lax.rem(self.dp // 4, 2),
            "z1": lax.rem(self.dp // 8, 2),
        }
        self.far = {
            axis: (self.dp + step - 2 * step * self.bits[axis], self.core)
            for axis, step in (("x", 1), ("y", 2), ("z0", 4), ("z1", 8))
        }
        self.far["core"] = (self.dp, 1 - self.core)
        self.items, self.opened = [], 0
        self.flights, self.merged, self.now, self.free = 0, 0, 0.0, {}

    def greet(self):
        barrier = pltpu.get_barrier_semaphore()
        for device in self.far.values():
            pl.semaphore_signal(barrier, inc=1, device_id=device, device_id_type=MESH)
        pl.semaphore_wait(barrier, len(self.far))

    def send(self, item, source, target, axis):
        copy = pltpu.make_async_remote_copy(
            src_ref=source, dst_ref=target, send_sem=self.send_sem.at[self.flights],
            recv_sem=self.recv_sem.at[self.flights], device_id=self.far[axis], device_id_type=MESH,
        )
        self.flights += 1
        copy.start()
        link = axis[0]
        size = source.dtype.itemsize * math.prod(source.shape)
        self.free[link] = max(self.free.get(link, 0.0), self.now) + size / RATES[axis]
        item.copy, item.eta = copy, self.free[link] + LATENCY

    def open(self):
        index = self.opened
        for behind, stage in ((SLOTS, 1), (RING - SLOTS, 2)):
            while any(
                item.index == index - behind and item.stage < stage
                for item in self.items
                if isinstance(item, Piece)
            ):
                self.advance(min(self.under_way(), key=lambda item: item.eta))
        self.opened += 1
        return index

    def put(self, index, value, lane, axes):
        half = value.shape[1] // 2
        for side, role in ((0, self.core), (1, 1 - self.core)):
            target = self.both.at[index % SLOTS, role, :, :, pl.ds(lane, half)]
            put_blocks(value, target, side, axes)

    def start(self, index, shard, axes, lane, width):
        piece = Piece(index, shard, axes, pl.ds(lane, width))
        self.send(
            piece, piece.cut(self.both.at[index % SLOTS, 1]), piece.cut(self.inbox.at[index % RING]),
            "core",
        )
        self.items.append(piece)

    def halve(self, piece, held, held_at, arrived, count, axis, target):
        near = self.bits[axis] * count
        away = (1 - self.bits[axis]) * count
        span = pl.ds(away, count)
        arrived[span] = arrived[span] + held[pl.ds(held_at + away, count)]
        self.send(piece, arrived.at[span], target, axis)
        span = pl.ds(near, count)
        arrived[span] = arrived[span] + held[pl.ds(held_at + near, count)]

    def advance(self, piece):
        piece.copy.wait()
        self.now = max(self.now, piece.eta)
        piece.copy = None
        if isinstance(piece, Small):
            self.advance_small(piece)
            return
        k, shard, axes, cut = piece.index, piece.shard, piece.axes, piece.cut
        whole = isinstance(shard, int)
        in0, in1, in2 = cut(self.inbox.at[k % RING]), cut(self.in1.at[k]), cut(self.in2.at[k])
        if whole:
            in3, in4 = cut(self.in3.at[shard]), cut(self.in4.at[shard])
        if piece.stage == 0:
            self.halve(piece, cut(self.both.at[k % SLOTS, 0]), 0, in0, 8, axes[0], in1)
        elif piece.stage == 1:
            self.halve(piece, in0, self.bits[axes[0]] * 8, in1, 4, axes[1], in2)
        elif piece.stage == 2 and whole:
            self.halve(piece, in1, self.bits[axes[1]] * 4, in2, 2, axes[2], in3)
        elif piece.stage == 2:
            place = shard[0] % 2 * 2 + shard[0] // 2
            self.osum[place] = in2[...] + in1[pl.ds(self.bits[axes[1]] * 4, 4)]
            self.merged += 1
            if self.merged < self.chunks:
                piece.stage = 5
            else:
                far = pl.ds((1 - self.bits["z0"]) * 2, 2)
                self.send(piece, self.osum.at[far], self.oin3, "z0")
        elif piece.stage == 3 and whole:
            self.halve(piece, in2, self.bits[axes[2]] * 2, in3, 1, axes[3], in4)
        elif piece.stage == 3:
            self.halve(piece, self.osum, self.bits["z0"] * 2, self.oin3, 1, "z1", self.oin4)
        elif piece.stage == 4:
            if whole:
                final = self.fin.at[self.core, pl.ds(shard, 1), :, piece.lanes]
                final[...] = in4[...] + in3[pl.ds(self.bits[axes[3]], 1)]
            else:
                final = self.fin.at[self.core, pl.ds(self.fin.shape[1] - 4, 4)]
                final[...] = self.oin4[0] + self.oin3[self.bits["z1"]]
            self.send(piece, final, final, "core")
        piece.stage += 1

    def start_small(self):
        item = Small()
        self.send(item, self.small, self.small_in.at[0], "core")
        self.items.append(item)

    def advance_small(self, item):
        self.small[...] = self.small[...] + self.small_in[item.stage]
        item.stage += 1
        if item.stage < 5:
            axis = ("core", "x", "y", "z0", "z1")[item.stage]
            self.send(item, self.small, self.small_in.at[item.stage], axis)

    def under_way(self):
        return [item for item in self.items if item.copy is not None]

    def progress(self, cost):
        self.now += cost
        while True:
            due = [item for item in self.under_way() if item.eta <= self.now]
            if not due:
                return
            self.advance(min(due, key=lambda item: item.eta))

    def drain(self):
        while self.under_way():
            self.advance(min(self.under_way(), key=lambda item: item.eta))


def put_blocks(value, target, side, axes):
    half = value.shape[1] // 2
    for block in range(16):
        place = block
        if axes is not None and len(axes) == 4:
            bit = dict(x=block % 2, y=block // 2 % 2, z0=block // 4 % 2, z1=block // 8)
            place = sum(bit[axis] << (3 - i) for i, axis in enumerate(axes))
        target[place] = value[
            BLOCK * block : BLOCK * (block + 1), half * side : half * (side + 1)
        ].astype(BF16)


def make_flip():
    eye = jnp.where(
        lax.broadcasted_iota(jnp.int32, (GROUP, GROUP), 0)
        == lax.broadcasted_iota(jnp.int32, (GROUP, GROUP), 1),
        1.0,
        0.0,
    ).astype(BF16)

    def flip(source, target):
        for part in range(source.shape[1] // GROUP):
            lanes = pl.ds(part * GROUP, GROUP)
            target[lanes, :] = dot(eye, source[:, lanes], 1, 1).astype(BF16)

    return flip


class Parking:
    def __init__(self, stage, target, sem):
        self.stage, self.target, self.sem = stage, target, sem
        self.sent = []

    def put(self, value, index):
        slot = len(self.sent) % 2
        if len(self.sent) >= 2:
            self.sent[-2].wait()
        self.stage[slot] = value.astype(BF16)
        copy = pltpu.make_async_copy(self.stage.at[slot], self.target.at[index], self.sem.at[slot])
        copy.start()
        self.sent.append(copy)

    def finish(self):
        for copy in self.sent[-2:]:
            copy.wait()


def layer_kernel(
    wired,
    lengths_ref, tokens_hbm, cot_hbm, ln_gain_ref, w_qkv_hbm, b_qkv_ref, q_gain_ref, k_gain_ref,
    w_o_hbm, b_o_ref, w_in_hbm, b_in_ref, w_out_hbm, b_out_ref,
    output_hbm, grad_tokens_hbm, pieces_hbm, small_hbm,
    weights, tok, cot, packed, grow, normed, hid_even, gpre_even, hid_odd, gpre_odd,
    flipped, turned, fed, gnorm, qs, ks, vs, gm, rk, dq, dk, small_ref,
    load_sem, done_sem, *refs,
):
    rows, width = tok.shape
    hidden_width = w_in_hbm.shape[1]
    chunks = hidden_width // width
    groups = width // GROUP
    seqs = rows // SEQ
    images = seqs * IMAGES
    base = lax.axis_index("branch") * seqs
    assert chunks == 4 and groups == 3
    hid, gpre = (hid_even, hid_odd), (gpre_even, gpre_odd)
    mixed, gprojs = tok, (hid_even, gpre_even, cot)
    w_in = [weights.at[f % 3] for f in range(chunks)]
    w_out = [weights.at[3 + f % 3] for f in range(chunks)]
    w_qkv, w_o = [weights.at[1], weights.at[4], weights.at[2]], weights.at[5]
    nq, rq, nk = (fed.at[:, pl.ds(part * GROUP, GROUP)] for part in range(3))
    loads = {}

    def load(name, source, target):
        copy = pltpu.make_async_copy(source, target, load_sem.at[len(loads)])
        copy.start()
        loads[name] = copy

    def load_chunk(f):
        cols = pl.ds(f * width, width)
        load(("in", f), w_in_hbm.at[:, cols], w_in[f])
        load(("out", f), w_out_hbm.at[cols, :], w_out[f])

    def load_qkv(hg):
        for t in range(3):
            load(
                ("qkv", hg, t),
                w_qkv_hbm.at[:, pl.ds(t * width + hg * GROUP, GROUP)],
                w_qkv[hg].at[:, pl.ds(t * GROUP, GROUP)],
            )

    load("tok", tokens_hbm, tok)
    load("cot", cot_hbm, cot)
    for f in range(3):
        load_chunk(f)
    small_ref[...] = jnp.zeros_like(small_ref)
    net, parking = None, None
    if wired:
        net = Exchange(refs[:10] + (small_ref,) + refs[10:], chunks)
        net.greet()
    else:
        parking = Parking(refs[0], pieces_hbm, refs[1])

    def emit(value, shard, axes):
        if wired:
            index = net.open()
            net.put(index, value, 0, axes)
            net.start(index, shard, axes, 0, width // 2)
        else:
            parking.put(value, shard if isinstance(shard, int) else chunks + groups + 1 + shard[0])

    def point(cost):
        if wired:
            net.progress(cost)

    def cost(amount):
        if wired:
            net.now += amount

    def lanes_of(part):
        return pl.ds(part * GROUP, GROUP)

    ones_row = jnp.where(lax.broadcasted_iota(jnp.int32, (16, rows), 0) == 0, 1.0, 0.0)
    flipped[pl.ds(width, 16), :] = ones_row.astype(BF16)
    eye = jnp.where(
        lax.broadcasted_iota(jnp.int32, (GROUP, GROUP), 0)
        == lax.broadcasted_iota(jnp.int32, (GROUP, GROUP), 1),
        1.0,
        0.0,
    ).astype(BF16)

    def flip(source, target, part):
        target[lanes_of(part), :] = dot(eye, source[:, lanes_of(part)], 1, 1).astype(BF16)

    for name in ("tok", "cot", ("in", 0), ("out", 0)):
        loads[name].wait()
    grad_sum = jnp.zeros((1, width), F32)
    for s in range(seqs):
        span = pl.ds(s * SEQ, SEQ)
        held = slot_positions([lengths_ref[base + s, j] for j in range(IMAGES)])
        rows_here = pick_rows(held, tok[span, :])
        packed[span, :] = rows_here.astype(BF16)
        unit, _ = row_stats(rows_here)
        normed[span, :] = (unit * ln_gain_ref[...].reshape(1, width)).astype(BF16)
        grads_here = pick_rows(held, cot[span, :])
        grow[span, :] = grads_here.astype(BF16)
        grad_sum = grad_sum + jnp.sum(grads_here, axis=0, keepdims=True)
    small_ref[pl.ds(7, 1), pl.ds(0, width)] = grad_sum
    for part in range(groups):
        flip(normed, flipped, part)
    cost(6.0)

    def add_fed(f):
        for part in range(groups):
            lanes = lanes_of(part)
            up = dot(hid[f % 2][...], w_out[f][:, lanes])
            fed[:, lanes] = up if f == 0 else fed[:, lanes] + up

    def add_gnorm(source, target, first):
        for part in range(groups):
            lanes = lanes_of(part)
            down = dot(source[...], target[lanes, :], 1, 1)
            gnorm[:, lanes] = down if first else gnorm[:, lanes] + down

    b_in = b_in_ref[...].reshape(1, hidden_width)
    ready = None

    def activate():
        f, c, pre, back = ready
        hidden, grad_pre = gelu_pair(pre, back)
        hid[f % 2][:, lanes_of(c)] = hidden.astype(BF16)
        gpre[f % 2][:, lanes_of(c)] = grad_pre.astype(BF16)

    def send_w_in(f):
        sums = dot(flipped[...], gpre[f % 2][...])
        cost(2.2)
        emit(sums[:width], f, XY)
        small_ref[pl.ds(f, 1), pl.ds(0, width)] = sums[width : width + 1]
        point(0.0)

    def send_w_out(f):
        cost(1.9)
        emit(dot(turned[...], grow[...]), (f,), YX[:2])
        point(0.0)

    for f in range(chunks):
        if f > 0:
            loads["in", f].wait()
            loads["out", f].wait()
        for c in range(groups):
            place = f * width + c * GROUP
            lanes = lanes_of(c)
            pre = dot(normed[...], w_in[f][:, lanes]) + b_in[:, place : place + GROUP]
            back = dot(grow[...], w_out[f][lanes, :], 1, 1)
            if ready is not None:
                activate()
            ready = (f, c, pre, back)
            if f > 0 and c == 0:
                for part in range(groups):
                    flip(hid[1 - f % 2], turned, part)
            if f > 0 and c == 2:
                add_fed(f - 1)
                add_gnorm(gpre[1 - f % 2], w_in[f - 1], f == 1)
            point((1.7, 1.2, 4.6)[c] if f > 0 else 1.2)
            if f > 0 and c == 0:
                send_w_in(f - 1)
            if f > 0 and c == 1:
                send_w_out(f - 1)
        if f == 1:
            load_chunk(3)
        if f == 2:
            load_qkv(0)
            load_qkv(1)
        if f == 3:
            load_qkv(2)
            load("wo", w_o_hbm, w_o)
    activate()
    for part in range(groups):
        flip(hid_odd, turned, part)
    send_w_in(chunks - 1)
    send_w_out(chunks - 1)

    add_fed(chunks - 1)
    hid_odd[...] = (fed[...] + b_out_ref[...].reshape(1, width)).astype(BF16)
    point(1.9)

    same_head = (
        lax.broadcasted_iota(jnp.int32, (GROUP, GROUP), 0) // HEAD
        == lax.broadcasted_iota(jnp.int32, (GROUP, GROUP), 1) // HEAD
    )
    average = jnp.where(same_head, 1.0 / HEAD, 0.0).astype(BF16)
    average_twice = jnp.concatenate([average, average], axis=0)
    q_gain = SCALE * jnp.concatenate([q_gain_ref[...].reshape(1, HEAD)] * (GROUP // HEAD), axis=1)
    k_gain = jnp.concatenate([k_gain_ref[...].reshape(1, HEAD)] * (GROUP // HEAD), axis=1)
    b_qkv = b_qkv_ref[...].reshape(1, 3 * width)
    lane = lax.broadcasted_iota(jnp.int32, (1, KEYS), 1)
    pair_lane = jnp.concatenate([lane, lane], axis=1)
    first_head = jnp.where(lane < HEAD, 1.0, 0.0).astype(BF16)
    second_head = jnp.where(lane < HEAD, 0.0, 1.0).astype(BF16)

    def head_mean(values, split):
        high = values.astype(BF16)
        if not split:
            return dot(high, average)
        rest = (values - high.astype(F32)).astype(BF16)
        return dot(jnp.concatenate([high, rest], axis=1), average_twice)

    def head_norm(raw):
        centered = raw - head_mean(raw, True)
        inverse = lax.rsqrt(head_mean(centered * centered, False) + EPS)
        return centered * inverse, inverse

    def two_heads(block):
        return jnp.concatenate([block * first_head, block * second_head], axis=0)

    def stacked(block):
        return jnp.concatenate([block[:, :KEYS], block[:, KEYS:]], axis=0)

    def invert(total):
        guess = pl.reciprocal(total, approx=True)
        return guess * (2.0 - total * guess)

    def over_heads(block, change):
        parts = []
        for head in range(2):
            part = block[:, head * KEYS : (head + 1) * KEYS]
            total = change(jnp.sum(part, axis=1, keepdims=True))
            parts.append(jnp.broadcast_to(total, part.shape))
        return jnp.concatenate(parts, axis=1)

    ks[pl.ds(rows, KEYS - SLOT), :] = jnp.zeros((KEYS - SLOT, GROUP), BF16)
    vs[pl.ds(rows, KEYS - SLOT), :] = jnp.zeros((KEYS - SLOT, GROUP), BF16)

    for hg in range(groups):
        gproj = gprojs[hg]
        bias_q, bias_k, bias_v = (
            b_qkv[:, t * width + hg * GROUP : t * width + (hg + 1) * GROUP] for t in range(3)
        )
        for t in range(3):
            loads["qkv", hg, t].wait()
        if hg == 0:
            loads["wo"].wait()
        raw = dot(normed[...], w_qkv[hg][:, lanes_of(0)]) + bias_q
        unit, inverse = head_norm(raw)
        nq[...] = unit
        rq[...] = inverse
        qs[...] = (unit * q_gain).astype(BF16)
        raw = dot(normed[...], w_qkv[hg][:, lanes_of(1)]) + bias_k
        unit, inverse = head_norm(raw)
        nk[...] = unit
        rk[...] = inverse
        ks[pl.ds(0, rows), :] = (unit * k_gain).astype(BF16)
        raw = dot(normed[...], w_qkv[hg][:, lanes_of(2)]) + bias_v
        vs[pl.ds(0, rows), :] = raw.astype(BF16)
        gm[...] = dot(grow[...], w_o[lanes_of(hg), :], 1, 1).astype(BF16)
        point(4.5)

        def one_image(image):
            start = image * SLOT
            span = pl.ds(start, SLOT)
            window = pl.ds(start, KEYS)
            seen = pair_lane < lengths_ref[base + image // IMAGES, image % IMAGES]
            for pair in range(GROUP // KEYS):
                lanes = pl.ds(pair * KEYS, KEYS)
                query, grad = qs[span, lanes], gm[span, lanes]
                keys, values = two_heads(ks[window, lanes]), two_heads(vs[window, lanes])
                weight = jnp.where(seen, jnp.exp(dot(query, keys, 1, 1)), 0.0)
                probs = weight * over_heads(weight, invert)
                grad_probs = dot(grad, values, 1, 1)
                inner = over_heads(probs * grad_probs, lambda total: total)
                grad_scores = (probs * (grad_probs - inner)).astype(BF16)
                probs_low = probs.astype(BF16)
                mixed[span, pl.ds(hg * GROUP + pair * KEYS, KEYS)] = dot(probs_low, values).astype(
                    BF16
                )
                dq[span, lanes] = dot(grad_scores, keys)
                dk[span, lanes] = dot(stacked(grad_scores), two_heads(query), 0, 0)[:SLOT]
                gproj[span, pl.ds(2 * GROUP + pair * KEYS, KEYS)] = dot(
                    stacked(probs_low), two_heads(grad), 0, 0
                )[:SLOT].astype(BF16)

        for image in range(images):
            one_image(image)
            if image % 4 == 3:
                point(2.6)
        if hg == groups - 1:
            for part in range(groups):
                flip(mixed, turned, part)
            if wired:
                index = net.open()
                for lane, size, part_axes in ((0, KEYS, XY), (KEYS, 2 * KEYS, YX)):
                    sums = dot(turned[...], grow[:, pl.ds(2 * lane, 2 * size)])
                    net.put(index, sums, lane, part_axes)
                    cost(1.1)
                    net.start(index, chunks + groups, part_axes, lane, size)
                point(0.0)
            else:
                parking.put(dot(turned[...], grow[...]), chunks + groups)

        axes = (XY, YX, YX)[hg]
        last = hg == groups - 1
        index = net.open() if wired else None
        parts = {}

        def part_grad(t, part_axes):
            sums = dot(flipped[...], gproj[:, lanes_of(t)])
            small_ref[pl.ds(4 + hg, 1), lanes_of(t)] = sums[width : width + 1]
            if wired:
                net.put(index, sums[:width], t * KEYS, part_axes)
                if last:
                    net.start(index, chunks + hg, part_axes, t * KEYS, KEYS)
            else:
                parts[t] = sums[:width]

        def norm_back(side, grad_ref, unit_ref, inverse_ref, gain):
            grad, unit = grad_ref[...], unit_ref[...]
            gain_sum = jnp.sum(grad * unit, axis=0, keepdims=True)
            small_ref[pl.ds(3 + side, 1), pl.ds(width, GROUP)] += gain_sum * (SCALE, 1.0)[side]
            grad = grad * gain
            back = grad - head_mean(grad, False) - unit * head_mean(grad * unit, False)
            gproj[:, lanes_of(side)] = (back * inverse_ref[...]).astype(BF16)

        cost(0.7)
        part_grad(2, ZX if last else axes)
        norm_back(0, dq, nq, rq, q_gain)
        cost(1.5)
        if last:
            point(0.0)
        part_grad(0, XY if last else axes)
        norm_back(1, dk, nk, rk, k_gain)
        cost(1.5)
        if last:
            point(0.0)
        part_grad(1, YX if last else axes)
        if not wired:
            parking.put(jnp.concatenate([parts[t] for t in range(3)], axis=1), chunks + hg)
        elif not last:
            net.start(index, chunks + hg, axes, 0, width // 2)
        point(0.0)

    add_gnorm(gpre_odd, w_in[chunks - 1], False)
    point(1.7)
    for hg in range(groups):
        add_gnorm(gprojs[hg], w_qkv[hg], False)
        if hg == 0:
            load("tok again", tokens_hbm, hid_even)
        if hg == 1:
            load("cot again", cot_hbm, gpre_even)
        point(1.7)
    ln_gain = ln_gain_ref[...].reshape(1, width)
    b_o = b_o_ref[...].reshape(1, width)
    gain_grad = jnp.zeros((1, width), F32)
    for s in range(seqs):
        span = pl.ds(s * SEQ, SEQ)
        unit, inverse = row_stats(packed[span, :].astype(F32))
        grad = gnorm[span, :]
        gain_grad = gain_grad + jnp.sum(grad * unit, axis=0, keepdims=True)
        grad = grad * ln_gain
        back = grad - jnp.mean(grad, axis=1, keepdims=True)
        back = (back - unit * jnp.mean(grad * unit, axis=1, keepdims=True)) * inverse
        normed[span, :] = (grow[span, :].astype(F32) + back).astype(BF16)
    for t in range(width // GROUP):
        small_ref[pl.ds(t, 1), pl.ds(width, GROUP)] = gain_grad[:, t * GROUP : (t + 1) * GROUP]
    if wired:
        net.start_small()
    point(1.5)
    finals = []
    loads["tok again"].wait()
    loads["cot again"].wait()

    def hand_over(source, target):
        copy = pltpu.make_async_copy(source, target, done_sem.at[len(finals)])
        copy.start()
        finals.append(copy)

    for s in range(seqs):
        span = pl.ds(s * SEQ, SEQ)
        place = position_slots([lengths_ref[base + s, j] for j in range(IMAGES)])
        put = one_hot(place)
        padding = jnp.where(place < 0, 1.0, 0.0)
        attended = (dot(mixed[span, :], w_o[...]) + b_o).astype(BF16).astype(F32)
        result = packed[span, :].astype(F32) + (attended + hid_odd[span, :].astype(F32))
        result = dot(put, result.astype(BF16)) + padding * hid_even[span, :].astype(F32)
        hid_even[span, :] = result.astype(BF16)
        hand_over(hid_even.at[span], output_hbm.at[span])
        point(1.2)
        grads = dot(put, normed[span, :]) + padding * gpre_even[span, :].astype(F32)
        gpre_even[span, :] = grads.astype(BF16)
        hand_over(gpre_even.at[span], grad_tokens_hbm.at[span])
        point(0.8)
    if wired:
        net.drain()
        hand_over(net.fin, pieces_hbm)
    else:
        parking.finish()
    hand_over(small_ref, small_hbm)
    for copy in finals:
        copy.wait()


def split_lanes(block, groups):
    width = block.shape[1] // 3
    return jnp.concatenate(
        [
            block[:, hg * width + t * GROUP : hg * width + (t + 1) * GROUP]
            for t in range(3)
            for hg in range(groups)
        ],
        axis=1,
    )


def fold_heads(gains):
    return sum(gains[:, h * HEAD : (h + 1) * HEAD] for h in range(GROUP // HEAD))


def small_parts(small, chunks, groups, width):
    b_in = jnp.concatenate([small[f : f + 1, :width] for f in range(chunks)], axis=1)
    b_qkv = jnp.concatenate([small[4 + hg : 5 + hg, :width] for hg in range(groups)], axis=1)
    ln = jnp.concatenate([small[t : t + 1, width:] for t in range(width // GROUP)], axis=1)
    gains = [fold_heads(small[3 + side : 4 + side, width:]) for side in range(2)]
    return ln, split_lanes(b_qkv, groups), gains[0], gains[1], small[7:8, :width], b_in


def finish_kernel(
    rows_hbm, grads_hbm, fin_hbm, small_hbm, output_hbm, grad_tokens_hbm, g_ln, g_qkv_hbm, g_b_qkv,
    g_q, g_k, g_o_hbm, g_b_o, g_in_hbm, g_b_in, g_out_hbm, g_b_out, held, fin, small, g_qkv, g_o, g_in,
    g_out, sem,
):
    comes = [
        pltpu.make_async_copy(source, target, sem.at[0, i])
        for i, (source, target) in enumerate(
            ((fin_hbm, fin), (small_hbm, small), (rows_hbm, held.at[0]), (grads_hbm, held.at[1]))
        )
    ]
    goes = [
        pltpu.make_async_copy(source, target, sem.at[1, i])
        for i, (source, target) in enumerate(
            (
                (held.at[0], output_hbm), (held.at[1], grad_tokens_hbm), (g_in, g_in_hbm),
                (g_qkv, g_qkv_hbm), (g_out, g_out_hbm), (g_o, g_o_hbm),
            )
        )
    ]
    for copy in comes:
        copy.start()
    width = g_o.shape[1]
    chunks, groups = g_in.shape[1] // width, width // GROUP

    def whole(shard, lane, size):
        return jnp.concatenate(
            [fin[side, shard, :, lane : lane + size].astype(F32) for side in range(2)], axis=1
        )

    comes[0].wait()
    for f in range(chunks):
        g_in[:, f * width : (f + 1) * width] = whole(f, 0, width // 2)
    goes[2].start()
    for hg in range(groups):
        for t in range(3):
            place = t * width + hg * GROUP
            g_qkv[:, place : place + GROUP] = whole(chunks + hg, t * KEYS, KEYS)
    goes[3].start()
    for i in range(2):
        comes[2 + i].wait()
        goes[i].start()
    for j in range(4):
        g_out[j * BLOCK : (j + 1) * BLOCK, :] = whole(chunks + groups + 1 + j, 0, width // 2)
    goes[4].start()
    g_o[:, :GROUP] = whole(chunks + groups, 0, KEYS)
    g_o[:, GROUP:] = whole(chunks + groups, KEYS, 2 * KEYS)
    goes[5].start()
    comes[1].wait()
    ln, b_qkv, q, k, b_out, b_in = small_parts(small[...], chunks, groups, width)
    for ref, value in (
        (g_ln, ln), (g_b_qkv, b_qkv), (g_q, q), (g_k, k), (g_b_o, b_out), (g_b_in, b_in), (g_b_out, b_out)
    ):
        ref[...] = value.reshape(value.shape[1])
    for copy in goes:
        copy.wait()


def local(n_dp, tokens, lengths, cotangent, ln_gain, w_qkv, b_qkv, q_gain, k_gain, w_o, b_o, w_in, b_in, w_out, b_out):
    rows, width = tokens.shape
    hidden_width = w_in.shape[1]
    chunks = hidden_width // width
    groups = width // GROUP
    seqs = rows // SEQ
    shards = chunks + groups + 1
    everyone = shards + chunks
    wired = n_dp * BLOCK == width and n_dp == 4 * chunks
    half = width // 2
    extra = KEYS - SLOT
    anywhere = pl.BlockSpec(memory_space=pl.ANY)
    vmem = pl.BlockSpec(memory_space=pltpu.VMEM)
    smem = pl.BlockSpec(memory_space=pltpu.SMEM)
    wide = lambda *shape: pltpu.VMEM(shape, F32)
    slim = lambda *shape: pltpu.VMEM(shape, BF16)
    flags = lambda *shape: pltpu.SemaphoreType.DMA(shape)
    low = lambda *shape: jax.ShapeDtypeStruct(shape, BF16)
    full = lambda *shape: jax.ShapeDtypeStruct(shape, F32)
    small_shape = (8, width + GROUP)

    if wired:
        out_piece = low(2, shards + 4, BLOCK, half)
        flights = 6 * (shards + 3) + 3 * chunks + 3 + 5
        others = [
            slim(SLOTS, 2, 16, BLOCK, half), slim(RING, 16, BLOCK, half),
            slim(everyone, 8, BLOCK, half), slim(everyone, 4, BLOCK, half),
            slim(shards, 2, BLOCK, half), slim(shards, 1, BLOCK, half), slim(4, 4, BLOCK, half),
            slim(2, 4, BLOCK, half), slim(1, 4, BLOCK, half), slim(2, shards + 4, BLOCK, half),
            wide(5, *small_shape), flags(flights), flags(flights),
        ]
        settings = dict(collective_id=0, has_side_effects=True)
    else:
        out_piece = low(everyone, width, width)
        others = [slim(2, width, width), flags(2)]
        settings = {}
    output, grad_tokens, pieces, small = pl.pallas_call(
        functools.partial(layer_kernel, wired),
        out_shape=(low(rows, width), low(rows, width), out_piece, full(*small_shape)),
        in_specs=[
            smem, anywhere, anywhere, vmem, anywhere, vmem, vmem, vmem, anywhere, vmem, anywhere,
            vmem, anywhere, vmem,
        ],
        out_specs=(anywhere,) * 4,
        scratch_shapes=[slim(6, width, width)]
        + [slim(rows, width)] * 9
        + [
            slim(width + 16, rows), slim(width, rows), wide(rows, width), wide(rows, width),
            slim(rows, GROUP), slim(rows + extra, GROUP), slim(rows + extra, GROUP),
            slim(rows, GROUP),
        ]
        + [wide(rows, GROUP)] * 3
        + [wide(*small_shape), flags(5 + 2 * chunks + 3 * groups), flags(2 * seqs + 2)]
        + others,
        compiler_params=pltpu.CompilerParams(vmem_limit_bytes=62 << 20, **settings),
    )(
        lengths, tokens, cotangent, ln_gain, w_qkv, b_qkv, q_gain, k_gain, w_o, b_o, w_in, b_in,
        w_out, b_out,
    )

    if wired:
        return pl.pallas_call(
            finish_kernel,
            out_shape=(
                low(rows, width), low(rows, width), full(width), full(BLOCK, 3 * width),
                full(3 * width), full(HEAD), full(HEAD), full(BLOCK, width), full(width),
                full(BLOCK, hidden_width), full(hidden_width), full(4 * BLOCK, width), full(width),
            ),
            in_specs=[anywhere] * 4,
            out_specs=(
                anywhere, anywhere, vmem, anywhere, vmem, vmem, vmem, anywhere, vmem, anywhere, vmem,
                anywhere, vmem,
            ),
            scratch_shapes=[
                slim(2, rows, width), slim(2, shards + 4, BLOCK, half), wide(*small_shape),
                wide(BLOCK, 3 * width), wide(BLOCK, width), wide(BLOCK, hidden_width),
                wide(4 * BLOCK, width), flags(2, 6),
            ],
        )(output, grad_tokens, pieces, small)

    def scatter(block, dim):
        part = lax.psum_scatter(block, "dp", scatter_dimension=dim, tiled=True)
        return lax.psum(part, "branch").astype(F32)

    grad_out = scatter(pieces[shards:].reshape(hidden_width, width), 0)
    reduced = scatter(pieces[:shards], 1)
    grad_in = jnp.concatenate([reduced[f] for f in range(chunks)], axis=1)
    qkv = jnp.concatenate([reduced[chunks + hg] for hg in range(groups)], axis=1)
    small = lax.psum(small, ("dp", "branch"))
    ln, g_b_qkv, g_q, g_k, g_b_out, g_b_in = (
        part[0] for part in small_parts(small, chunks, groups, width)
    )
    return (
        output, grad_tokens, ln, split_lanes(qkv, groups), g_b_qkv, g_q, g_k,
        reduced[chunks + groups], g_b_out, grad_in, g_b_in, grad_out, g_b_out,
    )


def solution(mesh):
    rows, split, whole = P(("dp", "branch"), None), P("dp", None), P()
    return jax.shard_map(
        functools.partial(local, mesh.shape["dp"]),
        mesh=mesh,
        in_specs=(rows, split, rows) + (whole,) * 11,
        out_specs=(
            rows, rows, whole, split, whole, whole, whole, split, whole, split, whole, split, whole,
        ),
        check_vma=False,
    )
```

```python
import functools
import math

import jax
import jax.numpy as jnp
from jax import lax
from jax.experimental import pallas as pl
from jax.experimental.pallas import tpu as pltpu
from jax.sharding import PartitionSpec as P

HEAD = 64
SEQ = 448
IMAGES = 4
SLOT = SEQ // IMAGES
LEAST = 32
KEYS = 128
GROUP = 256
EPS = 1e-06
SCALE = 0.125
F32 = jnp.float32
BF16 = jnp.bfloat16
GELU_A = math.sqrt(2.0 / math.pi)
GELU_B = 0.044715


def dot(left, right, left_dim=1, right_dim=0):
    return lax.dot_general(
        left, right, (((left_dim,), (right_dim,)), ((), ())), preferred_element_type=F32
    )


def slot_positions(lens):
    row = lax.broadcasted_iota(jnp.int32, (SEQ, 1), 0)
    held = jnp.full((SEQ, 1), -1, jnp.int32)
    start = jnp.int32(0)
    for image in range(IMAGES):
        place = row - SLOT * image
        held = jnp.where((place >= 0) & (place < lens[image]), place + start, held)
        start = start + lens[image]
    return held


def position_slots(lens):
    row = lax.broadcasted_iota(jnp.int32, (SEQ, 1), 0)
    held = jnp.full((SEQ, 1), -1, jnp.int32)
    start = jnp.int32(0)
    for image in range(IMAGES):
        place = row - start
        held = jnp.where((place >= 0) & (place < lens[image]), place + SLOT * image, held)
        start = start + lens[image]
    return held


def one_hot(index, first=0, size=SEQ):
    lanes = lax.broadcasted_iota(jnp.int32, (index.shape[0], size), 1) + first
    return jnp.where(lanes == index, 1.0, 0.0).astype(BF16)


def pick_rows(held, block):
    parts = []
    for image in range(0, IMAGES, 2):
        first, end = LEAST * image, SLOT * (image + 2)
        pick = one_hot(held[SLOT * image : end], first, end - first)
        parts.append(dot(pick, block[first:end]))
    return jnp.concatenate(parts, axis=0)


def row_stats(values):
    centered = values - jnp.mean(values, axis=1, keepdims=True)
    spread = jnp.mean(centered * centered, axis=1, keepdims=True)
    inverse = lax.rsqrt(spread + EPS)
    return centered * inverse, inverse


def gelu_pair(pre, grad):
    square = pre * pre
    up = 0.5 * jnp.tanh(pre * (GELU_A + (GELU_A * GELU_B) * square)) + 0.5
    hidden = pre * up
    slope = 2.0 * GELU_A + (6.0 * GELU_A * GELU_B) * square
    return hidden, (up + (hidden * (1.0 - up)) * slope) * grad


MESH = pl.DeviceIdType.MESH
BLOCK = 48
SLOTS = 2
RING = 8
XY, YX = ("x", "y", "z0", "z1"), ("y", "x", "z0", "z1")
ZX, ZY = ("z0", "z1", "x", "y"), ("z0", "z1", "y", "x")
RATES = {"core": 400e3, "x": 42e3, "y": 42e3, "z0": 42e3, "z1": 21e3}
LATENCY = 2.0


class Piece:
    def __init__(self, index, shard, axes, lanes):
        self.index, self.shard, self.axes, self.lanes = index, shard, axes, lanes
        self.stage, self.copy, self.eta = 0, None, 0.0

    def cut(self, ref):
        return ref.at[:, :, self.lanes]


class Small:
    def __init__(self):
        self.stage, self.copy, self.eta = 0, None, 0.0


class Exchange:
    def __init__(self, refs, chunks):
        (self.both, self.inbox, self.in1, self.in2, self.in3, self.in4, self.osum, self.oin3,
         self.oin4, self.fin, self.small, self.small_in, self.send_sem, self.recv_sem) = refs
        self.chunks = chunks
        self.dp, self.core = lax.axis_index("dp"), lax.axis_index("branch")
        self.bits = {
            "x": lax.rem(self.dp, 2),
            "y": lax.rem(self.dp // 2, 2),
            "z0": lax.rem(self.dp // 4, 2),
            "z1": lax.rem(self.dp // 8, 2),
        }
        self.far = {
            axis: (self.dp + step - 2 * step * self.bits[axis], self.core)
            for axis, step in (("x", 1), ("y", 2), ("z0", 4), ("z1", 8))
        }
        self.far["core"] = (self.dp, 1 - self.core)
        self.items, self.opened = [], 0
        self.flights, self.merged, self.now, self.free = 0, 0, 0.0, {}

    def greet(self):
        barrier = pltpu.get_barrier_semaphore()
        for device in self.far.values():
            pl.semaphore_signal(barrier, inc=1, device_id=device, device_id_type=MESH)
        pl.semaphore_wait(barrier, len(self.far))

    def send(self, item, source, target, axis):
        copy = pltpu.make_async_remote_copy(
            src_ref=source, dst_ref=target, send_sem=self.send_sem.at[self.flights],
            recv_sem=self.recv_sem.at[self.flights], device_id=self.far[axis], device_id_type=MESH,
        )
        self.flights += 1
        copy.start()
        link = axis[0]
        size = source.dtype.itemsize * math.prod(source.shape)
        self.free[link] = max(self.free.get(link, 0.0), self.now) + size / RATES[axis]
        item.copy, item.eta = copy, self.free[link] + LATENCY

    def open(self):
        index = self.opened
        for behind, stage in ((SLOTS, 1), (RING - SLOTS, 2)):
            while any(
                item.index == index - behind and item.stage < stage
                for item in self.items
                if isinstance(item, Piece)
            ):
                self.advance(min(self.under_way(), key=lambda item: item.eta))
        self.opened += 1
        return index

    def put(self, index, value, lane, axes):
        half = value.shape[1] // 2
        for side, role in ((0, self.core), (1, 1 - self.core)):
            target = self.both.at[index % SLOTS, role, :, :, pl.ds(lane, half)]
            put_blocks(value, target, side, axes)

    def start(self, index, shard, axes, lane, width):
        piece = Piece(index, shard, axes, pl.ds(lane, width))
        self.send(
            piece, piece.cut(self.both.at[index % SLOTS, 1]), piece.cut(self.inbox.at[index % RING]),
            "core",
        )
        self.items.append(piece)

    def halve(self, piece, held, held_at, arrived, count, axis, target):
        near = self.bits[axis] * count
        away = (1 - self.bits[axis]) * count
        span = pl.ds(away, count)
        arrived[span] = arrived[span] + held[pl.ds(held_at + away, count)]
        self.send(piece, arrived.at[span], target, axis)
        span = pl.ds(near, count)
        arrived[span] = arrived[span] + held[pl.ds(held_at + near, count)]

    def advance(self, piece):
        piece.copy.wait()
        self.now = max(self.now, piece.eta)
        piece.copy = None
        if isinstance(piece, Small):
            self.advance_small(piece)
            return
        k, shard, axes, cut = piece.index, piece.shard, piece.axes, piece.cut
        whole = isinstance(shard, int)
        in0, in1, in2 = cut(self.inbox.at[k % RING]), cut(self.in1.at[k]), cut(self.in2.at[k])
        if whole:
            in3, in4 = cut(self.in3.at[shard]), cut(self.in4.at[shard])
        if piece.stage == 0:
            self.halve(piece, cut(self.both.at[k % SLOTS, 0]), 0, in0, 8, axes[0], in1)
        elif piece.stage == 1:
            self.halve(piece, in0, self.bits[axes[0]] * 8, in1, 4, axes[1], in2)
        elif piece.stage == 2 and whole:
            self.halve(piece, in1, self.bits[axes[1]] * 4, in2, 2, axes[2], in3)
        elif piece.stage == 2:
            place = shard[0] % 2 * 2 + shard[0] // 2
            self.osum[place] = in2[...] + in1[pl.ds(self.bits[axes[1]] * 4, 4)]
            self.merged += 1
            if self.merged < self.chunks:
                piece.stage = 5
            else:
                far = pl.ds((1 - self.bits["z0"]) * 2, 2)
                self.send(piece, self.osum.at[far], self.oin3, "z0")
        elif piece.stage == 3 and whole:
            self.halve(piece, in2, self.bits[axes[2]] * 2, in3, 1, axes[3], in4)
        elif piece.stage == 3:
            self.halve(piece, self.osum, self.bits["z0"] * 2, self.oin3, 1, "z1", self.oin4)
        elif piece.stage == 4:
            if whole:
                final = self.fin.at[self.core, pl.ds(shard, 1), :, piece.lanes]
                final[...] = in4[...] + in3[pl.ds(self.bits[axes[3]], 1)]
            else:
                final = self.fin.at[self.core, pl.ds(self.fin.shape[1] - 4, 4)]
                final[...] = self.oin4[0] + self.oin3[self.bits["z1"]]
            self.send(piece, final, final, "core")
        piece.stage += 1

    def start_small(self):
        item = Small()
        self.send(item, self.small, self.small_in.at[0], "core")
        self.items.append(item)

    def advance_small(self, item):
        self.small[...] = self.small[...] + self.small_in[item.stage]
        item.stage += 1
        if item.stage < 5:
            axis = ("core", "x", "y", "z0", "z1")[item.stage]
            self.send(item, self.small, self.small_in.at[item.stage], axis)

    def under_way(self):
        return [item for item in self.items if item.copy is not None]

    def progress(self, cost):
        self.now += cost
        while True:
            due = [item for item in self.under_way() if item.eta <= self.now]
            if not due:
                return
            self.advance(min(due, key=lambda item: item.eta))

    def drain(self):
        while self.under_way():
            self.advance(min(self.under_way(), key=lambda item: item.eta))


def put_blocks(value, target, side, axes):
    half = value.shape[1] // 2
    for block in range(16):
        place = block
        if axes is not None and len(axes) == 4:
            bit = dict(x=block % 2, y=block // 2 % 2, z0=block // 4 % 2, z1=block // 8)
            place = sum(bit[axis] << (3 - i) for i, axis in enumerate(axes))
        target[place] = value[
            BLOCK * block : BLOCK * (block + 1), half * side : half * (side + 1)
        ].astype(BF16)


def make_flip():
    eye = jnp.where(
        lax.broadcasted_iota(jnp.int32, (GROUP, GROUP), 0)
        == lax.broadcasted_iota(jnp.int32, (GROUP, GROUP), 1),
        1.0,
        0.0,
    ).astype(BF16)

    def flip(source, target):
        for part in range(source.shape[1] // GROUP):
            lanes = pl.ds(part * GROUP, GROUP)
            target[lanes, :] = dot(eye, source[:, lanes], 1, 1).astype(BF16)

    return flip


class Parking:
    def __init__(self, stage, target, sem):
        self.stage, self.target, self.sem = stage, target, sem
        self.sent = []

    def put(self, value, index):
        slot = len(self.sent) % 2
        if len(self.sent) >= 2:
            self.sent[-2].wait()
        self.stage[slot] = value.astype(BF16)
        copy = pltpu.make_async_copy(self.stage.at[slot], self.target.at[index], self.sem.at[slot])
        copy.start()
        self.sent.append(copy)

    def finish(self):
        for copy in self.sent[-2:]:
            copy.wait()


def layer_kernel(
    wired,
    lengths_ref, tokens_hbm, cot_hbm, ln_gain_ref, w_qkv_hbm, b_qkv_ref, q_gain_ref, k_gain_ref,
    w_o_hbm, b_o_ref, w_in_hbm, b_in_ref, w_out_hbm, b_out_ref,
    output_hbm, grad_tokens_hbm, pieces_hbm, small_hbm,
    weights, tok, cot, packed, grow, normed, hid_even, gpre_even, hid_odd, gpre_odd,
    flipped, turned, fed, gnorm, qs, ks, vs, gm, rk, dq, dk, small_ref,
    load_sem, done_sem, *refs,
):
    rows, width = tok.shape
    hidden_width = w_in_hbm.shape[1]
    chunks = hidden_width // width
    groups = width // GROUP
    seqs = rows // SEQ
    images = seqs * IMAGES
    base = lax.axis_index("branch") * seqs
    assert chunks == 4 and groups == 3
    hid, gpre = (hid_even, hid_odd), (gpre_even, gpre_odd)
    mixed, gprojs = tok, (hid_even, gpre_even, cot)
    w_in = [weights.at[f % 3] for f in range(chunks)]
    w_out = [weights.at[3 + f % 3] for f in range(chunks)]
    w_qkv, w_o = [weights.at[1], weights.at[4], weights.at[2]], weights.at[5]
    nq, rq, nk = (fed.at[:, pl.ds(part * GROUP, GROUP)] for part in range(3))
    loads = {}

    def load(name, source, target):
        copy = pltpu.make_async_copy(source, target, load_sem.at[len(loads)])
        copy.start()
        loads[name] = copy

    def load_chunk(f):
        cols = pl.ds(f * width, width)
        load(("in", f), w_in_hbm.at[:, cols], w_in[f])
        load(("out", f), w_out_hbm.at[cols, :], w_out[f])

    def load_qkv(hg):
        for t in range(3):
            load(
                ("qkv", hg, t),
                w_qkv_hbm.at[:, pl.ds(t * width + hg * GROUP, GROUP)],
                w_qkv[hg].at[:, pl.ds(t * GROUP, GROUP)],
            )

    load("tok", tokens_hbm, tok)
    load("cot", cot_hbm, cot)
    for f in range(3):
        load_chunk(f)
    small_ref[...] = jnp.zeros_like(small_ref)
    net, parking = None, None
    if wired:
        net = Exchange(refs[:10] + (small_ref,) + refs[10:], chunks)
        net.greet()
    else:
        parking = Parking(refs[0], pieces_hbm, refs[1])

    def emit(value, shard, axes):
        if wired:
            index = net.open()
            net.put(index, value, 0, axes)
            net.start(index, shard, axes, 0, width // 2)
        else:
            parking.put(value, shard if isinstance(shard, int) else chunks + groups + 1 + shard[0])

    def point(cost):
        if wired:
            net.progress(cost)

    def cost(amount):
        if wired:
            net.now += amount

    def lanes_of(part):
        return pl.ds(part * GROUP, GROUP)

    ones_row = jnp.where(lax.broadcasted_iota(jnp.int32, (16, rows), 0) == 0, 1.0, 0.0)
    flipped[pl.ds(width, 16), :] = ones_row.astype(BF16)
    eye = jnp.where(
        lax.broadcasted_iota(jnp.int32, (GROUP, GROUP), 0)
        == lax.broadcasted_iota(jnp.int32, (GROUP, GROUP), 1),
        1.0,
        0.0,
    ).astype(BF16)

    def flip(source, target, part):
        target[lanes_of(part), :] = dot(eye, source[:, lanes_of(part)], 1, 1).astype(BF16)

    for name in ("tok", "cot", ("in", 0), ("out", 0)):
        loads[name].wait()
    grad_sum = jnp.zeros((1, width), F32)
    for s in range(seqs):
        span = pl.ds(s * SEQ, SEQ)
        held = slot_positions([lengths_ref[base + s, j] for j in range(IMAGES)])
        rows_here = pick_rows(held, tok[span, :])
        packed[span, :] = rows_here.astype(BF16)
        unit, _ = row_stats(rows_here)
        normed[span, :] = (unit * ln_gain_ref[...].reshape(1, width)).astype(BF16)
        grads_here = pick_rows(held, cot[span, :])
        grow[span, :] = grads_here.astype(BF16)
        grad_sum = grad_sum + jnp.sum(grads_here, axis=0, keepdims=True)
    small_ref[pl.ds(7, 1), pl.ds(0, width)] = grad_sum
    for part in range(groups):
        flip(normed, flipped, part)
    cost(6.0)

    def add_fed(f):
        for part in range(groups):
            lanes = lanes_of(part)
            up = dot(hid[f % 2][...], w_out[f][:, lanes])
            fed[:, lanes] = up if f == 0 else fed[:, lanes] + up

    def add_gnorm(source, target, first):
        for part in range(groups):
            lanes = lanes_of(part)
            down = dot(source[...], target[lanes, :], 1, 1)
            gnorm[:, lanes] = down if first else gnorm[:, lanes] + down

    b_in = b_in_ref[...].reshape(1, hidden_width)
    ready = None

    def activate():
        f, c, pre, back = ready
        hidden, grad_pre = gelu_pair(pre, back)
        hid[f % 2][:, lanes_of(c)] = hidden.astype(BF16)
        gpre[f % 2][:, lanes_of(c)] = grad_pre.astype(BF16)

    def send_w_in(f):
        sums = dot(flipped[...], gpre[f % 2][...])
        cost(2.2)
        emit(sums[:width], f, (XY, ZX, XY, ZY)[f])
        small_ref[pl.ds(f, 1), pl.ds(0, width)] = sums[width : width + 1]
        point(0.0)

    def send_w_out(f):
        cost(1.9)
        emit(dot(turned[...], grow[...]), (f,), YX[:2])
        point(0.0)

    for f in range(chunks):
        if f > 0:
            loads["in", f].wait()
            loads["out", f].wait()
        for c in range(groups):
            place = f * width + c * GROUP
            lanes = lanes_of(c)
            pre = dot(normed[...], w_in[f][:, lanes]) + b_in[:, place : place + GROUP]
            back = dot(grow[...], w_out[f][lanes, :], 1, 1)
            if ready is not None:
                activate()
            ready = (f, c, pre, back)
            if f > 0 and c == 0:
                for part in range(groups):
                    flip(hid[1 - f % 2], turned, part)
            if f > 0 and c == 2:
                add_fed(f - 1)
                add_gnorm(gpre[1 - f % 2], w_in[f - 1], f == 1)
            point((1.7, 1.2, 4.6)[c] if f > 0 else 1.2)
            if f > 0 and c == 0:
                send_w_in(f - 1)
            if f > 0 and c == 1:
                send_w_out(f - 1)
        if f == 1:
            load_chunk(3)
        if f == 2:
            load_qkv(0)
            load_qkv(1)
        if f == 3:
            load_qkv(2)
            load("wo", w_o_hbm, w_o)
    activate()
    for part in range(groups):
        flip(hid_odd, turned, part)
    send_w_in(chunks - 1)
    send_w_out(chunks - 1)

    add_fed(chunks - 1)
    hid_odd[...] = (fed[...] + b_out_ref[...].reshape(1, width)).astype(BF16)
    point(1.9)

    same_head = (
        lax.broadcasted_iota(jnp.int32, (GROUP, GROUP), 0) // HEAD
        == lax.broadcasted_iota(jnp.int32, (GROUP, GROUP), 1) // HEAD
    )
    average = jnp.where(same_head, 1.0 / HEAD, 0.0).astype(BF16)
    average_twice = jnp.concatenate([average, average], axis=0)
    q_gain = SCALE * jnp.concatenate([q_gain_ref[...].reshape(1, HEAD)] * (GROUP // HEAD), axis=1)
    k_gain = jnp.concatenate([k_gain_ref[...].reshape(1, HEAD)] * (GROUP // HEAD), axis=1)
    b_qkv = b_qkv_ref[...].reshape(1, 3 * width)
    lane = lax.broadcasted_iota(jnp.int32, (1, KEYS), 1)
    pair_lane = jnp.concatenate([lane, lane], axis=1)
    first_head = jnp.where(lane < HEAD, 1.0, 0.0).astype(BF16)
    second_head = jnp.where(lane < HEAD, 0.0, 1.0).astype(BF16)

    def head_mean(values, split):
        high = values.astype(BF16)
        if not split:
            return dot(high, average)
        rest = (values - high.astype(F32)).astype(BF16)
        return dot(jnp.concatenate([high, rest], axis=1), average_twice)

    def head_norm(raw):
        centered = raw - head_mean(raw, True)
        inverse = lax.rsqrt(head_mean(centered * centered, False) + EPS)
        return centered * inverse, inverse

    def two_heads(block):
        return jnp.concatenate([block * first_head, block * second_head], axis=0)

    def stacked(block):
        return jnp.concatenate([block[:, :KEYS], block[:, KEYS:]], axis=0)

    def invert(total):
        guess = pl.reciprocal(total, approx=True)
        return guess * (2.0 - total * guess)

    def over_heads(block, change):
        parts = []
        for head in range(2):
            part = block[:, head * KEYS : (head + 1) * KEYS]
            total = change(jnp.sum(part, axis=1, keepdims=True))
            parts.append(jnp.broadcast_to(total, part.shape))
        return jnp.concatenate(parts, axis=1)

    ks[pl.ds(rows, KEYS - SLOT), :] = jnp.zeros((KEYS - SLOT, GROUP), BF16)
    vs[pl.ds(rows, KEYS - SLOT), :] = jnp.zeros((KEYS - SLOT, GROUP), BF16)

    for hg in range(groups):
        gproj = gprojs[hg]
        bias_q, bias_k, bias_v = (
            b_qkv[:, t * width + hg * GROUP : t * width + (hg + 1) * GROUP] for t in range(3)
        )
        for t in range(3):
            loads["qkv", hg, t].wait()
        if hg == 0:
            loads["wo"].wait()
        raw = dot(normed[...], w_qkv[hg][:, lanes_of(0)]) + bias_q
        unit, inverse = head_norm(raw)
        nq[...] = unit
        rq[...] = inverse
        qs[...] = (unit * q_gain).astype(BF16)
        raw = dot(normed[...], w_qkv[hg][:, lanes_of(1)]) + bias_k
        unit, inverse = head_norm(raw)
        nk[...] = unit
        rk[...] = inverse
        ks[pl.ds(0, rows), :] = (unit * k_gain).astype(BF16)
        raw = dot(normed[...], w_qkv[hg][:, lanes_of(2)]) + bias_v
        vs[pl.ds(0, rows), :] = raw.astype(BF16)
        gm[...] = dot(grow[...], w_o[lanes_of(hg), :], 1, 1).astype(BF16)
        point(4.5)

        def one_image(image):
            start = image * SLOT
            span = pl.ds(start, SLOT)
            window = pl.ds(start, KEYS)
            seen = pair_lane < lengths_ref[base + image // IMAGES, image % IMAGES]
            for pair in range(GROUP // KEYS):
                lanes = pl.ds(pair * KEYS, KEYS)
                query, grad = qs[span, lanes], gm[span, lanes]
                keys, values = two_heads(ks[window, lanes]), two_heads(vs[window, lanes])
                weight = jnp.where(seen, jnp.exp(dot(query, keys, 1, 1)), 0.0)
                probs = weight * over_heads(weight, invert)
                grad_probs = dot(grad, values, 1, 1)
                inner = over_heads(probs * grad_probs, lambda total: total)
                grad_scores = (probs * (grad_probs - inner)).astype(BF16)
                probs_low = probs.astype(BF16)
                mixed[span, pl.ds(hg * GROUP + pair * KEYS, KEYS)] = dot(probs_low, values).astype(
                    BF16
                )
                dq[span, lanes] = dot(grad_scores, keys)
                dk[span, lanes] = dot(stacked(grad_scores), two_heads(query), 0, 0)[:SLOT]
                gproj[span, pl.ds(2 * GROUP + pair * KEYS, KEYS)] = dot(
                    stacked(probs_low), two_heads(grad), 0, 0
                )[:SLOT].astype(BF16)

        for image in range(images):
            one_image(image)
            if image % 4 == 3:
                point(2.6)
        if hg == groups - 1:
            for part in range(groups):
                flip(mixed, turned, part)
            if wired:
                index = net.open()
                for lane, size, part_axes in ((0, KEYS, XY), (KEYS, 2 * KEYS, YX)):
                    sums = dot(turned[...], grow[:, pl.ds(2 * lane, 2 * size)])
                    net.put(index, sums, lane, part_axes)
                    cost(1.1)
                    net.start(index, chunks + groups, part_axes, lane, size)
                point(0.0)
            else:
                parking.put(dot(turned[...], grow[...]), chunks + groups)

        axes = (XY, YX, YX)[hg]
        last = hg == groups - 1
        index = net.open() if wired else None
        parts = {}

        def part_grad(t, part_axes):
            sums = dot(flipped[...], gproj[:, lanes_of(t)])
            small_ref[pl.ds(4 + hg, 1), lanes_of(t)] = sums[width : width + 1]
            if wired:
                net.put(index, sums[:width], t * KEYS, part_axes)
                if last:
                    net.start(index, chunks + hg, part_axes, t * KEYS, KEYS)
            else:
                parts[t] = sums[:width]

        def norm_back(side, grad_ref, unit_ref, inverse_ref, gain):
            grad, unit = grad_ref[...], unit_ref[...]
            gain_sum = jnp.sum(grad * unit, axis=0, keepdims=True)
            small_ref[pl.ds(3 + side, 1), pl.ds(width, GROUP)] += gain_sum * (SCALE, 1.0)[side]
            grad = grad * gain
            back = grad - head_mean(grad, False) - unit * head_mean(grad * unit, False)
            gproj[:, lanes_of(side)] = (back * inverse_ref[...]).astype(BF16)

        cost(0.7)
        part_grad(2, ZX if last else axes)
        norm_back(0, dq, nq, rq, q_gain)
        cost(1.5)
        if last:
            point(0.0)
        part_grad(0, XY if last else axes)
        norm_back(1, dk, nk, rk, k_gain)
        cost(1.5)
        if last:
            point(0.0)
        part_grad(1, YX if last else axes)
        if not wired:
            parking.put(jnp.concatenate([parts[t] for t in range(3)], axis=1), chunks + hg)
        elif not last:
            net.start(index, chunks + hg, axes, 0, width // 2)
        point(0.0)

    add_gnorm(gpre_odd, w_in[chunks - 1], False)
    point(1.7)
    for hg in range(groups):
        add_gnorm(gprojs[hg], w_qkv[hg], False)
        if hg == 0:
            load("tok again", tokens_hbm, hid_even)
        if hg == 1:
            load("cot again", cot_hbm, gpre_even)
        point(1.7)
    ln_gain = ln_gain_ref[...].reshape(1, width)
    b_o = b_o_ref[...].reshape(1, width)
    gain_grad = jnp.zeros((1, width), F32)
    for s in range(seqs):
        span = pl.ds(s * SEQ, SEQ)
        unit, inverse = row_stats(packed[span, :].astype(F32))
        grad = gnorm[span, :]
        gain_grad = gain_grad + jnp.sum(grad * unit, axis=0, keepdims=True)
        grad = grad * ln_gain
        back = grad - jnp.mean(grad, axis=1, keepdims=True)
        back = (back - unit * jnp.mean(grad * unit, axis=1, keepdims=True)) * inverse
        normed[span, :] = (grow[span, :].astype(F32) + back).astype(BF16)
    for t in range(width // GROUP):
        small_ref[pl.ds(t, 1), pl.ds(width, GROUP)] = gain_grad[:, t * GROUP : (t + 1) * GROUP]
    if wired:
        net.start_small()
    point(1.5)
    finals = []
    loads["tok again"].wait()
    loads["cot again"].wait()

    def hand_over(source, target):
        copy = pltpu.make_async_copy(source, target, done_sem.at[len(finals)])
        copy.start()
        finals.append(copy)

    for s in range(seqs):
        span = pl.ds(s * SEQ, SEQ)
        place = position_slots([lengths_ref[base + s, j] for j in range(IMAGES)])
        put = one_hot(place)
        padding = jnp.where(place < 0, 1.0, 0.0)
        attended = (dot(mixed[span, :], w_o[...]) + b_o).astype(BF16).astype(F32)
        result = packed[span, :].astype(F32) + (attended + hid_odd[span, :].astype(F32))
        result = dot(put, result.astype(BF16)) + padding * hid_even[span, :].astype(F32)
        hid_even[span, :] = result.astype(BF16)
        hand_over(hid_even.at[span], output_hbm.at[span])
        point(1.2)
        grads = dot(put, normed[span, :]) + padding * gpre_even[span, :].astype(F32)
        gpre_even[span, :] = grads.astype(BF16)
        hand_over(gpre_even.at[span], grad_tokens_hbm.at[span])
        point(0.8)
    if wired:
        net.drain()
        hand_over(net.fin, pieces_hbm)
    else:
        parking.finish()
    hand_over(small_ref, small_hbm)
    for copy in finals:
        copy.wait()


def split_lanes(block, groups):
    width = block.shape[1] // 3
    return jnp.concatenate(
        [
            block[:, hg * width + t * GROUP : hg * width + (t + 1) * GROUP]
            for t in range(3)
            for hg in range(groups)
        ],
        axis=1,
    )


def fold_heads(gains):
    return sum(gains[:, h * HEAD : (h + 1) * HEAD] for h in range(GROUP // HEAD))


def small_parts(small, chunks, groups, width):
    b_in = jnp.concatenate([small[f : f + 1, :width] for f in range(chunks)], axis=1)
    b_qkv = jnp.concatenate([small[4 + hg : 5 + hg, :width] for hg in range(groups)], axis=1)
    ln = jnp.concatenate([small[t : t + 1, width:] for t in range(width // GROUP)], axis=1)
    gains = [fold_heads(small[3 + side : 4 + side, width:]) for side in range(2)]
    return ln, split_lanes(b_qkv, groups), gains[0], gains[1], small[7:8, :width], b_in


def finish_kernel(
    rows_hbm, grads_hbm, fin_hbm, small_hbm, output_hbm, grad_tokens_hbm, g_ln, g_qkv_hbm, g_b_qkv,
    g_q, g_k, g_o_hbm, g_b_o, g_in_hbm, g_b_in, g_out_hbm, g_b_out, held, fin, small, g_qkv, g_o, g_in,
    g_out, sem,
):
    comes = [
        pltpu.make_async_copy(source, target, sem.at[0, i])
        for i, (source, target) in enumerate(
            ((fin_hbm, fin), (small_hbm, small), (rows_hbm, held.at[0]), (grads_hbm, held.at[1]))
        )
    ]
    goes = [
        pltpu.make_async_copy(source, target, sem.at[1, i])
        for i, (source, target) in enumerate(
            (
                (held.at[0], output_hbm), (held.at[1], grad_tokens_hbm), (g_in, g_in_hbm),
                (g_qkv, g_qkv_hbm), (g_out, g_out_hbm), (g_o, g_o_hbm),
            )
        )
    ]
    for copy in comes:
        copy.start()
    width = g_o.shape[1]
    chunks, groups = g_in.shape[1] // width, width // GROUP

    def whole(shard, lane, size):
        return jnp.concatenate(
            [fin[side, shard, :, lane : lane + size].astype(F32) for side in range(2)], axis=1
        )

    comes[0].wait()
    for f in range(chunks):
        g_in[:, f * width : (f + 1) * width] = whole(f, 0, width // 2)
    goes[2].start()
    for hg in range(groups):
        for t in range(3):
            place = t * width + hg * GROUP
            g_qkv[:, place : place + GROUP] = whole(chunks + hg, t * KEYS, KEYS)
    goes[3].start()
    for i in range(2):
        comes[2 + i].wait()
        goes[i].start()
    for j in range(4):
        g_out[j * BLOCK : (j + 1) * BLOCK, :] = whole(chunks + groups + 1 + j, 0, width // 2)
    goes[4].start()
    g_o[:, :GROUP] = whole(chunks + groups, 0, KEYS)
    g_o[:, GROUP:] = whole(chunks + groups, KEYS, 2 * KEYS)
    goes[5].start()
    comes[1].wait()
    ln, b_qkv, q, k, b_out, b_in = small_parts(small[...], chunks, groups, width)
    for ref, value in (
        (g_ln, ln), (g_b_qkv, b_qkv), (g_q, q), (g_k, k), (g_b_o, b_out), (g_b_in, b_in), (g_b_out, b_out)
    ):
        ref[...] = value.reshape(value.shape[1])
    for copy in goes:
        copy.wait()


def local(n_dp, tokens, lengths, cotangent, ln_gain, w_qkv, b_qkv, q_gain, k_gain, w_o, b_o, w_in, b_in, w_out, b_out):
    rows, width = tokens.shape
    hidden_width = w_in.shape[1]
    chunks = hidden_width // width
    groups = width // GROUP
    seqs = rows // SEQ
    shards = chunks + groups + 1
    everyone = shards + chunks
    wired = n_dp * BLOCK == width and n_dp == 4 * chunks
    half = width // 2
    extra = KEYS - SLOT
    anywhere = pl.BlockSpec(memory_space=pl.ANY)
    vmem = pl.BlockSpec(memory_space=pltpu.VMEM)
    smem = pl.BlockSpec(memory_space=pltpu.SMEM)
    wide = lambda *shape: pltpu.VMEM(shape, F32)
    slim = lambda *shape: pltpu.VMEM(shape, BF16)
    flags = lambda *shape: pltpu.SemaphoreType.DMA(shape)
    low = lambda *shape: jax.ShapeDtypeStruct(shape, BF16)
    full = lambda *shape: jax.ShapeDtypeStruct(shape, F32)
    small_shape = (8, width + GROUP)

    if wired:
        out_piece = low(2, shards + 4, BLOCK, half)
        flights = 6 * (shards + 3) + 3 * chunks + 3 + 5
        others = [
            slim(SLOTS, 2, 16, BLOCK, half), slim(RING, 16, BLOCK, half),
            slim(everyone, 8, BLOCK, half), slim(everyone, 4, BLOCK, half),
            slim(shards, 2, BLOCK, half), slim(shards, 1, BLOCK, half), slim(4, 4, BLOCK, half),
            slim(2, 4, BLOCK, half), slim(1, 4, BLOCK, half), slim(2, shards + 4, BLOCK, half),
            wide(5, *small_shape), flags(flights), flags(flights),
        ]
        settings = dict(collective_id=0, has_side_effects=True)
    else:
        out_piece = low(everyone, width, width)
        others = [slim(2, width, width), flags(2)]
        settings = {}
    output, grad_tokens, pieces, small = pl.pallas_call(
        functools.partial(layer_kernel, wired),
        out_shape=(low(rows, width), low(rows, width), out_piece, full(*small_shape)),
        in_specs=[
            smem, anywhere, anywhere, vmem, anywhere, vmem, vmem, vmem, anywhere, vmem, anywhere,
            vmem, anywhere, vmem,
        ],
        out_specs=(anywhere,) * 4,
        scratch_shapes=[slim(6, width, width)]
        + [slim(rows, width)] * 9
        + [
            slim(width + 16, rows), slim(width, rows), wide(rows, width), wide(rows, width),
            slim(rows, GROUP), slim(rows + extra, GROUP), slim(rows + extra, GROUP),
            slim(rows, GROUP),
        ]
        + [wide(rows, GROUP)] * 3
        + [wide(*small_shape), flags(5 + 2 * chunks + 3 * groups), flags(2 * seqs + 2)]
        + others,
        compiler_params=pltpu.CompilerParams(vmem_limit_bytes=62 << 20, **settings),
    )(
        lengths, tokens, cotangent, ln_gain, w_qkv, b_qkv, q_gain, k_gain, w_o, b_o, w_in, b_in,
        w_out, b_out,
    )

    if wired:
        return pl.pallas_call(
            finish_kernel,
            out_shape=(
                low(rows, width), low(rows, width), full(width), full(BLOCK, 3 * width),
                full(3 * width), full(HEAD), full(HEAD), full(BLOCK, width), full(width),
                full(BLOCK, hidden_width), full(hidden_width), full(4 * BLOCK, width), full(width),
            ),
            in_specs=[anywhere] * 4,
            out_specs=(
                anywhere, anywhere, vmem, anywhere, vmem, vmem, vmem, anywhere, vmem, anywhere, vmem,
                anywhere, vmem,
            ),
            scratch_shapes=[
                slim(2, rows, width), slim(2, shards + 4, BLOCK, half), wide(*small_shape),
                wide(BLOCK, 3 * width), wide(BLOCK, width), wide(BLOCK, hidden_width),
                wide(4 * BLOCK, width), flags(2, 6),
            ],
        )(output, grad_tokens, pieces, small)

    def scatter(block, dim):
        part = lax.psum_scatter(block, "dp", scatter_dimension=dim, tiled=True)
        return lax.psum(part, "branch").astype(F32)

    grad_out = scatter(pieces[shards:].reshape(hidden_width, width), 0)
    reduced = scatter(pieces[:shards], 1)
    grad_in = jnp.concatenate([reduced[f] for f in range(chunks)], axis=1)
    qkv = jnp.concatenate([reduced[chunks + hg] for hg in range(groups)], axis=1)
    small = lax.psum(small, ("dp", "branch"))
    ln, g_b_qkv, g_q, g_k, g_b_out, g_b_in = (
        part[0] for part in small_parts(small, chunks, groups, width)
    )
    return (
        output, grad_tokens, ln, split_lanes(qkv, groups), g_b_qkv, g_q, g_k,
        reduced[chunks + groups], g_b_out, grad_in, g_b_in, grad_out, g_b_out,
    )


def solution(mesh):
    rows, split, whole = P(("dp", "branch"), None), P("dp", None), P()
    return jax.shard_map(
        functools.partial(local, mesh.shape["dp"]),
        mesh=mesh,
        in_specs=(rows, split, rows) + (whole,) * 11,
        out_specs=(
            rows, rows, whole, split, whole, whole, whole, split, whole, split, whole, split, whole,
        ),
        check_vma=False,
    )
```
